32 devices in a mesh: blk: 8 (over y, x, core), dp: 4 (over z).
Axes of the slice: x: 2, y: 2, z: 4, core: 2. Of those that a mesh axis runs over, the one named last changes fastest.
Arguments:
- inputs: bfloat16 [8, 1024, 768], P('dp', 'blk'), may hold values from -6 to 6
- lengths: int32 [8], P('dp'), may hold values from 64 to 1024, as said below
- prenorm: bfloat16 [768], P(('blk', 'dp')), may hold values from 0.099609375 to 1.8984375
- midnorm: bfloat16 [768], P(('blk', 'dp')), may hold values from 0.099609375 to 1.8984375
- query_proj: bfloat16 [768, 768], P(('blk', 'dp')), may hold values from -0.21875 to 0.21875
- key_proj: bfloat16 [768, 768], P(('blk', 'dp')), may hold values from -0.21875 to 0.21875
- value_proj: bfloat16 [768, 768], P(('blk', 'dp')), may hold values from -0.21875 to 0.21875
- output_proj: bfloat16 [768, 768], P(('blk', 'dp')), may hold values from -0.875 to 0.875
- premix: float32 [12, 12], replicated, may hold values from -1.75 to 1.75
- postmix: float32 [12, 12], replicated, may hold values from -1.75 to 1.75
- inner_proj: bfloat16 [768, 3072], P(('blk', 'dp')), may hold values from -0.21875 to 0.21875
- outer_proj: bfloat16 [3072, 768], P(('blk', 'dp')), may hold values from -0.109375 to 0.109375
- cotangent: bfloat16 [8, 1024, 768], P('dp', 'blk'), may hold values from -6 to 6
Outputs:
- outputs: bfloat16 [8, 1024, 768], P('dp', 'blk')
- grad_inputs: bfloat16 [8, 1024, 768], P('dp', 'blk')
- grad_prenorm: float32 [768], P(('blk', 'dp'))
- grad_midnorm: float32 [768], P(('blk', 'dp'))
- grad_query: float32 [768, 768], P(('blk', 'dp'))
- grad_key: float32 [768, 768], P(('blk', 'dp'))
- grad_value: float32 [768, 768], P(('blk', 'dp'))
- grad_output: float32 [768, 768], P(('blk', 'dp'))
- grad_premix: float32 [12, 12], replicated
- grad_postmix: float32 [12, 12], replicated
- grad_inner: float32 [768, 3072], P(('blk', 'dp'))
- grad_outer: float32 [3072, 768], P(('blk', 'dp'))
The draws below stay inside these ranges and needn't reach their ends.
Inputs may be any that keep to these rules, and one draw needn't show every extreme that they name: `lengths`: in each aligned group of 2 rows (the rows of one index of dp) one row, chosen by the seed, has length 1024; positions at or past a row's length are padding.
All inputs are finite; a program needn't handle non-finite values.
Results may differ from the reference program's by a relative error of at most 0.017.
Values may be sent and summed in bfloat16 or wider, within the bound.
No kernel may reach another device: no remote copies, remote signals or barrier semaphores. Data moves between devices by JAX's collectives and lax.ppermute only.
A program may use at most 128 MiB of HBM per device.

```python
import math
import jax
import jax.numpy as jnp
from jax import lax

D = 768
HEADS = 12
HEAD_DIM = 64
FF = 3072
ROWS_DEV = 2
LEN_MIN = 64
SEQ = 1024
ROWS = 8


def draw_lengths(key, part):
    key = jax.random.fold_in(key, 7)
    first_key, second_key, third_key = jax.random.split(key, 3)
    span = SEQ - LEN_MIN + 1
    sample_one = jax.random.randint(first_key, (ROWS,), 0, span)
    sample_two = jax.random.randint(second_key, (ROWS,), 0, 2 * span)
    drawn = LEN_MIN + jnp.minimum(sample_one, jnp.minimum(sample_two, span - 1))
    chosen = jax.random.randint(third_key, (ROWS // ROWS_DEV,), 0, ROWS_DEV)
    slots = jnp.arange(ROWS, dtype=jnp.int32)
    longest = slots % ROWS_DEV == jnp.repeat(chosen, ROWS_DEV)
    return jnp.where(longest, SEQ, drawn).astype(jnp.int32)


def shard_levels(own_key, dims, cuts, least, high):
    def one(dim, shards_of):
        steps = jax.random.uniform(jax.random.fold_in(jax.random.fold_in(own_key, 6), dim), (shards_of,), jnp.float32, least / len(cuts), high / len(cuts))
        return jnp.repeat(jnp.exp(steps), dims[dim] // shards_of).reshape((-1,) + (1,) * (len(dims) - dim - 1))

    level = one(*cuts[0])
    for cut in cuts[1:]:
        level = level * one(*cut)
    return level


def normal_values(stream_key, shape, scale, limit, cuts=(), kind=jnp.bfloat16):
    loudness = shard_levels(stream_key, shape, cuts, -0.22, 0.18) if cuts else 1.0
    values = jax.random.normal(stream_key, shape, jnp.float32) * scale * loudness
    return jnp.minimum(jnp.maximum(values, -limit), limit).astype(kind)


def setup_inputs(seed: int = 0) -> dict:
    key_list = jax.random.split(jax.random.key(seed), 14)
    inputs = normal_values(key_list[0], (ROWS, SEQ, D), 1.0, 6.0, ((0, 4), (1, 8)))
    lengths = draw_lengths(jax.random.fold_in(key_list[13], 71), 0)
    prenorm = jnp.clip(1.0 + 0.18 * jax.random.normal(key_list[2], (D,), jnp.float32), 0.099609375, 1.8984375).astype(jnp.bfloat16)
    midnorm = jnp.clip(1.0 + 0.18 * jax.random.normal(key_list[3], (D,), jnp.float32), 0.099609375, 1.8984375).astype(jnp.bfloat16)
    query_proj = normal_values(key_list[4], (D, D), D ** -0.5, 0.21875, ((0, 32),))
    key_proj = normal_values(key_list[5], (D, D), D ** -0.5, 0.21875, ((0, 32),))
    value_proj = normal_values(key_list[6], (D, D), D ** -0.5, 0.21875, ((0, 32),))
    output_proj = normal_values(key_list[7], (D, D), (D // 16) ** -0.5, 0.875, ((0, 32),))
    premix = normal_values(key_list[8], (HEADS, HEADS), HEADS ** -0.5, 1.75, (), jnp.float32)
    postmix = normal_values(key_list[9], (HEADS, HEADS), HEADS ** -0.5, 1.75, (), jnp.float32)
    inner_proj = normal_values(key_list[10], (D, FF), D ** -0.5, 0.21875, ((0, 32),))
    outer_proj = normal_values(key_list[11], (FF, D), FF ** -0.5, 0.109375, ((0, 32),))
    cotangent = normal_values(key_list[12], (ROWS, SEQ, D), 1.0, 6.0, ((0, 4), (1, 8)))
    return dict(inputs=inputs, lengths=lengths, prenorm=prenorm, midnorm=midnorm, query_proj=query_proj, key_proj=key_proj, value_proj=value_proj, output_proj=output_proj, premix=premix, postmix=postmix, inner_proj=inner_proj, outer_proj=outer_proj, cotangent=cotangent)


@jax.custom_vjp
def low(v):
    return lax.optimization_barrier(v.astype(jnp.bfloat16)).astype(jnp.float32)

@jax.custom_vjp
def low_back(v):
    return v

def low_keep(v):
    return (low(v), None)

def low_pass(kept, grad):
    return (grad,)

def back_keep(v):
    return (v, None)

def back_low(kept, grad):
    return (low(grad),)
low.defvjp(low_keep, low_pass)
low_back.defvjp(back_keep, back_low)
NEGATIVE = -1e+30
EPSILON = 1e-06
HIGH = lax.Precision.HIGHEST

def normalize(values, gain):
    return values * lax.rsqrt(lax.optimization_barrier(jnp.mean(values * values, axis=-1, keepdims=True)) + EPSILON) * gain

def attend_block(start, queries, keys, values, premix, postmix, length):
    block = min(512, SEQ)
    query_rows = lax.dynamic_slice_in_dim(queries, start, block, 0)
    query_pos = start + jnp.arange(block, dtype=jnp.int32)
    key_pos = jnp.arange(SEQ, dtype=jnp.int32)
    scores = low_back(jnp.einsum('ihd,jhd->hij', query_rows, keys, precision=HIGH) * 0.125)
    logits = jnp.einsum('gh,gij->hij', premix, scores, precision=HIGH)
    allowed = (key_pos[None, :] <= query_pos[:, None]) & (key_pos[None, :] < length)
    logits = jnp.where(allowed[None], logits, NEGATIVE)
    peak = lax.optimization_barrier(jnp.max(logits, axis=-1, keepdims=True))
    exponents = jnp.where(allowed[None], jnp.exp(logits - peak), 0.0)
    softmax_out = exponents / lax.optimization_barrier(jnp.sum(exponents, axis=-1, keepdims=True))
    mixed = low(jnp.einsum('hk,hij->kij', postmix, softmax_out, precision=HIGH))
    return jnp.einsum('kij,jkd->ikd', mixed, values, precision=HIGH)

def attend_row(queries, keys, values, premix, postmix, length):
    block = min(512, SEQ)
    starts = jnp.arange(SEQ // block, dtype=jnp.int32) * block
    checked = jax.checkpoint(attend_block)
    pieces = lax.map(lambda start: checked(start, queries, keys, values, premix, postmix, length), starts)
    return pieces.reshape(SEQ, HEADS, HEAD_DIM)

def forward(inputs, prenorm, midnorm, query_proj, key_proj, value_proj, output_proj, premix, postmix, inner_proj, outer_proj, row_lengths):
    groups = inputs.shape[0]
    normed = low(normalize(inputs, prenorm))

    def project(weight):
        made = jnp.einsum('rtd,de->rte', normed, weight, precision=HIGH)
        return low(low_back(made)).reshape(groups, SEQ, HEADS, HEAD_DIM)
    queries = project(query_proj)
    keys = project(key_proj)
    values = project(value_proj)
    attended = lax.map(lambda item: attend_row(item[0], item[1], item[2], premix, postmix, item[3]), (queries, keys, values, row_lengths))
    joined = low(low_back(attended.reshape(groups, SEQ, D)))
    attn_out = low_back(jnp.einsum('rtd,de->rte', joined, output_proj, precision=HIGH))
    middle = inputs + attn_out
    second = low(normalize(middle, midnorm))
    inner = low_back(jnp.einsum('rtd,df->rtf', second, inner_proj, precision=HIGH))
    hidden = low(jax.nn.gelu(inner, approximate=True))
    outer = jnp.einsum('rtf,fd->rtd', hidden, outer_proj, precision=HIGH)
    valid = (jnp.arange(SEQ, dtype=jnp.int32)[None, :] < row_lengths[:, None]).astype(jnp.float32)[..., None]
    return valid * (middle + outer)

def reference(inputs, lengths, prenorm, midnorm, query_proj, key_proj, value_proj, output_proj, premix, postmix, inner_proj, outer_proj, cotangent):
    weights_all = tuple((item.astype(jnp.float32) for item in (prenorm, midnorm, query_proj, key_proj, value_proj, output_proj, premix, postmix, inner_proj, outer_proj)))
    group = math.gcd(ROWS, max(1, 4096 // SEQ))
    number = ROWS // group
    inputs_grouped = inputs.astype(jnp.float32).reshape(number, group, SEQ, D)
    row_lengths = lengths.reshape(number, group)
    cotangents = cotangent.astype(jnp.float32).reshape(number, group, SEQ, D)

    def one_group(totals, item):
        group_inputs, group_lengths, group_cot = item
        layer_out, pullback = jax.vjp(lambda values, *weights: forward(values, *weights, group_lengths), group_inputs, *weights_all)
        grads = pullback(group_cot)
        totals = tuple((first + second for first, second in zip(totals, grads[1:])))
        return (totals, (layer_out, grads[0]))
    start_totals = tuple((jnp.zeros_like(item) for item in weights_all))
    totals, (layer_outs, input_grads) = lax.scan(one_group, start_totals, (inputs_grouped, row_lengths, cotangents))
    outputs = layer_outs.reshape(ROWS, SEQ, D).astype(jnp.bfloat16)
    grad_inputs = input_grads.reshape(ROWS, SEQ, D).astype(jnp.bfloat16)
    return (outputs, grad_inputs, totals[0], totals[1], totals[2], totals[3], totals[4], totals[5], totals[6], totals[7], totals[8], totals[9])
```

```python
import jax
import jax.numpy as jnp
from jax import lax
from jax.experimental import pallas as pl
from jax.experimental.pallas import tpu as pltpu
from jax.sharding import PartitionSpec as P

EPSILON = 1e-06
GROUP = 4
HEADS = 12
f32 = jnp.float32
bf16 = jnp.bfloat16
CH=256

def dot(a,b,ca=1,cb=0):
    return lax.dot_general(a,b,(((ca,),(cb,)),((),())),preferred_element_type=f32)

def masked(tile, chunk, qb, width, fill):
    rows,lanes=tile.shape
    key=chunk*CH+lax.broadcasted_iota(jnp.int32,(rows,lanes),0)
    query=qb*width+lax.broadcasted_iota(jnp.int32,(rows,lanes),1)%width
    return jnp.where(key<=query,tile,fill)

def scaled_queries_t(vec_t, mix, out_ref, heads, width, size, scale, swap):
    for h in range(heads):
        for g in range(heads):
            m = mix[h,g] if swap else mix[g,h]
            out_ref[g*size:(g+1)*size, h*width:(h+1)*width] = (vec_t[g*size:(g+1)*size,:]*(m*scale)).astype(bf16)

def fwd_kernel(meta, premix, postmix, q_ref, k_ref, v_ref, joined_ref, ut_ref, lse_ref, qst, s_ref, acc, mx):
    width,model=q_ref.shape
    heads=HEADS; size=model//heads
    qb=meta[0]; active=meta[1]>0
    last=(qb*width)//CH
    pair=2*width
    @pl.when(jnp.logical_not(active))
    def _():
        joined_ref[...]=jnp.zeros(joined_ref.shape,bf16)
    @pl.when(active)
    def _():
        qt=q_ref[...].astype(f32).T
        scaled_queries_t(qt, premix, qst, heads, width, size, 0.125, False)
        mx[...]=jnp.full(mx.shape,-1e30,f32)
        def scores(c,diag):
            kc=k_ref[pl.ds(c*CH,CH),:]
            for t in range(heads//2):
                sl=slice(t*pair,(t+1)*pair)
                s=dot(kc,qst[:,sl])
                if diag: s=masked(s,c,qb,width,-1e30)
                s_ref[pl.ds(c*CH,CH),sl]=s
                m=jnp.max(s.reshape(CH//8,8,pair),axis=0)
                mx[:,sl]=jnp.maximum(mx[:,sl],m)
        def body(c,_):
            scores(c,False); return 0
        lax.fori_loop(0,last,body,0)
        scores(last,True)
        peak=jnp.max(mx[...],axis=0,keepdims=True)
        acc[...]=jnp.zeros(acc.shape,f32)
        mx[...]=jnp.zeros(mx.shape,f32)
        def pv(c,_):
            vc=v_ref[pl.ds(c*CH,CH),:]
            for t in range(heads//2):
                sl=slice(t*pair,(t+1)*pair)
                p=jnp.exp(s_ref[pl.ds(c*CH,CH),sl]-peak[:,sl])
                mx[:,sl]+=jnp.sum(p.reshape(CH//8,8,pair),axis=0)
                acc[:,sl]+=dot(vc,p.astype(bf16),0,0)
            return 0
        lax.fori_loop(0,last+1,pv,0)
        total=jnp.sum(mx[...],axis=0,keepdims=True)
        lse_ref[...]=peak+jnp.log(total)
        inv=1.0/total
        for k in range(heads):
            rows=slice(k*size,(k+1)*size)
            out=jnp.zeros((size,width),f32)
            for h in range(heads):
                u=acc[rows,h*width:(h+1)*width]*inv[:,h*width:(h+1)*width]
                ut_ref[rows,h*width:(h+1)*width]=u.astype(bf16)
                out+=u*postmix[h,k]
            acc[rows,0:width]=out
        joined_ref[...]=acc[:,0:width].T.astype(bf16)

VM=60*1024*1024
def att_fwd(meta,premix,postmix,q,k,v):
    width,model=q.shape; seq=k.shape[0]; hw=HEADS*width
    smem=pl.BlockSpec(memory_space=pltpu.SMEM); vmem=pl.BlockSpec(memory_space=pltpu.VMEM)
    return pl.pallas_call(fwd_kernel,
        out_shape=(jax.ShapeDtypeStruct((width,model),bf16),jax.ShapeDtypeStruct((model,hw),bf16),jax.ShapeDtypeStruct((1,hw),f32)),
        in_specs=[smem]*3+[vmem]*3,out_specs=[vmem]*3,
        scratch_shapes=[pltpu.VMEM((model,hw),bf16),pltpu.VMEM((seq,hw),f32),pltpu.VMEM((model,hw),f32),pltpu.VMEM((8,hw),f32)],
        compiler_params=pltpu.CompilerParams(vmem_limit_bytes=VM),
        name="attend_forward",
    )(meta,premix,postmix,q,k,v)

def bwd_kernel(meta,premix,postmix,prerow,postrow,q_ref,up_ref,k_ref,v_ref,ut_ref,lse_ref,
               dq_ref,dk_ref,dv_ref,gpre_ref,gpost_ref,qst,qs,ust,us,acc,pbuf,lbuf,dots):
    width,model=q_ref.shape
    heads=HEADS; size=model//heads
    qb=meta[0]; active=meta[1]>0
    last=(qb*width)//CH
    pair=2*width
    @pl.when(jnp.logical_not(active))
    def _():
        dq_ref[...]=jnp.zeros(dq_ref.shape,bf16)
        gpre_ref[...]=jnp.zeros(gpre_ref.shape,f32)
        gpost_ref[...]=jnp.zeros(gpost_ref.shape,f32)
        dk_ref[...]=jnp.zeros(dk_ref.shape,bf16)
        dv_ref[...]=jnp.zeros(dv_ref.shape,bf16)
    @pl.when(active)
    def _():
        def clear(c,_):
            dk_ref[pl.ds(c*CH,CH),:]=jnp.zeros((CH,model),bf16)
            dv_ref[pl.ds(c*CH,CH),:]=jnp.zeros((CH,model),bf16)
            return 0
        lax.fori_loop(last+1,k_ref.shape[0]//CH,clear,0)
        q=q_ref[...].astype(f32); up=up_ref[...].astype(f32)
        qt=q.T; upt=up.T
        scaled_queries_t(qt, premix, qst, heads, width, size, 0.125, False)
        scaled_queries_t(upt, postmix, ust, heads, width, size, 1.0, True)
        for h in range(heads):
            qs[h*width:(h+1)*width,:]=(q*(prerow[h:h+1,:]*0.125)).astype(bf16)
            us[h*width:(h+1)*width,:]=(up*postrow[h:h+1,:]).astype(bf16)
            ul=ut_ref[:,h*width:(h+1)*width].astype(f32)
            t=jnp.sum((ul*upt).reshape(heads,size,width),axis=1)
            gpost_ref[h]=t
            d=jnp.zeros((1,width),f32)
            for k in range(heads): d+=t[k:k+1,:]*postmix[h,k]
            dots[:,h*width:(h+1)*width]=d
        acc[...]=jnp.zeros(acc.shape,f32)
        def chunk(c,diag):
            kc=k_ref[pl.ds(c*CH,CH),:]
            vc=v_ref[pl.ds(c*CH,CH),:]
            for t in range(heads//2):
                sl=slice(t*pair,(t+1)*pair)
                s=dot(kc,qst[:,sl])
                p=jnp.exp(s-lse_ref[:,sl])
                if diag: p=masked(p,c,qb,width,0.0)
                dp=dot(vc,ust[:,sl])
                l=(p*(dp-dots[:,sl])).astype(bf16)
                pbuf[:,sl]=p.astype(bf16)
                lbuf[:,sl]=l
                acc[:,sl]+=dot(kc,l,0,0)
            dv_ref[pl.ds(c*CH,CH),:]=dot(pbuf[...],us[...]).astype(bf16)
            dk_ref[pl.ds(c*CH,CH),:]=dot(lbuf[...],qs[...]).astype(bf16)
        def body(c,_):
            chunk(c,False); return 0
        lax.fori_loop(0,last,body,0)
        chunk(last,True)
        for g in range(heads):
            rows=slice(g*size,(g+1)*size)
            out=jnp.zeros((size,width),f32)
            qg=qt[rows,:]*0.125
            for h in range(heads):
                a=acc[rows,h*width:(h+1)*width]
                out+=a*premix[g,h]
                gpre_ref[g,h:h+1,:]=jnp.sum(a*qg,axis=0,keepdims=True)
            acc[rows,0:width]=out*0.125
        dq_ref[...]=acc[:,0:width].T.astype(bf16)

def att_bwd(meta,premix,postmix,q,up,k,v,ut,lse):
    width,model=q.shape; seq=k.shape[0]; hw=HEADS*width; size=model//HEADS
    prerow=jnp.repeat(premix.T,size,axis=1); postrow=jnp.repeat(postmix,size,axis=1)
    smem=pl.BlockSpec(memory_space=pltpu.SMEM); vmem=pl.BlockSpec(memory_space=pltpu.VMEM)
    S=jax.ShapeDtypeStruct
    return pl.pallas_call(bwd_kernel,
        out_shape=(S((width,model),bf16),S((seq,model),bf16),S((seq,model),bf16),S((HEADS,HEADS,width),f32),S((HEADS,HEADS,width),f32)),
        in_specs=[smem]*3+[vmem]*8,out_specs=[vmem]*5,
        scratch_shapes=[pltpu.VMEM((model,hw),bf16),pltpu.VMEM((hw,model),bf16),pltpu.VMEM((model,hw),bf16),pltpu.VMEM((hw,model),bf16),
            pltpu.VMEM((model,hw),f32),pltpu.VMEM((CH,hw),bf16),pltpu.VMEM((CH,hw),bf16),pltpu.VMEM((1,hw),f32)],
        compiler_params=pltpu.CompilerParams(vmem_limit_bytes=VM),
        name="attend_backward",
    )(meta,premix,postmix,prerow,postrow,q,up,k,v,ut,lse)


def swap(value, axis, mask):
    count = lax.axis_size(axis)
    return lax.ppermute(value, axis, [(i, i ^ mask) for i in range(count)])


def gather_cores(value, step=2):
    count = lax.axis_size("blk")
    pieces = {}
    for k in range(0, count, 2):
        pieces[k] = value if k == 0 else swap(value, "blk", k)
        pieces[k + 1] = swap(pieces[k], "blk", 1)
    return [pieces[k] for k in range(count)]


def place_rows(pieces, index, axis=0):
    size = pieces[0].shape[axis]
    shape = list(pieces[0].shape)
    shape[axis] = size * len(pieces)
    out = jnp.zeros(shape, pieces[0].dtype)
    for k, piece in enumerate(pieces):
        out = lax.dynamic_update_slice_in_dim(out, piece, (index ^ k) * size, axis)
    return out


def cut(value, index, count, axis=0):
    size = value.shape[axis] // count
    return lax.dynamic_slice_in_dim(value, index * size, size, axis)


def gather_dp(value, zplace):
    count = lax.axis_size("dp")
    return place_rows([value] + [swap(value, "dp", k) for k in range(1, count)], zplace)


def gather_all(value, place, zplace):
    return place_rows(gather_cores(gather_dp(value, zplace)), place)


def scatter_blk(value, place, axis=0):
    count = lax.axis_size("blk")
    keep = [cut(value, place ^ k, count, axis) for k in range(0, count, 2)]
    give = [cut(value, place ^ k ^ 1, count, axis) for k in range(0, count, 2)]
    got = [swap(g.astype(bf16), "blk", 1) for g in give]
    pair = [a.astype(f32) + b.astype(f32) for a, b in zip(keep, got)]
    total = pair[0]
    for i in range(1, count // 2):
        total = total + swap(pair[i].astype(bf16), "blk", 2 * i).astype(f32)
    return total


def scatter_dp(value, zplace):
    count = lax.axis_size("dp")
    total = cut(value, zplace, count)
    for k in range(1, count):
        total = total + swap(cut(value, zplace ^ k, count).astype(bf16), "dp", k).astype(f32)
    return total


def scatter_all(value, place, zplace):
    return scatter_dp(scatter_blk(value, place), zplace)


def gather_group(value):
    one, two = swap(value, "blk", 1), swap(value, "blk", 2)
    return jnp.concatenate([value, one, two, swap(two, "blk", 1)], axis=0)


def scatter_group(value):
    parts = [part.astype(bf16) for part in jnp.split(value, GROUP, axis=0)]
    own = parts[0].astype(f32) + swap(parts[1], "blk", 1).astype(f32)
    across = parts[2].astype(f32) + swap(parts[3], "blk", 1).astype(f32)
    return own + swap(across.astype(bf16), "blk", 2).astype(f32)


def sum_small(value):
    for axis in ("blk", "dp"):
        k = 1
        while k < lax.axis_size(axis):
            value = value + swap(value, axis, k)
            k *= 2
    return value


def inverse_rms(values):
    return lax.rsqrt(jnp.mean(values * values, axis=-1, keepdims=True) + EPSILON)


def norm_back(values, inverse, gain, grad):
    scaled = grad * gain
    back = inverse * (scaled - values * (inverse * inverse * jnp.mean(scaled * values, axis=-1, keepdims=True)))
    return back, jnp.sum(grad * values * inverse, axis=tuple(range(values.ndim - 1)))


def mm(a, b, ca, cb):
    return lax.dot_general(a, b, (((ca,), (cb,)), ((), ())), preferred_element_type=f32)


def on_device(
    inputs, lengths, prenorm, midnorm, query_proj, key_proj, value_proj, output_proj,
    premix, postmix, inner_proj, outer_proj, cotangent,
):
    count, depth = lax.axis_size("blk"), lax.axis_size("dp")
    place, zplace = lax.axis_index("blk"), lax.axis_index("dp")
    rows, width, model = inputs.shape
    mirror = [(i, count - 1 - i) for i in range(count)]
    blocks = [place, count - 1 - place]

    gains = jnp.stack([prenorm, midnorm], axis=1)
    gains = gather_all(gains, place, zplace).astype(f32)
    gain_first, gain_second = gains[:, 0], gains[:, 1]
    x_all = place_rows(gather_cores(inputs), place, axis=1)
    wqkv = gather_all(jnp.concatenate([query_proj, key_proj, value_proj], axis=1), place, zplace)
    output_w = gather_all(output_proj, place, zplace)
    query_w, key_w, value_w = wqkv[:, :model], wqkv[:, model:2 * model], wqkv[:, 2 * model:]

    bands = count // GROUP
    band_ff = depth * outer_proj.shape[0]
    outer_rows = gather_dp(outer_proj, zplace)
    outer_w = place_rows(
        [outer_rows] + [swap(outer_rows, "blk", GROUP * j) for j in range(1, bands)], place // GROUP
    )
    inner_rows = gather_dp(inner_proj, zplace)
    wide = inner_rows.reshape(inner_rows.shape[0], bands, GROUP, band_ff)
    inner_parts = []
    for k in range(count):
        part = lax.dynamic_index_in_dim(wide, (place ^ k) % GROUP, 2, keepdims=False)
        part = part.reshape(part.shape[0], bands * band_ff)
        inner_parts.append(part if k == 0 else swap(part, "blk", k))
    inner_w = place_rows(inner_parts, place)

    cot = jnp.stack([cotangent[0], lax.ppermute(cotangent[1], "blk", mirror)])
    offsets = jnp.arange(width, dtype=jnp.int32)
    valid = jnp.stack([(blocks[r] * width + offsets < lengths[r]) for r in range(rows)]).astype(f32)[..., None]
    upgrad = cot.astype(f32) * valid
    up_all = gather_group(upgrad.astype(bf16).reshape(rows * width, model))

    residual_all = x_all.astype(f32)
    inverse_all = inverse_rms(residual_all)
    normed_all = (residual_all * inverse_all * gain_first).astype(bf16)

    def own(value):
        return jnp.stack([lax.dynamic_slice_in_dim(value[r], blocks[r] * width, width, 0) for r in range(rows)])

    keys = mm(normed_all, key_w, 2, 0).astype(bf16)
    values = mm(normed_all, value_w, 2, 0).astype(bf16)
    normed_own = own(normed_all)
    residual = own(residual_all)
    queries = mm(normed_own, query_w, 2, 0).astype(bf16)
    metas = [
        jnp.stack([blocks[r], (blocks[r] * width < lengths[r]).astype(jnp.int32)]) for r in range(rows)
    ]
    forward = [att_fwd(metas[r], premix, postmix, queries[r], keys[r], values[r]) for r in range(rows)]
    joined = jnp.stack([f[0] for f in forward])
    middle = residual + mm(joined, output_w, 2, 0)
    inverse_mid = inverse_rms(middle)
    second = (middle * inverse_mid * gain_second).astype(bf16)
    second_all = gather_group(second.reshape(rows * width, model))
    inner = mm(second_all, inner_w, 1, 0)
    activated, act_back = jax.vjp(lambda v: jax.nn.gelu(v, approximate=True), inner)
    hidden = activated.astype(bf16)
    outer = scatter_group(mm(hidden, outer_w, 1, 0)).reshape(rows, width, model)
    result = (valid * (middle + outer)).astype(bf16)
    outputs = jnp.stack([result[0], lax.ppermute(result[1], "blk", mirror)])
    hidden_grad = mm(up_all, outer_w, 1, 1)
    inner_cast = act_back(hidden_grad)[0].astype(bf16)
    second_grad = scatter_group(mm(inner_cast, inner_w, 1, 1)).reshape(rows, width, model)
    outer_wgrad = mm(hidden, up_all, 0, 0)
    inner_wgrad = mm(second_all, inner_cast, 0, 0)
    middle_part, gain_second_grad = norm_back(middle, inverse_mid, gain_second, second_grad)
    middle_grad = upgrad + middle_part
    middle_cast = middle_grad.astype(bf16)
    flat = rows * width
    output_wgrad = mm(joined.reshape(flat, model), middle_cast.reshape(flat, model), 0, 0)
    upstream = mm(middle_cast, output_w, 2, 1).astype(bf16)

    back = [
        att_bwd(metas[r], premix, postmix, queries[r], upstream[r], keys[r], values[r], forward[r][1], forward[r][2])
        for r in range(rows)
    ]
    query_cast = jnp.stack([b[0] for b in back])
    key_cast = jnp.stack([b[1] for b in back])
    value_cast = jnp.stack([b[2] for b in back])
    pre_grad = jnp.sum(back[0][3] + back[1][3], axis=-1)
    post_grad = jnp.sum(back[0][4] + back[1][4], axis=-1)
    length = keys.shape[1]
    normed_flat = normed_all.reshape(rows * length, model)
    query_wgrad = mm(normed_own.reshape(flat, model), query_cast.reshape(flat, model), 0, 0)
    key_wgrad = mm(normed_flat, key_cast.reshape(rows * length, model), 0, 0)
    value_wgrad = mm(normed_flat, value_cast.reshape(rows * length, model), 0, 0)
    normed_grad = mm(key_cast, key_w, 2, 1) + mm(value_cast, value_w, 2, 1)
    query_part = mm(query_cast, query_w, 2, 1)

    def put(base, part):
        return jnp.stack([
            lax.dynamic_update_slice_in_dim(
                base[r],
                lax.dynamic_slice_in_dim(base[r], blocks[r] * width, width, 0) + part[r],
                blocks[r] * width, 0,
            )
            for r in range(rows)
        ])

    normed_grad = put(normed_grad, query_part)
    input_part, gain_first_grad = norm_back(residual_all, inverse_all, gain_first, normed_grad)
    input_part = put(input_part, middle_grad)
    grad_inputs = scatter_blk(input_part, place, axis=1).astype(bf16)

    output_sum = scatter_all(output_wgrad, place, zplace)
    qkv_sum = scatter_all(jnp.concatenate([query_wgrad, key_wgrad, value_wgrad], axis=1), place, zplace)
    outer_sum = cut(outer_wgrad, place // GROUP, bands)
    for j in range(1, bands):
        outer_sum = outer_sum + swap(
            cut(outer_wgrad, (place // GROUP) ^ j, bands).astype(bf16), "blk", GROUP * j
        ).astype(f32)
    outer_sum = scatter_dp(outer_sum, zplace)
    member = [None] * GROUP
    for k in range(count):
        part = cut(inner_wgrad, place ^ k, count)
        part = part if k == 0 else swap(part.astype(bf16), "blk", k).astype(f32)
        member[k % GROUP] = part if member[k % GROUP] is None else member[k % GROUP] + part
    inner_sum = jnp.zeros((model // count, bands, GROUP, band_ff), f32)
    for i in range(GROUP):
        inner_sum = lax.dynamic_update_slice_in_dim(
            inner_sum, member[i].reshape(model // count, bands, 1, band_ff), (place % GROUP) ^ i, 2
        )
    inner_sum = scatter_dp(inner_sum.reshape(model // count, inner_proj.shape[1]), zplace)

    small = jnp.concatenate([gain_first_grad, gain_second_grad, pre_grad.reshape(-1), post_grad.reshape(-1)])
    small = sum_small(jnp.pad(small, (0, -small.shape[0] % 1024)).reshape(-1, 128)).reshape(-1)
    shard = prenorm.shape[0]
    start = (place * depth + zplace) * shard
    heads = premix.shape[0]
    mixes = small[2 * model:2 * model + 2 * heads * heads].reshape(2, heads, heads)
    return (
        outputs,
        grad_inputs,
        lax.dynamic_slice_in_dim(small, start, shard, 0),
        lax.dynamic_slice_in_dim(small, model + start, shard, 0),
        qkv_sum[:, :model],
        qkv_sum[:, model:2 * model],
        qkv_sum[:, 2 * model:],
        output_sum,
        mixes[0],
        mixes[1],
        inner_sum,
        outer_sum,
    )


def solution(mesh):
    weight = P(("blk", "dp"), None)
    vector = P(("blk", "dp"))
    tokens = P("dp", "blk", None)
    in_specs = (
        tokens, P("dp"), vector, vector, weight, weight, weight, weight, P(), P(), weight, weight, tokens,
    )
    out_specs = (
        tokens, tokens, vector, vector, weight, weight, weight, weight, P(), P(), weight, weight,
    )
    return jax.shard_map(on_device, mesh=mesh, in_specs=in_specs, out_specs=out_specs, check_vma=False)
```

```python
import jax
import jax.numpy as jnp
from jax import lax
from jax.experimental import pallas as pl
from jax.experimental.pallas import tpu as pltpu
from jax.sharding import PartitionSpec as P

EPSILON = 1e-06
GROUP = 4
CHUNK = 256
NEGATIVE = -1e30
VMEM_MOST = 60 * 1024 * 1024
VMEM_SPARE = 8 * 1024 * 1024
f32 = jnp.float32
bf16 = jnp.bfloat16
ANY_SPEC = pl.BlockSpec(memory_space=pl.ANY)
SMEM_SPEC = pl.BlockSpec(memory_space=pltpu.SMEM)
VMEM_SPEC = pl.BlockSpec(memory_space=pltpu.VMEM)


def shaped(shape, dtype=bf16):
    return jax.ShapeDtypeStruct(shape, dtype)


def vmem_bytes(shape, dtype):
    lead, (rows, columns) = shape[:-2], shape[-2:]
    size = jnp.dtype(dtype).itemsize
    for extent in lead:
        size *= extent
    return size * -(-rows // 16) * 16 * -(-columns // 128) * 128


def call(body, name, outs, smem, args, scratch=(), flops=0, after=()):
    arrays = list(args) + list(outs)
    moved = sum(a.size * a.dtype.itemsize for a in arrays)
    held = sum(vmem_bytes(a.shape, a.dtype) for a in arrays + list(scratch))
    first = len(smem) + len(args)

    def kernel(*refs):
        body(*refs[:first], *refs[first + len(after):])

    return pl.pallas_call(
        kernel,
        out_shape=tuple(outs),
        in_specs=[SMEM_SPEC] * len(smem) + [VMEM_SPEC] * len(args) + [ANY_SPEC] * len(after),
        out_specs=tuple(VMEM_SPEC for _ in outs),
        scratch_shapes=list(scratch),
        compiler_params=pltpu.CompilerParams(vmem_limit_bytes=min(VMEM_MOST, held + VMEM_SPARE)),
        cost_estimate=pl.CostEstimate(flops=flops, bytes_accessed=moved, transcendentals=0),
        name=name,
    )(*smem, *args, *after)


def dot(a, b, ca=1, cb=0):
    return lax.dot_general(a, b, (((ca,), (cb,)), ((), ())), preferred_element_type=f32)


def picks(rows, columns, start_row, start_column=0):
    r = lax.broadcasted_iota(jnp.int32, (rows, columns), 0) - start_row
    c = lax.broadcasted_iota(jnp.int32, (rows, columns), 1) - start_column
    return r, c


def one_hot(mask):
    return jnp.where(mask, 1.0, 0.0).astype(bf16)


def inverse_rms(values):
    return lax.rsqrt(jnp.mean(values * values, axis=-1, keepdims=True) + EPSILON)


def norm_back(values, gain, grad):
    inverse = inverse_rms(values)
    scaled = grad * gain
    mean = jnp.mean(scaled * values, axis=-1, keepdims=True)
    return inverse * (scaled - values * (inverse * inverse * mean)), grad * values * inverse


def aligned(index, size):
    return pl.ds(pl.multiple_of(index * size, size), size)


def join_dp(meta, pieces, later, name):
    size, columns = pieces[0].shape
    depth = len(pieces)

    def body(meta_ref, *refs):
        ins, later_ref, out, later_out = refs[:depth], refs[depth], refs[depth + 1], refs[depth + 2]
        total = jnp.zeros((size * depth, columns), f32)
        for m in range(depth):
            r, c = picks(size * depth, size, (meta_ref[1] ^ m) * size)
            total += dot(one_hot(r == c), ins[m][...])
        out[...] = total.astype(bf16)
        later_out[...] = later_ref[...]

    outs = [shaped((size * depth, columns)), shaped(later.shape)]
    return call(body, name, outs, [meta], list(pieces) + [later])


def join_dp_ffn(meta, pieces, size, count, name):
    depth = len(pieces)
    total_rows, model = pieces[0].shape
    band = total_rows - (1 + GROUP) * size
    joined = size * depth

    def body(meta_ref, *refs):
        ins, outer_w, send_k, sections = refs[:depth], refs[depth], refs[depth + 1:-1], refs[-1]
        zplace = meta_ref[1]
        total = jnp.zeros(((1 + GROUP) * joined, model), f32)
        outer = jnp.zeros((band * depth, model), f32)
        for m in range(depth):
            r = lax.broadcasted_iota(jnp.int32, ((1 + GROUP) * joined, total_rows), 0)
            c = lax.broadcasted_iota(jnp.int32, ((1 + GROUP) * joined, total_rows), 1)
            want = (r // joined) * size + (r % joined) - (zplace ^ m) * size
            inside = ((r % joined) // size) == (zplace ^ m)
            total += dot(one_hot(jnp.logical_and(inside, want == c)), ins[m][...])
            r = lax.broadcasted_iota(jnp.int32, (band * depth, total_rows), 0) - (zplace ^ m) * band
            c = lax.broadcasted_iota(jnp.int32, (band * depth, total_rows), 1) - (1 + GROUP) * size
            outer += dot(one_hot(jnp.logical_and(c >= 0, r == c)), ins[m][...])
        outer_w[...] = outer.astype(bf16)
        for t in range(GROUP):
            sections[t] = total[(1 + t) * joined:(2 + t) * joined].astype(bf16)
        for k in range(count):
            send_k[k][:joined, :] = total[:joined].astype(bf16)
            send_k[k][joined:, :] = sections[(meta_ref[0] ^ k) % GROUP]

    outs = [shaped((band * depth, model))] + [shaped((2 * joined, model))] * count
    made = call(body, name, outs, [meta], pieces, [pltpu.VMEM((GROUP, joined, model), bf16)])
    return made[0], list(made[1:])


def join_blk(meta, pieces, name):
    size, model = pieces[0].shape[0] // 2, pieces[0].shape[1]

    def body(meta_ref, *refs):
        ins, outs = refs[:len(pieces)], refs[len(pieces):]
        for k in range(len(pieces)):
            for i in range(2):
                outs[i][aligned(meta_ref[0] ^ k, size), :] = ins[k][i * size:(i + 1) * size, :]

    return call(body, name, [shaped((size * len(pieces), model))] * 2, [meta], pieces)


def join_bands(meta, pieces, name):
    size, model = pieces[0].shape

    def body(meta_ref, *refs):
        for j in range(len(pieces)):
            refs[-1][aligned((meta_ref[0] // GROUP) ^ j, size), :] = refs[j][...]

    return call(body, name, [shaped((size * len(pieces), model))], [meta], pieces)[0]


def slot_of(meta_ref, slot):
    return meta_ref[2 + 4 * slot], meta_ref[3 + 4 * slot] > 0, meta_ref[4 + 4 * slot]


def masked_cotangent(meta, own, far, after):
    rows, width, model = own.shape

    def body(meta_ref, own_ref, far_ref, out_ref):
        for slot in range(2):
            block, unused, row = slot_of(meta_ref, slot)
            length = meta_ref[5 + 4 * slot]
            position = block * width + lax.broadcasted_iota(jnp.int32, (width, model), 0)
            value = jnp.where(row == 0, own_ref[0].astype(f32), far_ref[...].astype(f32))
            out_ref[slot] = jnp.where(position < length, value, 0.0).astype(bf16)

    return call(body, "masked_cotangent", [shaped(own.shape)], [meta], [own, far], (), 0, after)[0]


def masked(tile, chunk, block, width, fill):
    rows, lanes = tile.shape
    key = chunk * CHUNK + lax.broadcasted_iota(jnp.int32, (rows, lanes), 0)
    query = block * width + lax.broadcasted_iota(jnp.int32, (rows, lanes), 1) % width
    return jnp.where(key <= query, tile, fill)


def mix_columns(vector_t, mix, out_ref, heads, scale, by_row):
    model, width = vector_t.shape
    size = model // heads
    for h in range(heads):
        for g in range(heads):
            factor = (mix[h, g] if by_row else mix[g, h]) * scale
            out_ref[g * size:(g + 1) * size, h * width:(h + 1) * width] = (
                vector_t[g * size:(g + 1) * size, :] * factor
            ).astype(bf16)


def attend_forward(meta, premix, postmix, slot, x_pieces, w_pieces, w, gains):
    count = len(x_pieces)
    width, model = x_pieces[0].shape[1:]
    length = count * width
    heads = premix.shape[0]
    size = model // heads
    pair = 2 * width
    lanes = heads * width
    first = w_pieces is not None
    w_rows = model // count

    def body(meta_ref, pre, post, *refs):
        x_refs, refs = refs[:count], refs[count:]
        if first:
            piece_refs, refs = refs[:count], refs[count:]
        else:
            (w_ref, gain_ref), refs = refs[:2], refs[2:]
        joined_ref, n_ref, k_ref, v_ref, q_ref, ut_ref, lse_ref = refs[:7]
        refs = refs[7:]
        if first:
            (w_ref, gain_ref), refs = refs[:2], refs[2:]
            columns_ref, refs = refs[0], refs[1:]
        qst, s_ref, acc, mx = refs
        place = meta_ref[0]
        block, active, row = slot_of(meta_ref, slot)
        last = block // 2
        if first:
            for k in range(count):
                spot = aligned(place ^ k, w_rows)
                w_ref[spot, :] = piece_refs[k][:, :3 * model]
                columns_ref[spot, :] = piece_refs[k][:, 3 * model:].astype(f32)
            gain_ref[...] = columns_ref[...].T[:8, :]

        @pl.when(jnp.logical_not(active))
        def _():
            joined_ref[...] = jnp.zeros(joined_ref.shape, bf16)

        @pl.when(active)
        def _():
            gain = gain_ref[0:1, :]
            for k in range(count):
                @pl.when((place ^ k) // 2 <= last)
                def _():
                    xb = x_refs[k][row].astype(f32)
                    n_ref[aligned(place ^ k, width), :] = (xb * inverse_rms(xb) * gain).astype(bf16)

            def project(c, unused):
                nc = n_ref[aligned(c, CHUNK), :]
                k_ref[aligned(c, CHUNK), :] = dot(nc, w_ref[:, model:2 * model]).astype(bf16)
                v_ref[aligned(c, CHUNK), :] = dot(nc, w_ref[:, 2 * model:3 * model]).astype(bf16)
                return 0

            lax.fori_loop(0, last + 1, project, 0)
            query = dot(n_ref[aligned(block, width), :], w_ref[:, :model]).astype(bf16)
            q_ref[...] = query
            mix_columns(query.astype(f32).T, pre, qst, heads, 0.125, False)
            mx[...] = jnp.full(mx.shape, NEGATIVE, f32)

            def scores(c, diagonal):
                kc = k_ref[aligned(c, CHUNK), :]
                for t in range(heads // 2):
                    part = slice(t * pair, (t + 1) * pair)
                    s = dot(kc, qst[:, part])
                    if diagonal:
                        s = masked(s, c, block, width, NEGATIVE)
                    s_ref[aligned(c, CHUNK), part] = s
                    mx[:, part] = jnp.maximum(mx[:, part], jnp.max(s.reshape(CHUNK // 8, 8, pair), axis=0))

            lax.fori_loop(0, last, lambda c, unused: (scores(c, False), 0)[1], 0)
            scores(last, True)
            peak = jnp.max(mx[...], axis=0, keepdims=True)
            acc[...] = jnp.zeros(acc.shape, f32)
            mx[...] = jnp.zeros(mx.shape, f32)

            def weigh(c, unused):
                vc = v_ref[aligned(c, CHUNK), :]
                for t in range(heads // 2):
                    part = slice(t * pair, (t + 1) * pair)
                    p = jnp.exp(s_ref[aligned(c, CHUNK), part] - peak[:, part])
                    mx[:, part] += jnp.sum(p.reshape(CHUNK // 8, 8, pair), axis=0)
                    acc[:, part] += dot(vc, p.astype(bf16), 0, 0)
                return 0

            lax.fori_loop(0, last + 1, weigh, 0)
            total = jnp.sum(mx[...], axis=0, keepdims=True)
            lse_ref[...] = peak + jnp.log(total)
            inverse = 1.0 / total
            for k in range(heads):
                rows = slice(k * size, (k + 1) * size)
                out = jnp.zeros((size, width), f32)
                for h in range(heads):
                    cols = slice(h * width, (h + 1) * width)
                    u = acc[rows, cols] * inverse[:, cols]
                    ut_ref[rows, cols] = u.astype(bf16)
                    out += u * post[h, k]
                acc[rows, 0:width] = out
            joined_ref[...] = acc[:, 0:width].T.astype(bf16)

    outs = [
        shaped((width, model)), shaped((length, model)), shaped((length, model)), shaped((length, model)),
        shaped((width, model)), shaped((model, lanes)), shaped((1, lanes), f32),
    ]
    scratch = [
        pltpu.VMEM((model, lanes), bf16), pltpu.VMEM((length, lanes), f32),
        pltpu.VMEM((model, lanes), f32), pltpu.VMEM((8, lanes), f32),
    ]
    if first:
        outs += [shaped((model, 3 * model)), shaped((8, model), f32)]
        scratch = [pltpu.VMEM((model, 128), f32)] + scratch
        args = list(x_pieces) + list(w_pieces)
    else:
        args = list(x_pieces) + [w, gains]
    flops = 2 * length * model * (lanes + 2 * model)
    return call(body, f"attend_forward_{slot}", outs, [meta, premix, postmix], args, scratch, flops)


def after_attention(meta, slot, joined, near, far, gains, w):
    width, model = joined.shape

    def body(meta_ref, joined_ref, near_ref, far_ref, gain_ref, w_ref, middle_ref, second_ref):
        row = slot_of(meta_ref, slot)[2]
        residual = jnp.where(row == 0, near_ref[0].astype(f32), far_ref[1].astype(f32))
        middle = residual + dot(joined_ref[...], w_ref[...])
        middle_ref[...] = middle
        second_ref[...] = (middle * inverse_rms(middle) * gain_ref[1:2, :]).astype(bf16)

    outs = [shaped((width, model), f32), shaped((width, model))]
    args = [joined, near, far, gains, w]
    return call(body, f"after_attention_{slot}", outs, [meta], args, (), 2 * width * model * model)


def feed_forward(slot, seconds, ups, inner_w, outer_w):
    width, model = seconds[0].shape
    units = inner_w.shape[1]
    tokens = GROUP * width
    root = 0.7978845608028654
    tile = 256

    def body(*refs):
        s_refs, u_refs = refs[:GROUP], refs[GROUP:2 * GROUP]
        w1, w2, hidden_ref, inner_ref, own_ref, give_ref, across_ref, tok, up = refs[2 * GROUP:]
        for i in range(GROUP):
            tok[i * width:(i + 1) * width, :] = s_refs[i][...]
            up[i * width:(i + 1) * width, :] = u_refs[i][slot]
        for t in range(units // tile):
            part = slice(t * tile, (t + 1) * tile)
            v = dot(tok[...], w1[:, part])
            squared = v * v
            th = jnp.tanh(root * (v + 0.044715 * (squared * v)))
            hidden_ref[:, part] = (0.5 * v * (1.0 + th)).astype(bf16)
            slope = 0.5 * (1.0 + th) + 0.5 * v * (1.0 - th * th) * (root * (1.0 + 0.134145 * squared))
            inner_ref[:, part] = (dot(up[...], w2[part, :], 1, 1) * slope).astype(bf16)
        grad = dot(inner_ref[...], w1[...], 1, 1).astype(bf16)
        own_ref[...] = grad[:width]
        give_ref[:width, :] = grad[width:2 * width]
        give_ref[width:, :] = grad[3 * width:]
        across_ref[...] = grad[2 * width:3 * width]

    outs = [
        shaped((tokens, units)), shaped((tokens, units)), shaped((width, model)), shaped((2 * width, model)),
        shaped((width, model)),
    ]
    scratch = [pltpu.VMEM((tokens, model), bf16)] * 2
    args = list(seconds) + list(ups) + [inner_w, outer_w]
    return call(body, f"feed_forward_{slot}", outs, [], args, scratch, 6 * tokens * model * units)


def feed_weights(meta, seconds, ups, hiddens, inners, outer_w, count):
    width, model = seconds[0][0].shape
    units = hiddens[0].shape[1]
    tokens = 2 * GROUP * width
    half = GROUP * width
    bands = count // GROUP
    rows_in, rows_out = model // count, units // bands

    def body(meta_ref, *refs):
        s_refs, u_refs = refs[:2 * GROUP], refs[2 * GROUP:3 * GROUP]
        h_refs, i_refs, w2 = refs[3 * GROUP:3 * GROUP + 2], refs[3 * GROUP + 2:3 * GROUP + 4], refs[3 * GROUP + 4]
        refs = refs[3 * GROUP + 5:]
        own_ref, give_ref, across_ref = refs[:3]
        inner_k, outer_j = refs[3:3 + count], refs[3 + count:3 + count + bands]
        tok, up, hid, inn, grad = refs[3 + count + bands:]
        for r in range(2):
            for i in range(GROUP):
                spot = slice(r * half + i * width, r * half + (i + 1) * width)
                tok[spot, :] = s_refs[r * GROUP + i][...]
                up[spot, :] = u_refs[i][r]
            hid[r * half:(r + 1) * half, :] = h_refs[r][...]
            inn[r * half:(r + 1) * half, :] = i_refs[r][...]
            out = dot(h_refs[r][...], w2[...]).astype(bf16)
            spot = slice(r * width, (r + 1) * width)
            own_ref[spot, :] = out[:width]
            give_ref[spot, :] = out[width:2 * width]
            give_ref[2 * width + r * width:2 * width + (r + 1) * width, :] = out[3 * width:]
            across_ref[spot, :] = out[2 * width:3 * width]
        grad[...] = dot(tok[...], inn[...], 0, 0).astype(bf16)
        for k in range(count):
            inner_k[k][...] = grad[aligned(meta_ref[0] ^ k, rows_in), :]
        grad[:units, :] = dot(hid[...], up[...], 0, 0).astype(bf16)
        for j in range(bands):
            outer_j[j][...] = grad[aligned((meta_ref[0] // GROUP) ^ j, rows_out), :]

    outs = (
        [shaped((2 * width, model)), shaped((4 * width, model)), shaped((2 * width, model))]
        + [shaped((rows_in, units))] * count + [shaped((rows_out, model))] * bands
    )
    args = list(seconds[0]) + list(seconds[1]) + list(ups) + list(hiddens) + list(inners) + [outer_w]
    scratch = [
        pltpu.VMEM((tokens, model), bf16), pltpu.VMEM((tokens, model), bf16), pltpu.VMEM((tokens, units), bf16),
        pltpu.VMEM((tokens, units), bf16), pltpu.VMEM((max(model, units), max(model, units)), bf16),
    ]
    made = call(
        body, "feed_weights", outs, [meta], args, scratch, 6 * tokens * model * units
    )
    return made[:3], list(made[3:3 + count]), list(made[3 + count:])


def before_attention_back(meta, slot, own, got, came, middle, up, gains, w, after):
    width, model = own.shape

    def body(meta_ref, own_ref, got_ref, came_ref, middle_ref, up_ref, gain_ref, w_ref,
             grad_ref, cast_ref, upstream_ref, gain_out):
        second = own_ref[...].astype(f32) + got_ref[:width, :].astype(f32) + came_ref[...].astype(f32)
        back, gain_rows = norm_back(middle_ref[...], gain_ref[1:2, :], second)
        grad = up_ref[slot].astype(f32) + back
        grad_ref[...] = grad
        cast = grad.astype(bf16)
        cast_ref[...] = cast
        upstream_ref[...] = dot(cast, w_ref[...], 1, 1).astype(bf16)
        gain_out[...] = jnp.sum(gain_rows, axis=0, keepdims=True)

    outs = [shaped((width, model), f32), shaped((width, model)), shaped((width, model)), shaped((1, model), f32)]
    args = [own, got, came, middle, up, gains, w]
    return call(
        body, f"before_attention_back_{slot}", outs, [meta], args, (), 2 * width * model * model, after
    )


def attend_back(meta, premix, postmix, slot, query, upstream, keys, values, ut, lse, after):
    width, model = query.shape
    length = keys.shape[0]
    heads = premix.shape[0]
    size = model // heads
    pair = 2 * width
    lanes = heads * width

    def body(meta_ref, pre, post, pre_row, post_row, q_ref, up_ref, k_ref, v_ref, ut_ref, lse_ref,
             dq_ref, dk_ref, dv_ref, mix_ref, qst, qs, ust, us, acc, pbuf, lbuf, dots):
        block, active, unused_row = slot_of(meta_ref, slot)
        last = block // 2

        @pl.when(jnp.logical_not(active))
        def _():
            dq_ref[...] = jnp.zeros(dq_ref.shape, bf16)
            mix_ref[...] = jnp.zeros(mix_ref.shape, f32)

        @pl.when(active)
        def _():
            q = q_ref[...].astype(f32)
            up = up_ref[...].astype(f32)
            qt, upt = q.T, up.T
            mix_columns(qt, pre, qst, heads, 0.125, False)
            mix_columns(upt, post, ust, heads, 1.0, True)
            for h in range(heads):
                spot = slice(h * width, (h + 1) * width)
                qs[spot, :] = (q * (pre_row[h:h + 1, :] * 0.125)).astype(bf16)
                us[spot, :] = (up * post_row[h:h + 1, :]).astype(bf16)
                t = jnp.sum((ut_ref[:, spot].astype(f32) * upt).reshape(heads, size, width), axis=1)
                mix_ref[heads + h] = t
                d = jnp.zeros((1, width), f32)
                for k in range(heads):
                    d += t[k:k + 1, :] * post[h, k]
                dots[:, spot] = d
            acc[...] = jnp.zeros(acc.shape, f32)

            def visit(c, diagonal):
                kc = k_ref[aligned(c, CHUNK), :]
                vc = v_ref[aligned(c, CHUNK), :]
                for t in range(heads // 2):
                    part = slice(t * pair, (t + 1) * pair)
                    p = jnp.exp(dot(kc, qst[:, part]) - lse_ref[:, part])
                    if diagonal:
                        p = masked(p, c, block, width, 0.0)
                    grad = (p * (dot(vc, ust[:, part]) - dots[:, part])).astype(bf16)
                    pbuf[:, part] = p.astype(bf16)
                    lbuf[:, part] = grad
                    acc[:, part] += dot(kc, grad, 0, 0)
                dv_ref[aligned(c, CHUNK), :] = dot(pbuf[...], us[...]).astype(bf16)
                dk_ref[aligned(c, CHUNK), :] = dot(lbuf[...], qs[...]).astype(bf16)

            lax.fori_loop(0, last, lambda c, unused: (visit(c, False), 0)[1], 0)
            visit(last, True)
            for g in range(heads):
                rows = slice(g * size, (g + 1) * size)
                out = jnp.zeros((size, width), f32)
                qg = qt[rows, :] * 0.125
                for h in range(heads):
                    a = acc[rows, h * width:(h + 1) * width]
                    out += a * pre[g, h]
                    mix_ref[g, h:h + 1, :] = jnp.sum(a * qg, axis=0, keepdims=True)
                acc[rows, 0:width] = out * 0.125
            dq_ref[...] = acc[:, 0:width].T.astype(bf16)

    pre_row = jnp.repeat(premix.T, size, axis=1)
    post_row = jnp.repeat(postmix, size, axis=1)
    outs = [
        shaped((width, model)), shaped((length, model)), shaped((length, model)),
        shaped((2 * heads, heads, width), f32),
    ]
    scratch = [
        pltpu.VMEM((model, lanes), bf16), pltpu.VMEM((lanes, model), bf16), pltpu.VMEM((model, lanes), bf16),
        pltpu.VMEM((lanes, model), bf16), pltpu.VMEM((model, lanes), f32), pltpu.VMEM((CHUNK, lanes), bf16),
        pltpu.VMEM((CHUNK, lanes), bf16), pltpu.VMEM((1, lanes), f32),
    ]
    args = [pre_row, post_row, query, upstream, keys, values, ut, lse]
    return call(
        body, f"attend_back_{slot}", outs, [meta, premix, postmix], args, scratch, 5 * length * model * lanes, after
    )


def input_back(meta, dqs, dks, dvs, w, x_pieces, gains, grads, after):
    count = len(x_pieces)
    width, model = dqs[0].shape
    length = dks[0].shape[0]

    def body(meta_ref, *refs):
        dq_refs, dk_refs, dv_refs, grad_refs = refs[:2], refs[2:4], refs[4:6], refs[6:8]
        w_ref, gain_ref, refs = refs[8], refs[9], refs[10:]
        x_refs, refs = refs[:count], refs[count:]
        keep_ref, give_ref, gain_out, normed = refs
        place = meta_ref[0]
        gain_out[...] = jnp.zeros(gain_out.shape, f32)
        for slot in range(2):
            block, active, row = slot_of(meta_ref, slot)

            @pl.when(active)
            def _():
                def visit(c, unused):
                    spot = aligned(c, CHUNK)
                    normed[spot, :] = dot(dk_refs[slot][spot, :], w_ref[:, model:2 * model], 1, 1) + dot(
                        dv_refs[slot][spot, :], w_ref[:, 2 * model:3 * model], 1, 1
                    )
                    return 0

                lax.fori_loop(0, block // 2 + 1, visit, 0)
                normed[aligned(block, width), :] += dot(dq_refs[slot][...], w_ref[:, :model], 1, 1)

            for k in range(count):
                out_ref = (keep_ref, give_ref)[k % 2]
                spot = aligned((k // 2) * 2 + row, width)
                used = jnp.logical_and(active, (place ^ k) <= block)

                @pl.when(jnp.logical_not(used))
                def _():
                    out_ref[spot, :] = jnp.zeros((width, model), bf16)

                @pl.when(used)
                def _():
                    back, gain_rows = norm_back(
                        x_refs[k][row].astype(f32), gain_ref[0:1, :], normed[aligned(place ^ k, width), :]
                    )
                    factor = jnp.where((place ^ k) == block, 1.0, 0.0)
                    out_ref[spot, :] = (back + grad_refs[slot][...] * factor).astype(bf16)
                    gain_out[...] += jnp.sum(gain_rows, axis=0, keepdims=True)

    half = count * width
    outs = [shaped((half, model)), shaped((half, model)), shaped((1, model), f32)]
    args = list(dqs) + list(dks) + list(dvs) + list(grads) + [w, gains] + list(x_pieces)
    scratch = [pltpu.VMEM((length, model), f32)]
    return call(body, "input_back", outs, [meta], args, scratch, 8 * length * model * model, after)


def project_weights(meta, normeds, dqs, dks, dvs, joineds, casts, count):
    width, model = dqs[0].shape
    rows = model // count

    def body(meta_ref, *refs):
        n_refs, q_refs, k_refs, v_refs, j_refs, c_refs = (refs[2 * i:2 * i + 2] for i in range(6))
        keep_ref, give_ref, acc, cast = refs[12:]
        acc[...] = jnp.zeros(acc.shape, f32)
        for slot in range(2):
            block, active, unused_row = slot_of(meta_ref, slot)

            @pl.when(active)
            def _():
                def visit(c, unused):
                    spot = aligned(c, CHUNK)
                    nc = n_refs[slot][spot, :]
                    acc[:, model:2 * model] += dot(nc, k_refs[slot][spot, :], 0, 0)
                    acc[:, 2 * model:] += dot(nc, v_refs[slot][spot, :], 0, 0)
                    return 0

                lax.fori_loop(0, block // 2 + 1, visit, 0)
                acc[:, :model] += dot(n_refs[slot][aligned(block, width), :], q_refs[slot][...], 0, 0)

        cast[:, :3 * model] = acc[...].astype(bf16)
        out = dot(j_refs[0][...], c_refs[0][...], 0, 0) + dot(j_refs[1][...], c_refs[1][...], 0, 0)
        cast[:, 3 * model:] = out.astype(bf16)
        for k in range(count):
            (keep_ref, give_ref)[k % 2][k // 2 * rows:(k // 2 + 1) * rows, :] = cast[
                aligned(meta_ref[0] ^ k, rows), :
            ]

    outs = [shaped((count // 2 * rows, 4 * model))] * 2
    args = list(normeds) + list(dqs) + list(dks) + list(dvs) + list(joineds) + list(casts)
    scratch = [pltpu.VMEM((model, 3 * model), f32), pltpu.VMEM((model, 4 * model), bf16)]
    length = normeds[0].shape[0]
    return call(body, "project_weights", outs, [meta], args, scratch, 8 * length * model * model)


def pair_sums(keep, got, count, name):
    blocks = count // 2
    rows, columns = keep.shape[0] // blocks, keep.shape[1]

    def body(keep_ref, got_ref, *outs):
        for i in range(blocks):
            spot = slice(i * rows, (i + 1) * rows)
            outs[i][...] = (keep_ref[spot, :].astype(f32) + got_ref[spot, :].astype(f32)).astype(outs[i].dtype)

    outs = [shaped((rows, columns), f32)] + [shaped((rows, columns))] * (blocks - 1)
    return call(body, name, outs, [], [keep, got])


def split_dp(meta, depth, parts):
    joined, wide = parts[0].shape
    size = joined // depth

    def body(meta_ref, *refs):
        ins, outs = refs[:len(parts)], refs[len(parts):]
        total = ins[0][...].astype(f32)
        for ref in ins[1:]:
            total += ref[...].astype(f32)
        total = total.astype(bf16)
        for m in range(depth):
            r, c = picks(size, joined, 0, (meta_ref[1] ^ m) * size)
            outs[m][...] = dot(one_hot(r == c), total).astype(bf16)

    return call(body, "split_dp", [shaped((size, wide))] * depth, [meta], list(parts))


def split_dp_ffn(meta, depth, inner, outer, size):
    count, bands = len(inner), len(outer)
    joined, units = inner[0].shape
    band = outer[0].shape[0]
    shard = band // depth
    out_rows = GROUP * size + shard

    def body(meta_ref, *refs):
        i_refs, o_refs, outs, total = refs[:count], refs[count:count + bands], refs[count + bands:-1], refs[-1]
        for i in range(GROUP):
            section = i_refs[i][...].astype(f32)
            for j in range(1, bands):
                section += i_refs[j * GROUP + i][...].astype(f32)
            total[aligned((meta_ref[0] % GROUP) ^ i, joined), :] = section.astype(bf16)
        rest = o_refs[0][...].astype(f32)
        for j in range(1, bands):
            rest += o_refs[j][...].astype(f32)
        total[GROUP * joined:, :] = rest.astype(bf16)
        for m in range(depth):
            zplace = meta_ref[1] ^ m
            r = lax.broadcasted_iota(jnp.int32, (out_rows, GROUP * joined + band), 0)
            c = lax.broadcasted_iota(jnp.int32, (out_rows, GROUP * joined + band), 1)
            inner_c = (r // size) * joined + zplace * size + r % size
            outer_c = GROUP * joined + zplace * shard + r - GROUP * size
            outs[m][...] = dot(one_hot(c == jnp.where(r < GROUP * size, inner_c, outer_c)), total[...]).astype(bf16)

    args = list(inner) + list(outer)
    scratch = [pltpu.VMEM((GROUP * joined + band, units), bf16)]
    return call(body, "split_dp_ffn", [shaped((out_rows, units))] * depth, [meta], args, scratch)


def finish_projections(pieces):
    size, wide = pieces[0].shape
    parts = 4
    model = wide // parts

    def body(*refs):
        ins, outs = refs[:len(pieces)], refs[len(pieces):]
        for i in range(parts):
            part = slice(i * model, (i + 1) * model)
            total = ins[0][:, part].astype(f32)
            for ref in ins[1:]:
                total += ref[:, part].astype(f32)
            outs[i][...] = total

    outs = [shaped((size, model), f32)] * parts
    return call(body, "finish_projections", outs, [], pieces)


def finish_feed(pieces, size, bands):
    rows, units = pieces[0].shape
    band = units // bands

    def body(*refs):
        ins, inner_ref, outer_ref = refs[:len(pieces)], refs[-2], refs[-1]
        total = ins[0][...].astype(f32)
        for ref in ins[1:]:
            total += ref[...].astype(f32)
        for t in range(GROUP):
            for y in range(bands):
                inner_ref[:, (y * GROUP + t) * band:(y * GROUP + t + 1) * band] = total[
                    t * size:(t + 1) * size, y * band:(y + 1) * band
                ]
        outer_ref[...] = total[GROUP * size:, :]

    outs = [shaped((size, GROUP * units), f32), shaped((rows - GROUP * size, units), f32)]
    return call(body, "finish_feed", outs, [], pieces)


def swap(value, axis, mask):
    count = lax.axis_size(axis)
    return lax.ppermute(value, axis, [(i, i ^ mask) for i in range(count)])


def gather_dp(value):
    return [value] + [swap(value, "dp", m) for m in range(1, lax.axis_size("dp"))]


def gather_blk(value):
    pieces = {}
    for k in range(0, lax.axis_size("blk"), 2):
        pieces[k] = value if k == 0 else swap(value, "blk", k)
        pieces[k + 1] = swap(pieces[k], "blk", 1)
    return [pieces[k] for k in range(len(pieces))]


def gather_group(value):
    two = swap(value, "blk", 2)
    return [value, swap(value, "blk", 1), two, swap(two, "blk", 1)]


def scatter_chips(parts):
    return [parts[0]] + [swap(part, "blk", 2 * i) for i, part in enumerate(parts) if i]


def sum_small(value):
    for axis in ("blk", "dp"):
        k = 1
        while k < lax.axis_size(axis):
            value = value + swap(value, axis, k)
            k *= 2
    return value


def on_device(
    inputs, lengths, prenorm, midnorm, query_proj, key_proj, value_proj, output_proj,
    premix, postmix, inner_proj, outer_proj, cotangent,
):
    count, depth = lax.axis_size("blk"), lax.axis_size("dp")
    place, zplace = lax.axis_index("blk"), lax.axis_index("dp")
    rows, width, model = inputs.shape
    shard = prenorm.shape[0]
    low = place < count // 2
    mirror = count - 1
    slot_rows = [jnp.where(low, 1, 0), jnp.where(low, 0, 1)]
    blocks = [jnp.maximum(place, place ^ mirror), jnp.minimum(place, place ^ mirror)]
    spans = [jnp.where(slot_rows[i] == 0, lengths[0], lengths[1]) for i in range(2)]
    meta = [place, zplace]
    for i in range(2):
        meta += [blocks[i], (blocks[i] * width < spans[i]).astype(jnp.int32), slot_rows[i], spans[i]]
    meta = jnp.stack(meta).astype(jnp.int32)

    gains = jnp.pad(jnp.stack([prenorm, midnorm], axis=1), ((0, 0), (0, 126)))
    first_w = jnp.concatenate([query_proj, key_proj, value_proj, gains], axis=1)
    first_pieces = gather_dp(first_w)
    x_pieces = gather_blk(inputs)
    bands = count // GROUP
    band_ff = depth * outer_proj.shape[0]
    sections = inner_proj.reshape(shard, bands, GROUP, band_ff).transpose(2, 0, 1, 3)
    second_w = jnp.concatenate(
        [output_proj, sections.reshape(GROUP * shard, bands * band_ff), outer_proj], axis=0
    )
    first_rows, second_w = join_dp(meta, first_pieces, second_w, "join_dp")
    w_pieces = gather_blk(first_rows)

    outer_rows, sent = join_dp_ffn(meta, gather_dp(second_w), shard, count, "join_dp_ffn")
    output_w, inner_w = join_blk(
        meta, [sent[0]] + [swap(sent[k], "blk", k) for k in range(1, count)], "join_blk"
    )
    outer_w = join_bands(
        meta, [outer_rows] + [swap(outer_rows, "blk", GROUP * j) for j in range(1, bands)], "join_bands"
    )
    up = masked_cotangent(meta, cotangent, swap(cotangent[1], "blk", mirror), [w_pieces[count - 2]])
    ups = gather_group(up)

    fwd = [None] * 2
    fwd[0] = attend_forward(meta, premix, postmix, 0, x_pieces, w_pieces, None, None)
    w, gain_rows = fwd[0][7], fwd[0][8]
    fwd[1] = attend_forward(meta, premix, postmix, 1, x_pieces, None, w, gain_rows)
    mid = [
        after_attention(meta, i, fwd[i][0], x_pieces[0], x_pieces[mirror], gain_rows, output_w) for i in range(2)
    ]
    seconds = [gather_group(mid[i][1]) for i in range(2)]
    feed = [feed_forward(i, seconds[i], ups, inner_w, outer_w) for i in range(2)]
    gots, came = [], []
    for i in range(2):
        gots.append(swap(feed[i][3], "blk", 1))
        across = (feed[i][4].astype(f32) + gots[i][width:].astype(f32)).astype(bf16)
        came.append(swap(across, "blk", 2))
    (out_own, out_give, out_across), inner_grads, outer_grads = feed_weights(
        meta, seconds, ups, [f[0] for f in feed], [f[1] for f in feed], outer_w, count
    )

    pre = [
        before_attention_back(
            meta, i, feed[i][2], gots[i], came[i], mid[i][0], up, gain_rows, output_w, [out_own]
        )
        for i in range(2)
    ]
    back = [
        attend_back(
            meta, premix, postmix, i, fwd[i][4], pre[i][2], fwd[i][2], fwd[i][3], fwd[i][5], fwd[i][6], ()
        )
        for i in range(2)
    ]

    out_got = swap(out_give, "blk", 1)
    out_across = (out_across.astype(f32) + out_got[2 * width:].astype(f32)).astype(bf16)
    out_came = swap(out_across, "blk", 2)
    outer = out_own.astype(f32) + out_got[:2 * width].astype(f32) + out_came.astype(f32)
    results = []
    for i in range(2):
        position = blocks[i] * width + jnp.arange(width, dtype=jnp.int32)
        value = mid[i][0] + outer[i * width:(i + 1) * width]
        results.append(jnp.where((position < spans[i])[:, None], value, 0.0).astype(bf16))
    outputs = jnp.stack([
        jnp.where(low, results[1], results[0]),
        swap(jnp.where(low, results[0], results[1]), "blk", mirror),
    ])
    inner_grads = [inner_grads[0]] + [swap(inner_grads[k], "blk", k) for k in range(1, count)]
    outer_grads = [outer_grads[0]] + [swap(outer_grads[j], "blk", GROUP * j) for j in range(1, bands)]
    cuts = split_dp_ffn(meta, depth, inner_grads, outer_grads, shard)
    inner_sum, outer_sum = finish_feed(
        [cuts[0]] + [swap(cuts[m], "dp", m) for m in range(1, depth)], shard, bands
    )

    keep, give = project_weights(
        meta, [f[1] for f in fwd], [b[0] for b in back], [b[1] for b in back], [b[2] for b in back],
        [f[0] for f in fwd], [p[1] for p in pre], count,
    )
    input_keep, input_give, gain_first = input_back(
        meta, [b[0] for b in back], [b[1] for b in back], [b[2] for b in back], w, x_pieces, gain_rows,
        [p[0] for p in pre], [keep],
    )
    projected = scatter_chips(pair_sums(keep, swap(give, "blk", 1), count, "pair_sums_w"))
    cuts = split_dp(meta, depth, projected)
    query_sum, key_sum, value_sum, output_sum = finish_projections(
        [cuts[0]] + [swap(cuts[m], "dp", m) for m in range(1, depth)]
    )
    parts = scatter_chips(pair_sums(input_keep, swap(input_give, "blk", 1), count, "pair_sums_x"))
    grad_inputs = sum([part.astype(f32) for part in parts[1:]], parts[0]).astype(bf16).reshape(inputs.shape)

    heads = premix.shape[0]
    mixes = jnp.sum(back[0][3] + back[1][3], axis=-1).reshape(-1)
    small = jnp.concatenate([gain_first.reshape(-1), (pre[0][3] + pre[1][3]).reshape(-1), mixes])
    small = sum_small(jnp.pad(small, (0, -small.shape[0] % 1024)).reshape(-1, 128)).reshape(-1)
    start = (place * depth + zplace) * shard
    mixes = small[2 * model:2 * model + 2 * heads * heads].reshape(2, heads, heads)
    return (
        outputs,
        grad_inputs,
        lax.dynamic_slice_in_dim(small, start, shard, 0),
        lax.dynamic_slice_in_dim(small, model + start, shard, 0),
        query_sum,
        key_sum,
        value_sum,
        output_sum,
        mixes[0],
        mixes[1],
        inner_sum,
        outer_sum,
    )


def solution(mesh):
    weight = P(("blk", "dp"), None)
    vector = P(("blk", "dp"))
    tokens = P("dp", "blk", None)
    in_specs = (
        tokens, P("dp"), vector, vector, weight, weight, weight, weight, P(), P(), weight, weight, tokens,
    )
    out_specs = (
        tokens, tokens, vector, vector, weight, weight, weight, weight, P(), P(), weight, weight,
    )
    return jax.shard_map(on_device, mesh=mesh, in_specs=in_specs, out_specs=out_specs, check_vma=False)
```

```python
import jax
import jax.numpy as jnp
from jax import lax
from jax.experimental import pallas as pl
from jax.experimental.pallas import tpu as pltpu
from jax.sharding import PartitionSpec as P

EPSILON = 1e-06
GROUP = 4
CHUNK = 256
NEGATIVE = -1e30
VMEM_MOST = 60 * 1024 * 1024
VMEM_SPARE = 7 * 1024 * 1024
VMEM_WINDOWS = 18 * 1024 * 1024
GAIN_ROWS = 16
f32 = jnp.float32
bf16 = jnp.bfloat16
HIGH = lax.Precision.HIGHEST
ANY_SPEC = pl.BlockSpec(memory_space=pl.ANY)
VMEM_SPEC = pl.BlockSpec(memory_space=pltpu.VMEM)
HBM_SPEC = pl.BlockSpec(memory_space=pltpu.HBM)
SMEM_SPEC = pl.BlockSpec(memory_space=pltpu.SMEM)


def shaped(shape, dtype=bf16):
    return jax.ShapeDtypeStruct(shape, dtype)


def vmem_bytes(shape, dtype):
    lead, (rows, columns) = shape[:-2], shape[-2:]
    size = jnp.dtype(dtype).itemsize
    for extent in lead:
        size *= extent
    return size * -(-rows // 16) * 16 * -(-columns // 128) * 128


def call(body, name, outs, smem, args, scratch=(), flops=0, after=(), raw_args=(), raw_outs=()):
    n_smem, n_args = len(smem), len(args)
    arrays = list(args) + list(outs)
    windows = [a for i, a in enumerate(args) if i not in raw_args] + [a for i, a in enumerate(outs) if i not in raw_outs]
    windows = sum(vmem_bytes(a.shape, a.dtype) for a in windows)
    held = sum(vmem_bytes(a.shape, a.dtype) for a in scratch if getattr(a, "memory_space", None) == pltpu.VMEM)
    held += VMEM_SPARE + (windows if windows > VMEM_WINDOWS else 0)

    def kernel(*refs):
        first = n_smem + n_args
        body(*refs[:first], *refs[first + len(after):])

    return pl.pallas_call(
        kernel,
        out_shape=tuple(pltpu.HBM(a.shape, a.dtype) if i in raw_outs else a for i, a in enumerate(outs)),
        in_specs=[SMEM_SPEC] * n_smem
        + [HBM_SPEC if i in raw_args else VMEM_SPEC for i in range(n_args)] + [ANY_SPEC] * len(after),
        out_specs=tuple(HBM_SPEC if i in raw_outs else VMEM_SPEC for i in range(len(outs))),
        scratch_shapes=list(scratch),
        compiler_params=pltpu.CompilerParams(vmem_limit_bytes=min(VMEM_MOST, held)),
        cost_estimate=pl.CostEstimate(
            flops=flops, bytes_accessed=sum(a.size * a.dtype.itemsize for a in arrays), transcendentals=0
        ),
        name=name,
    )(
        *smem,
        *[pltpu.with_memory_space_constraint(a, pltpu.HBM) if i in raw_args else a for i, a in enumerate(args)],
        *after,
    )


def dot(a, b, ca=1, cb=0):
    return lax.dot_general(a, b, (((ca,), (cb,)), ((), ())), preferred_element_type=f32)


def picks(rows, columns, start_row, start_column=0):
    r = lax.broadcasted_iota(jnp.int32, (rows, columns), 0) - start_row
    c = lax.broadcasted_iota(jnp.int32, (rows, columns), 1) - start_column
    return r, c


def one_hot(mask):
    return jnp.where(mask, 1.0, 0.0).astype(bf16)


def inverse_rms(values):
    return lax.rsqrt(jnp.mean(values * values, axis=-1, keepdims=True) + EPSILON)


def norm_back(values, gain, grad):
    inverse = inverse_rms(values)
    scaled = grad * gain
    mean = jnp.mean(scaled * values, axis=-1, keepdims=True)
    return inverse * (scaled - values * (inverse * inverse * mean))


def aligned(index, size):
    return pl.ds(pl.multiple_of(index * size, size), size)


def pack_first(weights, gains):
    size, model = weights[0].shape
    parts = len(weights)

    def body(*refs):
        gain_ref, out_ref = refs[parts], refs[parts + 1]
        for i in range(parts):
            out_ref[i * size:(i + 1) * size, :] = refs[i][...]
        r, c = picks(size, model, 0)
        along = dot(gain_ref[...], one_hot(r == c)).astype(bf16)
        r, c = picks(GAIN_ROWS, 2, 0)
        out_ref[parts * size:, :] = dot(one_hot(r == c), along).astype(bf16)

    return call(body, "pack_first", [shaped((parts * size + GAIN_ROWS, model))], [], list(weights) + [gains])[0]


def join_dp(meta, pieces, x_links):
    depth = len(pieces)
    total_rows, model = pieces[0].shape
    size = (total_rows - GAIN_ROWS) // 4
    joined = size * depth
    links = len(x_links)
    lanes = 128

    def body(meta_ref, *refs):
        ins, x_refs, outs = refs[:depth], refs[depth:depth + links], refs[depth + links:]
        total = jnp.zeros((4 * joined, model), f32)
        gains = jnp.zeros((GAIN_ROWS, lanes), f32)
        for m in range(depth):
            d = meta_ref[1] ^ m
            r = lax.broadcasted_iota(jnp.int32, (4 * joined, total_rows), 0)
            c = lax.broadcasted_iota(jnp.int32, (4 * joined, total_rows), 1)
            want = jnp.where((r % joined) // size == d, (r // joined) * size + r % size, -1)
            total += dot(one_hot(c == want), ins[m][...])
            r, c = picks(lanes, lanes, 0, d * size)
            gains += dot(ins[m][4 * size:, :lanes], one_hot(jnp.logical_and(r == c, r < size)))
        outs[0][:4 * joined, :] = total.astype(bf16)
        outs[0][4 * joined:, :] = jnp.zeros((GAIN_ROWS, model), bf16)
        outs[0][4 * joined:, :lanes] = gains.astype(bf16)
        outs[1][...] = x_refs[2][0]
        outs[2][...] = x_refs[1][1]
        for i in range(links):
            outs[3][i] = x_refs[i][...]

    rows, width, model = x_links[0].shape
    outs = [
        shaped((4 * joined + GAIN_ROWS, model)), shaped((width, model)), shaped((width, model)),
        shaped((links, rows, width, model)),
    ]
    return call(body, "join_dp", outs, [meta], list(pieces) + list(x_links))


def forward_across(w_links, x_halves):
    total_rows, model = w_links[0].shape
    cut_at = (total_rows - GAIN_ROWS) // 2
    links = len(w_links)

    def body(*refs):
        w_refs, h_refs, outs = refs[:links], refs[links:links + 2], refs[links + 2:]
        outs[0][...] = w_refs[2][:cut_at, :]
        outs[1][...] = w_refs[1][cut_at:, :]
        for i in range(links):
            outs[2][i] = w_refs[i][...]
        for i in range(2):
            outs[3][i] = h_refs[i][...]

    outs = [
        shaped((cut_at, model)), shaped((total_rows - cut_at, model)), shaped((links, total_rows, model)),
        shaped((2, *x_halves[0].shape)),
    ]
    return call(body, "forward_across", outs, [], list(w_links) + list(x_halves))


def join_feed(pieces, size, count, after):
    depth, total_rows, model = pieces.shape
    band = total_rows - GROUP * size
    joined = size * depth

    def body(in_ref, inner_ref, outer_ref):
        total = jnp.zeros((GROUP * joined + band * depth, model), f32)
        for d in range(depth):
            r = lax.broadcasted_iota(jnp.int32, (GROUP * joined + band * depth, total_rows), 0)
            c = lax.broadcasted_iota(jnp.int32, (GROUP * joined + band * depth, total_rows), 1)
            inner = jnp.where((r % joined) // size == d, (r // joined) * size + r % size, -1)
            rest = r - GROUP * joined
            outer = jnp.where(rest // band == d, GROUP * size + rest % band, -1)
            total += dot(one_hot(c == jnp.where(rest < 0, inner, outer)), in_ref[d])
        cast = total.astype(bf16)
        for j in range(count):
            inner_ref[j] = cast[(j % GROUP) * joined:(j % GROUP + 1) * joined, :]
        outer_ref[...] = cast[GROUP * joined:, :]

    outs = [shaped((count, joined, model)), shaped((band * depth, model))]
    return call(body, "join_feed", outs, [], [pieces], (), 0, after)


def join_bands(meta, pieces, name):
    size, model = pieces[0].shape

    def body(meta_ref, *refs):
        for j in range(len(pieces)):
            refs[-1][aligned((meta_ref[0] // GROUP) ^ j, size), :] = refs[j][...]

    return call(body, name, [shaped((size * len(pieces), model))], [meta], pieces)[0]


def pack(pieces, name):
    def body(*refs):
        for i in range(len(pieces)):
            refs[-1][i] = refs[i][...]

    return call(body, name, [shaped((len(pieces), *pieces[0].shape))], [], pieces)[0]


def slot_of(meta_ref, slot):
    return meta_ref[2 + 4 * slot], meta_ref[3 + 4 * slot] > 0, meta_ref[4 + 4 * slot]


def masked_cotangent(meta, own, far, after):
    rows, width, model = own.shape

    def body(meta_ref, own_ref, far_ref, out_ref):
        for slot in range(2):
            block, unused, row = slot_of(meta_ref, slot)
            length = meta_ref[5 + 4 * slot]
            position = block * width + lax.broadcasted_iota(jnp.int32, (width, model), 0)
            value = jnp.where(row == 0, own_ref[0].astype(f32), far_ref[...].astype(f32))
            out_ref[slot] = jnp.where(position < length, value, 0.0).astype(bf16)

    return call(body, "masked_cotangent", [shaped(own.shape)], [meta], [own, far], (), 0, after)[0]


def masked(tile, chunk, block, width, fill):
    rows, lanes = tile.shape
    key = chunk * CHUNK + lax.broadcasted_iota(jnp.int32, (rows, lanes), 0)
    query = block * width + lax.broadcasted_iota(jnp.int32, (rows, lanes), 1) % width
    return jnp.where(key <= query, tile, fill)


def mix_columns(vector_t, mix, out_ref, heads, heads_in, scale, by_row):
    model, width = vector_t.shape
    size = model // heads
    for i, h in enumerate(heads_in):
        for g in range(heads):
            factor = (mix[h, g] if by_row else mix[g, h]) * scale
            out_ref[g * size:(g + 1) * size, i * width:(i + 1) * width] = (
                vector_t[g * size:(g + 1) * size, :] * factor
            ).astype(bf16)


def listed(pieces):
    arrays, spots = [], []
    for parts in pieces:
        spot = []
        for array, index in parts:
            known = [i for i, a in enumerate(arrays) if a is array]
            if not known:
                arrays.append(array)
            spot.append((known[0] if known else len(arrays) - 1, index))
        spots.append(spot)
    return arrays, spots


def views(refs, spot):
    return [refs[i] if index is None else refs[i].at[index] for i, index in spot]


def attend_forward(meta, premix, postmix, slot, x_pieces, w_pieces, w, gains):
    count = len(x_pieces)
    x_arrays, x_spots = listed(x_pieces)
    width, model = x_arrays[0].shape[1:]
    length = count * width
    heads = premix.shape[0]
    size = model // heads
    pair = 2 * width
    lanes = heads * width
    half = heads // 2 * width
    first = w_pieces is not None
    w_rows = model // count
    if first:
        w_arrays, w_spots = listed(w_pieces)

    def body(meta_ref, pre, post, *refs):
        x_refs, refs = refs[:len(x_arrays)], refs[len(x_arrays):]
        if first:
            piece_refs, refs = refs[:len(w_arrays)], refs[len(w_arrays):]
        else:
            (w_out, gain_ref), refs = refs[:2], refs[2:]
        joined_ref, n_out, k_out, v_out, q_ref, ut_a, ut_b, lse_ref = refs[:8]
        refs = refs[8:]
        if first:
            (w_out, wo_ref, gain_ref), refs = refs[:3], refs[3:]
        qst, s_ref, acc, mx, total_out, n_ref, k_ref, v_ref, w_ref, ut_ref, sems, w_sem, ut_sems = refs
        w_copy = pltpu.make_async_copy(w_ref, w_out, w_sem) if first else pltpu.make_async_copy(w_out, w_ref, w_sem)
        ut_copies = [pltpu.make_async_copy(ut_ref.at[i], (ut_a, ut_b)[i], ut_sems.at[i]) for i in range(2)]
        if not first:
            w_copy.start()
        place = meta_ref[0]
        block, active, row = slot_of(meta_ref, slot)
        last = block // 2
        if first:
            gain = jnp.zeros((GAIN_ROWS, model), f32)
            for k in range(count):
                at = 0
                for ref in views(piece_refs, w_spots[k]):
                    for start in range(0, ref.shape[0], w_rows):
                        if at == 3:
                            wo_ref[aligned(place ^ k, w_rows), :] = ref[start:start + w_rows, :]
                        elif at < 3:
                            w_ref[aligned(place ^ k, w_rows), at * model:(at + 1) * model] = ref[
                                start:start + w_rows, :
                            ]
                        else:
                            r, c = picks(128, model, 0, (place ^ k) * w_rows)
                            gain += dot(ref[start:, :128], one_hot(jnp.logical_and(r == c, r < w_rows)))
                        at += 1
            gain_ref[...] = gain[:8, :]
            w_copy.start()

        def leave(c):
            spot = aligned(c, CHUNK)
            pairs = ((n_ref, n_out), (k_ref, k_out), (v_ref, v_out))
            return [pltpu.make_async_copy(a.at[spot, :], b.at[spot, :], sems.at[i, c]) for i, (a, b) in enumerate(pairs)]

        @pl.when(jnp.logical_not(active))
        def _():
            joined_ref[...] = jnp.zeros(joined_ref.shape, bf16)
            if not first:
                w_copy.wait()

        @pl.when(active)
        def _():
            gain = gain_ref[0:1, :]
            for k in range(count):
                @pl.when((place ^ k) // 2 <= last)
                def _():
                    xb = views(x_refs, x_spots[k])[0][row].astype(f32)
                    n_ref[aligned(place ^ k, width), :] = (xb * inverse_rms(xb) * gain).astype(bf16)

            if not first:
                w_copy.wait()

            def project(c, unused):
                nc = n_ref[aligned(c, CHUNK), :]
                k_ref[aligned(c, CHUNK), :] = dot(nc, w_ref[:, model:2 * model]).astype(bf16)
                v_ref[aligned(c, CHUNK), :] = dot(nc, w_ref[:, 2 * model:3 * model]).astype(bf16)
                for copy in leave(c):
                    copy.start()
                return 0

            lax.fori_loop(0, last + 1, project, 0)
            query = dot(n_ref[aligned(block, width), :], w_ref[:, :model]).astype(bf16)
            q_ref[...] = query
            query_t = query.astype(f32).T
            for part_of in range(2):
                heads_in = range(part_of * heads // 2, (part_of + 1) * heads // 2)
                mix_columns(query_t, pre, qst, heads, heads_in, 0.125, False)
                mx[...] = jnp.full(mx.shape, NEGATIVE, f32)

                def scores(c, diagonal):
                    kc = k_ref[aligned(c, CHUNK), :]
                    for t in range(half // pair):
                        part = slice(t * pair, (t + 1) * pair)
                        s = dot(kc, qst[:, part])
                        if diagonal:
                            s = masked(s, c, block, width, NEGATIVE)
                        s_ref[aligned(c, CHUNK), part] = s
                        mx[:, part] = jnp.maximum(mx[:, part], jnp.max(s.reshape(CHUNK // 8, 8, pair), axis=0))

                lax.fori_loop(0, last, lambda c, unused: (scores(c, False), 0)[1], 0)
                scores(last, True)
                peak = jnp.max(mx[...], axis=0, keepdims=True)
                acc[...] = jnp.zeros(acc.shape, f32)
                mx[...] = jnp.zeros(mx.shape, f32)

                def weigh(c, unused):
                    vc = v_ref[aligned(c, CHUNK), :]
                    for t in range(half // pair):
                        part = slice(t * pair, (t + 1) * pair)
                        p = jnp.exp(s_ref[aligned(c, CHUNK), part] - peak[:, part])
                        mx[:, part] += jnp.sum(p.reshape(CHUNK // 8, 8, pair), axis=0)
                        acc[:, part] += dot(vc, p.astype(bf16), 0, 0)
                    return 0

                lax.fori_loop(0, last + 1, weigh, 0)
                total = jnp.sum(mx[...], axis=0, keepdims=True)
                lse_ref[:, part_of * half:(part_of + 1) * half] = peak + jnp.log(total)
                inverse = 1.0 / total
                for k in range(heads):
                    rows = slice(k * size, (k + 1) * size)
                    out = jnp.zeros((size, width), f32)
                    for i, h in enumerate(heads_in):
                        cols = slice(i * width, (i + 1) * width)
                        u = acc[rows, cols] * inverse[:, cols]
                        ut_ref[part_of, rows, cols] = u.astype(bf16)
                        out += u * post[h, k]
                    if part_of == 0:
                        total_out[rows, :] = out
                    else:
                        total_out[rows, :] += out
                ut_copies[part_of].start()
            joined_ref[...] = total_out[...].T.astype(bf16)

            def gone(c, unused):
                for copy in leave(c):
                    copy.wait()
                return 0

            lax.fori_loop(0, last + 1, gone, 0)
            for copy in ut_copies:
                copy.wait()

        if first:
            w_copy.wait()

    outs = [
        shaped((width, model)), shaped((length, model)), shaped((length, model)), shaped((length, model)),
        shaped((width, model)), shaped((model, half)), shaped((model, half)), shaped((1, lanes), f32),
    ]
    scratch = [
        pltpu.VMEM((model, half), bf16), pltpu.VMEM((length, half), f32),
        pltpu.VMEM((model, half), f32), pltpu.VMEM((8, half), f32), pltpu.VMEM((model, width), f32),
    ] + [pltpu.VMEM((length, model), bf16)] * 3 + [
        pltpu.VMEM((model, 3 * model), bf16), pltpu.VMEM((2, model, half), bf16),
        pltpu.SemaphoreType.DMA((3, length // CHUNK)), pltpu.SemaphoreType.DMA, pltpu.SemaphoreType.DMA((2,)),
    ]
    if first:
        outs += [shaped((model, 3 * model)), shaped((model, model)), shaped((8, model), f32)]
        args = x_arrays + w_arrays
    else:
        args = x_arrays + [w, gains]
    flops = 2 * length * model * (lanes + 2 * model)
    raw_args = () if first else (len(x_arrays),)
    raw_outs = (1, 2, 3, 5, 6) + ((8,) if first else ())
    return call(
        body, f"attend_forward_{slot}", outs, [meta, premix, postmix], args, scratch, flops, (), raw_args, raw_outs
    )


def after_attention(meta, slot, joined, near, far, gains, w):
    width, model = joined.shape

    def body(meta_ref, joined_ref, near_ref, far_ref, gain_ref, w_ref, middle_ref, second_ref):
        row = slot_of(meta_ref, slot)[2]
        residual = jnp.where(row == 0, near_ref[0].astype(f32), far_ref[1].astype(f32))
        middle = residual + dot(joined_ref[...], w_ref[...])
        middle_ref[...] = middle
        second_ref[...] = (middle * inverse_rms(middle) * gain_ref[1:2, :]).astype(bf16)

    outs = [shaped((width, model), f32), shaped((width, model))]
    args = [joined, near, far, gains, w]
    return call(body, f"after_attention_{slot}", outs, [meta], args, (), 2 * width * model * model)


def feed_forward(slot, seconds, ups, inner_w, outer_w):
    width, model = seconds[0].shape
    units = inner_w.shape[1]
    tokens = GROUP * width
    root = 0.7978845608028654
    tile = 256

    def body(*refs):
        s_refs, u_refs = refs[:GROUP], refs[GROUP:2 * GROUP]
        w1, w2, hidden_ref, inner_ref, own_ref, give_ref, across_ref, tok, up = refs[2 * GROUP:]
        for i in range(GROUP):
            tok[i * width:(i + 1) * width, :] = s_refs[i][...]
            up[i * width:(i + 1) * width, :] = u_refs[i][slot]
        for t in range(units // tile):
            part = slice(t * tile, (t + 1) * tile)
            v = dot(tok[...], w1[:, part])
            squared = v * v
            th = jnp.tanh(root * (v + 0.044715 * (squared * v)))
            hidden_ref[:, part] = (0.5 * v * (1.0 + th)).astype(bf16)
            slope = 0.5 * (1.0 + th) + 0.5 * v * (1.0 - th * th) * (root * (1.0 + 0.134145 * squared))
            inner_ref[:, part] = (dot(up[...], w2[part, :], 1, 1) * slope).astype(bf16)
        grad = dot(inner_ref[...], w1[...], 1, 1).astype(bf16)
        own_ref[...] = grad[:width]
        give_ref[:width, :] = grad[width:2 * width]
        give_ref[width:, :] = grad[3 * width:]
        across_ref[...] = grad[2 * width:3 * width]

    outs = [
        shaped((tokens, units)), shaped((tokens, units)), shaped((width, model)), shaped((2 * width, model)),
        shaped((width, model)),
    ]
    scratch = [pltpu.VMEM((tokens, model), bf16)] * 2
    args = list(seconds) + list(ups) + [inner_w, outer_w]
    return call(body, f"feed_forward_{slot}", outs, [], args, scratch, 6 * tokens * model * units)


def feed_weights(meta, seconds, ups, hiddens, inners, outer_w, count):
    width, model = seconds[0][0].shape
    units = hiddens[0].shape[1]
    tokens = 2 * GROUP * width
    half = GROUP * width
    bands = count // GROUP
    rows_out = units // bands

    def body(meta_ref, *refs):
        s_refs, u_refs = refs[:2 * GROUP], refs[2 * GROUP:3 * GROUP]
        h_refs, i_refs, w2 = refs[3 * GROUP:3 * GROUP + 2], refs[3 * GROUP + 2:3 * GROUP + 4], refs[3 * GROUP + 4]
        refs = refs[3 * GROUP + 5:]
        own_ref, give_ref, across_ref = refs[:3]
        inner_out, outer_j = refs[3], refs[4:4 + bands]
        tok, up, hid, inn, grad = refs[4 + bands:]
        for r in range(2):
            for i in range(GROUP):
                spot = slice(r * half + i * width, r * half + (i + 1) * width)
                tok[spot, :] = s_refs[r * GROUP + i][...]
                up[spot, :] = u_refs[i][r]
            hid[r * half:(r + 1) * half, :] = h_refs[r][...]
            inn[r * half:(r + 1) * half, :] = i_refs[r][...]
            out = dot(h_refs[r][...], w2[...]).astype(bf16)
            spot = slice(r * width, (r + 1) * width)
            own_ref[spot, :] = out[:width]
            give_ref[spot, :] = out[width:2 * width]
            give_ref[2 * width + r * width:2 * width + (r + 1) * width, :] = out[3 * width:]
            across_ref[spot, :] = out[2 * width:3 * width]
        inner_out[...] = dot(tok[...], inn[...], 0, 0).astype(bf16)
        grad[...] = dot(hid[...], up[...], 0, 0).astype(bf16)
        for j in range(bands):
            outer_j[j][...] = grad[aligned((meta_ref[0] // GROUP) ^ j, rows_out), :]

    outs = (
        [shaped((2 * width, model)), shaped((4 * width, model)), shaped((2 * width, model))]
        + [shaped((model, units))] + [shaped((rows_out, model))] * bands
    )
    args = list(seconds[0]) + list(seconds[1]) + list(ups) + list(hiddens) + list(inners) + [outer_w]
    scratch = [
        pltpu.VMEM((tokens, model), bf16), pltpu.VMEM((tokens, model), bf16), pltpu.VMEM((tokens, units), bf16),
        pltpu.VMEM((tokens, units), bf16), pltpu.VMEM((units, model), bf16),
    ]
    made = call(
        body, "feed_weights", outs, [meta], args, scratch, 6 * tokens * model * units
    )
    return made[:3], made[3], list(made[4:])


def before_attention_back(meta, slot, own, got, came, middle, up, gains, w, joineds, casts, inner_grads, count, after):
    width, model = own.shape
    last = joineds is not None
    rows = model // count

    def body(meta_ref, own_ref, got_ref, came_ref, middle_ref, up_ref, gain_ref, w_ref, *refs):
        if last:
            joined_refs, cast_in, inner_ref, refs = refs[:2], refs[2], refs[3], refs[4:]
        grad_ref, cast_ref, upstream_ref = refs[:3]
        second = own_ref[...].astype(f32) + got_ref[:width, :].astype(f32) + came_ref[...].astype(f32)
        back = norm_back(middle_ref[...], gain_ref[1:2, :], second)
        grad = up_ref[slot].astype(f32) + back
        grad_ref[...] = grad
        cast = grad.astype(bf16)
        cast_ref[...] = cast
        upstream_ref[...] = dot(cast, w_ref[...], 1, 1).astype(bf16)
        if last:
            total = dot(joined_refs[0][...], cast_in[...], 0, 0) + dot(joined_refs[1][...], cast, 0, 0)
            for j in range(count):
                refs[3][j, :rows, :] = total[j * rows:(j + 1) * rows, :].astype(bf16)
                refs[3][j, rows:, :] = inner_ref[j * rows:(j + 1) * rows, :]

    outs = [shaped((width, model), f32), shaped((width, model)), shaped((width, model))]
    args = [own, got, came, middle, up, gains, w]
    if last:
        outs.append(shaped((count, 2 * rows, model)))
        args += list(joineds) + [casts, inner_grads]
    return call(
        body, f"before_attention_back_{slot}", outs, [meta], args, (), 4 * width * model * model, after
    )


def attend_back(meta, premix, postmix, queries, upstreams, normeds, keys, values, uts, lses, count, after):
    width, model = queries[0].shape
    length = keys[0].shape[0]
    heads = premix.shape[0]
    size = model // heads
    pair = 2 * width
    lanes = heads * width
    half = lanes // 2
    w_rows = model // count

    def body(meta_ref, pre, post, pre_ref, post_ref, *refs):
        q_refs, up_refs, n_refs, k_refs, v_refs, lse_refs = (refs[2 * i:2 * i + 2] for i in range(6))
        ut_refs, refs = refs[12:16], refs[16:]
        dq_refs, dk_refs, dv_refs, (mix_ref, keep_ref, give_ref), refs = (
            refs[:2], refs[2:4], refs[4:6], refs[6:9], refs[9:]
        )
        qst, qs, ust, us, acc, pbuf, lbuf, dots, wacc, cin, cout, n_own, ut_held, in_sems, out_sems, own_sem, ut_sems = refs
        ut_copies = [pltpu.make_async_copy(ut_refs[i], ut_held.at[i], ut_sems.at[i]) for i in range(4)]
        wacc[...] = jnp.zeros(wacc.shape, f32)
        head = lax.broadcasted_iota(jnp.int32, (heads, model), 1) // size
        spread = jnp.where(head == lax.broadcasted_iota(jnp.int32, (heads, model), 0), 1.0, 0.0)
        pre_row = lax.dot_general(
            pre_ref[...], spread, (((0,), (0,)), ((), ())), precision=HIGH, preferred_element_type=f32
        )
        post_row = lax.dot_general(
            post_ref[...], spread, (((1,), (0,)), ((), ())), precision=HIGH, preferred_element_type=f32
        )
        mix_ref[...] = jnp.zeros(mix_ref.shape, f32)
        for slot in range(2):
            block, active, unused_row = slot_of(meta_ref, slot)
            last = block // 2

            @pl.when(jnp.logical_not(active))
            def _():
                dq_refs[slot][...] = jnp.zeros(dq_refs[slot].shape, bf16)

            @pl.when(active)
            def _():
                def fetch(c):
                    sources = (k_refs[slot], v_refs[slot], n_refs[slot])
                    return [
                        pltpu.make_async_copy(a.at[aligned(c, CHUNK), :], cin.at[c % 2, i], in_sems.at[c % 2, i])
                        for i, a in enumerate(sources)
                    ]

                def leave(c):
                    targets = (dk_refs[slot], dv_refs[slot])
                    return [
                        pltpu.make_async_copy(cout.at[c % 2, i], a.at[aligned(c, CHUNK), :], out_sems.at[c % 2, i])
                        for i, a in enumerate(targets)
                    ]

                own = pltpu.make_async_copy(n_refs[slot].at[aligned(block, width), :], n_own, own_sem)
                own.start()
                for copy in fetch(0) + ut_copies[2 * slot:2 * slot + 2]:
                    copy.start()
                q = q_refs[slot][...].astype(f32)
                up = up_refs[slot][...].astype(f32)
                qt, upt = q.T, up.T
                mix_columns(qt, pre, qst, heads, range(heads), 0.125, False)
                mix_columns(upt, post, ust, heads, range(heads), 1.0, True)
                for copy in ut_copies[2 * slot:2 * slot + 2]:
                    copy.wait()
                for h in range(heads):
                    spot = slice(h * width, (h + 1) * width)
                    qs[spot, :] = (q * (pre_row[h:h + 1, :] * 0.125)).astype(bf16)
                    us[spot, :] = (up * post_row[h:h + 1, :]).astype(bf16)
                    column = h % (heads // 2) * width
                    u = ut_held[2 * slot + (h >= heads // 2), :, column:column + width].astype(f32)
                    t = jnp.sum((u * upt).reshape(heads, size, width), axis=1)
                    mix_ref[heads + h] += t
                    d = jnp.zeros((1, width), f32)
                    for k in range(heads):
                        d += t[k:k + 1, :] * post[h, k]
                    dots[:, spot] = d
                acc[...] = jnp.zeros(acc.shape, f32)

                def visit(c, diagonal):
                    for copy in fetch(c):
                        copy.wait()
                    if not diagonal:
                        for copy in fetch(c + 1):
                            copy.start()
                    kc, vc = cin[c % 2, 0], cin[c % 2, 1]
                    for t in range(heads // 2):
                        part = slice(t * pair, (t + 1) * pair)
                        p = jnp.exp(dot(kc, qst[:, part]) - lse_refs[slot][:, part])
                        if diagonal:
                            p = masked(p, c, block, width, 0.0)
                        grad = (p * (dot(vc, ust[:, part]) - dots[:, part])).astype(bf16)
                        pbuf[:, part] = p.astype(bf16)
                        lbuf[:, part] = grad
                        acc[:, part] += dot(kc, grad, 0, 0)

                    @pl.when(c >= 2)
                    def _():
                        for copy in leave(c - 2):
                            copy.wait()

                    dk = dot(lbuf[...], qs[...]).astype(bf16)
                    dv = dot(pbuf[...], us[...]).astype(bf16)
                    cout[c % 2, 0] = dk
                    cout[c % 2, 1] = dv
                    for copy in leave(c):
                        copy.start()
                    nc = cin[c % 2, 2]
                    wacc[:, model:2 * model] += dot(nc, dk, 0, 0)
                    wacc[:, 2 * model:] += dot(nc, dv, 0, 0)

                lax.fori_loop(0, last, lambda c, unused: (visit(c, False), 0)[1], 0)
                visit(last, True)
                for g in range(heads):
                    rows = slice(g * size, (g + 1) * size)
                    out = jnp.zeros((size, width), f32)
                    qg = qt[rows, :] * 0.125
                    for h in range(heads):
                        a = acc[rows, h * width:(h + 1) * width]
                        out += a * pre[g, h]
                        mix_ref[g, h:h + 1, :] += jnp.sum(a * qg, axis=0, keepdims=True)
                    acc[rows, 0:width] = out * 0.125
                dq = acc[:, 0:width].T.astype(bf16)
                dq_refs[slot][...] = dq
                own.wait()
                wacc[:, :model] += dot(n_own[...], dq, 0, 0)

                @pl.when(last >= 1)
                def _():
                    for copy in leave(last - 1):
                        copy.wait()

                for copy in leave(last):
                    copy.wait()

        for k in range(count):
            (keep_ref, give_ref)[k % 2][k // 2 * w_rows:(k // 2 + 1) * w_rows, :] = wacc[
                aligned(meta_ref[0] ^ k, w_rows), :
            ].astype(bf16)

    outs = (
        [shaped((width, model))] * 2 + [shaped((length, model))] * 4
        + [shaped((2 * heads, heads, width), f32)] + [shaped((count // 2 * w_rows, 3 * model))] * 2
    )
    scratch = [
        pltpu.VMEM((model, lanes), bf16), pltpu.VMEM((lanes, model), bf16), pltpu.VMEM((model, lanes), bf16),
        pltpu.VMEM((lanes, model), bf16), pltpu.VMEM((model, lanes), f32), pltpu.VMEM((CHUNK, lanes), bf16),
        pltpu.VMEM((CHUNK, lanes), bf16), pltpu.VMEM((1, lanes), f32), pltpu.VMEM((model, 3 * model), f32),
        pltpu.VMEM((2, 3, CHUNK, model), bf16), pltpu.VMEM((2, 2, CHUNK, model), bf16), pltpu.VMEM((width, model), bf16),
        pltpu.VMEM((4, model, half), bf16), pltpu.SemaphoreType.DMA((2, 3)), pltpu.SemaphoreType.DMA((2, 2)),
        pltpu.SemaphoreType.DMA, pltpu.SemaphoreType.DMA((4,)),
    ]
    args = (
        [premix, postmix] + list(queries) + list(upstreams) + list(normeds) + list(keys) + list(values) + list(lses)
        + list(uts)
    )
    made = call(
        body, "attend_back", outs, [meta, premix, postmix], args, scratch, 15 * length * model * lanes, after,
        tuple(range(6, 12)) + tuple(range(14, 18)), range(2, 6),
    )
    return made[:2], made[2:4], made[4:6], made[6], made[7], made[8]


def input_back(meta, dqs, dks, dvs, w, x_pieces, gains, grads, after):
    count = len(x_pieces)
    x_arrays, x_spots = listed(x_pieces)
    width, model = dqs[0].shape
    length = dks[0].shape[0]

    def body(meta_ref, *refs):
        dq_refs, dk_refs, dv_refs, grad_refs = refs[:2], refs[2:4], refs[4:6], refs[6:8]
        w_in, gain_ref, refs = refs[8], refs[9], refs[10:]
        x_refs, refs = refs[:len(x_arrays)], refs[len(x_arrays):]
        keep_ref, give_ref, normed, dk_held, dv_held, w_ref, sems, w_sem = refs
        w_copy = pltpu.make_async_copy(w_in, w_ref, w_sem)
        w_copy.start()
        place = meta_ref[0]

        def fetch(slot, c):
            spot = aligned(c, CHUNK)
            return [
                pltpu.make_async_copy(a.at[spot, :], b.at[slot, spot, :], sems.at[slot, c, i])
                for i, (a, b) in enumerate(((dk_refs[slot], dk_held), (dv_refs[slot], dv_held)))
            ]

        def begin(slot, c):
            for copy in fetch(slot, c):
                copy.start()
            return 0

        for slot in range(2):
            block, active, row = slot_of(meta_ref, slot)
            chunks = jnp.where(active, block // 2 + 1, 0)
            lax.fori_loop(0, chunks, lambda c, unused, slot=slot: begin(slot, c), 0)
        w_copy.wait()

        for slot in range(2):
            block, active, row = slot_of(meta_ref, slot)

            @pl.when(active)
            def _():
                def visit(c, unused):
                    spot = aligned(c, CHUNK)
                    for copy in fetch(slot, c):
                        copy.wait()
                    normed[spot, :] = dot(dk_held[slot, spot, :], w_ref[:, model:2 * model], 1, 1) + dot(
                        dv_held[slot, spot, :], w_ref[:, 2 * model:3 * model], 1, 1
                    )
                    return 0

                lax.fori_loop(0, block // 2 + 1, visit, 0)
                normed[aligned(block, width), :] += dot(dq_refs[slot][...], w_ref[:, :model], 1, 1)

            for k in range(count):
                out_ref = (keep_ref, give_ref)[k % 2]
                spot = aligned((k // 2) * 2 + row, width)
                used = jnp.logical_and(active, (place ^ k) <= block)

                @pl.when(jnp.logical_not(used))
                def _():
                    out_ref[spot, :] = jnp.zeros((width, model), bf16)

                @pl.when(used)
                def _():
                    back = norm_back(
                        views(x_refs, x_spots[k])[0][row].astype(f32), gain_ref[0:1, :], normed[aligned(place ^ k, width), :]
                    )
                    factor = jnp.where((place ^ k) == block, 1.0, 0.0)
                    out_ref[spot, :] = (back + grad_refs[slot][...] * factor).astype(bf16)

    half = count * width
    outs = [shaped((half, model)), shaped((half, model))]
    args = list(dqs) + list(dks) + list(dvs) + list(grads) + [w, gains] + x_arrays
    scratch = [
        pltpu.VMEM((length, model), f32), pltpu.VMEM((2, length, model), bf16), pltpu.VMEM((2, length, model), bf16),
        pltpu.VMEM((model, 3 * model), bf16), pltpu.SemaphoreType.DMA((2, length // CHUNK, 2)), pltpu.SemaphoreType.DMA,
    ]
    return call(body, "input_back", outs, [meta], args, scratch, 8 * length * model * model, after, (2, 3, 4, 5, 8))


def pair_sums(keep, got, count, later, after, name):
    blocks = count // 2
    rows, columns = keep.shape[0] // blocks, keep.shape[1]

    def body(keep_ref, got_ref, *refs):
        outs = refs[len(later):]
        for source, target in zip(refs, outs[blocks:]):
            target[...] = source[...]
        for i in range(blocks):
            spot = slice(i * rows, (i + 1) * rows)
            outs[i][...] = (keep_ref[spot, :].astype(f32) + got_ref[spot, :].astype(f32)).astype(outs[i].dtype)

    outs = [shaped((rows, columns), f32)] + [shaped((rows, columns))] * (blocks - 1)
    outs += [shaped(a.shape, a.dtype) for a in later]
    made = call(body, name, outs, [], [keep, got] + list(later), (), 0, after)
    return made[:blocks], made[blocks:]


def split_dp(meta, depth, parts, after):
    joined, wide = parts[0].shape
    size = joined // depth

    def body(meta_ref, *refs):
        ins, outs = refs[:len(parts)], refs[len(parts):]
        total = ins[0][...].astype(f32)
        for ref in ins[1:]:
            total += ref[...].astype(f32)
        total = total.astype(bf16)
        for m in range(depth):
            r, c = picks(size, joined, 0, (meta_ref[1] ^ m) * size)
            outs[m][...] = dot(one_hot(r == c), total).astype(bf16)

    return call(body, "split_dp", [shaped((size, wide))] * depth, [meta], list(parts), (), 0, after)


def split_feed(meta, depth, grads, outer, size, after):
    count, joined, units = grads.shape
    joined //= 2
    bands = len(outer)
    band = outer[0].shape[0]
    shard = band // depth
    parts = 1 + GROUP
    out_rows = parts * size + shard

    def body(meta_ref, grad_ref, *refs):
        o_refs, outs, total = refs[:bands], refs[bands:-1], refs[-1]
        section = grad_ref[0, :joined, :].astype(f32)
        for j in range(1, count):
            section += grad_ref[j, :joined, :].astype(f32)
        total[:joined, :] = section.astype(bf16)
        for t in range(GROUP):
            section = grad_ref[t, joined:, :].astype(f32)
            for j in range(1, bands):
                section += grad_ref[j * GROUP + t, joined:, :].astype(f32)
            total[(1 + t) * joined:(2 + t) * joined, :] = section.astype(bf16)
        rest = o_refs[0][...].astype(f32)
        for j in range(1, bands):
            rest += o_refs[j][...].astype(f32)
        total[parts * joined:, :] = rest.astype(bf16)
        for d in range(depth):
            r = lax.broadcasted_iota(jnp.int32, (out_rows, parts * joined + band), 0)
            c = lax.broadcasted_iota(jnp.int32, (out_rows, parts * joined + band), 1)
            inner_c = (r // size) * joined + d * size + r % size
            outer_c = parts * joined + d * shard + r - parts * size
            outs[0][d] = dot(one_hot(c == jnp.where(r < parts * size, inner_c, outer_c)), total[...]).astype(bf16)

    scratch = [pltpu.VMEM((parts * joined + band, units), bf16)]
    return call(body, "split_feed", [shaped((depth, out_rows, units))], [meta], [grads] + list(outer), scratch, 0, after)[0]


def finish_projections(pieces, weights, gain):
    size, wide = pieces[0].shape
    parts = 3
    model = wide // parts

    def body(*refs):
        ins, w_refs, gain_ref, outs = refs[:len(pieces)], refs[len(pieces):-5], refs[-5], refs[-4:]
        along = jnp.zeros((size, 1), f32)
        for i in range(parts):
            part = slice(i * model, (i + 1) * model)
            total = ins[0][:, part].astype(f32)
            for ref in ins[1:]:
                total += ref[:, part].astype(f32)
            outs[i][...] = total
            along += jnp.sum(total * w_refs[i][...].astype(f32), axis=1, keepdims=True)
        outs[3][...] = along / gain_ref[...]

    outs = [shaped((size, model), f32)] * parts + [shaped((size, 1), f32)]
    return call(body, "finish_projections", outs, [], list(pieces) + list(weights) + [gain])


def finish_feed(pieces, weight, gain, bands):
    size = weight.shape[0]
    depth, rows, units = pieces.shape
    band = units // bands

    def body(in_ref, w_ref, gain_ref, output_ref, inner_ref, outer_ref, gain_out):
        total = in_ref[0].astype(f32)
        for d in range(1, depth):
            total += in_ref[d].astype(f32)
        output_ref[...] = total[:size, :]
        for t in range(GROUP):
            for y in range(bands):
                inner_ref[:, (y * GROUP + t) * band:(y * GROUP + t + 1) * band] = total[
                    (1 + t) * size:(2 + t) * size, y * band:(y + 1) * band
                ]
        outer_ref[...] = total[(1 + GROUP) * size:, :]
        along = jnp.sum(inner_ref[...] * w_ref[...].astype(f32), axis=1, keepdims=True)
        gain_out[...] = along / gain_ref[...]

    outs = [
        shaped((size, units), f32), shaped((size, GROUP * units), f32),
        shaped((rows - (1 + GROUP) * size, units), f32), shaped((size, 1), f32),
    ]
    return call(body, "finish_feed", outs, [], [pieces, weight, gain])


def swap(value, axis, mask):
    count = lax.axis_size(axis)
    return lax.ppermute(value, axis, [(i, i ^ mask) for i in range(count)])


def gather_dp(value):
    return [value] + [swap(value, "dp", m) for m in range(1, lax.axis_size("dp"))]


def gather_first(meta, inputs, first_w):
    count, depth = lax.axis_size("blk"), lax.axis_size("dp")
    pieces = gather_dp(first_w)
    x_links = [inputs, swap(inputs, "blk", 2), swap(inputs, "blk", 4)]
    w_own, x_on_two, x_on_four, x_core = join_dp(meta, pieces, x_links)
    w_links = [w_own, swap(w_own, "blk", 2), swap(w_own, "blk", 4)]
    if count == 8:
        halves = [swap(x_on_two, "blk", 2), swap(x_on_four, "blk", 4)]
        x_core = swap(x_core, "blk", 1)
        w_on_two, w_on_four, w_core, x_across = forward_across(w_links, halves)
        w_across = [swap(w_on_two, "blk", 2), swap(w_on_four, "blk", 4)]
        w_core, x_far = swap(w_core, "blk", 1), swap(x_across, "blk", 1)
        w_far = [swap(part, "blk", 1) for part in w_across]
        xs = [[(a, None)] for a in x_links] + [[(x_across, None)]]
        ws = [[(a, None)] for a in w_links] + [[(a, None) for a in w_across]]
        xs_core = [[(x_core, i)] for i in range(3)] + [[(x_far, None)]]
        ws_core = [[(w_core, i)] for i in range(3)] + [[(a, None) for a in w_far]]
    else:
        x_links += [swap(inputs, "blk", k) for k in range(6, count, 2)]
        w_links += [swap(w_own, "blk", k) for k in range(6, count, 2)]
        xs, ws = [[(a, None)] for a in x_links], [[(a, None)] for a in w_links]
        xs_core, ws_core = [[(swap(a, "blk", 1), None)] for a in x_links], [[(swap(a, "blk", 1), None)] for a in w_links]
    x_pieces = [part for pair in zip(xs, xs_core) for part in pair]
    w_pieces = [part for pair in zip(ws, ws_core) for part in pair]
    return x_pieces, w_pieces


def all_to_all(value, axis):
    return lax.all_to_all(value, axis, 0, 0, tiled=True)


def gather_group(value):
    two = swap(value, "blk", 2)
    return [value, swap(value, "blk", 1), two, swap(two, "blk", 1)]


def scatter_chips(parts):
    return [parts[0]] + [swap(part, "blk", 2 * i) for i, part in enumerate(parts) if i]


def on_device(
    inputs, lengths, prenorm, midnorm, query_proj, key_proj, value_proj, output_proj,
    premix, postmix, inner_proj, outer_proj, cotangent,
):
    count, depth = lax.axis_size("blk"), lax.axis_size("dp")
    place, zplace = lax.axis_index("blk"), lax.axis_index("dp")
    rows, width, model = inputs.shape
    shard = prenorm.shape[0]
    low = place < count // 2
    mirror = count - 1
    slot_rows = [jnp.where(low, 1, 0), jnp.where(low, 0, 1)]
    blocks = [jnp.maximum(place, place ^ mirror), jnp.minimum(place, place ^ mirror)]
    spans = [jnp.where(slot_rows[i] == 0, lengths[0], lengths[1]) for i in range(2)]
    meta = [place, zplace]
    for i in range(2):
        meta += [blocks[i], (blocks[i] * width < spans[i]).astype(jnp.int32), slot_rows[i], spans[i]]
    meta = jnp.stack(meta).astype(jnp.int32)

    bands = count // GROUP
    band_ff = depth * outer_proj.shape[0]
    sections = inner_proj.reshape(shard, bands, GROUP, band_ff).transpose(2, 0, 1, 3)
    second_w = jnp.concatenate([sections.reshape(GROUP * shard, bands * band_ff), outer_proj], axis=0)
    second_w = lax.all_gather(second_w, "dp")
    first_w = pack_first([query_proj, key_proj, value_proj, output_proj], jnp.stack([prenorm, midnorm]))
    x_pieces, w_pieces = gather_first(meta, inputs, first_w)

    fwd = [None] * 2
    fwd[0] = attend_forward(meta, premix, postmix, 0, x_pieces, w_pieces, None, None)
    w, output_w, gain_rows = fwd[0][8:]
    sent, outer_rows = join_feed(second_w, shard, count, [fwd[0][0]])
    inner_w = all_to_all(sent, "blk").reshape(model, -1)
    outer_w = join_bands(
        meta, [outer_rows] + [swap(outer_rows, "blk", GROUP * j) for j in range(1, bands)], "join_bands"
    )
    up = masked_cotangent(meta, cotangent, swap(cotangent[1], "blk", mirror), [fwd[0][0]])
    ups = gather_group(up)
    fwd[1] = attend_forward(meta, premix, postmix, 1, x_pieces, None, w, gain_rows)
    mid = [
        after_attention(meta, i, fwd[i][0], inputs, x_pieces[mirror][0][0], gain_rows, output_w) for i in range(2)
    ]
    seconds = [gather_group(mid[i][1]) for i in range(2)]
    feed = [feed_forward(i, seconds[i], ups, inner_w, outer_w) for i in range(2)]
    gots, came = [], []
    for i in range(2):
        gots.append(swap(feed[i][3], "blk", 1))
        across = (feed[i][4].astype(f32) + gots[i][width:].astype(f32)).astype(bf16)
        came.append(swap(across, "blk", 2))
    (out_own, out_give, out_across), inner_grads, outer_grads = feed_weights(
        meta, seconds, ups, [f[0] for f in feed], [f[1] for f in feed], outer_w, count
    )

    pre = []
    for i in range(2):
        last = i == 1
        pre.append(before_attention_back(
            meta, i, feed[i][2], gots[i], came[i], mid[i][0], up, gain_rows, output_w,
            [fwd[0][0], fwd[1][0]] if last else None, pre[0][1] if last else None, inner_grads, count, [out_own],
        ))

    out_got = swap(out_give, "blk", 1)
    out_across = (out_across.astype(f32) + out_got[2 * width:].astype(f32)).astype(bf16)
    feed_grads = all_to_all(pre[1][3], "blk")
    outer_grads = [outer_grads[0]] + [swap(outer_grads[j], "blk", GROUP * j) for j in range(1, bands)]

    dqs, dks, dvs, mixes, keep, give = attend_back(
        meta, premix, postmix, [f[4] for f in fwd], [p[2] for p in pre], [f[1] for f in fwd], [f[2] for f in fwd],
        [f[3] for f in fwd], [fwd[0][5], fwd[0][6], fwd[1][5], fwd[1][6]], [f[7] for f in fwd], count, [out_across],
    )
    out_came = swap(out_across, "blk", 2)
    outer = out_own.astype(f32) + out_got[:2 * width].astype(f32) + out_came.astype(f32)
    results = []
    for i in range(2):
        position = blocks[i] * width + jnp.arange(width, dtype=jnp.int32)
        value = mid[i][0] + outer[i * width:(i + 1) * width]
        results.append(jnp.where((position < spans[i])[:, None], value, 0.0).astype(bf16))
    near, far = jnp.where(low, results[1], results[0]), jnp.where(low, results[0], results[1])
    outputs = jnp.stack([near, swap(far, "blk", mirror)])

    heads = premix.shape[0]
    mixes = jnp.sum(mixes, axis=-1).reshape(-1)
    mixes = jnp.pad(mixes, (0, -mixes.shape[0] % 1024)).reshape(-1, 128)
    input_keep, input_give = input_back(
        meta, dqs, dks, dvs, w, x_pieces, gain_rows, [p[0] for p in pre], [keep, feed_grads, out_came]
    )
    projected, (mixes,) = pair_sums(keep, swap(give, "blk", 1), count, [mixes], [], "pair_sums_w")
    cuts = split_feed(meta, depth, feed_grads, outer_grads, shard, [projected[0]])
    output_sum, inner_sum, outer_sum, mid_gain = finish_feed(
        all_to_all(cuts, "dp"), inner_proj, midnorm.astype(f32)[:, None], bands
    )
    everyone = count * depth
    mixes = lax.all_to_all(jnp.broadcast_to(mixes, (everyone, *mixes.shape)), ("blk", "dp"), 0, 0, tiled=True)
    mixes = jnp.sum(mixes, axis=0).reshape(-1)[:2 * heads * heads].reshape(2, heads, heads)
    projected = scatter_chips(projected)
    input_parts, unused = pair_sums(input_keep, swap(input_give, "blk", 1), count, [], [outputs], "pair_sums_x")
    input_parts = scatter_chips(input_parts)
    cuts = split_dp(meta, depth, projected, [])
    query_sum, key_sum, value_sum, pre_gain = finish_projections(
        [cuts[0]] + [swap(cuts[m], "dp", m) for m in range(1, depth)],
        [query_proj, key_proj, value_proj], prenorm.astype(f32)[:, None],
    )
    grad_inputs = sum([part.astype(f32) for part in input_parts[1:]], input_parts[0]).astype(bf16).reshape(inputs.shape)
    return (
        outputs,
        grad_inputs,
        pre_gain.reshape(-1),
        mid_gain.reshape(-1),
        query_sum,
        key_sum,
        value_sum,
        output_sum,
        mixes[0],
        mixes[1],
        inner_sum,
        outer_sum,
    )


def solution(mesh):
    weight = P(("blk", "dp"), None)
    vector = P(("blk", "dp"))
    tokens = P("dp", "blk", None)
    in_specs = (
        tokens, P("dp"), vector, vector, weight, weight, weight, weight, P(), P(), weight, weight, tokens,
    )
    out_specs = (
        tokens, tokens, vector, vector, weight, weight, weight, weight, P(), P(), weight, weight,
    )
    return jax.shard_map(on_device, mesh=mesh, in_specs=in_specs, out_specs=out_specs, check_vma=False)
```

```python
import jax
import jax.numpy as jnp
from jax import lax
from jax.experimental import pallas as pl
from jax.experimental.pallas import tpu as pltpu
from jax.sharding import PartitionSpec as P

EPSILON = 1e-06
GROUP = 4
CHUNK = 256
NEGATIVE = -1e30
VMEM_MOST = 60 * 1024 * 1024
VMEM_SPARE = 8 * 1024 * 1024
VMEM_WINDOWS = 18 * 1024 * 1024
GAIN_ROWS = 16
f32 = jnp.float32
bf16 = jnp.bfloat16
HIGH = lax.Precision.HIGHEST
ANY_SPEC = pl.BlockSpec(memory_space=pl.ANY)
VMEM_SPEC = pl.BlockSpec(memory_space=pltpu.VMEM)
HBM_SPEC = pl.BlockSpec(memory_space=pltpu.HBM)
SMEM_SPEC = pl.BlockSpec(memory_space=pltpu.SMEM)


def shaped(shape, dtype=bf16):
    return jax.ShapeDtypeStruct(shape, dtype)


def vmem_bytes(shape, dtype):
    lead, (rows, columns) = shape[:-2], shape[-2:]
    size = jnp.dtype(dtype).itemsize
    for extent in lead:
        size *= extent
    return size * -(-rows // 16) * 16 * -(-columns // 128) * 128


def call(body, name, outs, smem, args, scratch=(), flops=0, after=(), raw_args=(), raw_outs=(), extra=0):
    n_smem, n_args = len(smem), len(args)
    arrays = list(args) + list(outs)
    windows = [a for i, a in enumerate(args) if i not in raw_args] + [a for i, a in enumerate(outs) if i not in raw_outs]
    windows = sum(vmem_bytes(a.shape, a.dtype) for a in windows)
    held = sum(vmem_bytes(a.shape, a.dtype) for a in scratch if getattr(a, "memory_space", None) == pltpu.VMEM)
    held += VMEM_SPARE + extra + (windows if windows > VMEM_WINDOWS else 0)

    def kernel(*refs):
        first = n_smem + n_args
        body(*refs[:first], *refs[first + len(after):])

    return pl.pallas_call(
        kernel,
        out_shape=tuple(pltpu.HBM(a.shape, a.dtype) if i in raw_outs else a for i, a in enumerate(outs)),
        in_specs=[SMEM_SPEC] * n_smem
        + [HBM_SPEC if i in raw_args else VMEM_SPEC for i in range(n_args)] + [ANY_SPEC] * len(after),
        out_specs=tuple(HBM_SPEC if i in raw_outs else VMEM_SPEC for i in range(len(outs))),
        scratch_shapes=list(scratch),
        compiler_params=pltpu.CompilerParams(vmem_limit_bytes=min(VMEM_MOST, held)),
        cost_estimate=pl.CostEstimate(
            flops=flops, bytes_accessed=sum(a.size * a.dtype.itemsize for a in arrays), transcendentals=0
        ),
        name=name,
    )(
        *smem,
        *[pltpu.with_memory_space_constraint(a, pltpu.HBM) if i in raw_args else a for i, a in enumerate(args)],
        *after,
    )


def begin(pairs, sems):
    copies = [pltpu.make_async_copy(a, b, sems.at[i]) for i, (a, b) in enumerate(pairs)]
    for copy in copies:
        copy.start()
    return copies


def finish(copies):
    for copy in copies:
        copy.wait()


def dma(count):
    return pltpu.SemaphoreType.DMA((count,))


def dot(a, b, ca=1, cb=0):
    return lax.dot_general(a, b, (((ca,), (cb,)), ((), ())), preferred_element_type=f32)


def picks(rows, columns, start_row, start_column=0):
    r = lax.broadcasted_iota(jnp.int32, (rows, columns), 0) - start_row
    c = lax.broadcasted_iota(jnp.int32, (rows, columns), 1) - start_column
    return r, c


def one_hot(mask):
    return jnp.where(mask, 1.0, 0.0).astype(bf16)


def inverse_rms(values):
    return lax.rsqrt(jnp.mean(values * values, axis=-1, keepdims=True) + EPSILON)


def norm_back(values, gain, grad):
    inverse = inverse_rms(values)
    scaled = grad * gain
    mean = jnp.mean(scaled * values, axis=-1, keepdims=True)
    return inverse * (scaled - values * (inverse * inverse * mean))


def aligned(index, size):
    return pl.ds(pl.multiple_of(index * size, size), size)


def pack_first(weights, gains):
    size, model = weights[0].shape
    parts = len(weights)

    def body(*refs):
        gain_ref, out_ref, held, sems = refs[parts:]
        copies = begin([(refs[i], held.at[i]) for i in range(parts)], sems)
        r, c = picks(size, model, 0)
        along = dot(gain_ref[...], one_hot(r == c)).astype(bf16)
        r, c = picks(GAIN_ROWS, 2, 0)
        out_ref[parts * size:, :] = dot(one_hot(r == c), along).astype(bf16)
        finish(copies)
        for i in range(parts):
            out_ref[i * size:(i + 1) * size, :] = held[i]

    scratch = [pltpu.VMEM((parts, size, model), bf16), dma(parts)]
    outs = [shaped((parts * size + GAIN_ROWS, model))]
    return call(
        body, "pack_first", outs, [], list(weights) + [gains], scratch, raw_args=tuple(range(parts))
    )[0]


def join_dp(meta, pieces, x_links):
    depth = len(pieces)
    total_rows, model = pieces[0].shape
    size = (total_rows - GAIN_ROWS) // 4
    joined = size * depth
    links = len(x_links)
    lanes = 128

    def body(meta_ref, *refs):
        ins, x_refs, outs, sems = refs[:depth], refs[depth:depth + links], refs[depth + links:-1], refs[-1]
        pairs = [(x_refs[2].at[0], outs[1]), (x_refs[1].at[1], outs[2])]
        copies = begin(pairs + [(x_refs[i], outs[3].at[i]) for i in range(links)], sems)
        total = jnp.zeros((4 * joined, model), f32)
        gains = jnp.zeros((GAIN_ROWS, lanes), f32)
        for m in range(depth):
            d = meta_ref[1] ^ m
            r = lax.broadcasted_iota(jnp.int32, (4 * joined, total_rows), 0)
            c = lax.broadcasted_iota(jnp.int32, (4 * joined, total_rows), 1)
            want = jnp.where((r % joined) // size == d, (r // joined) * size + r % size, -1)
            total += dot(one_hot(c == want), ins[m][...])
            r, c = picks(lanes, lanes, 0, d * size)
            gains += dot(ins[m][4 * size:, :lanes], one_hot(jnp.logical_and(r == c, r < size)))
        outs[0][:4 * joined, :] = total.astype(bf16)
        outs[0][4 * joined:, :] = jnp.zeros((GAIN_ROWS, model), bf16)
        outs[0][4 * joined:, :lanes] = gains.astype(bf16)
        finish(copies)

    rows, width, model = x_links[0].shape
    outs = [
        shaped((4 * joined + GAIN_ROWS, model)), shaped((width, model)), shaped((width, model)),
        shaped((links, rows, width, model)),
    ]
    return call(
        body, "join_dp", outs, [meta], list(pieces) + list(x_links), [dma(2 + links)],
        raw_args=tuple(range(depth, depth + links)),
    )


def forward_across(w_links, x_halves):
    total_rows, model = w_links[0].shape
    cut_at = (total_rows - GAIN_ROWS) // 2
    links = len(w_links)

    def body(*refs):
        w_refs, h_refs, outs = refs[:links], refs[links:links + 2], refs[links + 2:]
        outs[0][...] = w_refs[2][:cut_at, :]
        outs[1][...] = w_refs[1][cut_at:, :]
        for i in range(links):
            outs[2][i] = w_refs[i][...]
        for i in range(2):
            outs[3][i] = h_refs[i][...]

    outs = [
        shaped((cut_at, model)), shaped((total_rows - cut_at, model)), shaped((links, total_rows, model)),
        shaped((2, *x_halves[0].shape)),
    ]
    return call(body, "forward_across", outs, [], list(w_links) + list(x_halves))


def join_feed(meta, pieces, size, count, after):
    depth, total_rows, model = pieces.shape
    bands = count // GROUP
    band = (total_rows - count * size) // bands

    def body(meta_ref, in_ref, inner_ref, outer_ref, held, joined, sems):
        copies = begin([(in_ref.at[d], held.at[d]) for d in range(depth)], sems)
        for d in range(depth):
            copies[d].wait()
            for k in range(count):
                inner_ref[(k * depth + d) * size:(k * depth + d + 1) * size, :] = held[d, k * size:(k + 1) * size, :]
            for j in range(bands):
                start = count * size + j * band
                joined[j, d * band:(d + 1) * band, :] = held[d, start:start + band, :]
        for j in range(bands):
            outer_ref[aligned((meta_ref[0] // GROUP) ^ j, band * depth), :] = joined[j]

    outs = [shaped((count * depth * size, model)), shaped((bands * band * depth, model))]
    scratch = [
        pltpu.VMEM((depth, total_rows, model), bf16), pltpu.VMEM((bands, band * depth, model), bf16), dma(depth),
    ]
    return call(body, "join_feed", outs, [meta], [pieces], scratch, 0, after, (0,))


def slot_of(meta_ref, slot):
    return meta_ref[2 + 4 * slot], meta_ref[3 + 4 * slot] > 0, meta_ref[4 + 4 * slot]


def masked_cotangent(meta, own, far, after):
    rows, width, model = own.shape

    def body(meta_ref, own_ref, far_ref, out_ref):
        for slot in range(2):
            block, unused, row = slot_of(meta_ref, slot)
            length = meta_ref[5 + 4 * slot]
            position = block * width + lax.broadcasted_iota(jnp.int32, (width, model), 0)
            value = jnp.where(row == 0, own_ref[0].astype(f32), far_ref[...].astype(f32))
            out_ref[slot * width:(slot + 1) * width, :] = jnp.where(position < length, value, 0.0).astype(bf16)

    outs = [shaped((rows * width, model))]
    return call(body, "masked_cotangent", outs, [meta], [own, far], (), 0, after)[0]


def masked(tile, chunk, block, width, fill):
    rows, lanes = tile.shape
    key = chunk * CHUNK + lax.broadcasted_iota(jnp.int32, (rows, lanes), 0)
    query = block * width + lax.broadcasted_iota(jnp.int32, (rows, lanes), 1) % width
    return jnp.where(key <= query, tile, fill)


def mix_columns(vector_t, mix, out_ref, heads, heads_in, scale, by_row):
    model, width = vector_t.shape
    size = model // heads
    for i, h in enumerate(heads_in):
        for g in range(heads):
            factor = (mix[h, g] if by_row else mix[g, h]) * scale
            out_ref[g * size:(g + 1) * size, i * width:(i + 1) * width] = (
                vector_t[g * size:(g + 1) * size, :] * factor
            ).astype(bf16)


def listed(pieces):
    arrays, spots = [], []
    for parts in pieces:
        spot = []
        for array, index in parts:
            known = [i for i, a in enumerate(arrays) if a is array]
            if not known:
                arrays.append(array)
            spot.append((known[0] if known else len(arrays) - 1, index))
        spots.append(spot)
    return arrays, spots


def views(refs, spot):
    return [refs[i] if index is None else refs[i].at[index] for i, index in spot]


def attend_forward(meta, premix, postmix, x_pieces, w_pieces, after):
    count = len(x_pieces)
    x_arrays, x_spots = listed(x_pieces)
    w_arrays, w_spots = listed(w_pieces)
    width, model = x_arrays[0].shape[1:]
    length = count * width
    chunks = length // CHUNK
    heads = premix.shape[0]
    size = model // heads
    pair = 2 * width
    lanes = heads * width
    half = lanes // 2
    w_rows = model // count
    mirror = count - 1

    def body(meta_ref, pre, post, *refs):
        x_refs, refs = refs[:len(x_arrays)], refs[len(x_arrays):]
        w_refs, refs = refs[:len(w_arrays)], refs[len(w_arrays):]
        joined_ref, second_ref, middle_ref, n_out, k_out, v_out, q_ref, ut_out, lse_ref, w_out, wo_out, gain_ref = refs[:12]
        qst, s_ref, acc, mx, total_out, n_ref, k_ref, v_ref, w_ref, wo_ref, ut_ref, xs, gains = refs[12:25]
        vt_ref, refs = refs[-1], refs[:-1]
        x_sems, w_sems, sems, w_sem, ut_sems = refs[25:]
        place = meta_ref[0]
        x_copies = begin([(views(x_refs, x_spots[k])[0], xs.at[k]) for k in range(count)], x_sems)
        pairs, gain_pairs = [], []
        for k in range(count):
            at, spot = 0, aligned(place ^ k, w_rows)
            for ref in views(w_refs, w_spots[k]):
                for start in range(0, ref.shape[0], w_rows):
                    if at < 3:
                        target = w_ref.at[spot, at * model:(at + 1) * model]
                        pairs.append((ref.at[start:start + w_rows, :], target))
                    elif at == 3:
                        pairs.append((ref.at[start:start + w_rows, :], wo_ref.at[spot, :]))
                    else:
                        gain_pairs.append((ref.at[start:start + GAIN_ROWS, :128], gains.at[k]))
                    at += 1
        w_copies = begin(gain_pairs + pairs, w_sems)
        finish(x_copies + w_copies[:count])
        gain = jnp.zeros((GAIN_ROWS, model), f32)
        for k in range(count):
            r, c = picks(128, model, 0, (place ^ k) * w_rows)
            gain += dot(gains[k], one_hot(jnp.logical_and(r == c, r < w_rows)))
        gain_ref[...] = gain[:8, :]
        out_copies = [
            pltpu.make_async_copy(w_ref, w_out, w_sem.at[0]), pltpu.make_async_copy(wo_ref, wo_out, w_sem.at[1])
        ]

        finish(w_copies[count:])
        for copy in out_copies:
            copy.start()

        def attend(slot, unused):
            block, active, row = slot_of(meta_ref, slot)
            last = block // 2
            mine = aligned(slot, width)
            ut_copies = [
                pltpu.make_async_copy(ut_ref.at[2 * slot + i], ut_out.at[2 * slot + i], ut_sems.at[2 * slot + i])
                for i in range(2)
            ]

            def leave(c):
                spot = aligned(c, CHUNK)
                pairs = ((n_ref, n_out), (k_ref, k_out), (v_ref, v_out))
                return [
                    pltpu.make_async_copy(a.at[spot, :], b.at[slot, spot, :], sems.at[i, c])
                    for i, (a, b) in enumerate(pairs)
                ]

            @pl.when(active)
            def _():
                for k in range(count):
                    @pl.when((place ^ k) // 2 <= last)
                    def _():
                        xb = xs[k, row].astype(f32)
                        n_ref[aligned(place ^ k, width), :] = (xb * inverse_rms(xb) * gain_ref[0:1, :]).astype(bf16)

            @pl.when(jnp.logical_not(active))
            def _():
                joined_ref[mine, :] = jnp.zeros((width, model), bf16)

            @pl.when(active)
            def _():
                def project(c, unused):
                    nc = n_ref[aligned(c, CHUNK), :]
                    k_ref[aligned(c, CHUNK), :] = dot(nc, w_ref[:, model:2 * model]).astype(bf16)
                    vc = dot(nc, w_ref[:, 2 * model:3 * model]).astype(bf16)
                    v_ref[aligned(c, CHUNK), :] = vc
                    vt_ref[c] = vc.T
                    for copy in leave(c):
                        copy.start()
                    return 0

                lax.fori_loop(0, last + 1, project, 0)
                query = dot(n_ref[aligned(block, width), :], w_ref[:, :model]).astype(bf16)
                q_ref[mine, :] = query
                query_t = query.astype(f32).T
                for part_of in range(2):
                    heads_in = range(part_of * heads // 2, (part_of + 1) * heads // 2)
                    mix_columns(query_t, pre, qst, heads, heads_in, 0.125, False)
                    mx[...] = jnp.full(mx.shape, NEGATIVE, f32)

                    def scores(c, unused):
                        kc = k_ref[aligned(c, CHUNK), :]
                        for t in range(half // pair):
                            part = slice(t * pair, (t + 1) * pair)
                            s = masked(dot(kc, qst[:, part]), c, block, width, NEGATIVE)
                            s_ref[aligned(c, CHUNK), part] = s
                            mx[:, part] = jnp.maximum(mx[:, part], jnp.max(s.reshape(CHUNK // 8, 8, pair), axis=0))
                        return 0

                    lax.fori_loop(0, last + 1, scores, 0)
                    peak = jnp.max(mx[...], axis=0, keepdims=True)
                    acc[...] = jnp.zeros(acc.shape, f32)
                    mx[...] = jnp.zeros(mx.shape, f32)

                    def weigh(c, unused):
                        vt = vt_ref[c]
                        for t in range(half // pair):
                            part = slice(t * pair, (t + 1) * pair)
                            p = jnp.exp(s_ref[aligned(c, CHUNK), part] - peak[:, part])
                            mx[:, part] += jnp.sum(p.reshape(CHUNK // 8, 8, pair), axis=0)
                            acc[:, part] += dot(vt, p.astype(bf16))
                        return 0

                    lax.fori_loop(0, last + 1, weigh, 0)
                    total = jnp.sum(mx[...], axis=0, keepdims=True)
                    lse_ref[slot, :, part_of * half:(part_of + 1) * half] = peak + jnp.log(total)
                    inverse = 1.0 / total
                    for k in range(heads):
                        rows = slice(k * size, (k + 1) * size)
                        out = jnp.zeros((size, width), f32)
                        for i, h in enumerate(heads_in):
                            cols = slice(i * width, (i + 1) * width)
                            u = acc[rows, cols] * inverse[:, cols]
                            ut_ref[2 * slot + part_of, rows, cols] = u.astype(bf16)
                            out += u * post[h, k]
                        if part_of == 0:
                            total_out[rows, :] = out
                        else:
                            total_out[rows, :] += out
                    ut_copies[part_of].start()
                joined_ref[mine, :] = total_out[...].T.astype(bf16)

                def gone(c, unused):
                    finish(leave(c))
                    return 0

                lax.fori_loop(0, last + 1, gone, 0)

            residual = jnp.where(row == 0, xs[0, 0].astype(f32), xs[mirror, 1].astype(f32))
            middle = residual + dot(joined_ref[mine, :], wo_ref[...])
            middle_ref[mine, :] = middle
            second_ref[mine, :] = (middle * inverse_rms(middle) * gain_ref[1:2, :]).astype(bf16)

            @pl.when(active)
            def _():
                finish(ut_copies)

            return 0

        lax.fori_loop(0, 2, attend, 0)
        finish(out_copies)

    tokens = 2 * width
    outs = [
        shaped((tokens, model)), shaped((tokens, model)), shaped((tokens, model), f32), shaped((2, length, model)),
        shaped((2, length, model)), shaped((2, length, model)), shaped((tokens, model)), shaped((4, model, half)),
        shaped((2, 1, lanes), f32), shaped((model, 3 * model)), shaped((model, model)), shaped((8, model), f32),
    ]
    scratch = [
        pltpu.VMEM((model, half), bf16), pltpu.VMEM((length, half), f32), pltpu.VMEM((model, half), f32),
        pltpu.VMEM((8, half), f32), pltpu.VMEM((model, width), f32), pltpu.VMEM((length, model), bf16),
        pltpu.VMEM((length, model), bf16), pltpu.VMEM((length, model), bf16), pltpu.VMEM((model, 3 * model), bf16),
        pltpu.VMEM((model, model), bf16), pltpu.VMEM((4, model, half), bf16),
        pltpu.VMEM((count, 2, width, model), bf16), pltpu.VMEM((count, GAIN_ROWS, 128), bf16),
        dma(count), dma(5 * count), pltpu.SemaphoreType.DMA((3, chunks)), dma(2), dma(4),
        pltpu.VMEM((chunks, model, CHUNK), bf16),
    ]
    args = x_arrays + w_arrays
    flops = 4 * length * model * (lanes + 2 * model)
    return call(
        body, "attend_forward", outs, [meta, premix, postmix], args, scratch, flops, after,
        tuple(range(len(args))), (3, 4, 5, 7, 9, 10),
    )


def feed_forward(seconds, ups, inner_w, outer_w):
    width, model = seconds[0].shape
    units = inner_w.shape[1]
    tokens = GROUP * width
    root = 0.7978845608028654
    tile = 256

    def body(*refs):
        s_refs, u_refs, (w1, w2), refs = refs[:GROUP], refs[GROUP:2 * GROUP], refs[2 * GROUP:2 * GROUP + 2], refs[2 * GROUP + 2:]
        hidden_ref, inner_ref, grads, outs, (tok, up, sems) = refs[0], refs[1], refs[2:5], refs[5:8], refs[8:]
        spots = [slice(i * width, (i + 1) * width) for i in range(GROUP)]
        pairs = [(s_refs[i], tok.at[spots[i], :]) for i in range(GROUP)]
        pairs += [(u_refs[i], up.at[spots[i], :]) for i in range(GROUP)]
        copies = begin(pairs, sems)
        finish(copies[:GROUP])
        for t in range(units // tile):
            part = slice(t * tile, (t + 1) * tile)
            v = dot(tok[...], w1[:, part])
            squared = v * v
            th = jnp.tanh(root * (v + 0.044715 * (squared * v)))
            hidden_ref[:, part] = (0.5 * v * (1.0 + th)).astype(bf16)
            slope = 0.5 * (1.0 + th) + 0.5 * v * (1.0 - th * th) * (root * (1.0 + 0.134145 * squared))
            if t == 0:
                finish(copies[GROUP:])
            inner_ref[:, part] = (dot(up[...], w2[part, :], 1, 1) * slope).astype(bf16)
        for (own_ref, give_ref, across_ref), made in (
            (grads, dot(inner_ref[...], w1[...], 1, 1)), (outs, dot(hidden_ref[...], w2[...]))
        ):
            made = made.astype(bf16)
            own_ref[...] = made[:width]
            give_ref[:width, :] = made[width:2 * width]
            give_ref[width:, :] = made[3 * width:]
            across_ref[...] = made[2 * width:3 * width]

    outs = [shaped((tokens, units)), shaped((tokens, units))]
    outs += [shaped((width, model)), shaped((2 * width, model)), shaped((width, model))] * 2
    scratch = [pltpu.VMEM((tokens, model), bf16), pltpu.VMEM((tokens, model), bf16), dma(2 * GROUP)]
    args = list(seconds) + list(ups) + [inner_w, outer_w]
    made = call(
        body, "feed_forward", outs, [], args, scratch, 8 * tokens * model * units, (), tuple(range(2 * GROUP))
    )
    return made[0], made[1], made[2:5], made[5:8]


def feed_weights(meta, seconds, ups, hidden, inner, bands, after):
    width, model = seconds[0].shape
    units = hidden.shape[1]
    tokens = GROUP * width
    rows_out = units // bands

    def body(meta_ref, *refs):
        s_refs, u_refs, (h_ref, i_ref), refs = refs[:GROUP], refs[GROUP:2 * GROUP], refs[2 * GROUP:2 * GROUP + 2], refs[2 * GROUP + 2:]
        inner_out, outer_j, (tok, up, grad, sems) = refs[0], refs[1:1 + bands], refs[1 + bands:]
        pairs = [(s_refs[i], tok.at[i * width:(i + 1) * width, :]) for i in range(GROUP)]
        pairs += [(u_refs[i], up.at[i * width:(i + 1) * width, :]) for i in range(GROUP)]
        copies = begin(pairs, sems)
        finish(copies[:GROUP])
        inner_out[...] = dot(tok[...], i_ref[...], 0, 0).astype(bf16)
        finish(copies[GROUP:])
        grad[...] = dot(h_ref[...], up[...], 0, 0).astype(bf16)
        for j in range(bands):
            outer_j[j][...] = grad[aligned((meta_ref[0] // GROUP) ^ j, rows_out), :]

    outs = [shaped((model, units))] + [shaped((rows_out, model))] * bands
    args = list(seconds) + list(ups) + [hidden, inner]
    scratch = [
        pltpu.VMEM((tokens, model), bf16), pltpu.VMEM((tokens, model), bf16), pltpu.VMEM((units, model), bf16),
        dma(2 * GROUP),
    ]
    made = call(
        body, "feed_weights", outs, [meta], args, scratch, 4 * tokens * model * units, after, tuple(range(2 * GROUP))
    )
    return made[0], list(made[1:])


def before_attention_back(own, got, came, middle, up, gains, w, joined, inner_grads, count, after):
    tokens, model = own.shape
    rows = model // count

    def body(own_ref, got_ref, came_ref, middle_ref, up_ref, gain_ref, w_in, joined_ref, inner_ref,
             grad_ref, upstream_ref, packed_ref, w_ref, total_ref, sems):
        copies = begin([(w_in, w_ref), (inner_ref, total_ref.at[:, rows:, :])], sems)
        second = own_ref[...].astype(f32) + got_ref[:tokens, :].astype(f32) + came_ref[...].astype(f32)
        back = norm_back(middle_ref[...], gain_ref[1:2, :], second)
        grad = up_ref[...].astype(f32) + back
        grad_ref[...] = grad
        cast = grad.astype(bf16)
        total = dot(joined_ref[...], cast, 0, 0)
        for j in range(count):
            total_ref[j, :rows, :] = total[j * rows:(j + 1) * rows, :].astype(bf16)
        copies[1].wait()
        last = pltpu.make_async_copy(total_ref, packed_ref, sems.at[2])
        last.start()
        copies[0].wait()
        upstream_ref[...] = dot(cast, w_ref[...], 1, 1).astype(bf16)
        last.wait()

    outs = [shaped((tokens, model), f32), shaped((tokens, model)), shaped((count, 2 * rows, model))]
    args = [own, got, came, middle, up, gains, w, joined, inner_grads.reshape(count, rows, model)]
    scratch = [pltpu.VMEM((model, model), bf16), pltpu.VMEM((count, 2 * rows, model), bf16), dma(3)]
    return call(
        body, "before_attention_back", outs, [], args, scratch, 4 * tokens * model * model, after, (6, 8), (2,)
    )


def attend_back(meta, premix, postmix, pre_row, post_row, query, upstream, normed, keys, values, ut, lse, count, after):
    tokens, model = query.shape
    width = tokens // 2
    length = keys.shape[1]
    heads = premix.shape[0]
    size = model // heads
    pair = 2 * width
    lanes = heads * width
    half = lanes // 2
    w_rows = model // count

    def body(meta_ref, pre, post, pre_in, post_in, q_in, up_in, lse_in, n_hbm, k_hbm, v_hbm, ut_hbm,
             dq_ref, dk_hbm, dv_hbm, mix_ref, keep_ref, give_ref,
             qst, qs, ust, us, acc, pbuf, lbuf, dots, wacc, cin, cout, n_own, ut_held, in_sems, out_sems, own_sem, ut_sems,
             pre_row, post_row, q_ref, up_ref, lse_ref, arg_sems, kt_ref, nt_ref):
        args = begin(
            [(pre_in, pre_row), (post_in, post_row), (q_in, q_ref), (up_in, up_ref), (lse_in, lse_ref)], arg_sems
        )
        wacc[...] = jnp.zeros(wacc.shape, f32)
        mix_ref[...] = jnp.zeros(mix_ref.shape, f32)
        finish(args)

        def through(slot, unused):
            block, active, unused_row = slot_of(meta_ref, slot)
            last = block // 2
            mine = aligned(slot, width)
            ut_copies = [
                pltpu.make_async_copy(ut_hbm.at[2 * slot + i], ut_held.at[i], ut_sems.at[i]) for i in range(2)
            ]

            @pl.when(jnp.logical_not(active))
            def _():
                dq_ref[mine, :] = jnp.zeros((width, model), bf16)

            @pl.when(active)
            def _():
                def fetch(c):
                    return [
                        pltpu.make_async_copy(
                            a.at[slot, aligned(c, CHUNK), :], cin.at[c % 2, i], in_sems.at[c % 2, i]
                        )
                        for i, a in enumerate((k_hbm, v_hbm, n_hbm))
                    ]

                def leave(c):
                    return [
                        pltpu.make_async_copy(
                            cout.at[c % 2, i], a.at[slot, aligned(c, CHUNK), :], out_sems.at[c % 2, i]
                        )
                        for i, a in enumerate((dk_hbm, dv_hbm))
                    ]

                own = pltpu.make_async_copy(n_hbm.at[slot, aligned(block, width), :], n_own, own_sem)
                own.start()
                for copy in ut_copies + fetch(0):
                    copy.start()
                q = q_ref[mine, :].astype(f32)
                up = up_ref[mine, :].astype(f32)
                qt, upt = q.T, up.T
                mix_columns(qt, pre, qst, heads, range(heads), 0.125, False)
                mix_columns(upt, post, ust, heads, range(heads), 1.0, True)
                for h in range(heads):
                    spot = slice(h * width, (h + 1) * width)
                    qs[spot, :] = (q * (pre_row[h:h + 1, :] * 0.125)).astype(bf16)
                    us[spot, :] = (up * post_row[h:h + 1, :]).astype(bf16)
                finish(ut_copies)
                for h in range(heads):
                    spot = slice(h * width, (h + 1) * width)
                    column = h % (heads // 2) * width
                    u = ut_held[h // (heads // 2), :, column:column + width].astype(f32)
                    t = jnp.sum((u * upt).reshape(heads, size, width), axis=1)
                    mix_ref[heads + h] += t
                    d = jnp.zeros((1, width), f32)
                    for k in range(heads):
                        d += t[k:k + 1, :] * post[h, k]
                    dots[:, spot] = d
                acc[...] = jnp.zeros(acc.shape, f32)

                def visit(c, unused):
                    finish(fetch(c))

                    @pl.when(c < last)
                    def _():
                        for copy in fetch(c + 1):
                            copy.start()

                    kc, vc = cin[c % 2, 0], cin[c % 2, 1]
                    kt_ref[...] = kc.T
                    nt_ref[...] = cin[c % 2, 2].T
                    for t in range(heads // 2):
                        part = slice(t * pair, (t + 1) * pair)
                        p = masked(jnp.exp(dot(kc, qst[:, part]) - lse_ref[slot, :, part]), c, block, width, 0.0)
                        grad = (p * (dot(vc, ust[:, part]) - dots[:, part])).astype(bf16)
                        pbuf[:, part] = p.astype(bf16)
                        lbuf[:, part] = grad
                        acc[:, part] += dot(kt_ref[...], grad)

                    @pl.when(c >= 2)
                    def _():
                        finish(leave(c - 2))

                    dk = dot(lbuf[...], qs[...]).astype(bf16)
                    dv = dot(pbuf[...], us[...]).astype(bf16)
                    cout[c % 2, 0] = dk
                    cout[c % 2, 1] = dv
                    for copy in leave(c):
                        copy.start()
                    wacc[:, model:2 * model] += dot(nt_ref[...], dk)
                    wacc[:, 2 * model:] += dot(nt_ref[...], dv)
                    return 0

                lax.fori_loop(0, last + 1, visit, 0)
                for g in range(heads):
                    rows = slice(g * size, (g + 1) * size)
                    out = jnp.zeros((size, width), f32)
                    qg = qt[rows, :] * 0.125
                    for h in range(heads):
                        a = acc[rows, h * width:(h + 1) * width]
                        out += a * pre[g, h]
                        mix_ref[g, h:h + 1, :] += jnp.sum(a * qg, axis=0, keepdims=True)
                    acc[rows, 0:width] = out * 0.125
                dq = acc[:, 0:width].T.astype(bf16)
                dq_ref[mine, :] = dq
                own.wait()
                wacc[:, :model] += dot(n_own[...], dq, 0, 0)

                @pl.when(last >= 1)
                def _():
                    finish(leave(last - 1))

                finish(leave(last))

            return 0

        lax.fori_loop(0, 2, through, 0)
        for k in range(count):
            (keep_ref, give_ref)[k % 2][k // 2 * w_rows:(k // 2 + 1) * w_rows, :] = wacc[
                aligned(meta_ref[0] ^ k, w_rows), :
            ].astype(bf16)

    outs = [
        shaped((tokens, model)), shaped((2, length, model)), shaped((2, length, model)),
        shaped((2 * heads, heads, width), f32), shaped((count // 2 * w_rows, 3 * model)),
        shaped((count // 2 * w_rows, 3 * model)),
    ]
    scratch = [
        pltpu.VMEM((model, lanes), bf16), pltpu.VMEM((lanes, model), bf16), pltpu.VMEM((model, lanes), bf16),
        pltpu.VMEM((lanes, model), bf16), pltpu.VMEM((model, lanes), f32), pltpu.VMEM((CHUNK, lanes), bf16),
        pltpu.VMEM((CHUNK, lanes), bf16), pltpu.VMEM((1, lanes), f32), pltpu.VMEM((model, 3 * model), f32),
        pltpu.VMEM((2, 3, CHUNK, model), bf16), pltpu.VMEM((2, 2, CHUNK, model), bf16), pltpu.VMEM((width, model), bf16),
        pltpu.VMEM((2, model, half), bf16), pltpu.SemaphoreType.DMA((2, 3)), pltpu.SemaphoreType.DMA((2, 2)),
        pltpu.SemaphoreType.DMA, dma(2), pltpu.VMEM((heads, model), f32), pltpu.VMEM((heads, model), f32),
        pltpu.VMEM((tokens, model), bf16), pltpu.VMEM((tokens, model), bf16), pltpu.VMEM((2, 1, lanes), f32), dma(5),
        pltpu.VMEM((model, CHUNK), bf16), pltpu.VMEM((model, CHUNK), bf16),
    ]
    args = [pre_row, post_row, query, upstream, lse, normed, keys, values, ut]
    return call(
        body, "attend_back", outs, [meta, premix, postmix], args, scratch, 15 * length * model * lanes, after,
        tuple(range(9)), (1, 2),
    )


def input_back(meta, dq, dk, dv, w, x_pieces, gains, grad, after):
    count = len(x_pieces)
    x_arrays, x_spots = listed(x_pieces)
    width, model = x_arrays[0].shape[1:]
    length = dk.shape[1]
    chunks = length // CHUNK

    def body(meta_ref, dq_in, grad_in, gain_in, dk_hbm, dv_hbm, w_hbm, *refs):
        x_refs, refs = refs[:len(x_arrays)], refs[len(x_arrays):]
        keep_ref, give_ref, normed, dk_held, dv_held, w_ref, xs, sems, w_sem, x_sems = refs[:10]
        dq_ref, grad_ref, gain_ref, arg_sems, wt_ref = refs[10:]
        arg_copies = begin([(dq_in, dq_ref), (grad_in, grad_ref), (gain_in, gain_ref)], arg_sems)
        place = meta_ref[0]
        w_copy = pltpu.make_async_copy(w_hbm, w_ref, w_sem)
        w_copy.start()

        def fetch(slot, c):
            spot = aligned(c, CHUNK)
            return [
                pltpu.make_async_copy(a.at[slot, spot, :], b.at[slot, spot, :], sems.at[slot, c, i])
                for i, (a, b) in enumerate(((dk_hbm, dk_held), (dv_hbm, dv_held)))
            ]

        def start(slot, c):
            for copy in fetch(slot, c):
                copy.start()
            return 0

        for slot in range(2):
            block, active, row = slot_of(meta_ref, slot)
            needed = jnp.where(active, block // 2 + 1, 0)
            lax.fori_loop(0, needed, lambda c, unused, slot=slot: start(slot, c), 0)
        x_copies = begin([(views(x_refs, x_spots[k])[0], xs.at[k]) for k in range(count)], x_sems)
        w_copy.wait()
        for i in range(3):
            wt_ref[i] = w_ref[:, i * model:(i + 1) * model].T
        finish(arg_copies)

        finish(x_copies)

        def through(slot, unused):
            block, active, row = slot_of(meta_ref, slot)
            mine = aligned(slot, width)

            @pl.when(active)
            def _():
                def visit(c, unused):
                    spot = aligned(c, CHUNK)
                    finish(fetch(slot, c))
                    normed[spot, :] = dot(dk_held[slot, spot, :], wt_ref[1]) + dot(dv_held[slot, spot, :], wt_ref[2])
                    return 0

                lax.fori_loop(0, block // 2 + 1, visit, 0)
                normed[aligned(block, width), :] += dot(dq_ref[mine, :], wt_ref[0])

            def chip(i, unused):
                for k, out_ref in enumerate((keep_ref, give_ref)):
                    source = place ^ (2 * i + k)
                    spot = aligned(2 * i + row, width)
                    used = jnp.logical_and(active, source <= block)

                    @pl.when(jnp.logical_not(used))
                    def _():
                        out_ref[spot, :] = jnp.zeros((width, model), bf16)

                    @pl.when(used)
                    def _():
                        back = norm_back(
                            xs[2 * i + k, row].astype(f32), gain_ref[0:1, :], normed[aligned(source, width), :]
                        )
                        factor = jnp.where(source == block, 1.0, 0.0)
                        out_ref[spot, :] = (back + grad_ref[mine, :] * factor).astype(bf16)
                return 0

            lax.fori_loop(0, count // 2, chip, 0)
            return 0

        lax.fori_loop(0, 2, through, 0)

    half = count * width
    outs = [shaped((half, model)), shaped((half, model))]
    args = [dq, grad, gains, dk, dv, w] + x_arrays
    scratch = [
        pltpu.VMEM((length, model), f32), pltpu.VMEM((2, length, model), bf16), pltpu.VMEM((2, length, model), bf16),
        pltpu.VMEM((model, 3 * model), bf16), pltpu.VMEM((count, 2, width, model), bf16),
        pltpu.SemaphoreType.DMA((2, chunks, 2)), pltpu.SemaphoreType.DMA, dma(count),
        pltpu.VMEM(dq.shape, bf16), pltpu.VMEM(grad.shape, f32), pltpu.VMEM(gains.shape, f32), dma(3),
        pltpu.VMEM((3, model, model), bf16),
    ]
    return call(
        body, "input_back", outs, [meta], args, scratch, 8 * length * model * model, after,
        tuple(range(len(args))),
    )


def pair_sums(keep, got, count, later, after, name):
    blocks = count // 2
    rows, columns = keep.shape[0] // blocks, keep.shape[1]

    def body(keep_ref, got_ref, *refs):
        outs = refs[len(later):]
        for source, target in zip(refs, outs[blocks:]):
            target[...] = source[...]
        for i in range(blocks):
            spot = slice(i * rows, (i + 1) * rows)
            outs[i][...] = (keep_ref[spot, :].astype(f32) + got_ref[spot, :].astype(f32)).astype(outs[i].dtype)

    outs = [shaped((rows, columns))] * blocks
    outs += [shaped(a.shape, a.dtype) for a in later]
    made = call(body, name, outs, [], [keep, got] + list(later), (), 0, after)
    return made[:blocks], made[blocks:]


def halves_first(keep, got, pair, after, name):
    rows, columns = keep.shape[0] // 4, keep.shape[1]
    half = rows // 2

    def body(keep_ref, got_ref, one, other, two_ref, four_ref, rest_ref, sum_ref):
        sum_ref[...] = one[...] + other[...]

        def part(i, b):
            spot = slice(i * rows + b * half, i * rows + (b + 1) * half)
            return keep_ref[spot, :].astype(f32) + got_ref[spot, :].astype(f32)

        for n, (i, b) in enumerate(((1, 0), (3, 0))):
            two_ref[n * half:(n + 1) * half, :] = part(i, b).astype(bf16)
        for n, (i, b) in enumerate(((2, 1), (3, 1))):
            four_ref[n * half:(n + 1) * half, :] = part(i, b).astype(bf16)
        for n, (i, b) in enumerate(((0, 0), (2, 0), (0, 1), (1, 1))):
            rest_ref[n * half:(n + 1) * half, :] = part(i, b)

    outs = [
        shaped((rows, columns)), shaped((rows, columns)), shaped((2 * rows, columns), f32), shaped(pair[0].shape, f32),
    ]
    return call(body, name, outs, [], [keep, got, *pair], (), 0, after)


def halves_second(rest, from_two, from_four, pair, after, name):
    rows, columns = from_two.shape
    half = rows // 2

    def body(rest_ref, two_in, four_in, one, other, two_ref, four_ref, own_ref, sum_ref):
        sum_ref[...] = one[...] + other[...]
        own_ref[:half, :] = rest_ref[:half, :] + two_in[:half, :].astype(f32)
        four_ref[...] = (rest_ref[half:rows, :] + two_in[half:, :].astype(f32)).astype(bf16)
        own_ref[half:, :] = rest_ref[rows:rows + half, :] + four_in[:half, :].astype(f32)
        two_ref[...] = (rest_ref[rows + half:, :] + four_in[half:, :].astype(f32)).astype(bf16)

    outs = [
        shaped((half, columns)), shaped((half, columns)), shaped((rows, columns), f32), shaped(pair[0].shape, f32),
    ]
    return call(body, name, outs, [], [rest, from_two, from_four, *pair], (), 0, after)


def input_sum(own, from_four, from_two, shape):
    rows, width, model = shape

    def body(own_ref, four_ref, two_ref, out_ref):
        out_ref[0] = (own_ref[:width, :] + four_ref[...].astype(f32)).astype(bf16)
        out_ref[1] = (own_ref[width:, :] + two_ref[...].astype(f32)).astype(bf16)

    return call(body, "input_sum", [shaped(shape)], [], [own, from_four, from_two])[0]


def split_dp(meta, depth, parts, pair, after):
    joined, wide = parts[0].shape
    size = joined // depth
    halved = parts[1].shape[0] != joined

    def body(meta_ref, *refs):
        ins, (one, other), outs, sum_ref = refs[:len(parts)], refs[len(parts):len(parts) + 2], refs[len(parts) + 2:-2], refs[-2]
        total_ref = refs[-1]
        sum_ref[...] = one[...] + other[...]
        if halved:
            for i in range(2):
                spot = slice(i * joined // 2, (i + 1) * joined // 2)
                total_ref[spot, :] = (ins[0][spot, :] + ins[1 + i][...].astype(f32)).astype(bf16)
        else:
            total = ins[0][...].astype(f32)
            for ref in ins[1:]:
                total += ref[...].astype(f32)
            total_ref[...] = total.astype(bf16)
        for m in range(depth):
            r, c = picks(size, joined, 0, (meta_ref[1] ^ m) * size)
            outs[m][...] = dot(one_hot(r == c), total_ref[...]).astype(bf16)

    outs = [shaped((size, wide))] * depth + [shaped(pair[0].shape, f32)]
    scratch = [pltpu.VMEM((joined, wide), bf16)]
    made = call(body, "split_dp", outs, [meta], list(parts) + list(pair), scratch, 0, after)
    return made[:depth], made[depth]


def split_feed(meta, depth, grads, outer, size, after):
    count, joined, units = grads.shape
    joined //= 2
    bands = len(outer)
    band = outer[0].shape[0]
    shard = band // depth
    parts = 1 + GROUP
    out_rows = parts * size + shard

    def body(meta_ref, grad_in, *refs):
        o_ins, outs, (total, grad_ref, outer_ref, sems) = refs[:bands], refs[bands:-4], refs[-4:]
        o_refs = [outer_ref.at[j] for j in range(bands)]
        finish(begin([(grad_in, grad_ref)] + [(o_ins[j], o_refs[j]) for j in range(bands)], sems))
        section = grad_ref[0, :joined, :].astype(f32)
        for j in range(1, count):
            section += grad_ref[j, :joined, :].astype(f32)
        total[:joined, :] = section.astype(bf16)
        for t in range(GROUP):
            section = grad_ref[t, joined:, :].astype(f32)
            for j in range(1, bands):
                section += grad_ref[j * GROUP + t, joined:, :].astype(f32)
            total[(1 + t) * joined:(2 + t) * joined, :] = section.astype(bf16)
        rest = o_refs[0][...].astype(f32)
        for j in range(1, bands):
            rest += o_refs[j][...].astype(f32)
        total[parts * joined:, :] = rest.astype(bf16)
        for d in range(depth):
            for t in range(parts):
                outs[0][d, t * size:(t + 1) * size, :] = total[t * joined + d * size:t * joined + (d + 1) * size, :]
            start = parts * joined + d * shard
            outs[0][d, parts * size:, :] = total[start:start + shard, :]

    scratch = [
        pltpu.VMEM((parts * joined + band, units), bf16), pltpu.VMEM(grads.shape, bf16),
        pltpu.VMEM((bands, band, units), bf16), dma(1 + bands),
    ]
    args = [grads] + list(outer)
    outs = [shaped((depth, out_rows, units))]
    return call(body, "split_feed", outs, [meta], args, scratch, 0, after, tuple(range(len(args))))[0]


def finish_projections(pieces, weights, gain):
    size, wide = pieces[0].shape
    parts = 3
    model = wide // parts

    def body(*refs):
        ins, w_ins, gain_in, outs = refs[:len(pieces)], refs[len(pieces):-8], refs[-8], refs[-7:-3]
        w_held, gain_ref, sems = refs[-3:]
        w_refs = [w_held.at[i] for i in range(parts)]
        finish(begin([(w_ins[i], w_refs[i]) for i in range(parts)] + [(gain_in, gain_ref)], sems))
        along = jnp.zeros((size, 1), f32)
        for i in range(parts):
            part = slice(i * model, (i + 1) * model)
            total = ins[0][:, part].astype(f32)
            for ref in ins[1:]:
                total += ref[:, part].astype(f32)
            outs[i][...] = total
            along += jnp.sum(total * w_refs[i][...].astype(f32), axis=1, keepdims=True)
        outs[3][...] = along / gain_ref[...]

    outs = [shaped((size, model), f32)] * parts + [shaped((size, 1), f32)]
    scratch = [pltpu.VMEM((parts, size, model), bf16), pltpu.VMEM((size, 1), f32), dma(parts + 1)]
    args = list(pieces) + list(weights) + [gain]
    return call(
        body, "finish_projections", outs, [], args, scratch, raw_args=tuple(range(len(pieces), len(args)))
    )


def finish_feed(pieces, weight, gain, bands):
    size = weight.shape[0]
    rows, units = pieces.shape
    band = units // bands

    def body(in_hbm, w_in, gain_in, output_ref, inner_ref, outer_ref, gain_out, in_ref, w_ref, gain_ref, sems):
        finish(begin([(in_hbm, in_ref), (w_in, w_ref), (gain_in, gain_ref)], sems))
        total = in_ref[...].astype(f32)
        output_ref[...] = total[:size, :]
        for t in range(GROUP):
            for y in range(bands):
                inner_ref[:, (y * GROUP + t) * band:(y * GROUP + t + 1) * band] = total[
                    (1 + t) * size:(2 + t) * size, y * band:(y + 1) * band
                ]
        outer_ref[...] = total[(1 + GROUP) * size:, :]
        along = jnp.sum(inner_ref[...] * w_ref[...].astype(f32), axis=1, keepdims=True)
        gain_out[...] = along / gain_ref[...]

    outs = [
        shaped((size, units), f32), shaped((size, GROUP * units), f32),
        shaped((rows - (1 + GROUP) * size, units), f32), shaped((size, 1), f32),
    ]
    scratch = [pltpu.VMEM(pieces.shape, bf16), pltpu.VMEM(weight.shape, bf16), pltpu.VMEM((size, 1), f32), dma(3)]
    return call(body, "finish_feed", outs, [], [pieces, weight, gain], scratch, raw_args=(0, 1, 2))


def swap(value, axis, mask):
    count = lax.axis_size(axis)
    return lax.ppermute(value, axis, [(i, i ^ mask) for i in range(count)])


def gather_dp(value):
    return [value] + [swap(value, "dp", m) for m in range(1, lax.axis_size("dp"))]


def gather_first(meta, inputs, first_w):
    count, depth = lax.axis_size("blk"), lax.axis_size("dp")
    pieces = gather_dp(first_w)
    x_links = [inputs, swap(inputs, "blk", 2), swap(inputs, "blk", 4)]
    w_own, x_on_two, x_on_four, x_core = join_dp(meta, pieces, x_links)
    w_links = [w_own, swap(w_own, "blk", 2), swap(w_own, "blk", 4)]
    if count == 8:
        halves = [swap(x_on_two, "blk", 2), swap(x_on_four, "blk", 4)]
        x_core = swap(x_core, "blk", 1)
        w_on_two, w_on_four, w_core, x_across = forward_across(w_links, halves)
        w_across = [swap(w_on_two, "blk", 2), swap(w_on_four, "blk", 4)]
        w_core, x_far = swap(w_core, "blk", 1), swap(x_across, "blk", 1)
        w_far = [swap(part, "blk", 1) for part in w_across]
        xs = [[(a, None)] for a in x_links] + [[(x_across, None)]]
        ws = [[(a, None)] for a in w_links] + [[(a, None) for a in w_across]]
        xs_core = [[(x_core, i)] for i in range(3)] + [[(x_far, None)]]
        ws_core = [[(w_core, i)] for i in range(3)] + [[(a, None) for a in w_far]]
    else:
        x_links += [swap(inputs, "blk", k) for k in range(6, count, 2)]
        w_links += [swap(w_own, "blk", k) for k in range(6, count, 2)]
        xs, ws = [[(a, None)] for a in x_links], [[(a, None)] for a in w_links]
        xs_core, ws_core = [[(swap(a, "blk", 1), None)] for a in x_links], [[(swap(a, "blk", 1), None)] for a in w_links]
    x_pieces = [part for pair in zip(xs, xs_core) for part in pair]
    w_pieces = [part for pair in zip(ws, ws_core) for part in pair]
    return x_pieces, w_pieces


def all_to_all(value, axis):
    return lax.all_to_all(value, axis, 0, 0, tiled=True)


def gather_group(value):
    two = swap(value, "blk", 2)
    return [value, swap(value, "blk", 1), two, swap(two, "blk", 1)]


def scatter_chips(parts):
    return [parts[0]] + [swap(part, "blk", 2 * i) for i, part in enumerate(parts) if i]


def on_device(
    inputs, lengths, prenorm, midnorm, query_proj, key_proj, value_proj, output_proj,
    premix, postmix, inner_proj, outer_proj, cotangent,
):
    count, depth = lax.axis_size("blk"), lax.axis_size("dp")
    place, zplace = lax.axis_index("blk"), lax.axis_index("dp")
    rows, width, model = inputs.shape
    shard = prenorm.shape[0]
    low = place < count // 2
    mirror = count - 1
    slot_rows = [jnp.where(low, 1, 0), jnp.where(low, 0, 1)]
    blocks = [jnp.maximum(place, place ^ mirror), jnp.minimum(place, place ^ mirror)]
    spans = [jnp.where(slot_rows[i] == 0, lengths[0], lengths[1]) for i in range(2)]
    meta = [place, zplace]
    for i in range(2):
        meta += [blocks[i], (blocks[i] * width < spans[i]).astype(jnp.int32), slot_rows[i], spans[i]]
    meta = jnp.stack(meta).astype(jnp.int32)

    head_size = model // premix.shape[0]
    pre_row = jnp.repeat(premix.T, head_size, axis=1)
    post_row = jnp.repeat(postmix, head_size, axis=1)
    bands = count // GROUP
    band_ff = depth * outer_proj.shape[0]
    first_w = pack_first([query_proj, key_proj, value_proj, output_proj], jnp.stack([prenorm, midnorm]))
    x_pieces, w_pieces = gather_first(meta, inputs, first_w)

    sections = inner_proj.reshape(shard, bands, GROUP, band_ff).transpose(2, 0, 1, 3).reshape(GROUP, shard, -1)
    sections = all_to_all(jnp.concatenate([sections] * bands), "blk")
    outer_shards = [outer_proj] + [swap(outer_proj, "blk", GROUP * j) for j in range(1, bands)]
    second_w = jnp.concatenate([sections.reshape(count * shard, -1)] + outer_shards, axis=0)
    second_w = lax.all_gather(second_w, "dp")
    up = masked_cotangent(meta, cotangent, swap(cotangent[1], "blk", mirror), [w_pieces[2][0][0]])
    ups = gather_group(up)

    joined, second, middle, normed, keys, values, query, ut, lse, w, output_w, gain_rows = attend_forward(
        meta, premix, postmix, x_pieces, w_pieces, [up]
    )
    seconds = gather_group(second)
    inner_w, outer_w = join_feed(meta, second_w, shard, count, [second, ups[2]])
    hidden, inner, (own, give, across), (out_own, out_give, out_across) = feed_forward(
        seconds, ups, inner_w, outer_w
    )
    got = swap(give, "blk", 1)
    tokens = rows * width
    across = (across.astype(f32) + got[tokens:].astype(f32)).astype(bf16)
    came = swap(across, "blk", 2)
    out_got = swap(out_give, "blk", 1)
    inner_grads, outer_grads = feed_weights(meta, seconds, ups, hidden, inner, bands, [across])

    grad, upstream, packed = before_attention_back(
        own, got, came, middle, up, gain_rows, output_w, joined, inner_grads, count, []
    )
    feed_grads = all_to_all(packed, "blk")
    outer_grads = [outer_grads[0]] + [swap(outer_grads[j], "blk", GROUP * j) for j in range(1, bands)]
    out_across = (out_across.astype(f32) + out_got[tokens:].astype(f32)).astype(bf16)
    out_came = swap(out_across, "blk", 2)
    dq, dk, dv, mixes, keep, give = attend_back(
        meta, premix, postmix, pre_row, post_row, query, upstream, normed, keys, values, ut, lse, count, [out_across]
    )
    outer = out_own.astype(f32) + out_got[:tokens].astype(f32) + out_came.astype(f32)
    results = []
    for i in range(2):
        position = blocks[i] * width + jnp.arange(width, dtype=jnp.int32)
        value = middle[i * width:(i + 1) * width] + outer[i * width:(i + 1) * width]
        results.append(jnp.where((position < spans[i])[:, None], value, 0.0).astype(bf16))
    near, far = jnp.where(low, results[1], results[0]), jnp.where(low, results[0], results[1])
    outputs = jnp.stack([near, swap(far, "blk", mirror)])

    heads = premix.shape[0]
    cuts = split_feed(meta, depth, feed_grads, outer_grads, shard, [out_came])
    input_keep, input_give = input_back(meta, dq, dk, dv, w, x_pieces, gain_rows, grad, [cuts])
    cuts = lax.psum_scatter(cuts.reshape(-1, cuts.shape[2]), "dp", scatter_dimension=0, tiled=True)
    mixes = jnp.sum(mixes, axis=-1).reshape(-1)
    mixes = jnp.pad(mixes, (0, -mixes.shape[0] % 1024)).reshape(-1, 128)
    give, input_give = swap(give, "blk", 1), swap(input_give, "blk", 1)
    steps = [("dp", 1 << i) for i in range(depth.bit_length() - 1)] + [("blk", 1 << i) for i in range(count.bit_length() - 1)]

    def step(value):
        return value, swap(value, *steps.pop(0))

    if count == 8:
        two, four, rest, mixes = halves_first(keep, give, step(mixes), [input_keep], "halves_first_w")
        two, four = swap(two, "blk", 2), swap(four, "blk", 4)
        x_two, x_four, x_rest, mixes = halves_first(input_keep, input_give, step(mixes), [rest], "halves_first_x")
        x_two, x_four = swap(x_two, "blk", 2), swap(x_four, "blk", 4)
        two, four, rest, mixes = halves_second(rest, two, four, step(mixes), [x_rest], "halves_second_w")
        two, four = swap(two, "blk", 2), swap(four, "blk", 4)
        x_two, x_four, x_rest, mixes = halves_second(x_rest, x_two, x_four, step(mixes), [rest], "halves_second_x")
        x_two, x_four = swap(x_two, "blk", 2), swap(x_four, "blk", 4)
        cuts_w, mixes = split_dp(meta, depth, [rest, four, two], step(mixes), [x_rest])
        grad_inputs = input_sum(x_rest, x_four, x_two, inputs.shape)
    else:
        projected, unused = pair_sums(keep, give, count, [], [input_keep], "pair_sums_w")
        cuts_w, mixes = split_dp(meta, depth, scatter_chips(projected), step(mixes), [])
        parts, unused = pair_sums(input_keep, input_give, count, [], [], "pair_sums_x")
        grad_inputs = sum([part.astype(f32) for part in scatter_chips(parts)]).astype(bf16).reshape(inputs.shape)
    while steps:
        mixes = sum(step(mixes))
    mixes = mixes.reshape(-1)[:2 * heads * heads].reshape(2, heads, heads)
    output_sum, inner_sum, outer_sum, mid_gain = finish_feed(
        cuts, inner_proj, midnorm.astype(f32)[:, None], bands
    )
    cuts = cuts_w
    query_sum, key_sum, value_sum, pre_gain = finish_projections(
        [cuts[0]] + [swap(cuts[m], "dp", m) for m in range(1, depth)],
        [query_proj, key_proj, value_proj], prenorm.astype(f32)[:, None],
    )
    return (
        outputs,
        grad_inputs,
        pre_gain.reshape(-1),
        mid_gain.reshape(-1),
        query_sum,
        key_sum,
        value_sum,
        output_sum,
        mixes[0],
        mixes[1],
        inner_sum,
        outer_sum,
    )


def solution(mesh):
    weight = P(("blk", "dp"), None)
    vector = P(("blk", "dp"))
    tokens = P("dp", "blk", None)
    in_specs = (
        tokens, P("dp"), vector, vector, weight, weight, weight, weight, P(), P(), weight, weight, tokens,
    )
    out_specs = (
        tokens, tokens, vector, vector, weight, weight, weight, weight, P(), P(), weight, weight,
    )
    return jax.shard_map(on_device, mesh=mesh, in_specs=in_specs, out_specs=out_specs, check_vma=False)
```

```python
import jax
import jax.numpy as jnp
from jax import lax
from jax.experimental import pallas as pl
from jax.experimental.pallas import tpu as pltpu
from jax.sharding import PartitionSpec as P

EPSILON = 1e-06
GROUP = 4
CHUNK = 256
NEGATIVE = -1e30
VMEM_MOST = 60 * 1024 * 1024
VMEM_SPARE = 8 * 1024 * 1024
VMEM_WINDOWS = 18 * 1024 * 1024
GAIN_ROWS = 16
f32 = jnp.float32
bf16 = jnp.bfloat16
HIGH = lax.Precision.HIGHEST
ANY_SPEC = pl.BlockSpec(memory_space=pl.ANY)
VMEM_SPEC = pl.BlockSpec(memory_space=pltpu.VMEM)
HBM_SPEC = pl.BlockSpec(memory_space=pltpu.HBM)
SMEM_SPEC = pl.BlockSpec(memory_space=pltpu.SMEM)


def shaped(shape, dtype=bf16):
    return jax.ShapeDtypeStruct(shape, dtype)


def vmem_bytes(shape, dtype):
    lead, (rows, columns) = shape[:-2], shape[-2:]
    size = jnp.dtype(dtype).itemsize
    for extent in lead:
        size *= extent
    return size * -(-rows // 16) * 16 * -(-columns // 128) * 128


def call(body, name, outs, smem, args, scratch=(), flops=0, after=(), raw_args=(), raw_outs=(), extra=0):
    n_smem, n_args = len(smem), len(args)
    arrays = list(args) + list(outs)
    windows = [a for i, a in enumerate(args) if i not in raw_args] + [a for i, a in enumerate(outs) if i not in raw_outs]
    windows = sum(vmem_bytes(a.shape, a.dtype) for a in windows)
    held = sum(vmem_bytes(a.shape, a.dtype) for a in scratch if getattr(a, "memory_space", None) == pltpu.VMEM)
    held += VMEM_SPARE + extra + (windows if windows > VMEM_WINDOWS else 0)

    def kernel(*refs):
        first = n_smem + n_args
        body(*refs[:first], *refs[first + len(after):])

    return pl.pallas_call(
        kernel,
        out_shape=tuple(pltpu.HBM(a.shape, a.dtype) if i in raw_outs else a for i, a in enumerate(outs)),
        in_specs=[SMEM_SPEC] * n_smem
        + [HBM_SPEC if i in raw_args else VMEM_SPEC for i in range(n_args)] + [ANY_SPEC] * len(after),
        out_specs=tuple(HBM_SPEC if i in raw_outs else VMEM_SPEC for i in range(len(outs))),
        scratch_shapes=list(scratch),
        compiler_params=pltpu.CompilerParams(vmem_limit_bytes=min(VMEM_MOST, held)),
        cost_estimate=pl.CostEstimate(
            flops=flops, bytes_accessed=sum(a.size * a.dtype.itemsize for a in arrays), transcendentals=0
        ),
        name=name,
    )(
        *smem,
        *[pltpu.with_memory_space_constraint(a, pltpu.HBM) if i in raw_args else a for i, a in enumerate(args)],
        *after,
    )


def begin(pairs, sems):
    copies = [pltpu.make_async_copy(a, b, sems.at[i]) for i, (a, b) in enumerate(pairs)]
    for copy in copies:
        copy.start()
    return copies


def finish(copies):
    for copy in copies:
        copy.wait()


def dma(count):
    return pltpu.SemaphoreType.DMA((count,))


def dot(a, b, ca=1, cb=0):
    return lax.dot_general(a, b, (((ca,), (cb,)), ((), ())), preferred_element_type=f32)


def picks(rows, columns, start_row, start_column=0):
    r = lax.broadcasted_iota(jnp.int32, (rows, columns), 0) - start_row
    c = lax.broadcasted_iota(jnp.int32, (rows, columns), 1) - start_column
    return r, c


def one_hot(mask):
    return jnp.where(mask, 1.0, 0.0).astype(bf16)


def inverse_rms(values):
    return lax.rsqrt(jnp.mean(values * values, axis=-1, keepdims=True) + EPSILON)


def norm_back(values, gain, grad):
    inverse = inverse_rms(values)
    scaled = grad * gain
    mean = jnp.mean(scaled * values, axis=-1, keepdims=True)
    return inverse * (scaled - values * (inverse * inverse * mean))


def aligned(index, size):
    return pl.ds(pl.multiple_of(index * size, size), size)


def pack_first(weights, gains):
    size, model = weights[0].shape
    parts = len(weights)

    def body(*refs):
        gain_ref, out_ref, held, sems = refs[parts:]
        copies = begin([(refs[i], held.at[i]) for i in range(parts)], sems)
        r, c = picks(size, model, 0)
        along = dot(gain_ref[...], one_hot(r == c)).astype(bf16)
        r, c = picks(GAIN_ROWS, 2, 0)
        out_ref[parts * size:, :] = dot(one_hot(r == c), along).astype(bf16)
        finish(copies)
        for i in range(parts):
            out_ref[i * size:(i + 1) * size, :] = held[i]

    scratch = [pltpu.VMEM((parts, size, model), bf16), dma(parts)]
    outs = [shaped((parts * size + GAIN_ROWS, model))]
    return call(
        body, "pack_first", outs, [], list(weights) + [gains], scratch, raw_args=tuple(range(parts))
    )[0]


def join_dp(meta, pieces, x_links, outer):
    depth = len(pieces)
    total_rows, model = pieces[0].shape
    size = (total_rows - GAIN_ROWS) // 4
    joined = size * depth
    links = len(x_links)
    lanes = 128

    def body(meta_ref, *refs):
        ins, x_refs, outer_ref, outs, sems = (
            refs[:depth], refs[depth:depth + links], refs[depth + links], refs[depth + links + 1:-1], refs[-1]
        )
        pairs = [(x_refs[2].at[0], outs[1]), (x_refs[1].at[1], outs[2])]
        copies = begin(pairs + [(x_refs[i], outs[3].at[i]) for i in range(links)], sems)
        total = jnp.zeros((4 * joined, model), f32)
        gains = jnp.zeros((GAIN_ROWS, lanes), f32)
        for m in range(depth):
            d = meta_ref[1] ^ m
            r = lax.broadcasted_iota(jnp.int32, (4 * joined, total_rows), 0)
            c = lax.broadcasted_iota(jnp.int32, (4 * joined, total_rows), 1)
            want = jnp.where((r % joined) // size == d, (r // joined) * size + r % size, -1)
            total += dot(one_hot(c == want), ins[m][...])
            r, c = picks(lanes, lanes, 0, d * size)
            gains += dot(ins[m][4 * size:, :lanes], one_hot(jnp.logical_and(r == c, r < size)))
        outs[0][:4 * joined, :] = total.astype(bf16)
        outs[0][4 * joined:, :] = jnp.zeros((GAIN_ROWS, model), bf16)
        outs[0][4 * joined:, :lanes] = gains.astype(bf16)
        outs[4][:whole, :] = outs[0][...]
        outs[4][whole:, :] = outer_ref[...]
        finish(copies)

    rows, width, model = x_links[0].shape
    whole = 4 * joined + GAIN_ROWS
    outs = [
        shaped((whole, model)), shaped((width, model)), shaped((width, model)), shaped((links, rows, width, model)),
        shaped((whole + outer.shape[0], model)),
    ]
    return call(
        body, "join_dp", outs, [meta], list(pieces) + list(x_links) + [outer], [dma(2 + links)],
        raw_args=tuple(range(depth, depth + links)),
    )


def forward_across(w_links, x_halves, rest):
    total_rows, model = w_links[0].shape
    cut_at = (total_rows - GAIN_ROWS) // 2
    links = len(w_links)

    def body(*refs):
        w_refs, h_refs, outs = refs[:links], refs[links:links + 2], refs[links + 2:]
        outs[4][...] = w_refs[2][total_rows:, :]
        outs[0][...] = w_refs[2][:cut_at, :]
        outs[1][...] = w_refs[1][cut_at:, :]
        for i in range(links):
            outs[2][i] = w_refs[i][:total_rows, :]
        for i in range(2):
            outs[3][i] = h_refs[i][...]

    outs = [
        shaped((cut_at, model)), shaped((total_rows - cut_at, model)), shaped((links, total_rows, model)),
        shaped((2, *x_halves[0].shape)), shaped((rest, model)),
    ]
    return call(body, "forward_across", outs, [], list(w_links) + list(x_halves))


def join_feed(meta, pieces, size, count, after):
    depth, total_rows, model = pieces.shape
    bands = count // GROUP
    band = (total_rows - count * size) // bands

    def body(meta_ref, in_ref, inner_ref, outer_ref, held, joined, sems):
        copies = begin([(in_ref.at[d], held.at[d]) for d in range(depth)], sems)
        for d in range(depth):
            copies[d].wait()
            for k in range(count):
                inner_ref[(k * depth + d) * size:(k * depth + d + 1) * size, :] = held[d, k * size:(k + 1) * size, :]
            for j in range(bands):
                start = count * size + j * band
                joined[j, d * band:(d + 1) * band, :] = held[d, start:start + band, :]
        for j in range(bands):
            outer_ref[aligned((meta_ref[0] // GROUP) ^ j, band * depth), :] = joined[j]

    outs = [shaped((count * depth * size, model)), shaped((bands * band * depth, model))]
    scratch = [
        pltpu.VMEM((depth, total_rows, model), bf16), pltpu.VMEM((bands, band * depth, model), bf16), dma(depth),
    ]
    return call(body, "join_feed", outs, [meta], [pieces], scratch, 0, after, (0,))


def slot_of(meta_ref, slot):
    return meta_ref[2 + 4 * slot], meta_ref[3 + 4 * slot] > 0, meta_ref[4 + 4 * slot]


def masked_cotangent(meta, own, far, after):
    rows, width, model = own.shape

    def body(meta_ref, own_ref, far_ref, out_ref):
        for slot in range(2):
            block, unused, row = slot_of(meta_ref, slot)
            length = meta_ref[5 + 4 * slot]
            position = block * width + lax.broadcasted_iota(jnp.int32, (width, model), 0)
            value = jnp.where(row == 0, own_ref[0].astype(f32), far_ref[...].astype(f32))
            out_ref[slot * width:(slot + 1) * width, :] = jnp.where(position < length, value, 0.0).astype(bf16)

    outs = [shaped((rows * width, model))]
    return call(body, "masked_cotangent", outs, [meta], [own, far], (), 0, after)[0]


def masked(tile, chunk, block, width, fill):
    rows, lanes = tile.shape
    key = chunk * CHUNK + lax.broadcasted_iota(jnp.int32, (rows, lanes), 0)
    query = block * width + lax.broadcasted_iota(jnp.int32, (rows, lanes), 1) % width
    return jnp.where(key <= query, tile, fill)


def mix_columns(vector_t, mix, out_ref, heads, heads_in, scale, by_row):
    model, width = vector_t.shape
    size = model // heads
    for i, h in enumerate(heads_in):
        for g in range(heads):
            factor = (mix[h, g] if by_row else mix[g, h]) * scale
            out_ref[g * size:(g + 1) * size, i * width:(i + 1) * width] = (
                vector_t[g * size:(g + 1) * size, :] * factor
            ).astype(bf16)


def listed(pieces):
    arrays, spots = [], []
    for parts in pieces:
        spot = []
        for array, index in parts:
            known = [i for i, a in enumerate(arrays) if a is array]
            if not known:
                arrays.append(array)
            spot.append((known[0] if known else len(arrays) - 1, index))
        spots.append(spot)
    return arrays, spots


def views(refs, spot):
    return [refs[i] if index is None else refs[i].at[index] for i, index in spot]


def attend_forward(meta, premix, postmix, x_pieces, w_pieces, after):
    count = len(x_pieces)
    x_arrays, x_spots = listed(x_pieces)
    w_arrays, w_spots = listed(w_pieces)
    width, model = x_arrays[0].shape[1:]
    length = count * width
    chunks = length // CHUNK
    heads = premix.shape[0]
    size = model // heads
    pair = 2 * width
    lanes = heads * width
    half = lanes // 2
    w_rows = model // count
    mirror = count - 1

    def body(meta_ref, pre, post, *refs):
        x_refs, refs = refs[:len(x_arrays)], refs[len(x_arrays):]
        w_refs, refs = refs[:len(w_arrays)], refs[len(w_arrays):]
        joined_ref, second_ref, middle_ref, n_out, k_out, v_out, q_ref, ut_out, lse_ref, w_out, wo_out, gain_ref = refs[:12]
        qst, s_ref, acc, mx, total_out, n_ref, k_ref, v_ref, w_ref, wo_ref, ut_ref, xs, gains = refs[12:25]
        vt_ref, refs = refs[-1], refs[:-1]
        x_sems, w_sems, sems, w_sem, ut_sems = refs[25:]
        place = meta_ref[0]
        x_copies = begin([(views(x_refs, x_spots[k])[0], xs.at[k]) for k in range(count)], x_sems)
        pairs, gain_pairs = [], []
        for k in range(count):
            at, spot = 0, aligned(place ^ k, w_rows)
            for ref in views(w_refs, w_spots[k]):
                for start in range(0, ref.shape[0], w_rows):
                    if at > 4:
                        continue
                    if at < 3:
                        target = w_ref.at[spot, at * model:(at + 1) * model]
                        pairs.append((ref.at[start:start + w_rows, :], target))
                    elif at == 3:
                        pairs.append((ref.at[start:start + w_rows, :], wo_ref.at[spot, :]))
                    else:
                        gain_pairs.append((ref.at[start:start + GAIN_ROWS, :128], gains.at[k]))
                    at += 1
        w_copies = begin(gain_pairs + pairs, w_sems)
        finish(x_copies + w_copies[:count])
        gain = jnp.zeros((GAIN_ROWS, model), f32)
        for k in range(count):
            r, c = picks(128, model, 0, (place ^ k) * w_rows)
            gain += dot(gains[k], one_hot(jnp.logical_and(r == c, r < w_rows)))
        gain_ref[...] = gain[:8, :]
        out_copies = [
            pltpu.make_async_copy(w_ref, w_out, w_sem.at[0]), pltpu.make_async_copy(wo_ref, wo_out, w_sem.at[1])
        ]

        finish(w_copies[count:])
        for copy in out_copies:
            copy.start()

        def attend(slot, unused):
            block, active, row = slot_of(meta_ref, slot)
            last = block // 2
            mine = aligned(slot, width)
            ut_copies = [
                pltpu.make_async_copy(ut_ref.at[2 * slot + i], ut_out.at[2 * slot + i], ut_sems.at[2 * slot + i])
                for i in range(2)
            ]

            def leave(c):
                spot = aligned(c, CHUNK)
                pairs = ((n_ref, n_out), (k_ref, k_out), (v_ref, v_out))
                return [
                    pltpu.make_async_copy(a.at[spot, :], b.at[slot, spot, :], sems.at[i, c])
                    for i, (a, b) in enumerate(pairs)
                ]

            @pl.when(active)
            def _():
                for k in range(count):
                    @pl.when((place ^ k) // 2 <= last)
                    def _():
                        xb = xs[k, row].astype(f32)
                        n_ref[aligned(place ^ k, width), :] = (xb * inverse_rms(xb) * gain_ref[0:1, :]).astype(bf16)

            @pl.when(jnp.logical_not(active))
            def _():
                joined_ref[mine, :] = jnp.zeros((width, model), bf16)

            @pl.when(active)
            def _():
                def project(c, unused):
                    nc = n_ref[aligned(c, CHUNK), :]
                    k_ref[aligned(c, CHUNK), :] = dot(nc, w_ref[:, model:2 * model]).astype(bf16)
                    vc = dot(nc, w_ref[:, 2 * model:3 * model]).astype(bf16)
                    v_ref[aligned(c, CHUNK), :] = vc
                    vt_ref[c] = vc.T
                    for copy in leave(c):
                        copy.start()
                    return 0

                lax.fori_loop(0, last + 1, project, 0)
                query = dot(n_ref[aligned(block, width), :], w_ref[:, :model]).astype(bf16)
                q_ref[mine, :] = query
                query_t = query.astype(f32).T
                for part_of in range(2):
                    heads_in = range(part_of * heads // 2, (part_of + 1) * heads // 2)
                    mix_columns(query_t, pre, qst, heads, heads_in, 0.125, False)
                    mx[...] = jnp.full(mx.shape, NEGATIVE, f32)

                    def scores(c, unused):
                        kc = k_ref[aligned(c, CHUNK), :]
                        for t in range(half // pair):
                            part = slice(t * pair, (t + 1) * pair)
                            s = masked(dot(kc, qst[:, part]), c, block, width, NEGATIVE)
                            s_ref[aligned(c, CHUNK), part] = s
                            mx[:, part] = jnp.maximum(mx[:, part], jnp.max(s.reshape(CHUNK // 8, 8, pair), axis=0))
                        return 0

                    lax.fori_loop(0, last + 1, scores, 0)
                    peak = jnp.max(mx[...], axis=0, keepdims=True)
                    acc[...] = jnp.zeros(acc.shape, f32)
                    mx[...] = jnp.zeros(mx.shape, f32)

                    def weigh(c, unused):
                        vt = vt_ref[c]
                        for t in range(half // pair):
                            part = slice(t * pair, (t + 1) * pair)
                            p = jnp.exp(s_ref[aligned(c, CHUNK), part] - peak[:, part])
                            mx[:, part] += jnp.sum(p.reshape(CHUNK // 8, 8, pair), axis=0)
                            acc[:, part] += dot(vt, p.astype(bf16))
                        return 0

                    lax.fori_loop(0, last + 1, weigh, 0)
                    total = jnp.sum(mx[...], axis=0, keepdims=True)
                    lse_ref[slot, :, part_of * half:(part_of + 1) * half] = peak + jnp.log(total)
                    inverse = 1.0 / total
                    for k in range(heads):
                        rows = slice(k * size, (k + 1) * size)
                        out = jnp.zeros((size, width), f32)
                        for i, h in enumerate(heads_in):
                            cols = slice(i * width, (i + 1) * width)
                            u = acc[rows, cols] * inverse[:, cols]
                            ut_ref[2 * slot + part_of, rows, cols] = u.astype(bf16)
                            out += u * post[h, k]
                        if part_of == 0:
                            total_out[rows, :] = out
                        else:
                            total_out[rows, :] += out
                    ut_copies[part_of].start()
                joined_ref[mine, :] = total_out[...].T.astype(bf16)

                def gone(c, unused):
                    finish(leave(c))
                    return 0

                lax.fori_loop(0, last + 1, gone, 0)

            residual = jnp.where(row == 0, xs[0, 0].astype(f32), xs[mirror, 1].astype(f32))
            middle = residual + dot(joined_ref[mine, :], wo_ref[...])
            middle_ref[mine, :] = middle
            second_ref[mine, :] = (middle * inverse_rms(middle) * gain_ref[1:2, :]).astype(bf16)

            @pl.when(active)
            def _():
                finish(ut_copies)

            return 0

        lax.fori_loop(0, 2, attend, 0)
        finish(out_copies)

    tokens = 2 * width
    outs = [
        shaped((tokens, model)), shaped((tokens, model)), shaped((tokens, model), f32), shaped((2, length, model)),
        shaped((2, length, model)), shaped((2, length, model)), shaped((tokens, model)), shaped((4, model, half)),
        shaped((2, 1, lanes), f32), shaped((model, 3 * model)), shaped((model, model)), shaped((8, model), f32),
    ]
    scratch = [
        pltpu.VMEM((model, half), bf16), pltpu.VMEM((length, half), f32), pltpu.VMEM((model, half), f32),
        pltpu.VMEM((8, half), f32), pltpu.VMEM((model, width), f32), pltpu.VMEM((length, model), bf16),
        pltpu.VMEM((length, model), bf16), pltpu.VMEM((length, model), bf16), pltpu.VMEM((model, 3 * model), bf16),
        pltpu.VMEM((model, model), bf16), pltpu.VMEM((4, model, half), bf16),
        pltpu.VMEM((count, 2, width, model), bf16), pltpu.VMEM((count, GAIN_ROWS, 128), bf16),
        dma(count), dma(5 * count), pltpu.SemaphoreType.DMA((3, chunks)), dma(2), dma(4),
        pltpu.VMEM((chunks, model, CHUNK), bf16),
    ]
    args = x_arrays + w_arrays
    flops = 4 * length * model * (lanes + 2 * model)
    return call(
        body, "attend_forward", outs, [meta, premix, postmix], args, scratch, flops, after,
        tuple(range(len(args))), (3, 4, 5, 7, 9, 10),
    )


def feed_forward(seconds, ups, inner_w, outer_w):
    width, model = seconds[0].shape
    units = inner_w.shape[1]
    tokens = GROUP * width
    root = 0.7978845608028654
    tile = 256

    def body(*refs):
        s_refs, u_refs, (w1, w2), refs = refs[:GROUP], refs[GROUP:2 * GROUP], refs[2 * GROUP:2 * GROUP + 2], refs[2 * GROUP + 2:]
        hidden_ref, inner_ref, grads, outs, (tok, up, sems) = refs[0], refs[1], refs[2:5], refs[5:8], refs[8:]
        spots = [slice(i * width, (i + 1) * width) for i in range(GROUP)]
        pairs = [(s_refs[i], tok.at[spots[i], :]) for i in range(GROUP)]
        pairs += [(u_refs[i], up.at[spots[i], :]) for i in range(GROUP)]
        copies = begin(pairs, sems)
        finish(copies[:GROUP])
        for t in range(units // tile):
            part = slice(t * tile, (t + 1) * tile)
            v = dot(tok[...], w1[:, part])
            squared = v * v
            th = jnp.tanh(root * (v + 0.044715 * (squared * v)))
            hidden_ref[:, part] = (0.5 * v * (1.0 + th)).astype(bf16)
            slope = 0.5 * (1.0 + th) + 0.5 * v * (1.0 - th * th) * (root * (1.0 + 0.134145 * squared))
            if t == 0:
                finish(copies[GROUP:])
            inner_ref[:, part] = (dot(up[...], w2[part, :], 1, 1) * slope).astype(bf16)
        for (own_ref, give_ref, across_ref), made in (
            (grads, dot(inner_ref[...], w1[...], 1, 1)), (outs, dot(hidden_ref[...], w2[...]))
        ):
            made = made.astype(bf16)
            own_ref[...] = made[:width]
            give_ref[:width, :] = made[width:2 * width]
            give_ref[width:, :] = made[3 * width:]
            across_ref[...] = made[2 * width:3 * width]

    outs = [shaped((tokens, units)), shaped((tokens, units))]
    outs += [shaped((width, model)), shaped((2 * width, model)), shaped((width, model))] * 2
    scratch = [pltpu.VMEM((tokens, model), bf16), pltpu.VMEM((tokens, model), bf16), dma(2 * GROUP)]
    args = list(seconds) + list(ups) + [inner_w, outer_w]
    made = call(
        body, "feed_forward", outs, [], args, scratch, 8 * tokens * model * units, (), tuple(range(2 * GROUP))
    )
    return made[0], made[1], made[2:5], made[5:8]


def feed_weights(meta, seconds, ups, hidden, inner, bands, after):
    width, model = seconds[0].shape
    units = hidden.shape[1]
    tokens = GROUP * width
    rows_out = units // bands

    def body(meta_ref, *refs):
        s_refs, u_refs, (h_ref, i_ref), refs = refs[:GROUP], refs[GROUP:2 * GROUP], refs[2 * GROUP:2 * GROUP + 2], refs[2 * GROUP + 2:]
        inner_out, outer_j, (tok, up, grad, sems) = refs[0], refs[1:1 + bands], refs[1 + bands:]
        pairs = [(s_refs[i], tok.at[i * width:(i + 1) * width, :]) for i in range(GROUP)]
        pairs += [(u_refs[i], up.at[i * width:(i + 1) * width, :]) for i in range(GROUP)]
        copies = begin(pairs, sems)
        finish(copies[:GROUP])
        inner_out[...] = dot(tok[...], i_ref[...], 0, 0).astype(bf16)
        finish(copies[GROUP:])
        grad[...] = dot(h_ref[...], up[...], 0, 0).astype(bf16)
        for j in range(bands):
            outer_j[j][...] = grad[aligned((meta_ref[0] // GROUP) ^ j, rows_out), :]

    outs = [shaped((model, units))] + [shaped((rows_out, model))] * bands
    args = list(seconds) + list(ups) + [hidden, inner]
    scratch = [
        pltpu.VMEM((tokens, model), bf16), pltpu.VMEM((tokens, model), bf16), pltpu.VMEM((units, model), bf16),
        dma(2 * GROUP),
    ]
    made = call(
        body, "feed_weights", outs, [meta], args, scratch, 4 * tokens * model * units, after, tuple(range(2 * GROUP))
    )
    return made[0], list(made[1:])


def before_attention_back(own, got, came, middle, up, gains, w, joined, inner_grads, out_got, out_across, count, after):
    tokens, model = own.shape
    rows = model // count

    def body(own_ref, got_ref, came_ref, middle_ref, up_ref, gain_ref, w_in, joined_ref, inner_ref, out_got_ref, out_ref,
             grad_ref, upstream_ref, packed_ref, across_ref, w_ref, total_ref, sems):
        across_ref[...] = (out_ref[...].astype(f32) + out_got_ref[tokens:, :].astype(f32)).astype(bf16)
        copies = begin([(w_in, w_ref), (inner_ref, total_ref.at[:, rows:, :])], sems)
        second = own_ref[...].astype(f32) + got_ref[:tokens, :].astype(f32) + came_ref[...].astype(f32)
        back = norm_back(middle_ref[...], gain_ref[1:2, :], second)
        grad = up_ref[...].astype(f32) + back
        grad_ref[...] = grad
        cast = grad.astype(bf16)
        total = dot(joined_ref[...], cast, 0, 0)
        for j in range(count):
            total_ref[j, :rows, :] = total[j * rows:(j + 1) * rows, :].astype(bf16)
        copies[1].wait()
        last = pltpu.make_async_copy(total_ref, packed_ref, sems.at[2])
        last.start()
        copies[0].wait()
        upstream_ref[...] = dot(cast, w_ref[...], 1, 1).astype(bf16)
        last.wait()

    outs = [
        shaped((tokens, model), f32), shaped((tokens, model)), shaped((count, 2 * rows, model)), shaped((tokens, model)),
    ]
    args = [own, got, came, middle, up, gains, w, joined, inner_grads.reshape(count, rows, model), out_got, out_across]
    scratch = [pltpu.VMEM((model, model), bf16), pltpu.VMEM((count, 2 * rows, model), bf16), dma(3)]
    return call(
        body, "before_attention_back", outs, [], args, scratch, 4 * tokens * model * model, after, (6, 8), (2,)
    )


def attend_back(meta, premix, postmix, pre_row, post_row, query, upstream, normed, keys, values, ut, lse, count, after):
    tokens, model = query.shape
    width = tokens // 2
    length = keys.shape[1]
    heads = premix.shape[0]
    size = model // heads
    pair = 2 * width
    lanes = heads * width
    half = lanes // 2
    w_rows = model // count

    def body(meta_ref, pre, post, pre_in, post_in, q_in, up_in, lse_in, n_hbm, k_hbm, v_hbm, ut_hbm,
             dq_ref, dk_hbm, dv_hbm, mix_out, keep_ref, give_ref,
             qst, qs, ust, us, acc, pbuf, lbuf, dots, wacc, cin, cout, n_own, ut_held, in_sems, out_sems, own_sem, ut_sems,
             pre_row, post_row, q_ref, up_ref, lse_ref, arg_sems, kt_ref, nt_ref, mix_ref):
        args = begin(
            [(pre_in, pre_row), (post_in, post_row), (q_in, q_ref), (up_in, up_ref), (lse_in, lse_ref)], arg_sems
        )
        wacc[...] = jnp.zeros(wacc.shape, f32)
        mix_ref[...] = jnp.zeros(mix_ref.shape, f32)
        finish(args)

        def through(slot, unused):
            block, active, unused_row = slot_of(meta_ref, slot)
            last = block // 2
            mine = aligned(slot, width)
            ut_copies = [
                pltpu.make_async_copy(ut_hbm.at[2 * slot + i], ut_held.at[i], ut_sems.at[i]) for i in range(2)
            ]

            @pl.when(jnp.logical_not(active))
            def _():
                dq_ref[mine, :] = jnp.zeros((width, model), bf16)

            @pl.when(active)
            def _():
                def fetch(c):
                    return [
                        pltpu.make_async_copy(
                            a.at[slot, aligned(c, CHUNK), :], cin.at[c % 2, i], in_sems.at[c % 2, i]
                        )
                        for i, a in enumerate((k_hbm, v_hbm, n_hbm))
                    ]

                def leave(c):
                    return [
                        pltpu.make_async_copy(
                            cout.at[c % 2, i], a.at[slot, aligned(c, CHUNK), :], out_sems.at[c % 2, i]
                        )
                        for i, a in enumerate((dk_hbm, dv_hbm))
                    ]

                own = pltpu.make_async_copy(n_hbm.at[slot, aligned(block, width), :], n_own, own_sem)
                own.start()
                for copy in ut_copies + fetch(0):
                    copy.start()
                q = q_ref[mine, :].astype(f32)
                up = up_ref[mine, :].astype(f32)
                qt, upt = q.T, up.T
                mix_columns(qt, pre, qst, heads, range(heads), 0.125, False)
                mix_columns(upt, post, ust, heads, range(heads), 1.0, True)
                for h in range(heads):
                    spot = slice(h * width, (h + 1) * width)
                    qs[spot, :] = (q * (pre_row[h:h + 1, :] * 0.125)).astype(bf16)
                    us[spot, :] = (up * post_row[h:h + 1, :]).astype(bf16)
                finish(ut_copies)
                for h in range(heads):
                    spot = slice(h * width, (h + 1) * width)
                    column = h % (heads // 2) * width
                    u = ut_held[h // (heads // 2), :, column:column + width].astype(f32)
                    t = jnp.sum((u * upt).reshape(heads, size, width), axis=1)
                    mix_ref[(heads + h) * heads:(heads + h + 1) * heads, :] += t
                    d = jnp.zeros((1, width), f32)
                    for k in range(heads):
                        d += t[k:k + 1, :] * post[h, k]
                    dots[:, spot] = d
                acc[...] = jnp.zeros(acc.shape, f32)

                def visit(c, unused):
                    finish(fetch(c))

                    @pl.when(c < last)
                    def _():
                        for copy in fetch(c + 1):
                            copy.start()

                    kc, vc = cin[c % 2, 0], cin[c % 2, 1]
                    kt_ref[...] = kc.T
                    nt_ref[...] = cin[c % 2, 2].T
                    for t in range(heads // 2):
                        part = slice(t * pair, (t + 1) * pair)
                        p = masked(jnp.exp(dot(kc, qst[:, part]) - lse_ref[slot, :, part]), c, block, width, 0.0)
                        grad = (p * (dot(vc, ust[:, part]) - dots[:, part])).astype(bf16)
                        pbuf[:, part] = p.astype(bf16)
                        lbuf[:, part] = grad
                        acc[:, part] += dot(kt_ref[...], grad)

                    @pl.when(c >= 2)
                    def _():
                        finish(leave(c - 2))

                    dk = dot(lbuf[...], qs[...]).astype(bf16)
                    dv = dot(pbuf[...], us[...]).astype(bf16)
                    cout[c % 2, 0] = dk
                    cout[c % 2, 1] = dv
                    for copy in leave(c):
                        copy.start()
                    wacc[:, model:2 * model] += dot(nt_ref[...], dk)
                    wacc[:, 2 * model:] += dot(nt_ref[...], dv)
                    return 0

                lax.fori_loop(0, last + 1, visit, 0)
                for g in range(heads):
                    rows = slice(g * size, (g + 1) * size)
                    out = jnp.zeros((size, width), f32)
                    qg = qt[rows, :] * 0.125
                    for h in range(heads):
                        a = acc[rows, h * width:(h + 1) * width]
                        out += a * pre[g, h]
                        mix_ref[g * heads + h:g * heads + h + 1, :] += jnp.sum(a * qg, axis=0, keepdims=True)
                    acc[rows, 0:width] = out * 0.125
                dq = acc[:, 0:width].T.astype(bf16)
                dq_ref[mine, :] = dq
                own.wait()
                wacc[:, :model] += dot(n_own[...], dq, 0, 0)

                @pl.when(last >= 1)
                def _():
                    finish(leave(last - 1))

                finish(leave(last))

            return 0

        lax.fori_loop(0, 2, through, 0)
        every = jnp.sum(mix_ref[...], axis=1, keepdims=True)
        r = lax.broadcasted_iota(jnp.int32, mix_ref.shape, 0)
        c = lax.broadcasted_iota(jnp.int32, mix_ref.shape, 1)
        every = jnp.where(r % 128 == c, every, 0.0)
        mix_out[...] = jnp.zeros(mix_out.shape, f32)
        for i in range(-(-mix_ref.shape[0] // 128)):
            mix_out[i:i + 1, :] = jnp.sum(every[i * 128:(i + 1) * 128, :], axis=0, keepdims=True)
        for k in range(count):
            (keep_ref, give_ref)[k % 2][k // 2 * w_rows:(k // 2 + 1) * w_rows, :] = wacc[
                aligned(meta_ref[0] ^ k, w_rows), :
            ].astype(bf16)

    outs = [
        shaped((tokens, model)), shaped((2, length, model)), shaped((2, length, model)),
        shaped((8, 128), f32), shaped((count // 2 * w_rows, 3 * model)),
        shaped((count // 2 * w_rows, 3 * model)),
    ]
    scratch = [
        pltpu.VMEM((model, lanes), bf16), pltpu.VMEM((lanes, model), bf16), pltpu.VMEM((model, lanes), bf16),
        pltpu.VMEM((lanes, model), bf16), pltpu.VMEM((model, lanes), f32), pltpu.VMEM((CHUNK, lanes), bf16),
        pltpu.VMEM((CHUNK, lanes), bf16), pltpu.VMEM((1, lanes), f32), pltpu.VMEM((model, 3 * model), f32),
        pltpu.VMEM((2, 3, CHUNK, model), bf16), pltpu.VMEM((2, 2, CHUNK, model), bf16), pltpu.VMEM((width, model), bf16),
        pltpu.VMEM((2, model, half), bf16), pltpu.SemaphoreType.DMA((2, 3)), pltpu.SemaphoreType.DMA((2, 2)),
        pltpu.SemaphoreType.DMA, dma(2), pltpu.VMEM((heads, model), f32), pltpu.VMEM((heads, model), f32),
        pltpu.VMEM((tokens, model), bf16), pltpu.VMEM((tokens, model), bf16), pltpu.VMEM((2, 1, lanes), f32), dma(5),
        pltpu.VMEM((model, CHUNK), bf16), pltpu.VMEM((model, CHUNK), bf16),
        pltpu.VMEM((2 * heads * heads, width), f32),
    ]
    args = [pre_row, post_row, query, upstream, lse, normed, keys, values, ut]
    return call(
        body, "attend_back", outs, [meta, premix, postmix], args, scratch, 15 * length * model * lanes, after,
        tuple(range(9)), (1, 2),
    )


def input_back(meta, dq, dk, dv, w, x_pieces, gains, grad, after):
    count = len(x_pieces)
    x_arrays, x_spots = listed(x_pieces)
    width, model = x_arrays[0].shape[1:]
    length = dk.shape[1]
    chunks = length // CHUNK

    def body(meta_ref, dq_in, grad_in, gain_in, dk_hbm, dv_hbm, w_hbm, *refs):
        x_refs, refs = refs[:len(x_arrays)], refs[len(x_arrays):]
        keep_ref, give_ref, normed, dk_held, dv_held, w_ref, xs, sems, w_sem, x_sems = refs[:10]
        dq_ref, grad_ref, gain_ref, arg_sems, wt_ref = refs[10:]
        arg_copies = begin([(dq_in, dq_ref), (grad_in, grad_ref), (gain_in, gain_ref)], arg_sems)
        place = meta_ref[0]
        w_copy = pltpu.make_async_copy(w_hbm, w_ref, w_sem)
        w_copy.start()

        def fetch(slot, c):
            spot = aligned(c, CHUNK)
            return [
                pltpu.make_async_copy(a.at[slot, spot, :], b.at[slot, spot, :], sems.at[slot, c, i])
                for i, (a, b) in enumerate(((dk_hbm, dk_held), (dv_hbm, dv_held)))
            ]

        def start(slot, c):
            for copy in fetch(slot, c):
                copy.start()
            return 0

        for slot in range(2):
            block, active, row = slot_of(meta_ref, slot)
            needed = jnp.where(active, block // 2 + 1, 0)
            lax.fori_loop(0, needed, lambda c, unused, slot=slot: start(slot, c), 0)
        x_copies = begin([(views(x_refs, x_spots[k])[0], xs.at[k]) for k in range(count)], x_sems)
        w_copy.wait()
        for i in range(3):
            wt_ref[i] = w_ref[:, i * model:(i + 1) * model].T
        finish(arg_copies)

        finish(x_copies)

        def through(slot, unused):
            block, active, row = slot_of(meta_ref, slot)
            mine = aligned(slot, width)

            @pl.when(active)
            def _():
                def visit(c, unused):
                    spot = aligned(c, CHUNK)
                    finish(fetch(slot, c))
                    normed[spot, :] = dot(dk_held[slot, spot, :], wt_ref[1]) + dot(dv_held[slot, spot, :], wt_ref[2])
                    return 0

                lax.fori_loop(0, block // 2 + 1, visit, 0)
                normed[aligned(block, width), :] += dot(dq_ref[mine, :], wt_ref[0])

            def chip(i, unused):
                for k, out_ref in enumerate((keep_ref, give_ref)):
                    source = place ^ (2 * i + k)
                    spot = aligned(2 * i + row, width)
                    used = jnp.logical_and(active, source <= block)

                    @pl.when(jnp.logical_not(used))
                    def _():
                        out_ref[spot, :] = jnp.zeros((width, model), bf16)

                    @pl.when(used)
                    def _():
                        back = norm_back(
                            xs[2 * i + k, row].astype(f32), gain_ref[0:1, :], normed[aligned(source, width), :]
                        )
                        factor = jnp.where(source == block, 1.0, 0.0)
                        out_ref[spot, :] = (back + grad_ref[mine, :] * factor).astype(bf16)
                return 0

            lax.fori_loop(0, count // 2, chip, 0)
            return 0

        lax.fori_loop(0, 2, through, 0)

    half = count * width
    outs = [shaped((half, model)), shaped((half, model))]
    args = [dq, grad, gains, dk, dv, w] + x_arrays
    scratch = [
        pltpu.VMEM((length, model), f32), pltpu.VMEM((2, length, model), bf16), pltpu.VMEM((2, length, model), bf16),
        pltpu.VMEM((model, 3 * model), bf16), pltpu.VMEM((count, 2, width, model), bf16),
        pltpu.SemaphoreType.DMA((2, chunks, 2)), pltpu.SemaphoreType.DMA, dma(count),
        pltpu.VMEM(dq.shape, bf16), pltpu.VMEM(grad.shape, f32), pltpu.VMEM(gains.shape, f32), dma(3),
        pltpu.VMEM((3, model, model), bf16),
    ]
    return call(
        body, "input_back", outs, [meta], args, scratch, 8 * length * model * model, after,
        tuple(range(len(args))),
    )


def pair_sums(keep, got, count, later, after, name):
    blocks = count // 2
    rows, columns = keep.shape[0] // blocks, keep.shape[1]

    def body(keep_ref, got_ref, *refs):
        outs = refs[len(later):]
        for source, target in zip(refs, outs[blocks:]):
            target[...] = source[...]
        for i in range(blocks):
            spot = slice(i * rows, (i + 1) * rows)
            outs[i][...] = (keep_ref[spot, :].astype(f32) + got_ref[spot, :].astype(f32)).astype(outs[i].dtype)

    outs = [shaped((rows, columns))] * blocks
    outs += [shaped(a.shape, a.dtype) for a in later]
    made = call(body, name, outs, [], [keep, got] + list(later), (), 0, after)
    return made[:blocks], made[blocks:]


def halves_first(keep, got, pair, after, name):
    rows, columns = keep.shape[0] // 4, keep.shape[1]
    half = rows // 2

    def body(keep_ref, got_ref, *refs):
        if pair:
            refs[-1][...] = refs[0][...] + refs[1][...]
        two_ref, four_ref, rest_ref = refs[len(pair):len(pair) + 3]

        def part(i, b):
            spot = slice(i * rows + b * half, i * rows + (b + 1) * half)
            return keep_ref[spot, :].astype(f32) + got_ref[spot, :].astype(f32)

        for n, (i, b) in enumerate(((1, 0), (3, 0))):
            two_ref[n * half:(n + 1) * half, :] = part(i, b).astype(bf16)
        for n, (i, b) in enumerate(((2, 1), (3, 1))):
            four_ref[n * half:(n + 1) * half, :] = part(i, b).astype(bf16)
        for n, (i, b) in enumerate(((0, 0), (2, 0), (0, 1), (1, 1))):
            rest_ref[n * half:(n + 1) * half, :] = part(i, b)

    outs = [
        shaped((rows, columns)), shaped((rows, columns)), shaped((2 * rows, columns), f32),
    ] + [shaped(a.shape, f32) for a in pair[:1]]
    return call(body, name, outs, [], [keep, got, *pair], (), 0, after)


def halves_second(rest, from_two, from_four, pair, after, name):
    rows, columns = from_two.shape
    half = rows // 2

    def body(rest_ref, two_in, four_in, one, other, two_ref, four_ref, own_ref, sum_ref):
        sum_ref[...] = one[...] + other[...]
        own_ref[:half, :] = rest_ref[:half, :] + two_in[:half, :].astype(f32)
        four_ref[...] = (rest_ref[half:rows, :] + two_in[half:, :].astype(f32)).astype(bf16)
        own_ref[half:, :] = rest_ref[rows:rows + half, :] + four_in[:half, :].astype(f32)
        two_ref[...] = (rest_ref[rows + half:, :] + four_in[half:, :].astype(f32)).astype(bf16)

    outs = [
        shaped((half, columns)), shaped((half, columns)), shaped((rows, columns), f32), shaped(pair[0].shape, f32),
    ]
    return call(body, name, outs, [], [rest, from_two, from_four, *pair], (), 0, after)


def input_sum(own, from_four, from_two, shape):
    rows, width, model = shape

    def body(own_ref, four_ref, two_ref, out_ref):
        out_ref[0] = (own_ref[:width, :] + four_ref[...].astype(f32)).astype(bf16)
        out_ref[1] = (own_ref[width:, :] + two_ref[...].astype(f32)).astype(bf16)

    return call(body, "input_sum", [shaped(shape)], [], [own, from_four, from_two])[0]


def split_dp(meta, depth, parts, pair, after):
    joined, wide = parts[0].shape
    size = joined // depth
    halved = parts[1].shape[0] != joined

    def body(meta_ref, *refs):
        ins, (one, other), outs, sum_ref = refs[:len(parts)], refs[len(parts):len(parts) + 2], refs[len(parts) + 2:-2], refs[-2]
        total_ref = refs[-1]
        sum_ref[...] = one[...] + other[...]
        if halved:
            for i in range(2):
                spot = slice(i * joined // 2, (i + 1) * joined // 2)
                total_ref[spot, :] = (ins[0][spot, :] + ins[1 + i][...].astype(f32)).astype(bf16)
        else:
            total = ins[0][...].astype(f32)
            for ref in ins[1:]:
                total += ref[...].astype(f32)
            total_ref[...] = total.astype(bf16)
        for m in range(depth):
            r, c = picks(size, joined, 0, (meta_ref[1] ^ m) * size)
            outs[m][...] = dot(one_hot(r == c), total_ref[...]).astype(bf16)

    outs = [shaped((size, wide))] * depth + [shaped(pair[0].shape, f32)]
    scratch = [pltpu.VMEM((joined, wide), bf16)]
    made = call(body, "split_dp", outs, [meta], list(parts) + list(pair), scratch, 0, after)
    return made[:depth], made[depth]


def split_feed(meta, depth, grads, outer, size, middle, parts_out):
    count, joined, units = grads.shape
    joined //= 2
    bands = len(outer)
    band = outer[0].shape[0]
    shard = band // depth
    parts = 1 + GROUP
    out_rows = parts * size + shard
    tokens = middle.shape[0]
    width = tokens // 2

    def body(meta_ref, grad_in, *refs):
        o_ins, out_ins, refs = refs[:bands], refs[bands:bands + 4], refs[bands + 4:]
        outs, (total, grad_ref, outer_ref, middle_ref, part_ref, sems) = refs[:3], refs[3:]
        o_refs = [outer_ref.at[j] for j in range(bands)]
        pairs = [(out_ins[0], middle_ref)] + [(out_ins[1 + i].at[:tokens, :], part_ref.at[i]) for i in range(3)]
        copies = begin(pairs + [(grad_in, grad_ref)] + [(o_ins[j], o_refs[j]) for j in range(bands)], sems)
        finish(copies[:4])
        for slot in range(2):
            block, unused, row = slot_of(meta_ref, slot)
            spot = slice(slot * width, (slot + 1) * width)
            position = block * width + lax.broadcasted_iota(jnp.int32, (width, units), 0)
            value = middle_ref[spot, :]
            for i in range(3):
                value += part_ref[i, spot, :].astype(f32)
            value = jnp.where(position < meta_ref[5 + 4 * slot], value, 0.0).astype(bf16)
            for n in range(2):
                @pl.when(row == n)
                def _():
                    outs[1 + n][...] = value

        finish(copies[4:])
        section = grad_ref[0, :joined, :].astype(f32)
        for j in range(1, count):
            section += grad_ref[j, :joined, :].astype(f32)
        total[:joined, :] = section.astype(bf16)
        for t in range(GROUP):
            section = grad_ref[t, joined:, :].astype(f32)
            for j in range(1, bands):
                section += grad_ref[j * GROUP + t, joined:, :].astype(f32)
            total[(1 + t) * joined:(2 + t) * joined, :] = section.astype(bf16)
        rest = o_refs[0][...].astype(f32)
        for j in range(1, bands):
            rest += o_refs[j][...].astype(f32)
        total[parts * joined:, :] = rest.astype(bf16)
        for d in range(depth):
            for t in range(parts):
                outs[0][d, t * size:(t + 1) * size, :] = total[t * joined + d * size:t * joined + (d + 1) * size, :]
            start = parts * joined + d * shard
            outs[0][d, parts * size:, :] = total[start:start + shard, :]

    scratch = [
        pltpu.VMEM((parts * joined + band, units), bf16), pltpu.VMEM(grads.shape, bf16),
        pltpu.VMEM((bands, band, units), bf16), pltpu.VMEM((tokens, units), f32), pltpu.VMEM((3, tokens, units), bf16),
        dma(5 + bands),
    ]
    args = [grads] + list(outer) + [middle] + list(parts_out)
    outs = [shaped((depth, out_rows, units)), shaped((width, units)), shaped((width, units))]
    return call(body, "split_feed", outs, [meta], args, scratch, 0, (), tuple(range(len(args))))


def finish_projections(pieces, weights):
    size, wide = pieces[0].shape
    parts = 3
    model = wide // parts

    def body(*refs):
        ins, w_ins, outs = refs[:len(pieces)], refs[len(pieces):-6], refs[-6:-2]
        w_held, sems = refs[-2:]
        w_refs = [w_held.at[i] for i in range(parts)]
        finish(begin([(w_ins[i], w_refs[i]) for i in range(parts)], sems))
        along = jnp.zeros((size, 1), f32)
        for i in range(parts):
            part = slice(i * model, (i + 1) * model)
            total = ins[0][:, part].astype(f32)
            for ref in ins[1:]:
                total += ref[:, part].astype(f32)
            outs[i][...] = total
            along += jnp.sum(total * w_refs[i][...].astype(f32), axis=1, keepdims=True)
        outs[3][...] = along

    outs = [shaped((size, model), f32)] * parts + [shaped((size, 1), f32)]
    scratch = [pltpu.VMEM((parts, size, model), bf16), dma(parts)]
    args = list(pieces) + list(weights)
    return call(
        body, "finish_projections", outs, [], args, scratch, raw_args=tuple(range(len(pieces), len(args)))
    )


def finish_feed(pieces, weight, bands):
    size = weight.shape[0]
    rows, units = pieces.shape
    band = units // bands

    def body(in_hbm, w_in, output_ref, inner_ref, outer_ref, along_ref, in_ref, w_ref, sems):
        finish(begin([(in_hbm, in_ref), (w_in, w_ref)], sems))
        total = in_ref[...].astype(f32)
        output_ref[...] = total[:size, :]
        for t in range(GROUP):
            for y in range(bands):
                inner_ref[:, (y * GROUP + t) * band:(y * GROUP + t + 1) * band] = total[
                    (1 + t) * size:(2 + t) * size, y * band:(y + 1) * band
                ]
        outer_ref[...] = total[(1 + GROUP) * size:, :]
        along_ref[...] = jnp.sum(inner_ref[...] * w_ref[...].astype(f32), axis=1, keepdims=True)

    outs = [
        shaped((size, units), f32), shaped((size, GROUP * units), f32),
        shaped((rows - (1 + GROUP) * size, units), f32), shaped((size, 1), f32),
    ]
    scratch = [pltpu.VMEM(pieces.shape, bf16), pltpu.VMEM(weight.shape, bf16), dma(2)]
    return call(body, "finish_feed", outs, [], [pieces, weight], scratch, raw_args=(0, 1))


def swap(value, axis, mask):
    count = lax.axis_size(axis)
    return lax.ppermute(value, axis, [(i, i ^ mask) for i in range(count)])


def gather_dp(value):
    return [value] + [swap(value, "dp", m) for m in range(1, lax.axis_size("dp"))]


def gather_first(meta, inputs, first_w, inner, outer):
    count, depth = lax.axis_size("blk"), lax.axis_size("dp")
    pieces = gather_dp(first_w)
    x_links = [inputs, swap(inputs, "blk", 2), swap(inputs, "blk", 4)]
    w_own, x_on_two, x_on_four, x_core, w_more = join_dp(meta, pieces, x_links, outer)
    if count == 8:
        w_links = [w_own, swap(w_own, "blk", 2), swap(w_more, "blk", 4)]
        halves = [swap(x_on_two, "blk", 2), swap(x_on_four, "blk", 4)]
        x_core = swap(x_core, "blk", 1)
        w_on_two, w_on_four, w_core, x_across, outer_far = forward_across(w_links, halves, outer.shape[0])
        feed = jnp.concatenate([inner, outer, outer_far], axis=0)
        w_across = [swap(w_on_two, "blk", 2), swap(w_on_four, "blk", 4)]
        w_core, x_far = swap(w_core, "blk", 1), swap(x_across, "blk", 1)
        w_far = [swap(part, "blk", 1) for part in w_across]
        xs = [[(a, None)] for a in x_links] + [[(x_across, None)]]
        ws = [[(a, None)] for a in w_links] + [[(a, None) for a in w_across]]
        xs_core = [[(x_core, i)] for i in range(3)] + [[(x_far, None)]]
        ws_core = [[(w_core, i)] for i in range(3)] + [[(a, None) for a in w_far]]
    else:
        x_links += [swap(inputs, "blk", k) for k in range(6, count, 2)]
        shards = [outer] + [swap(outer, "blk", GROUP * j) for j in range(1, count // GROUP)]
        feed = jnp.concatenate([inner] + shards, axis=0)
        w_links = [w_own, swap(w_own, "blk", 2), swap(w_own, "blk", 4)]
        w_links += [swap(w_own, "blk", k) for k in range(6, count, 2)]
        xs, ws = [[(a, None)] for a in x_links], [[(a, None)] for a in w_links]
        xs_core, ws_core = [[(swap(a, "blk", 1), None)] for a in x_links], [[(swap(a, "blk", 1), None)] for a in w_links]
    x_pieces = [part for pair in zip(xs, xs_core) for part in pair]
    w_pieces = [part for pair in zip(ws, ws_core) for part in pair]
    return x_pieces, w_pieces, feed


def all_to_all(value, axis):
    return lax.all_to_all(value, axis, 0, 0, tiled=True)


def gather_group(value):
    two = swap(value, "blk", 2)
    return [value, swap(value, "blk", 1), two, swap(two, "blk", 1)]


def scatter_chips(parts):
    return [parts[0]] + [swap(part, "blk", 2 * i) for i, part in enumerate(parts) if i]


def on_device(
    inputs, lengths, prenorm, midnorm, query_proj, key_proj, value_proj, output_proj,
    premix, postmix, inner_proj, outer_proj, cotangent,
):
    count, depth = lax.axis_size("blk"), lax.axis_size("dp")
    place, zplace = lax.axis_index("blk"), lax.axis_index("dp")
    rows, width, model = inputs.shape
    shard = prenorm.shape[0]
    low = place < count // 2
    mirror = count - 1
    slot_rows = [jnp.where(low, 1, 0), jnp.where(low, 0, 1)]
    blocks = [jnp.maximum(place, place ^ mirror), jnp.minimum(place, place ^ mirror)]
    spans = [jnp.where(slot_rows[i] == 0, lengths[0], lengths[1]) for i in range(2)]
    meta = [place, zplace]
    for i in range(2):
        meta += [blocks[i], (blocks[i] * width < spans[i]).astype(jnp.int32), slot_rows[i], spans[i]]
    meta = jnp.stack(meta).astype(jnp.int32)

    head_size = model // premix.shape[0]
    pre_row = jnp.repeat(premix.T, head_size, axis=1)
    post_row = jnp.repeat(postmix, head_size, axis=1)
    bands = count // GROUP
    band_ff = depth * outer_proj.shape[0]
    first_w = pack_first([query_proj, key_proj, value_proj, output_proj], jnp.stack([prenorm, midnorm]))
    sections = inner_proj.reshape(shard, bands, GROUP, band_ff).transpose(2, 0, 1, 3).reshape(GROUP, shard, -1)
    sections = all_to_all(jnp.concatenate([sections] * bands), "blk").reshape(count * shard, -1)
    x_pieces, w_pieces, second_w = gather_first(meta, inputs, first_w, sections, outer_proj)
    second_w = lax.all_gather(second_w, "dp")
    up = masked_cotangent(meta, cotangent, swap(cotangent[1], "blk", mirror), [w_pieces[2][0][0]])
    ups = gather_group(up)

    joined, second, middle, normed, keys, values, query, ut, lse, w, output_w, gain_rows = attend_forward(
        meta, premix, postmix, x_pieces, w_pieces, [up, pre_row, post_row]
    )
    seconds = gather_group(second)
    inner_w, outer_w = join_feed(meta, second_w, shard, count, [second, ups[2]])
    hidden, inner, (own, give, across), (out_own, out_give, out_across) = feed_forward(
        seconds, ups, inner_w, outer_w
    )
    got = swap(give, "blk", 1)
    tokens = rows * width
    across = (across.astype(f32) + got[tokens:].astype(f32)).astype(bf16)
    came = swap(across, "blk", 2)
    out_got = swap(out_give, "blk", 1)
    inner_grads, outer_grads = feed_weights(meta, seconds, ups, hidden, inner, bands, [across])

    grad, upstream, packed, out_across = before_attention_back(
        own, got, came, middle, up, gain_rows, output_w, joined, inner_grads, out_got, out_across, count, []
    )
    feed_grads = all_to_all(packed, "blk")
    outer_grads = [outer_grads[0]] + [swap(outer_grads[j], "blk", GROUP * j) for j in range(1, bands)]
    out_came = swap(out_across, "blk", 2)
    dq, dk, dv, mixes, keep, give = attend_back(
        meta, premix, postmix, pre_row, post_row, query, upstream, normed, keys, values, ut, lse, count, []
    )
    heads = premix.shape[0]
    cuts, near, far = split_feed(
        meta, depth, feed_grads, outer_grads, shard, middle, [out_own, out_got, out_came]
    )
    outputs = jnp.stack([near, swap(far, "blk", mirror)])
    input_keep, input_give = input_back(meta, dq, dk, dv, w, x_pieces, gain_rows, grad, [cuts])
    cuts = lax.psum_scatter(cuts.reshape(-1, cuts.shape[2]), "dp", scatter_dimension=0, tiled=True)
    give, input_give = swap(give, "blk", 1), swap(input_give, "blk", 1)
    steps = [("dp", 1 << i) for i in range(depth.bit_length() - 1)] + [("blk", 1 << i) for i in range(count.bit_length() - 1)]

    def step(value):
        return value, swap(value, *steps.pop(0))

    if count == 8:
        two, four, rest = halves_first(keep, give, (), [input_keep], "halves_first_w")
        two, four = swap(two, "blk", 2), swap(four, "blk", 4)
        x_two, x_four, x_rest, mixes = halves_first(input_keep, input_give, step(mixes), [rest], "halves_first_x")
        x_two, x_four = swap(x_two, "blk", 2), swap(x_four, "blk", 4)
        two, four, rest, mixes = halves_second(rest, two, four, step(mixes), [x_rest], "halves_second_w")
        two, four = swap(two, "blk", 2), swap(four, "blk", 4)
        x_two, x_four, x_rest, mixes = halves_second(x_rest, x_two, x_four, step(mixes), [rest], "halves_second_x")
        x_two, x_four = swap(x_two, "blk", 2), swap(x_four, "blk", 4)
        cuts_w, mixes = split_dp(meta, depth, [rest, four, two], step(mixes), [x_rest])
        grad_inputs = input_sum(x_rest, x_four, x_two, inputs.shape)
    else:
        projected, unused = pair_sums(keep, give, count, [], [input_keep], "pair_sums_w")
        cuts_w, mixes = split_dp(meta, depth, scatter_chips(projected), step(mixes), [])
        parts, unused = pair_sums(input_keep, input_give, count, [], [], "pair_sums_x")
        grad_inputs = sum([part.astype(f32) for part in scatter_chips(parts)]).astype(bf16).reshape(inputs.shape)
    while steps:
        mixes = sum(step(mixes))
    mixes = mixes.reshape(-1)[:2 * heads * heads].reshape(2, heads, heads)
    output_sum, inner_sum, outer_sum, mid_gain = finish_feed(
        cuts, inner_proj, bands
    )
    cuts = cuts_w
    query_sum, key_sum, value_sum, pre_gain = finish_projections(
        [cuts[0]] + [swap(cuts[m], "dp", m) for m in range(1, depth)],
        [query_proj, key_proj, value_proj],
    )
    return (
        outputs,
        grad_inputs,
        pre_gain.reshape(-1) / prenorm.astype(f32),
        mid_gain.reshape(-1) / midnorm.astype(f32),
        query_sum,
        key_sum,
        value_sum,
        output_sum,
        mixes[0],
        mixes[1],
        inner_sum,
        outer_sum,
    )


def solution(mesh):
    weight = P(("blk", "dp"), None)
    vector = P(("blk", "dp"))
    tokens = P("dp", "blk", None)
    in_specs = (
        tokens, P("dp"), vector, vector, weight, weight, weight, weight, P(), P(), weight, weight, tokens,
    )
    out_specs = (
        tokens, tokens, vector, vector, weight, weight, weight, weight, P(), P(), weight, weight,
    )
    return jax.shard_map(on_device, mesh=mesh, in_specs=in_specs, out_specs=out_specs, check_vma=False)
```

```python
import jax
import jax.numpy as jnp
from jax import lax
from jax.experimental import pallas as pl
from jax.experimental.pallas import tpu as pltpu
from jax.sharding import PartitionSpec as P

EPSILON = 1e-06
GROUP = 4
CHUNK = 256
NEGATIVE = -1e30
VMEM_MOST = 60 * 1024 * 1024
VMEM_SPARE = 8 * 1024 * 1024
VMEM_WINDOWS = 18 * 1024 * 1024
GAIN_ROWS = 16
f32 = jnp.float32
bf16 = jnp.bfloat16
HIGH = lax.Precision.HIGHEST
ANY_SPEC = pl.BlockSpec(memory_space=pl.ANY)
VMEM_SPEC = pl.BlockSpec(memory_space=pltpu.VMEM)
HBM_SPEC = pl.BlockSpec(memory_space=pltpu.HBM)
SMEM_SPEC = pl.BlockSpec(memory_space=pltpu.SMEM)


def shaped(shape, dtype=bf16):
    return jax.ShapeDtypeStruct(shape, dtype)


def vmem_bytes(shape, dtype):
    lead, (rows, columns) = shape[:-2], shape[-2:]
    size = jnp.dtype(dtype).itemsize
    for extent in lead:
        size *= extent
    return size * -(-rows // 16) * 16 * -(-columns // 128) * 128


def call(body, name, outs, smem, args, scratch=(), flops=0, after=(), raw_args=(), raw_outs=(), extra=0):
    n_smem, n_args = len(smem), len(args)
    arrays = list(args) + list(outs)
    windows = [a for i, a in enumerate(args) if i not in raw_args] + [a for i, a in enumerate(outs) if i not in raw_outs]
    windows = sum(vmem_bytes(a.shape, a.dtype) for a in windows)
    held = sum(vmem_bytes(a.shape, a.dtype) for a in scratch if getattr(a, "memory_space", None) == pltpu.VMEM)
    held += VMEM_SPARE + extra + (windows if windows > VMEM_WINDOWS else 0)

    def kernel(*refs):
        first = n_smem + n_args
        body(*refs[:first], *refs[first + len(after):])

    return pl.pallas_call(
        kernel,
        out_shape=tuple(pltpu.HBM(a.shape, a.dtype) if i in raw_outs else a for i, a in enumerate(outs)),
        in_specs=[SMEM_SPEC] * n_smem
        + [HBM_SPEC if i in raw_args else VMEM_SPEC for i in range(n_args)] + [ANY_SPEC] * len(after),
        out_specs=tuple(HBM_SPEC if i in raw_outs else VMEM_SPEC for i in range(len(outs))),
        scratch_shapes=list(scratch),
        compiler_params=pltpu.CompilerParams(vmem_limit_bytes=min(VMEM_MOST, held)),
        cost_estimate=pl.CostEstimate(
            flops=flops, bytes_accessed=sum(a.size * a.dtype.itemsize for a in arrays), transcendentals=0
        ),
        name=name,
    )(
        *smem,
        *[pltpu.with_memory_space_constraint(a, pltpu.HBM) if i in raw_args else a for i, a in enumerate(args)],
        *after,
    )


def begin(pairs, sems):
    copies = [pltpu.make_async_copy(a, b, sems.at[i]) for i, (a, b) in enumerate(pairs)]
    for copy in copies:
        copy.start()
    return copies


def finish(copies):
    for copy in copies:
        copy.wait()


def dma(count):
    return pltpu.SemaphoreType.DMA((count,))


def dot(a, b, ca=1, cb=0):
    return lax.dot_general(a, b, (((ca,), (cb,)), ((), ())), preferred_element_type=f32)


def picks(rows, columns, start_row, start_column=0):
    r = lax.broadcasted_iota(jnp.int32, (rows, columns), 0) - start_row
    c = lax.broadcasted_iota(jnp.int32, (rows, columns), 1) - start_column
    return r, c


def one_hot(mask):
    return jnp.where(mask, 1.0, 0.0).astype(bf16)


def inverse_rms(values):
    return lax.rsqrt(jnp.mean(values * values, axis=-1, keepdims=True) + EPSILON)


def norm_back(values, gain, grad):
    inverse = inverse_rms(values)
    scaled = grad * gain
    mean = jnp.mean(scaled * values, axis=-1, keepdims=True)
    return inverse * (scaled - values * (inverse * inverse * mean))


def aligned(index, size):
    return pl.ds(pl.multiple_of(index * size, size), size)


def pack_first(weights, gains):
    size, model = weights[0].shape
    parts = len(weights)

    def body(*refs):
        gain_ref, out_ref, held, sems = refs[parts:]
        copies = begin([(refs[i], held.at[i]) for i in range(parts)], sems)
        r, c = picks(size, model, 0)
        along = dot(gain_ref[...], one_hot(r == c)).astype(bf16)
        r, c = picks(GAIN_ROWS, 2, 0)
        out_ref[parts * size:, :] = dot(one_hot(r == c), along).astype(bf16)
        finish(copies)
        for i in range(parts):
            out_ref[i * size:(i + 1) * size, :] = held[i]

    scratch = [pltpu.VMEM((parts, size, model), bf16), dma(parts)]
    outs = [shaped((parts * size + GAIN_ROWS, model))]
    return call(
        body, "pack_first", outs, [], list(weights) + [gains], scratch, raw_args=tuple(range(parts))
    )[0]


def join_dp(meta, pieces, x_links, after):
    depth = len(pieces)
    total_rows, model = pieces[0].shape
    size = (total_rows - GAIN_ROWS) // 4
    joined = size * depth
    links = len(x_links)
    lanes = 128

    def body(meta_ref, *refs):
        ins, x_refs, outs, sems = refs[:depth], refs[depth:depth + links], refs[depth + links:-1], refs[-1]
        copies = begin([(x_refs[i], outs[1].at[i]) for i in range(links)], sems)
        total = jnp.zeros((4 * joined, model), f32)
        gains = jnp.zeros((GAIN_ROWS, lanes), f32)
        for m in range(depth):
            d = meta_ref[1] ^ m
            r = lax.broadcasted_iota(jnp.int32, (4 * joined, total_rows), 0)
            c = lax.broadcasted_iota(jnp.int32, (4 * joined, total_rows), 1)
            want = jnp.where((r % joined) // size == d, (r // joined) * size + r % size, -1)
            total += dot(one_hot(c == want), ins[m][...])
            r, c = picks(lanes, lanes, 0, d * size)
            gains += dot(ins[m][4 * size:, :lanes], one_hot(jnp.logical_and(r == c, r < size)))
        outs[0][:4 * joined, :] = total.astype(bf16)
        outs[0][4 * joined:, :] = jnp.zeros((GAIN_ROWS, model), bf16)
        outs[0][4 * joined:, :lanes] = gains.astype(bf16)
        finish(copies)

    rows, width, model = x_links[0].shape
    whole = 4 * joined + GAIN_ROWS
    outs = [shaped((whole, model)), shaped((links, rows, width, model))]
    return call(
        body, "join_dp", outs, [meta], list(pieces) + list(x_links), [dma(links)], after=after,
        raw_args=tuple(range(depth, depth + links)),
    )


def forward_across(w_links, x_halves):
    total_rows, model = w_links[0].shape
    cut_at = (total_rows - GAIN_ROWS) // 2
    links = len(w_links)

    def body(*refs):
        w_refs, h_refs, outs = refs[:links], refs[links:links + 2], refs[links + 2:]
        outs[0][...] = w_refs[2][:cut_at, :]
        outs[1][...] = w_refs[1][cut_at:, :]
        for i in range(links):
            outs[2][i] = w_refs[i][:total_rows, :]
        for i in range(2):
            outs[3][i] = h_refs[i][...]

    outs = [
        shaped((cut_at, model)), shaped((total_rows - cut_at, model)), shaped((links, total_rows, model)),
        shaped((2, *x_halves[0].shape)),
    ]
    return call(body, "forward_across", outs, [], list(w_links) + list(x_halves))


def join_feed(meta, pieces, size, count, after):
    depth, total_rows, model = pieces.shape
    bands = count // GROUP
    band = (total_rows - count * size) // bands

    def body(meta_ref, in_ref, inner_ref, outer_ref, held, joined, sems):
        copies = begin([(in_ref.at[d], held.at[d]) for d in range(depth)], sems)
        for d in range(depth):
            copies[d].wait()
            for k in range(count):
                inner_ref[(k * depth + d) * size:(k * depth + d + 1) * size, :] = held[d, k * size:(k + 1) * size, :]
            for j in range(bands):
                start = count * size + j * band
                joined[j, d * band:(d + 1) * band, :] = held[d, start:start + band, :]
        for j in range(bands):
            outer_ref[aligned((meta_ref[0] // GROUP) ^ j, band * depth), :] = joined[j]

    outs = [shaped((count * depth * size, model)), shaped((bands * band * depth, model))]
    scratch = [
        pltpu.VMEM((depth, total_rows, model), bf16), pltpu.VMEM((bands, band * depth, model), bf16), dma(depth),
    ]
    return call(body, "join_feed", outs, [meta], [pieces], scratch, 0, after, (0,))


def slot_of(meta_ref, slot):
    return meta_ref[2 + 4 * slot], meta_ref[3 + 4 * slot] > 0, meta_ref[4 + 4 * slot]


def masked_cotangent(meta, own, far, after):
    rows, width, model = own.shape

    def body(meta_ref, own_ref, far_ref, out_ref):
        for slot in range(2):
            block, unused, row = slot_of(meta_ref, slot)
            length = meta_ref[5 + 4 * slot]
            position = block * width + lax.broadcasted_iota(jnp.int32, (width, model), 0)
            value = jnp.where(row == 0, own_ref[0].astype(f32), far_ref[...].astype(f32))
            out_ref[slot * width:(slot + 1) * width, :] = jnp.where(position < length, value, 0.0).astype(bf16)

    outs = [shaped((rows * width, model))]
    return call(body, "masked_cotangent", outs, [meta], [own, far], (), 0, after)[0]


def masked(tile, chunk, block, width, fill):
    rows, lanes = tile.shape
    key = chunk * CHUNK + lax.broadcasted_iota(jnp.int32, (rows, lanes), 0)
    query = block * width + lax.broadcasted_iota(jnp.int32, (rows, lanes), 1) % width
    return jnp.where(key <= query, tile, fill)


def mix_columns(vector_t, mix, out_ref, heads, heads_in, scale, by_row):
    model, width = vector_t.shape
    size = model // heads
    for i, h in enumerate(heads_in):
        for g in range(heads):
            factor = (mix[h, g] if by_row else mix[g, h]) * scale
            out_ref[g * size:(g + 1) * size, i * width:(i + 1) * width] = (
                vector_t[g * size:(g + 1) * size, :] * factor
            ).astype(bf16)


def listed(pieces):
    arrays, spots = [], []
    for parts in pieces:
        spot = []
        for array, index in parts:
            known = [i for i, a in enumerate(arrays) if a is array]
            if not known:
                arrays.append(array)
            spot.append((known[0] if known else len(arrays) - 1, index))
        spots.append(spot)
    return arrays, spots


def views(refs, spot):
    return [refs[i] if index is None else refs[i].at[index] for i, index in spot]


def attend_forward(meta, premix, postmix, x_pieces, w_pieces, after):
    count = len(x_pieces)
    x_arrays, x_spots = listed(x_pieces)
    w_arrays, w_spots = listed(w_pieces)
    width, model = x_arrays[0].shape[1:]
    length = count * width
    chunks = length // CHUNK
    heads = premix.shape[0]
    size = model // heads
    pair = 2 * width
    lanes = heads * width
    half = lanes // 2
    w_rows = model // count
    mirror = count - 1

    def body(meta_ref, pre, post, *refs):
        x_refs, refs = refs[:len(x_arrays)], refs[len(x_arrays):]
        w_refs, refs = refs[:len(w_arrays)], refs[len(w_arrays):]
        joined_ref, second_ref, middle_ref, n_out, k_out, v_out, q_ref, ut_out, lse_ref, w_out, wo_out, gain_ref = refs[:12]
        qst, s_ref, acc, mx, total_out, n_ref, k_ref, v_ref, w_ref, wo_ref, ut_ref, xs, gains = refs[12:25]
        vt_ref, refs = refs[-1], refs[:-1]
        x_sems, w_sems, sems, w_sem, ut_sems = refs[25:]
        place = meta_ref[0]
        x_copies = begin([(views(x_refs, x_spots[k])[0], xs.at[k]) for k in range(count)], x_sems)
        pairs, gain_pairs = [], []
        for k in range(count):
            at, spot = 0, aligned(place ^ k, w_rows)
            for ref in views(w_refs, w_spots[k]):
                for start in range(0, ref.shape[0], w_rows):
                    if at > 4:
                        continue
                    if at < 3:
                        target = w_ref.at[spot, at * model:(at + 1) * model]
                        pairs.append((ref.at[start:start + w_rows, :], target))
                    elif at == 3:
                        pairs.append((ref.at[start:start + w_rows, :], wo_ref.at[spot, :]))
                    else:
                        gain_pairs.append((ref.at[start:start + GAIN_ROWS, :128], gains.at[k]))
                    at += 1
        w_copies = begin(gain_pairs + pairs, w_sems)
        finish(x_copies + w_copies[:count])
        gain = jnp.zeros((GAIN_ROWS, model), f32)
        for k in range(count):
            r, c = picks(128, model, 0, (place ^ k) * w_rows)
            gain += dot(gains[k], one_hot(jnp.logical_and(r == c, r < w_rows)))
        gain_ref[...] = gain[:8, :]
        out_copies = [
            pltpu.make_async_copy(w_ref, w_out, w_sem.at[0]), pltpu.make_async_copy(wo_ref, wo_out, w_sem.at[1])
        ]

        finish(w_copies[count:])
        for copy in out_copies:
            copy.start()

        def attend(slot, unused):
            block, active, row = slot_of(meta_ref, slot)
            last = block // 2
            mine = aligned(slot, width)
            ut_copies = [
                pltpu.make_async_copy(ut_ref.at[2 * slot + i], ut_out.at[2 * slot + i], ut_sems.at[2 * slot + i])
                for i in range(2)
            ]

            def leave(c):
                spot = aligned(c, CHUNK)
                pairs = ((n_ref, n_out), (k_ref, k_out), (v_ref, v_out))
                return [
                    pltpu.make_async_copy(a.at[spot, :], b.at[slot, spot, :], sems.at[i, c])
                    for i, (a, b) in enumerate(pairs)
                ]

            @pl.when(active)
            def _():
                for k in range(count):
                    @pl.when((place ^ k) // 2 <= last)
                    def _():
                        xb = xs[k, row].astype(f32)
                        n_ref[aligned(place ^ k, width), :] = (xb * inverse_rms(xb) * gain_ref[0:1, :]).astype(bf16)

            @pl.when(jnp.logical_not(active))
            def _():
                joined_ref[mine, :] = jnp.zeros((width, model), bf16)

            @pl.when(active)
            def _():
                def project(c, unused):
                    nc = n_ref[aligned(c, CHUNK), :]
                    k_ref[aligned(c, CHUNK), :] = dot(nc, w_ref[:, model:2 * model]).astype(bf16)
                    vc = dot(nc, w_ref[:, 2 * model:3 * model]).astype(bf16)
                    v_ref[aligned(c, CHUNK), :] = vc
                    vt_ref[c] = vc.T
                    for copy in leave(c):
                        copy.start()
                    return 0

                lax.fori_loop(0, last + 1, project, 0)
                query = dot(n_ref[aligned(block, width), :], w_ref[:, :model]).astype(bf16)
                q_ref[mine, :] = query
                query_t = query.astype(f32).T
                for part_of in range(2):
                    heads_in = range(part_of * heads // 2, (part_of + 1) * heads // 2)
                    mix_columns(query_t, pre, qst, heads, heads_in, 0.125, False)
                    mx[...] = jnp.full(mx.shape, NEGATIVE, f32)

                    def scores(c, unused):
                        kc = k_ref[aligned(c, CHUNK), :]
                        for t in range(half // pair):
                            part = slice(t * pair, (t + 1) * pair)
                            s = masked(dot(kc, qst[:, part]), c, block, width, NEGATIVE)
                            s_ref[aligned(c, CHUNK), part] = s
                            mx[:, part] = jnp.maximum(mx[:, part], jnp.max(s.reshape(CHUNK // 8, 8, pair), axis=0))
                        return 0

                    lax.fori_loop(0, last + 1, scores, 0)
                    peak = jnp.max(mx[...], axis=0, keepdims=True)
                    acc[...] = jnp.zeros(acc.shape, f32)
                    mx[...] = jnp.zeros(mx.shape, f32)

                    def weigh(c, unused):
                        vt = vt_ref[c]
                        for t in range(half // pair):
                            part = slice(t * pair, (t + 1) * pair)
                            p = jnp.exp(s_ref[aligned(c, CHUNK), part] - peak[:, part])
                            mx[:, part] += jnp.sum(p.reshape(CHUNK // 8, 8, pair), axis=0)
                            acc[:, part] += dot(vt, p.astype(bf16))
                        return 0

                    lax.fori_loop(0, last + 1, weigh, 0)
                    total = jnp.sum(mx[...], axis=0, keepdims=True)
                    lse_ref[slot, :, part_of * half:(part_of + 1) * half] = peak + jnp.log(total)
                    inverse = 1.0 / total
                    for k in range(heads):
                        rows = slice(k * size, (k + 1) * size)
                        out = jnp.zeros((size, width), f32)
                        for i, h in enumerate(heads_in):
                            cols = slice(i * width, (i + 1) * width)
                            u = acc[rows, cols] * inverse[:, cols]
                            ut_ref[2 * slot + part_of, rows, cols] = u.astype(bf16)
                            out += u * post[h, k]
                        if part_of == 0:
                            total_out[rows, :] = out
                        else:
                            total_out[rows, :] += out
                    ut_copies[part_of].start()
                joined_ref[mine, :] = total_out[...].T.astype(bf16)

                def gone(c, unused):
                    finish(leave(c))
                    return 0

                lax.fori_loop(0, last + 1, gone, 0)

            residual = jnp.where(row == 0, xs[0, 0].astype(f32), xs[mirror, 1].astype(f32))
            middle = residual + dot(joined_ref[mine, :], wo_ref[...])
            middle_ref[mine, :] = middle
            second_ref[mine, :] = (middle * inverse_rms(middle) * gain_ref[1:2, :]).astype(bf16)

            @pl.when(active)
            def _():
                finish(ut_copies)

            return 0

        lax.fori_loop(0, 2, attend, 0)
        finish(out_copies)

    tokens = 2 * width
    outs = [
        shaped((tokens, model)), shaped((tokens, model)), shaped((tokens, model), f32), shaped((2, length, model)),
        shaped((2, length, model)), shaped((2, length, model)), shaped((tokens, model)), shaped((4, model, half)),
        shaped((2, 1, lanes), f32), shaped((model, 3 * model)), shaped((model, model)), shaped((8, model), f32),
    ]
    scratch = [
        pltpu.VMEM((model, half), bf16), pltpu.VMEM((length, half), f32), pltpu.VMEM((model, half), f32),
        pltpu.VMEM((8, half), f32), pltpu.VMEM((model, width), f32), pltpu.VMEM((length, model), bf16),
        pltpu.VMEM((length, model), bf16), pltpu.VMEM((length, model), bf16), pltpu.VMEM((model, 3 * model), bf16),
        pltpu.VMEM((model, model), bf16), pltpu.VMEM((4, model, half), bf16),
        pltpu.VMEM((count, 2, width, model), bf16), pltpu.VMEM((count, GAIN_ROWS, 128), bf16),
        dma(count), dma(5 * count), pltpu.SemaphoreType.DMA((3, chunks)), dma(2), dma(4),
        pltpu.VMEM((chunks, model, CHUNK), bf16),
    ]
    args = x_arrays + w_arrays
    flops = 4 * length * model * (lanes + 2 * model)
    return call(
        body, "attend_forward", outs, [meta, premix, postmix], args, scratch, flops, after,
        tuple(range(len(args))), (3, 4, 5, 7, 9, 10),
    )


def feed_forward(seconds, ups, inner_w, outer_w):
    width, model = seconds[0].shape
    units = inner_w.shape[1]
    tokens = GROUP * width
    root = 0.7978845608028654
    tile = 256

    def body(*refs):
        s_refs, u_refs, (w1, w2), refs = refs[:GROUP], refs[GROUP:2 * GROUP], refs[2 * GROUP:2 * GROUP + 2], refs[2 * GROUP + 2:]
        hidden_ref, inner_ref, grads, outs, (tok, up, sems) = refs[0], refs[1], refs[2:5], refs[5:8], refs[8:]
        spots = [slice(i * width, (i + 1) * width) for i in range(GROUP)]
        pairs = [(s_refs[i], tok.at[spots[i], :]) for i in range(GROUP)]
        pairs += [(u_refs[i], up.at[spots[i], :]) for i in range(GROUP)]
        copies = begin(pairs, sems)
        finish(copies[:GROUP])
        for t in range(units // tile):
            part = slice(t * tile, (t + 1) * tile)
            v = dot(tok[...], w1[:, part])
            squared = v * v
            th = jnp.tanh(root * (v + 0.044715 * (squared * v)))
            hidden_ref[:, part] = (0.5 * v * (1.0 + th)).astype(bf16)
            slope = 0.5 * (1.0 + th) + 0.5 * v * (1.0 - th * th) * (root * (1.0 + 0.134145 * squared))
            if t == 0:
                finish(copies[GROUP:])
            inner_ref[:, part] = (dot(up[...], w2[part, :], 1, 1) * slope).astype(bf16)
        for (own_ref, give_ref, across_ref), made in (
            (grads, dot(inner_ref[...], w1[...], 1, 1)), (outs, dot(hidden_ref[...], w2[...]))
        ):
            made = made.astype(bf16)
            own_ref[...] = made[:width]
            give_ref[:width, :] = made[width:2 * width]
            give_ref[width:, :] = made[3 * width:]
            across_ref[...] = made[2 * width:3 * width]

    outs = [shaped((tokens, units)), shaped((tokens, units))]
    outs += [shaped((width, model)), shaped((2 * width, model)), shaped((width, model))] * 2
    scratch = [pltpu.VMEM((tokens, model), bf16), pltpu.VMEM((tokens, model), bf16), dma(2 * GROUP)]
    args = list(seconds) + list(ups) + [inner_w, outer_w]
    made = call(
        body, "feed_forward", outs, [], args, scratch, 8 * tokens * model * units, (), tuple(range(2 * GROUP))
    )
    return made[0], made[1], made[2:5], made[5:8]


def feed_weights(meta, seconds, ups, hidden, inner, bands, after):
    width, model = seconds[0].shape
    units = hidden.shape[1]
    tokens = GROUP * width
    rows_out = units // bands

    def body(meta_ref, *refs):
        s_refs, u_refs, (h_ref, i_ref), refs = refs[:GROUP], refs[GROUP:2 * GROUP], refs[2 * GROUP:2 * GROUP + 2], refs[2 * GROUP + 2:]
        inner_out, outer_j, (tok, up, grad, sems) = refs[0], refs[1:1 + bands], refs[1 + bands:]
        pairs = [(s_refs[i], tok.at[i * width:(i + 1) * width, :]) for i in range(GROUP)]
        pairs += [(u_refs[i], up.at[i * width:(i + 1) * width, :]) for i in range(GROUP)]
        copies = begin(pairs, sems)
        finish(copies[:GROUP])
        inner_out[...] = dot(tok[...], i_ref[...], 0, 0).astype(bf16)
        finish(copies[GROUP:])
        grad[...] = dot(h_ref[...], up[...], 0, 0).astype(bf16)
        for j in range(bands):
            outer_j[j][...] = grad[aligned((meta_ref[0] // GROUP) ^ j, rows_out), :]

    outs = [shaped((model, units))] + [shaped((rows_out, model))] * bands
    args = list(seconds) + list(ups) + [hidden, inner]
    scratch = [
        pltpu.VMEM((tokens, model), bf16), pltpu.VMEM((tokens, model), bf16), pltpu.VMEM((units, model), bf16),
        dma(2 * GROUP),
    ]
    made = call(
        body, "feed_weights", outs, [meta], args, scratch, 4 * tokens * model * units, after, tuple(range(2 * GROUP))
    )
    return made[0], list(made[1:])


def before_attention_back(own, got, came, middle, up, gains, w, joined, inner_grads, out_got, out_across, count, after):
    tokens, model = own.shape
    rows = model // count

    def body(own_ref, got_ref, came_ref, middle_ref, up_ref, gain_ref, w_in, joined_ref, inner_ref, out_got_ref, out_ref,
             grad_ref, upstream_ref, packed_ref, across_ref, w_ref, total_ref, sems):
        across_ref[...] = (out_ref[...].astype(f32) + out_got_ref[tokens:, :].astype(f32)).astype(bf16)
        copies = begin([(w_in, w_ref), (inner_ref, total_ref.at[:, rows:, :])], sems)
        second = own_ref[...].astype(f32) + got_ref[:tokens, :].astype(f32) + came_ref[...].astype(f32)
        back = norm_back(middle_ref[...], gain_ref[1:2, :], second)
        grad = up_ref[...].astype(f32) + back
        grad_ref[...] = grad
        cast = grad.astype(bf16)
        total = dot(joined_ref[...], cast, 0, 0)
        for j in range(count):
            total_ref[j, :rows, :] = total[j * rows:(j + 1) * rows, :].astype(bf16)
        copies[1].wait()
        last = pltpu.make_async_copy(total_ref, packed_ref, sems.at[2])
        last.start()
        copies[0].wait()
        upstream_ref[...] = dot(cast, w_ref[...], 1, 1).astype(bf16)
        last.wait()

    outs = [
        shaped((tokens, model), f32), shaped((tokens, model)), shaped((count, 2 * rows, model)), shaped((tokens, model)),
    ]
    args = [own, got, came, middle, up, gains, w, joined, inner_grads.reshape(count, rows, model), out_got, out_across]
    scratch = [pltpu.VMEM((model, model), bf16), pltpu.VMEM((count, 2 * rows, model), bf16), dma(3)]
    return call(
        body, "before_attention_back", outs, [], args, scratch, 4 * tokens * model * model, after, (6, 8), (2,)
    )


def attend_back(meta, premix, postmix, pre_row, post_row, query, upstream, normed, keys, values, ut, lse, count, after):
    tokens, model = query.shape
    width = tokens // 2
    length = keys.shape[1]
    heads = premix.shape[0]
    size = model // heads
    pair = 2 * width
    lanes = heads * width
    half = lanes // 2
    w_rows = model // count

    def body(meta_ref, pre, post, pre_in, post_in, q_in, up_in, lse_in, n_hbm, k_hbm, v_hbm, ut_hbm,
             dq_ref, dk_hbm, dv_hbm, mix_out, keep_ref, give_ref,
             qst, qs, ust, us, acc, pbuf, lbuf, dots, wacc, cin, cout, n_own, ut_held, in_sems, out_sems, own_sem, ut_sems,
             pre_row, post_row, q_ref, up_ref, lse_ref, arg_sems, kt_ref, nt_ref, mix_ref):
        args = begin(
            [(pre_in, pre_row), (post_in, post_row), (q_in, q_ref), (up_in, up_ref), (lse_in, lse_ref)], arg_sems
        )
        wacc[...] = jnp.zeros(wacc.shape, f32)
        mix_ref[...] = jnp.zeros(mix_ref.shape, f32)
        finish(args)

        def through(slot, unused):
            block, active, unused_row = slot_of(meta_ref, slot)
            last = block // 2
            mine = aligned(slot, width)
            ut_copies = [
                pltpu.make_async_copy(ut_hbm.at[2 * slot + i], ut_held.at[i], ut_sems.at[i]) for i in range(2)
            ]

            @pl.when(jnp.logical_not(active))
            def _():
                dq_ref[mine, :] = jnp.zeros((width, model), bf16)

            @pl.when(active)
            def _():
                def fetch(c):
                    return [
                        pltpu.make_async_copy(
                            a.at[slot, aligned(c, CHUNK), :], cin.at[c % 2, i], in_sems.at[c % 2, i]
                        )
                        for i, a in enumerate((k_hbm, v_hbm, n_hbm))
                    ]

                def leave(c):
                    return [
                        pltpu.make_async_copy(
                            cout.at[c % 2, i], a.at[slot, aligned(c, CHUNK), :], out_sems.at[c % 2, i]
                        )
                        for i, a in enumerate((dk_hbm, dv_hbm))
                    ]

                own = pltpu.make_async_copy(n_hbm.at[slot, aligned(block, width), :], n_own, own_sem)
                own.start()
                for copy in ut_copies + fetch(0):
                    copy.start()
                q = q_ref[mine, :].astype(f32)
                up = up_ref[mine, :].astype(f32)
                qt, upt = q.T, up.T
                mix_columns(qt, pre, qst, heads, range(heads), 0.125, False)
                mix_columns(upt, post, ust, heads, range(heads), 1.0, True)
                for h in range(heads):
                    spot = slice(h * width, (h + 1) * width)
                    qs[spot, :] = (q * (pre_row[h:h + 1, :] * 0.125)).astype(bf16)
                    us[spot, :] = (up * post_row[h:h + 1, :]).astype(bf16)
                finish(ut_copies)
                for h in range(heads):
                    spot = slice(h * width, (h + 1) * width)
                    column = h % (heads // 2) * width
                    u = ut_held[h // (heads // 2), :, column:column + width].astype(f32)
                    t = jnp.sum((u * upt).reshape(heads, size, width), axis=1)
                    mix_ref[(heads + h) * heads:(heads + h + 1) * heads, :] += t
                    d = jnp.zeros((1, width), f32)
                    for k in range(heads):
                        d += t[k:k + 1, :] * post[h, k]
                    dots[:, spot] = d
                acc[...] = jnp.zeros(acc.shape, f32)

                def visit(c, unused):
                    finish(fetch(c))

                    @pl.when(c < last)
                    def _():
                        for copy in fetch(c + 1):
                            copy.start()

                    kc, vc = cin[c % 2, 0], cin[c % 2, 1]
                    kt_ref[...] = kc.T
                    nt_ref[...] = cin[c % 2, 2].T
                    for t in range(heads // 2):
                        part = slice(t * pair, (t + 1) * pair)
                        p = masked(jnp.exp(dot(kc, qst[:, part]) - lse_ref[slot, :, part]), c, block, width, 0.0)
                        grad = (p * (dot(vc, ust[:, part]) - dots[:, part])).astype(bf16)
                        pbuf[:, part] = p.astype(bf16)
                        lbuf[:, part] = grad
                        acc[:, part] += dot(kt_ref[...], grad)

                    @pl.when(c >= 2)
                    def _():
                        finish(leave(c - 2))

                    dk = dot(lbuf[...], qs[...]).astype(bf16)
                    dv = dot(pbuf[...], us[...]).astype(bf16)
                    cout[c % 2, 0] = dk
                    cout[c % 2, 1] = dv
                    for copy in leave(c):
                        copy.start()
                    wacc[:, model:2 * model] += dot(nt_ref[...], dk)
                    wacc[:, 2 * model:] += dot(nt_ref[...], dv)
                    return 0

                lax.fori_loop(0, last + 1, visit, 0)
                for g in range(heads):
                    rows = slice(g * size, (g + 1) * size)
                    out = jnp.zeros((size, width), f32)
                    qg = qt[rows, :] * 0.125
                    for h in range(heads):
                        a = acc[rows, h * width:(h + 1) * width]
                        out += a * pre[g, h]
                        mix_ref[g * heads + h:g * heads + h + 1, :] += jnp.sum(a * qg, axis=0, keepdims=True)
                    acc[rows, 0:width] = out * 0.125
                dq = acc[:, 0:width].T.astype(bf16)
                dq_ref[mine, :] = dq
                own.wait()
                wacc[:, :model] += dot(n_own[...], dq, 0, 0)

                @pl.when(last >= 1)
                def _():
                    finish(leave(last - 1))

                finish(leave(last))

            return 0

        lax.fori_loop(0, 2, through, 0)
        every = jnp.sum(mix_ref[...], axis=1, keepdims=True)
        r = lax.broadcasted_iota(jnp.int32, mix_ref.shape, 0)
        c = lax.broadcasted_iota(jnp.int32, mix_ref.shape, 1)
        every = jnp.where(r % 128 == c, every, 0.0)
        mix_out[...] = jnp.zeros(mix_out.shape, f32)
        for i in range(-(-mix_ref.shape[0] // 128)):
            mix_out[i:i + 1, :] = jnp.sum(every[i * 128:(i + 1) * 128, :], axis=0, keepdims=True)
        for k in range(count):
            (keep_ref, give_ref)[k % 2][k // 2 * w_rows:(k // 2 + 1) * w_rows, :] = wacc[
                aligned(meta_ref[0] ^ k, w_rows), :
            ].astype(bf16)

    outs = [
        shaped((tokens, model)), shaped((2, length, model)), shaped((2, length, model)),
        shaped((8, 128), f32), shaped((count // 2 * w_rows, 3 * model)),
        shaped((count // 2 * w_rows, 3 * model)),
    ]
    scratch = [
        pltpu.VMEM((model, lanes), bf16), pltpu.VMEM((lanes, model), bf16), pltpu.VMEM((model, lanes), bf16),
        pltpu.VMEM((lanes, model), bf16), pltpu.VMEM((model, lanes), f32), pltpu.VMEM((CHUNK, lanes), bf16),
        pltpu.VMEM((CHUNK, lanes), bf16), pltpu.VMEM((1, lanes), f32), pltpu.VMEM((model, 3 * model), f32),
        pltpu.VMEM((2, 3, CHUNK, model), bf16), pltpu.VMEM((2, 2, CHUNK, model), bf16), pltpu.VMEM((width, model), bf16),
        pltpu.VMEM((2, model, half), bf16), pltpu.SemaphoreType.DMA((2, 3)), pltpu.SemaphoreType.DMA((2, 2)),
        pltpu.SemaphoreType.DMA, dma(2), pltpu.VMEM((heads, model), f32), pltpu.VMEM((heads, model), f32),
        pltpu.VMEM((tokens, model), bf16), pltpu.VMEM((tokens, model), bf16), pltpu.VMEM((2, 1, lanes), f32), dma(5),
        pltpu.VMEM((model, CHUNK), bf16), pltpu.VMEM((model, CHUNK), bf16),
        pltpu.VMEM((2 * heads * heads, width), f32),
    ]
    args = [pre_row, post_row, query, upstream, lse, normed, keys, values, ut]
    return call(
        body, "attend_back", outs, [meta, premix, postmix], args, scratch, 15 * length * model * lanes, after,
        tuple(range(9)), (1, 2),
    )


def input_back(meta, dq, dk, dv, w, x_pieces, gains, grad, after):
    count = len(x_pieces)
    x_arrays, x_spots = listed(x_pieces)
    width, model = x_arrays[0].shape[1:]
    length = dk.shape[1]
    chunks = length // CHUNK

    def body(meta_ref, dq_in, grad_in, gain_in, dk_hbm, dv_hbm, w_hbm, *refs):
        x_refs, refs = refs[:len(x_arrays)], refs[len(x_arrays):]
        keep_ref, give_ref, normed, dk_held, dv_held, w_ref, xs, sems, w_sem, x_sems = refs[:10]
        dq_ref, grad_ref, gain_ref, arg_sems, wt_ref = refs[10:]
        arg_copies = begin([(dq_in, dq_ref), (grad_in, grad_ref), (gain_in, gain_ref)], arg_sems)
        place = meta_ref[0]
        w_copy = pltpu.make_async_copy(w_hbm, w_ref, w_sem)
        w_copy.start()

        def fetch(slot, c):
            spot = aligned(c, CHUNK)
            return [
                pltpu.make_async_copy(a.at[slot, spot, :], b.at[slot, spot, :], sems.at[slot, c, i])
                for i, (a, b) in enumerate(((dk_hbm, dk_held), (dv_hbm, dv_held)))
            ]

        def start(slot, c):
            for copy in fetch(slot, c):
                copy.start()
            return 0

        for slot in range(2):
            block, active, row = slot_of(meta_ref, slot)
            needed = jnp.where(active, block // 2 + 1, 0)
            lax.fori_loop(0, needed, lambda c, unused, slot=slot: start(slot, c), 0)
        x_copies = begin([(views(x_refs, x_spots[k])[0], xs.at[k]) for k in range(count)], x_sems)
        w_copy.wait()
        for i in range(3):
            wt_ref[i] = w_ref[:, i * model:(i + 1) * model].T
        finish(arg_copies)

        finish(x_copies)

        def through(slot, unused):
            block, active, row = slot_of(meta_ref, slot)
            mine = aligned(slot, width)

            @pl.when(active)
            def _():
                def visit(c, unused):
                    spot = aligned(c, CHUNK)
                    finish(fetch(slot, c))
                    normed[spot, :] = dot(dk_held[slot, spot, :], wt_ref[1]) + dot(dv_held[slot, spot, :], wt_ref[2])
                    return 0

                lax.fori_loop(0, block // 2 + 1, visit, 0)
                normed[aligned(block, width), :] += dot(dq_ref[mine, :], wt_ref[0])

            def chip(i, unused):
                for k, out_ref in enumerate((keep_ref, give_ref)):
                    source = place ^ (2 * i + k)
                    spot = aligned(2 * i + row, width)
                    used = jnp.logical_and(active, source <= block)

                    @pl.when(jnp.logical_not(used))
                    def _():
                        out_ref[spot, :] = jnp.zeros((width, model), bf16)

                    @pl.when(used)
                    def _():
                        back = norm_back(
                            xs[2 * i + k, row].astype(f32), gain_ref[0:1, :], normed[aligned(source, width), :]
                        )
                        factor = jnp.where(source == block, 1.0, 0.0)
                        out_ref[spot, :] = (back + grad_ref[mine, :] * factor).astype(bf16)
                return 0

            lax.fori_loop(0, count // 2, chip, 0)
            return 0

        lax.fori_loop(0, 2, through, 0)

    half = count * width
    outs = [shaped((half, model)), shaped((half, model))]
    args = [dq, grad, gains, dk, dv, w] + x_arrays
    scratch = [
        pltpu.VMEM((length, model), f32), pltpu.VMEM((2, length, model), bf16), pltpu.VMEM((2, length, model), bf16),
        pltpu.VMEM((model, 3 * model), bf16), pltpu.VMEM((count, 2, width, model), bf16),
        pltpu.SemaphoreType.DMA((2, chunks, 2)), pltpu.SemaphoreType.DMA, dma(count),
        pltpu.VMEM(dq.shape, bf16), pltpu.VMEM(grad.shape, f32), pltpu.VMEM(gains.shape, f32), dma(3),
        pltpu.VMEM((3, model, model), bf16),
    ]
    return call(
        body, "input_back", outs, [meta], args, scratch, 8 * length * model * model, after,
        tuple(range(len(args))),
    )


def pair_sums(keep, got, count, later, after, name):
    blocks = count // 2
    rows, columns = keep.shape[0] // blocks, keep.shape[1]

    def body(keep_ref, got_ref, *refs):
        outs = refs[len(later):]
        for source, target in zip(refs, outs[blocks:]):
            target[...] = source[...]
        for i in range(blocks):
            spot = slice(i * rows, (i + 1) * rows)
            outs[i][...] = (keep_ref[spot, :].astype(f32) + got_ref[spot, :].astype(f32)).astype(outs[i].dtype)

    outs = [shaped((rows, columns))] * blocks
    outs += [shaped(a.shape, a.dtype) for a in later]
    made = call(body, name, outs, [], [keep, got] + list(later), (), 0, after)
    return made[:blocks], made[blocks:]


def halves_first(keep, got, pair, after, name):
    rows, columns = keep.shape[0] // 4, keep.shape[1]
    half = rows // 2

    def body(keep_ref, got_ref, *refs):
        if pair:
            refs[-1][...] = refs[0][...] + refs[1][...]
        two_ref, four_ref, rest_ref = refs[len(pair):len(pair) + 3]

        def part(i, b):
            spot = slice(i * rows + b * half, i * rows + (b + 1) * half)
            return keep_ref[spot, :].astype(f32) + got_ref[spot, :].astype(f32)

        for n, (i, b) in enumerate(((1, 0), (3, 0))):
            two_ref[n * half:(n + 1) * half, :] = part(i, b).astype(bf16)
        for n, (i, b) in enumerate(((2, 1), (3, 1))):
            four_ref[n * half:(n + 1) * half, :] = part(i, b).astype(bf16)
        for n, (i, b) in enumerate(((0, 0), (2, 0), (0, 1), (1, 1))):
            rest_ref[n * half:(n + 1) * half, :] = part(i, b)

    outs = [
        shaped((rows, columns)), shaped((rows, columns)), shaped((2 * rows, columns), f32),
    ] + [shaped(a.shape, f32) for a in pair[:1]]
    return call(body, name, outs, [], [keep, got, *pair], (), 0, after)


def halves_second(rest, from_two, from_four, pair, after, name):
    rows, columns = from_two.shape
    half = rows // 2

    def body(rest_ref, two_in, four_in, one, other, two_ref, four_ref, own_ref, sum_ref):
        sum_ref[...] = one[...] + other[...]
        own_ref[:half, :] = rest_ref[:half, :] + two_in[:half, :].astype(f32)
        four_ref[...] = (rest_ref[half:rows, :] + two_in[half:, :].astype(f32)).astype(bf16)
        own_ref[half:, :] = rest_ref[rows:rows + half, :] + four_in[:half, :].astype(f32)
        two_ref[...] = (rest_ref[rows + half:, :] + four_in[half:, :].astype(f32)).astype(bf16)

    outs = [
        shaped((half, columns)), shaped((half, columns)), shaped((rows, columns), f32), shaped(pair[0].shape, f32),
    ]
    return call(body, name, outs, [], [rest, from_two, from_four, *pair], (), 0, after)


def input_sum(own, from_four, from_two, shape):
    rows, width, model = shape

    def body(own_ref, four_ref, two_ref, out_ref):
        out_ref[0] = (own_ref[:width, :] + four_ref[...].astype(f32)).astype(bf16)
        out_ref[1] = (own_ref[width:, :] + two_ref[...].astype(f32)).astype(bf16)

    return call(body, "input_sum", [shaped(shape)], [], [own, from_four, from_two])[0]


def split_dp(meta, depth, parts, pair, after):
    joined, wide = parts[0].shape
    size = joined // depth
    halved = parts[1].shape[0] != joined

    def body(meta_ref, *refs):
        ins, (one, other), outs, sum_ref = refs[:len(parts)], refs[len(parts):len(parts) + 2], refs[len(parts) + 2:-2], refs[-2]
        total_ref = refs[-1]
        sum_ref[...] = one[...] + other[...]
        if halved:
            for i in range(2):
                spot = slice(i * joined // 2, (i + 1) * joined // 2)
                total_ref[spot, :] = (ins[0][spot, :] + ins[1 + i][...].astype(f32)).astype(bf16)
        else:
            total = ins[0][...].astype(f32)
            for ref in ins[1:]:
                total += ref[...].astype(f32)
            total_ref[...] = total.astype(bf16)
        for m in range(depth):
            r, c = picks(size, joined, 0, (meta_ref[1] ^ m) * size)
            outs[m][...] = dot(one_hot(r == c), total_ref[...]).astype(bf16)

    outs = [shaped((size, wide))] * depth + [shaped(pair[0].shape, f32)]
    scratch = [pltpu.VMEM((joined, wide), bf16)]
    made = call(body, "split_dp", outs, [meta], list(parts) + list(pair), scratch, 0, after)
    return made[:depth], made[depth]


def split_feed(meta, depth, grads, outer, size, middle, parts_out):
    count, joined, units = grads.shape
    joined //= 2
    bands = len(outer)
    band = outer[0].shape[0]
    shard = band // depth
    parts = 1 + GROUP
    out_rows = parts * size + shard
    tokens = middle.shape[0]
    width = tokens // 2

    def body(meta_ref, grad_in, *refs):
        o_ins, out_ins, refs = refs[:bands], refs[bands:bands + 4], refs[bands + 4:]
        outs, (total, grad_ref, outer_ref, middle_ref, part_ref, sems) = refs[:3], refs[3:]
        o_refs = [outer_ref.at[j] for j in range(bands)]
        pairs = [(out_ins[0], middle_ref)] + [(out_ins[1 + i].at[:tokens, :], part_ref.at[i]) for i in range(3)]
        copies = begin(pairs + [(grad_in, grad_ref)] + [(o_ins[j], o_refs[j]) for j in range(bands)], sems)
        finish(copies[:4])
        for slot in range(2):
            block, unused, row = slot_of(meta_ref, slot)
            spot = slice(slot * width, (slot + 1) * width)
            position = block * width + lax.broadcasted_iota(jnp.int32, (width, units), 0)
            value = middle_ref[spot, :]
            for i in range(3):
                value += part_ref[i, spot, :].astype(f32)
            value = jnp.where(position < meta_ref[5 + 4 * slot], value, 0.0).astype(bf16)
            for n in range(2):
                @pl.when(row == n)
                def _():
                    outs[1 + n][...] = value

        finish(copies[4:])
        section = grad_ref[0, :joined, :].astype(f32)
        for j in range(1, count):
            section += grad_ref[j, :joined, :].astype(f32)
        total[:joined, :] = section.astype(bf16)
        for t in range(GROUP):
            section = grad_ref[t, joined:, :].astype(f32)
            for j in range(1, bands):
                section += grad_ref[j * GROUP + t, joined:, :].astype(f32)
            total[(1 + t) * joined:(2 + t) * joined, :] = section.astype(bf16)
        rest = o_refs[0][...].astype(f32)
        for j in range(1, bands):
            rest += o_refs[j][...].astype(f32)
        total[parts * joined:, :] = rest.astype(bf16)
        for d in range(depth):
            for t in range(parts):
                outs[0][d, t * size:(t + 1) * size, :] = total[t * joined + d * size:t * joined + (d + 1) * size, :]
            start = parts * joined + d * shard
            outs[0][d, parts * size:, :] = total[start:start + shard, :]

    scratch = [
        pltpu.VMEM((parts * joined + band, units), bf16), pltpu.VMEM(grads.shape, bf16),
        pltpu.VMEM((bands, band, units), bf16), pltpu.VMEM((tokens, units), f32), pltpu.VMEM((3, tokens, units), bf16),
        dma(5 + bands),
    ]
    args = [grads] + list(outer) + [middle] + list(parts_out)
    outs = [shaped((depth, out_rows, units)), shaped((width, units)), shaped((width, units))]
    return call(body, "split_feed", outs, [meta], args, scratch, 0, (), tuple(range(len(args))))


def finish_projections(pieces, weights):
    size, wide = pieces[0].shape
    parts = 3
    model = wide // parts

    def body(*refs):
        ins, w_ins, outs = refs[:len(pieces)], refs[len(pieces):-6], refs[-6:-2]
        w_held, sems = refs[-2:]
        w_refs = [w_held.at[i] for i in range(parts)]
        finish(begin([(w_ins[i], w_refs[i]) for i in range(parts)], sems))
        along = jnp.zeros((size, 1), f32)
        for i in range(parts):
            part = slice(i * model, (i + 1) * model)
            total = ins[0][:, part].astype(f32)
            for ref in ins[1:]:
                total += ref[:, part].astype(f32)
            outs[i][...] = total
            along += jnp.sum(total * w_refs[i][...].astype(f32), axis=1, keepdims=True)
        outs[3][...] = along

    outs = [shaped((size, model), f32)] * parts + [shaped((size, 1), f32)]
    scratch = [pltpu.VMEM((parts, size, model), bf16), dma(parts)]
    args = list(pieces) + list(weights)
    return call(
        body, "finish_projections", outs, [], args, scratch, raw_args=tuple(range(len(pieces), len(args)))
    )


def finish_feed(pieces, weight, bands):
    size = weight.shape[0]
    depth, rows, units = pieces.shape
    band = units // bands

    def body(in_hbm, w_in, output_ref, inner_ref, outer_ref, along_ref, in_ref, w_ref, sems):
        finish(begin([(in_hbm, in_ref), (w_in, w_ref)], sems))
        total = in_ref[0].astype(f32)
        for d in range(1, depth):
            total += in_ref[d].astype(f32)
        output_ref[...] = total[:size, :]
        for t in range(GROUP):
            for y in range(bands):
                inner_ref[:, (y * GROUP + t) * band:(y * GROUP + t + 1) * band] = total[
                    (1 + t) * size:(2 + t) * size, y * band:(y + 1) * band
                ]
        outer_ref[...] = total[(1 + GROUP) * size:, :]
        along_ref[...] = jnp.sum(inner_ref[...] * w_ref[...].astype(f32), axis=1, keepdims=True)

    outs = [
        shaped((size, units), f32), shaped((size, GROUP * units), f32),
        shaped((rows - (1 + GROUP) * size, units), f32), shaped((size, 1), f32),
    ]
    scratch = [pltpu.VMEM(pieces.shape, bf16), pltpu.VMEM(weight.shape, bf16), dma(2)]
    return call(body, "finish_feed", outs, [], [pieces, weight], scratch, raw_args=(0, 1))


def swap(value, axis, mask):
    count = lax.axis_size(axis)
    return lax.ppermute(value, axis, [(i, i ^ mask) for i in range(count)])


def gather_dp(value):
    return [value] + [swap(value, "dp", m) for m in range(1, lax.axis_size("dp"))]


def gather_first(meta, inputs, first_w, inner, outer, after):
    count, depth = lax.axis_size("blk"), lax.axis_size("dp")
    pieces = gather_dp(first_w)
    x_links = [inputs, swap(inputs, "blk", 2), swap(inputs, "blk", 4)]
    shards = [outer] + [swap(outer, "blk", GROUP * j) for j in range(1, count // GROUP)]
    halves = [swap(x_links[2][0], "blk", 2), swap(x_links[1][1], "blk", 4)] if count == 8 else []
    w_own, x_core = join_dp(meta, pieces, x_links, after + shards[1:] + halves)
    feed = jnp.concatenate([inner] + shards, axis=0)
    if count == 8:
        w_links = [w_own, swap(w_own, "blk", 2), swap(w_own, "blk", 4)]
        x_core = swap(x_core, "blk", 1)
        w_on_two, w_on_four, w_core, x_across = forward_across(w_links, halves)
        w_across = [swap(w_on_two, "blk", 2), swap(w_on_four, "blk", 4)]
        w_core, x_far = swap(w_core, "blk", 1), swap(x_across, "blk", 1)
        w_far = [swap(part, "blk", 1) for part in w_across]
        xs = [[(a, None)] for a in x_links] + [[(x_across, None)]]
        ws = [[(a, None)] for a in w_links] + [[(a, None) for a in w_across]]
        xs_core = [[(x_core, i)] for i in range(3)] + [[(x_far, None)]]
        ws_core = [[(w_core, i)] for i in range(3)] + [[(a, None) for a in w_far]]
    else:
        x_links += [swap(inputs, "blk", k) for k in range(6, count, 2)]
        w_links = [w_own, swap(w_own, "blk", 2), swap(w_own, "blk", 4)]
        w_links += [swap(w_own, "blk", k) for k in range(6, count, 2)]
        xs, ws = [[(a, None)] for a in x_links], [[(a, None)] for a in w_links]
        xs_core, ws_core = [[(swap(a, "blk", 1), None)] for a in x_links], [[(swap(a, "blk", 1), None)] for a in w_links]
    x_pieces = [part for pair in zip(xs, xs_core) for part in pair]
    w_pieces = [part for pair in zip(ws, ws_core) for part in pair]
    return x_pieces, w_pieces, feed


def all_to_all(value, axis):
    return lax.all_to_all(value, axis, 0, 0, tiled=True)


def gather_group(value):
    two = swap(value, "blk", 2)
    return [value, swap(value, "blk", 1), two, swap(two, "blk", 1)]


def scatter_chips(parts):
    return [parts[0]] + [swap(part, "blk", 2 * i) for i, part in enumerate(parts) if i]


def on_device(
    inputs, lengths, prenorm, midnorm, query_proj, key_proj, value_proj, output_proj,
    premix, postmix, inner_proj, outer_proj, cotangent,
):
    count, depth = lax.axis_size("blk"), lax.axis_size("dp")
    place, zplace = lax.axis_index("blk"), lax.axis_index("dp")
    rows, width, model = inputs.shape
    shard = prenorm.shape[0]
    low = place < count // 2
    mirror = count - 1
    slot_rows = [jnp.where(low, 1, 0), jnp.where(low, 0, 1)]
    blocks = [jnp.maximum(place, place ^ mirror), jnp.minimum(place, place ^ mirror)]
    spans = [jnp.where(slot_rows[i] == 0, lengths[0], lengths[1]) for i in range(2)]
    meta = [place, zplace]
    for i in range(2):
        meta += [blocks[i], (blocks[i] * width < spans[i]).astype(jnp.int32), slot_rows[i], spans[i]]
    meta = jnp.stack(meta).astype(jnp.int32)

    head_size = model // premix.shape[0]
    pre_row = jnp.repeat(premix.T, head_size, axis=1)
    post_row = jnp.repeat(postmix, head_size, axis=1)
    bands = count // GROUP
    band_ff = depth * outer_proj.shape[0]
    first_w = pack_first([query_proj, key_proj, value_proj, output_proj], jnp.stack([prenorm, midnorm]))
    sections = inner_proj.reshape(shard, bands, GROUP, band_ff).transpose(2, 0, 1, 3).reshape(GROUP, shard, -1)
    sections = all_to_all(jnp.concatenate([sections] * bands), "blk").reshape(count * shard, -1)
    far_cotangent = swap(cotangent[1], "blk", mirror)
    x_pieces, w_pieces, second_w = gather_first(meta, inputs, first_w, sections, outer_proj, [sections])
    second_w = all_to_all(jnp.broadcast_to(second_w, (depth, *second_w.shape)), "dp")
    up = masked_cotangent(meta, cotangent, far_cotangent, [w_pieces[count - 2][0][0]])
    ups = gather_group(up)

    joined, second, middle, normed, keys, values, query, ut, lse, w, output_w, gain_rows = attend_forward(
        meta, premix, postmix, x_pieces, w_pieces, [up, pre_row, post_row]
    )
    seconds = gather_group(second)
    inner_w, outer_w = join_feed(meta, second_w, shard, count, [second, ups[2]])
    hidden, inner, (own, give, across), (out_own, out_give, out_across) = feed_forward(
        seconds, ups, inner_w, outer_w
    )
    got = swap(give, "blk", 1)
    tokens = rows * width
    across = (across.astype(f32) + got[tokens:].astype(f32)).astype(bf16)
    came = swap(across, "blk", 2)
    out_got = swap(out_give, "blk", 1)
    inner_grads, outer_grads = feed_weights(meta, seconds, ups, hidden, inner, bands, [across])

    grad, upstream, packed, out_across = before_attention_back(
        own, got, came, middle, up, gain_rows, output_w, joined, inner_grads, out_got, out_across, count, []
    )
    feed_grads = all_to_all(packed, "blk")
    outer_grads = [outer_grads[0]] + [swap(outer_grads[j], "blk", GROUP * j) for j in range(1, bands)]
    out_came = swap(out_across, "blk", 2)
    dq, dk, dv, mixes, keep, give = attend_back(
        meta, premix, postmix, pre_row, post_row, query, upstream, normed, keys, values, ut, lse, count, []
    )
    heads = premix.shape[0]
    cuts, near, far = split_feed(
        meta, depth, feed_grads, outer_grads, shard, middle, [out_own, out_got, out_came]
    )
    outputs = jnp.stack([near, swap(far, "blk", mirror)])
    input_keep, input_give = input_back(meta, dq, dk, dv, w, x_pieces, gain_rows, grad, [cuts])
    feed_sums = all_to_all(cuts, "dp")
    give, input_give = swap(give, "blk", 1), swap(input_give, "blk", 1)
    steps = [("blk", 1 << i) for i in range(count.bit_length() - 1)] + [("dp", 1 << i) for i in range(depth.bit_length() - 1)]

    def step(value):
        return value, swap(value, *steps.pop(0))

    if count == 8:
        two, four, rest = halves_first(keep, give, (), [input_keep], "halves_first_w")
        two, four = swap(two, "blk", 2), swap(four, "blk", 4)
        x_two, x_four, x_rest, mixes = halves_first(input_keep, input_give, step(mixes), [rest], "halves_first_x")
        x_two, x_four = swap(x_two, "blk", 2), swap(x_four, "blk", 4)
        two, four, rest, mixes = halves_second(rest, two, four, step(mixes), [x_rest], "halves_second_w")
        two, four = swap(two, "blk", 2), swap(four, "blk", 4)
        x_two, x_four, x_rest, mixes = halves_second(x_rest, x_two, x_four, step(mixes), [rest], "halves_second_x")
        x_two, x_four = swap(x_two, "blk", 2), swap(x_four, "blk", 4)
        cuts_w, mixes = split_dp(meta, depth, [rest, four, two], step(mixes), [x_rest])
        grad_inputs = input_sum(x_rest, x_four, x_two, inputs.shape)
    else:
        projected, unused = pair_sums(keep, give, count, [], [input_keep], "pair_sums_w")
        cuts_w, mixes = split_dp(meta, depth, scatter_chips(projected), step(mixes), [])
        parts, unused = pair_sums(input_keep, input_give, count, [], [], "pair_sums_x")
        grad_inputs = sum([part.astype(f32) for part in scatter_chips(parts)]).astype(bf16).reshape(inputs.shape)
    while steps:
        mixes = sum(step(mixes))
    mixes = mixes.reshape(-1)[:2 * heads * heads].reshape(2, heads, heads)
    output_sum, inner_sum, outer_sum, mid_gain = finish_feed(
        feed_sums, inner_proj, bands
    )
    cuts = cuts_w
    query_sum, key_sum, value_sum, pre_gain = finish_projections(
        [cuts[0]] + [swap(cuts[m], "dp", m) for m in range(1, depth)],
        [query_proj, key_proj, value_proj],
    )
    return (
        outputs,
        grad_inputs,
        pre_gain.reshape(-1) / prenorm.astype(f32),
        mid_gain.reshape(-1) / midnorm.astype(f32),
        query_sum,
        key_sum,
        value_sum,
        output_sum,
        mixes[0],
        mixes[1],
        inner_sum,
        outer_sum,
    )


def solution(mesh):
    weight = P(("blk", "dp"), None)
    vector = P(("blk", "dp"))
    tokens = P("dp", "blk", None)
    in_specs = (
        tokens, P("dp"), vector, vector, weight, weight, weight, weight, P(), P(), weight, weight, tokens,
    )
    out_specs = (
        tokens, tokens, vector, vector, weight, weight, weight, weight, P(), P(), weight, weight,
    )
    return jax.shard_map(on_device, mesh=mesh, in_specs=in_specs, out_specs=out_specs, check_vma=False)
```

```python
import jax
import jax.numpy as jnp
from jax import lax
from jax.experimental import pallas as pl
from jax.experimental.pallas import tpu as pltpu
from jax.sharding import PartitionSpec as P

EPSILON = 1e-06
GROUP = 4
CHUNK = 256
NEGATIVE = -1e30
VMEM_MOST = 60 * 1024 * 1024
VMEM_SPARE = 8 * 1024 * 1024
VMEM_WINDOWS = 18 * 1024 * 1024
GAIN_ROWS = 16
f32 = jnp.float32
bf16 = jnp.bfloat16
HIGH = lax.Precision.HIGHEST
ANY_SPEC = pl.BlockSpec(memory_space=pl.ANY)
VMEM_SPEC = pl.BlockSpec(memory_space=pltpu.VMEM)
HBM_SPEC = pl.BlockSpec(memory_space=pltpu.HBM)
SMEM_SPEC = pl.BlockSpec(memory_space=pltpu.SMEM)


def shaped(shape, dtype=bf16):
    return jax.ShapeDtypeStruct(shape, dtype)


def vmem_bytes(shape, dtype):
    lead, (rows, columns) = shape[:-2], shape[-2:]
    size = jnp.dtype(dtype).itemsize
    for extent in lead:
        size *= extent
    return size * -(-rows // 16) * 16 * -(-columns // 128) * 128


def call(body, name, outs, smem, args, scratch=(), flops=0, after=(), raw_args=(), raw_outs=(), extra=0):
    n_smem, n_args = len(smem), len(args)
    arrays = list(args) + list(outs)
    windows = [a for i, a in enumerate(args) if i not in raw_args] + [a for i, a in enumerate(outs) if i not in raw_outs]
    windows = sum(vmem_bytes(a.shape, a.dtype) for a in windows)
    held = sum(vmem_bytes(a.shape, a.dtype) for a in scratch if getattr(a, "memory_space", None) == pltpu.VMEM)
    held += VMEM_SPARE + extra + (windows if windows > VMEM_WINDOWS else 0)

    def kernel(*refs):
        first = n_smem + n_args
        body(*refs[:first], *refs[first + len(after):])

    return pl.pallas_call(
        kernel,
        out_shape=tuple(pltpu.HBM(a.shape, a.dtype) if i in raw_outs else a for i, a in enumerate(outs)),
        in_specs=[SMEM_SPEC] * n_smem
        + [HBM_SPEC if i in raw_args else VMEM_SPEC for i in range(n_args)] + [ANY_SPEC] * len(after),
        out_specs=tuple(HBM_SPEC if i in raw_outs else VMEM_SPEC for i in range(len(outs))),
        scratch_shapes=list(scratch),
        compiler_params=pltpu.CompilerParams(vmem_limit_bytes=min(VMEM_MOST, held)),
        cost_estimate=pl.CostEstimate(
            flops=flops, bytes_accessed=sum(a.size * a.dtype.itemsize for a in arrays), transcendentals=0
        ),
        name=name,
    )(
        *smem,
        *[pltpu.with_memory_space_constraint(a, pltpu.HBM) if i in raw_args else a for i, a in enumerate(args)],
        *after,
    )


def begin(pairs, sems):
    copies = [pltpu.make_async_copy(a, b, sems.at[i]) for i, (a, b) in enumerate(pairs)]
    for copy in copies:
        copy.start()
    return copies


def finish(copies):
    for copy in copies:
        copy.wait()


def dma(count):
    return pltpu.SemaphoreType.DMA((count,))


def dot(a, b, ca=1, cb=0):
    return lax.dot_general(a, b, (((ca,), (cb,)), ((), ())), preferred_element_type=f32)


def picks(rows, columns, start_row, start_column=0):
    r = lax.broadcasted_iota(jnp.int32, (rows, columns), 0) - start_row
    c = lax.broadcasted_iota(jnp.int32, (rows, columns), 1) - start_column
    return r, c


def one_hot(mask):
    return jnp.where(mask, 1.0, 0.0).astype(bf16)


def inverse_rms(values):
    return lax.rsqrt(jnp.mean(values * values, axis=-1, keepdims=True) + EPSILON)


def norm_back(values, gain, grad):
    inverse = inverse_rms(values)
    scaled = grad * gain
    mean = jnp.mean(scaled * values, axis=-1, keepdims=True)
    return inverse * (scaled - values * (inverse * inverse * mean))


def aligned(index, size):
    return pl.ds(pl.multiple_of(index * size, size), size)


def pack_first(weights, gains):
    size, model = weights[0].shape
    parts = len(weights)

    def body(*refs):
        gain_ref, out_ref, held, sems = refs[parts:]
        copies = begin([(refs[i], held.at[i]) for i in range(parts)], sems)
        r, c = picks(size, model, 0)
        along = dot(gain_ref[...], one_hot(r == c)).astype(bf16)
        r, c = picks(GAIN_ROWS, 2, 0)
        out_ref[parts * size:, :] = dot(one_hot(r == c), along).astype(bf16)
        finish(copies)
        for i in range(parts):
            out_ref[i * size:(i + 1) * size, :] = held[i]

    scratch = [pltpu.VMEM((parts, size, model), bf16), dma(parts)]
    outs = [shaped((parts * size + GAIN_ROWS, model))]
    return call(
        body, "pack_first", outs, [], list(weights) + [gains], scratch, raw_args=tuple(range(parts))
    )[0]


def join_dp(meta, pieces, x_links, after):
    depth = len(pieces)
    total_rows, model = pieces[0].shape
    size = (total_rows - GAIN_ROWS) // 4
    joined = size * depth
    links = len(x_links)
    lanes = 128

    def body(meta_ref, *refs):
        ins, x_refs, outs, sems = refs[:depth], refs[depth:depth + links], refs[depth + links:-1], refs[-1]
        copies = begin([(x_refs[i], outs[1].at[i]) for i in range(links)], sems)
        total = jnp.zeros((4 * joined, model), f32)
        gains = jnp.zeros((GAIN_ROWS, lanes), f32)
        for m in range(depth):
            d = meta_ref[1] ^ m
            r = lax.broadcasted_iota(jnp.int32, (4 * joined, total_rows), 0)
            c = lax.broadcasted_iota(jnp.int32, (4 * joined, total_rows), 1)
            want = jnp.where((r % joined) // size == d, (r // joined) * size + r % size, -1)
            total += dot(one_hot(c == want), ins[m][...])
            r, c = picks(lanes, lanes, 0, d * size)
            gains += dot(ins[m][4 * size:, :lanes], one_hot(jnp.logical_and(r == c, r < size)))
        outs[0][:4 * joined, :] = total.astype(bf16)
        outs[0][4 * joined:, :] = jnp.zeros((GAIN_ROWS, model), bf16)
        outs[0][4 * joined:, :lanes] = gains.astype(bf16)
        finish(copies)

    rows, width, model = x_links[0].shape
    whole = 4 * joined + GAIN_ROWS
    outs = [shaped((whole, model)), shaped((links, rows, width, model))]
    return call(
        body, "join_dp", outs, [meta], list(pieces) + list(x_links), [dma(links)], after=after,
        raw_args=tuple(range(depth, depth + links)),
    )


def forward_across(w_links, x_halves):
    total_rows, model = w_links[0].shape
    cut_at = (total_rows - GAIN_ROWS) // 2
    links = len(w_links)

    def body(*refs):
        w_refs, h_refs, outs = refs[:links], refs[links:links + 2], refs[links + 2:]
        outs[0][...] = w_refs[2][:cut_at, :]
        outs[1][...] = w_refs[1][cut_at:, :]
        for i in range(links):
            outs[2][i] = w_refs[i][:total_rows, :]
        for i in range(2):
            outs[3][i] = h_refs[i][...]

    outs = [
        shaped((cut_at, model)), shaped((total_rows - cut_at, model)), shaped((links, total_rows, model)),
        shaped((2, *x_halves[0].shape)),
    ]
    return call(body, "forward_across", outs, [], list(w_links) + list(x_halves))


def join_feed(meta, pieces, size, count, after):
    depth, total_rows, model = pieces.shape
    bands = count // GROUP
    band = (total_rows - count * size) // bands

    def body(meta_ref, in_ref, inner_ref, outer_ref, held, joined, sems):
        copies = begin([(in_ref.at[d], held.at[d]) for d in range(depth)], sems)
        for d in range(depth):
            copies[d].wait()
            for k in range(count):
                inner_ref[(k * depth + d) * size:(k * depth + d + 1) * size, :] = held[d, k * size:(k + 1) * size, :]
            for j in range(bands):
                start = count * size + j * band
                joined[j, d * band:(d + 1) * band, :] = held[d, start:start + band, :]
        for j in range(bands):
            outer_ref[aligned((meta_ref[0] // GROUP) ^ j, band * depth), :] = joined[j]

    outs = [shaped((count * depth * size, model)), shaped((bands * band * depth, model))]
    scratch = [
        pltpu.VMEM((depth, total_rows, model), bf16), pltpu.VMEM((bands, band * depth, model), bf16), dma(depth),
    ]
    return call(body, "join_feed", outs, [meta], [pieces], scratch, 0, after, (0,))


def slot_of(meta_ref, slot):
    return meta_ref[2 + 4 * slot], meta_ref[3 + 4 * slot] > 0, meta_ref[4 + 4 * slot]


def masked_cotangent(meta, own, far, after):
    rows, width, model = own.shape

    def body(meta_ref, own_ref, far_ref, out_ref):
        for slot in range(2):
            block, unused, row = slot_of(meta_ref, slot)
            length = meta_ref[5 + 4 * slot]
            position = block * width + lax.broadcasted_iota(jnp.int32, (width, model), 0)
            value = jnp.where(row == 0, own_ref[0].astype(f32), far_ref[...].astype(f32))
            out_ref[slot * width:(slot + 1) * width, :] = jnp.where(position < length, value, 0.0).astype(bf16)

    outs = [shaped((rows * width, model))]
    return call(body, "masked_cotangent", outs, [meta], [own, far], (), 0, after)[0]


def masked(tile, chunk, block, width, fill):
    rows, lanes = tile.shape
    key = chunk * CHUNK + lax.broadcasted_iota(jnp.int32, (rows, lanes), 0)
    query = block * width + lax.broadcasted_iota(jnp.int32, (rows, lanes), 1) % width
    return jnp.where(key <= query, tile, fill)


def mix_columns(vector_t, mix, out_ref, heads, heads_in, scale, by_row):
    model, width = vector_t.shape
    size = model // heads
    for i, h in enumerate(heads_in):
        for g in range(heads):
            factor = (mix[h, g] if by_row else mix[g, h]) * scale
            out_ref[g * size:(g + 1) * size, i * width:(i + 1) * width] = (
                vector_t[g * size:(g + 1) * size, :] * factor
            ).astype(bf16)


def lanes_at(index, size):
    return pl.ds(pl.multiple_of(index * size, size), size)


def over_keys(left_ref, right_ref, out_ref, used, lanes):
    for m in range(1, left_ref.shape[1] // CHUNK + 1):
        @pl.when(used == m)
        def _():
            def some(t, unused):
                part = lanes_at(t, lanes)
                out_ref[:, part] = dot(left_ref[:, :m * CHUNK], right_ref[:m * CHUNK, part])
                return 0

            lax.fori_loop(0, out_ref.shape[1] // lanes, some, 0)


def listed(pieces):
    arrays, spots = [], []
    for parts in pieces:
        spot = []
        for array, index in parts:
            known = [i for i, a in enumerate(arrays) if a is array]
            if not known:
                arrays.append(array)
            spot.append((known[0] if known else len(arrays) - 1, index))
        spots.append(spot)
    return arrays, spots


def views(refs, spot):
    return [refs[i] if index is None else refs[i].at[index] for i, index in spot]


def attend_forward(meta, premix, postmix, x_pieces, w_pieces, after):
    count = len(x_pieces)
    x_arrays, x_spots = listed(x_pieces)
    w_arrays, w_spots = listed(w_pieces)
    width, model = x_arrays[0].shape[1:]
    length = count * width
    chunks = length // CHUNK
    heads = premix.shape[0]
    size = model // heads
    pair = 2 * width
    lanes = heads * width
    half = lanes // 2
    w_rows = model // count
    mirror = count - 1

    def body(meta_ref, pre, post, *refs):
        x_refs, refs = refs[:len(x_arrays)], refs[len(x_arrays):]
        w_refs, refs = refs[:len(w_arrays)], refs[len(w_arrays):]
        joined_ref, second_ref, middle_ref, n_out, k_out, v_out, q_ref, ut_out, lse_ref, w_out, wo_out, gain_ref = refs[:12]
        qst, s_ref, acc, mx, total_out, n_ref, k_ref, v_ref, w_ref, wo_ref, ut_ref, xs, gains = refs[12:25]
        vt_ref, refs = refs[-1], refs[:-1]
        x_sems, w_sems, sems, w_sem, ut_sems = refs[25:]
        place = meta_ref[0]
        x_copies = begin([(views(x_refs, x_spots[k])[0], xs.at[k]) for k in range(count)], x_sems)
        pairs, gain_pairs = [], []
        for k in range(count):
            at, spot = 0, aligned(place ^ k, w_rows)
            for ref in views(w_refs, w_spots[k]):
                for start in range(0, ref.shape[0], w_rows):
                    if at > 4:
                        continue
                    if at < 3:
                        target = w_ref.at[spot, at * model:(at + 1) * model]
                        pairs.append((ref.at[start:start + w_rows, :], target))
                    elif at == 3:
                        pairs.append((ref.at[start:start + w_rows, :], wo_ref.at[spot, :]))
                    else:
                        gain_pairs.append((ref.at[start:start + GAIN_ROWS, :128], gains.at[k]))
                    at += 1
        w_copies = begin(gain_pairs + pairs, w_sems)
        finish(x_copies + w_copies[:count])
        gain = jnp.zeros((GAIN_ROWS, model), f32)
        for k in range(count):
            r, c = picks(128, model, 0, (place ^ k) * w_rows)
            gain += dot(gains[k], one_hot(jnp.logical_and(r == c, r < w_rows)))
        gain_ref[...] = gain[:8, :]
        out_copies = [
            pltpu.make_async_copy(w_ref, w_out, w_sem.at[0]), pltpu.make_async_copy(wo_ref, wo_out, w_sem.at[1])
        ]

        finish(w_copies[count:])
        for copy in out_copies:
            copy.start()

        def attend(slot, unused):
            block, active, row = slot_of(meta_ref, slot)
            last = block // 2
            mine = aligned(slot, width)
            ut_copies = [
                pltpu.make_async_copy(ut_ref.at[2 * slot + i], ut_out.at[2 * slot + i], ut_sems.at[2 * slot + i])
                for i in range(2)
            ]

            def leave(c):
                spot = aligned(c, CHUNK)
                pairs = ((n_ref, n_out), (k_ref, k_out), (v_ref, v_out))
                return [
                    pltpu.make_async_copy(a.at[spot, :], b.at[slot, spot, :], sems.at[i, c])
                    for i, (a, b) in enumerate(pairs)
                ]

            @pl.when(active)
            def _():
                for k in range(count):
                    @pl.when((place ^ k) // 2 <= last)
                    def _():
                        xb = xs[k, row].astype(f32)
                        n_ref[aligned(place ^ k, width), :] = (xb * inverse_rms(xb) * gain_ref[0:1, :]).astype(bf16)

            @pl.when(jnp.logical_not(active))
            def _():
                joined_ref[mine, :] = jnp.zeros((width, model), bf16)

            @pl.when(active)
            def _():
                def project(c, unused):
                    nc = n_ref[aligned(c, CHUNK), :]
                    k_ref[aligned(c, CHUNK), :] = dot(nc, w_ref[:, model:2 * model]).astype(bf16)
                    vc = dot(nc, w_ref[:, 2 * model:3 * model]).astype(bf16)
                    v_ref[aligned(c, CHUNK), :] = vc
                    vt_ref[c] = vc.T
                    for copy in leave(c):
                        copy.start()
                    return 0

                lax.fori_loop(0, last + 1, project, 0)
                query = dot(n_ref[aligned(block, width), :], w_ref[:, :model]).astype(bf16)
                q_ref[mine, :] = query
                query_t = query.astype(f32).T
                for part_of in range(2):
                    heads_in = range(part_of * heads // 2, (part_of + 1) * heads // 2)
                    mix_columns(query_t, pre, qst, heads, heads_in, 0.125, False)
                    mx[...] = jnp.full(mx.shape, NEGATIVE, f32)

                    def scores(c, unused):
                        kc = k_ref[aligned(c, CHUNK), :]
                        for t in range(half // pair):
                            part = slice(t * pair, (t + 1) * pair)
                            s = masked(dot(kc, qst[:, part]), c, block, width, NEGATIVE)
                            s_ref[aligned(c, CHUNK), part] = s
                            mx[:, part] = jnp.maximum(mx[:, part], jnp.max(s.reshape(CHUNK // 8, 8, pair), axis=0))
                        return 0

                    lax.fori_loop(0, last + 1, scores, 0)
                    peak = jnp.max(mx[...], axis=0, keepdims=True)
                    acc[...] = jnp.zeros(acc.shape, f32)
                    mx[...] = jnp.zeros(mx.shape, f32)

                    def weigh(c, unused):
                        vt = vt_ref[c]
                        for t in range(half // pair):
                            part = slice(t * pair, (t + 1) * pair)
                            p = jnp.exp(s_ref[aligned(c, CHUNK), part] - peak[:, part])
                            mx[:, part] += jnp.sum(p.reshape(CHUNK // 8, 8, pair), axis=0)
                            acc[:, part] += dot(vt, p.astype(bf16))
                        return 0

                    lax.fori_loop(0, last + 1, weigh, 0)
                    total = jnp.sum(mx[...], axis=0, keepdims=True)
                    lse_ref[slot, :, part_of * half:(part_of + 1) * half] = peak + jnp.log(total)
                    inverse = 1.0 / total
                    for k in range(heads):
                        rows = slice(k * size, (k + 1) * size)
                        out = jnp.zeros((size, width), f32)
                        for i, h in enumerate(heads_in):
                            cols = slice(i * width, (i + 1) * width)
                            u = acc[rows, cols] * inverse[:, cols]
                            ut_ref[2 * slot + part_of, rows, cols] = u.astype(bf16)
                            out += u * post[h, k]
                        if part_of == 0:
                            total_out[rows, :] = out
                        else:
                            total_out[rows, :] += out
                    ut_copies[part_of].start()
                joined_ref[mine, :] = total_out[...].T.astype(bf16)

                def gone(c, unused):
                    finish(leave(c))
                    return 0

                lax.fori_loop(0, last + 1, gone, 0)

            residual = jnp.where(row == 0, xs[0, 0].astype(f32), xs[mirror, 1].astype(f32))
            middle = residual + dot(joined_ref[mine, :], wo_ref[...])
            middle_ref[mine, :] = middle
            second_ref[mine, :] = (middle * inverse_rms(middle) * gain_ref[1:2, :]).astype(bf16)

            @pl.when(active)
            def _():
                finish(ut_copies)

            return 0

        lax.fori_loop(0, 2, attend, 0)
        finish(out_copies)

    tokens = 2 * width
    outs = [
        shaped((tokens, model)), shaped((tokens, model)), shaped((tokens, model), f32), shaped((2, length, model)),
        shaped((2, length, model)), shaped((2, length, model)), shaped((tokens, model)), shaped((4, model, half)),
        shaped((2, 1, lanes), f32), shaped((model, 3 * model)), shaped((model, model)), shaped((8, model), f32),
    ]
    scratch = [
        pltpu.VMEM((model, half), bf16), pltpu.VMEM((length, half), f32), pltpu.VMEM((model, half), f32),
        pltpu.VMEM((8, half), f32), pltpu.VMEM((model, width), f32), pltpu.VMEM((length, model), bf16),
        pltpu.VMEM((length, model), bf16), pltpu.VMEM((length, model), bf16), pltpu.VMEM((model, 3 * model), bf16),
        pltpu.VMEM((model, model), bf16), pltpu.VMEM((4, model, half), bf16),
        pltpu.VMEM((count, 2, width, model), bf16), pltpu.VMEM((count, GAIN_ROWS, 128), bf16),
        dma(count), dma(5 * count), pltpu.SemaphoreType.DMA((3, chunks)), dma(2), dma(4),
        pltpu.VMEM((chunks, model, CHUNK), bf16),
    ]
    args = x_arrays + w_arrays
    flops = 4 * length * model * (lanes + 2 * model)
    return call(
        body, "attend_forward", outs, [meta, premix, postmix], args, scratch, flops, after,
        tuple(range(len(args))), (3, 4, 5, 7, 9, 10),
    )


def feed_forward(seconds, ups, inner_w, outer_w):
    width, model = seconds[0].shape
    units = inner_w.shape[1]
    tokens = GROUP * width
    root = 0.7978845608028654
    tile = 256

    def body(*refs):
        s_refs, u_refs, (w1, w2), refs = refs[:GROUP], refs[GROUP:2 * GROUP], refs[2 * GROUP:2 * GROUP + 2], refs[2 * GROUP + 2:]
        hidden_ref, inner_ref, grads, outs, (tok, up, sems) = refs[0], refs[1], refs[2:5], refs[5:8], refs[8:]
        spots = [slice(i * width, (i + 1) * width) for i in range(GROUP)]
        pairs = [(s_refs[i], tok.at[spots[i], :]) for i in range(GROUP)]
        pairs += [(u_refs[i], up.at[spots[i], :]) for i in range(GROUP)]
        copies = begin(pairs, sems)
        finish(copies[:GROUP])
        for t in range(units // tile):
            part = slice(t * tile, (t + 1) * tile)
            v = dot(tok[...], w1[:, part])
            squared = v * v
            th = jnp.tanh(root * (v + 0.044715 * (squared * v)))
            hidden_ref[:, part] = (0.5 * v * (1.0 + th)).astype(bf16)
            slope = 0.5 * (1.0 + th) + 0.5 * v * (1.0 - th * th) * (root * (1.0 + 0.134145 * squared))
            if t == 0:
                finish(copies[GROUP:])
            inner_ref[:, part] = (dot(up[...], w2[part, :], 1, 1) * slope).astype(bf16)
        for (own_ref, give_ref, across_ref), made in (
            (grads, dot(inner_ref[...], w1[...], 1, 1)), (outs, dot(hidden_ref[...], w2[...]))
        ):
            made = made.astype(bf16)
            own_ref[...] = made[:width]
            give_ref[:width, :] = made[width:2 * width]
            give_ref[width:, :] = made[3 * width:]
            across_ref[...] = made[2 * width:3 * width]

    outs = [shaped((tokens, units)), shaped((tokens, units))]
    outs += [shaped((width, model)), shaped((2 * width, model)), shaped((width, model))] * 2
    scratch = [pltpu.VMEM((tokens, model), bf16), pltpu.VMEM((tokens, model), bf16), dma(2 * GROUP)]
    args = list(seconds) + list(ups) + [inner_w, outer_w]
    made = call(
        body, "feed_forward", outs, [], args, scratch, 8 * tokens * model * units, (), tuple(range(2 * GROUP))
    )
    return made[0], made[1], made[2:5], made[5:8]


def feed_weights(meta, seconds, ups, hidden, inner, bands, after):
    width, model = seconds[0].shape
    units = hidden.shape[1]
    tokens = GROUP * width
    rows_out = units // bands

    def body(meta_ref, *refs):
        s_refs, u_refs, (h_ref, i_ref), refs = refs[:GROUP], refs[GROUP:2 * GROUP], refs[2 * GROUP:2 * GROUP + 2], refs[2 * GROUP + 2:]
        inner_out, outer_j, (tok, up, grad, sems) = refs[0], refs[1:1 + bands], refs[1 + bands:]
        pairs = [(s_refs[i], tok.at[i * width:(i + 1) * width, :]) for i in range(GROUP)]
        pairs += [(u_refs[i], up.at[i * width:(i + 1) * width, :]) for i in range(GROUP)]
        copies = begin(pairs, sems)
        finish(copies[:GROUP])
        inner_out[...] = dot(tok[...], i_ref[...], 0, 0).astype(bf16)
        finish(copies[GROUP:])
        grad[...] = dot(h_ref[...], up[...], 0, 0).astype(bf16)
        for j in range(bands):
            outer_j[j][...] = grad[aligned((meta_ref[0] // GROUP) ^ j, rows_out), :]

    outs = [shaped((model, units))] + [shaped((rows_out, model))] * bands
    args = list(seconds) + list(ups) + [hidden, inner]
    scratch = [
        pltpu.VMEM((tokens, model), bf16), pltpu.VMEM((tokens, model), bf16), pltpu.VMEM((units, model), bf16),
        dma(2 * GROUP),
    ]
    made = call(
        body, "feed_weights", outs, [meta], args, scratch, 4 * tokens * model * units, after, tuple(range(2 * GROUP))
    )
    return made[0], list(made[1:])


def before_attention_back(own, got, came, middle, up, gains, w, joined, inner_grads, out_got, out_across, count, after):
    tokens, model = own.shape
    rows = model // count

    def body(own_ref, got_ref, came_ref, middle_ref, up_ref, gain_ref, w_in, joined_ref, inner_ref, out_got_ref, out_ref,
             grad_ref, upstream_ref, packed_ref, across_ref, w_ref, total_ref, sems):
        across_ref[...] = (out_ref[...].astype(f32) + out_got_ref[tokens:, :].astype(f32)).astype(bf16)
        copies = begin([(w_in, w_ref), (inner_ref, total_ref.at[:, rows:, :])], sems)
        second = own_ref[...].astype(f32) + got_ref[:tokens, :].astype(f32) + came_ref[...].astype(f32)
        back = norm_back(middle_ref[...], gain_ref[1:2, :], second)
        grad = up_ref[...].astype(f32) + back
        grad_ref[...] = grad
        cast = grad.astype(bf16)
        total = dot(joined_ref[...], cast, 0, 0)
        for j in range(count):
            total_ref[j, :rows, :] = total[j * rows:(j + 1) * rows, :].astype(bf16)
        copies[1].wait()
        last = pltpu.make_async_copy(total_ref, packed_ref, sems.at[2])
        last.start()
        copies[0].wait()
        upstream_ref[...] = dot(cast, w_ref[...], 1, 1).astype(bf16)
        last.wait()

    outs = [
        shaped((tokens, model), f32), shaped((tokens, model)), shaped((count, 2 * rows, model)), shaped((tokens, model)),
    ]
    args = [own, got, came, middle, up, gains, w, joined, inner_grads.reshape(count, rows, model), out_got, out_across]
    scratch = [pltpu.VMEM((model, model), bf16), pltpu.VMEM((count, 2 * rows, model), bf16), dma(3)]
    return call(
        body, "before_attention_back", outs, [], args, scratch, 4 * tokens * model * model, after, (6, 8), (2,)
    )


def attend_back(meta, premix, postmix, pre_row, post_row, query, upstream, normed, keys, values, ut, lse, count, after):
    tokens, model = query.shape
    width = tokens // 2
    length = keys.shape[1]
    heads = premix.shape[0]
    size = model // heads
    pair = 2 * width
    lanes = heads * width
    half = lanes // 2
    w_rows = model // count

    def body(meta_ref, pre, post, pre_in, post_in, q_in, up_in, lse_in, n_hbm, k_hbm, v_hbm, ut_hbm,
             dq_ref, dk_hbm, dv_hbm, mix_out, keep_ref, give_ref,
             qst, qs, ust, us, acc, pbuf, lbuf, dots, wacc, cin, cout, n_own, ut_held, in_sems, out_sems, own_sem, ut_sems,
             pre_row, post_row, q_ref, up_ref, lse_ref, arg_sems, kt_ref, nt_ref, mix_ref):
        args = begin(
            [(pre_in, pre_row), (post_in, post_row), (q_in, q_ref), (up_in, up_ref), (lse_in, lse_ref)], arg_sems
        )
        wacc[...] = jnp.zeros(wacc.shape, f32)
        mix_ref[...] = jnp.zeros(mix_ref.shape, f32)
        finish(args)

        def through(slot, unused):
            block, active, unused_row = slot_of(meta_ref, slot)
            last = block // 2
            mine = aligned(slot, width)
            ut_copies = [
                pltpu.make_async_copy(ut_hbm.at[2 * slot + i], ut_held.at[i], ut_sems.at[i]) for i in range(2)
            ]

            @pl.when(jnp.logical_not(active))
            def _():
                dq_ref[mine, :] = jnp.zeros((width, model), bf16)

            @pl.when(active)
            def _():
                def fetch(c):
                    return [
                        pltpu.make_async_copy(
                            a.at[slot, aligned(c, CHUNK), :], cin.at[c % 2, i], in_sems.at[c % 2, i]
                        )
                        for i, a in enumerate((k_hbm, v_hbm, n_hbm))
                    ]

                def leave(c):
                    return [
                        pltpu.make_async_copy(
                            cout.at[c % 2, i], a.at[slot, aligned(c, CHUNK), :], out_sems.at[c % 2, i]
                        )
                        for i, a in enumerate((dk_hbm, dv_hbm))
                    ]

                own = pltpu.make_async_copy(n_hbm.at[slot, aligned(block, width), :], n_own, own_sem)
                own.start()
                for copy in ut_copies + fetch(0):
                    copy.start()
                q = q_ref[mine, :].astype(f32)
                up = up_ref[mine, :].astype(f32)
                qt, upt = q.T, up.T
                mix_columns(qt, pre, qst, heads, range(heads), 0.125, False)
                mix_columns(upt, post, ust, heads, range(heads), 1.0, True)
                for h in range(heads):
                    spot = slice(h * width, (h + 1) * width)
                    qs[spot, :] = (q * (pre_row[h:h + 1, :] * 0.125)).astype(bf16)
                    us[spot, :] = (up * post_row[h:h + 1, :]).astype(bf16)
                finish(ut_copies)
                for h in range(heads):
                    spot = slice(h * width, (h + 1) * width)
                    column = h % (heads // 2) * width
                    u = ut_held[h // (heads // 2), :, column:column + width].astype(f32)
                    t = jnp.sum((u * upt).reshape(heads, size, width), axis=1)
                    mix_ref[(heads + h) * heads:(heads + h + 1) * heads, :] += t
                    d = jnp.zeros((1, width), f32)
                    for k in range(heads):
                        d += t[k:k + 1, :] * post[h, k]
                    dots[:, spot] = d

                def visit(c, unused):
                    finish(fetch(c))

                    @pl.when(c < last)
                    def _():
                        for copy in fetch(c + 1):
                            copy.start()

                    kc, vc = cin[c % 2, 0], cin[c % 2, 1]
                    kt_ref[:, lanes_at(c, CHUNK)] = kc.T
                    nt_ref[...] = cin[c % 2, 2].T
                    for t in range(heads // 2):
                        part = slice(t * pair, (t + 1) * pair)
                        p = masked(jnp.exp(dot(kc, qst[:, part]) - lse_ref[slot, :, part]), c, block, width, 0.0)
                        grad = (p * (dot(vc, ust[:, part]) - dots[:, part])).astype(bf16)
                        pbuf[:, part] = p.astype(bf16)
                        lbuf[aligned(c, CHUNK), part] = grad

                    @pl.when(c >= 2)
                    def _():
                        finish(leave(c - 2))

                    dk = dot(lbuf[aligned(c, CHUNK), :], qs[...]).astype(bf16)
                    dv = dot(pbuf[...], us[...]).astype(bf16)
                    cout[c % 2, 0] = dk
                    cout[c % 2, 1] = dv
                    for copy in leave(c):
                        copy.start()
                    wacc[:, model:2 * model] += dot(nt_ref[...], dk)
                    wacc[:, 2 * model:] += dot(nt_ref[...], dv)
                    return 0

                lax.fori_loop(0, last + 1, visit, 0)
                over_keys(kt_ref, lbuf, acc, last + 1, pair)
                for g in range(heads):
                    rows = slice(g * size, (g + 1) * size)
                    out = jnp.zeros((size, width), f32)
                    qg = qt[rows, :] * 0.125
                    for h in range(heads):
                        a = acc[rows, h * width:(h + 1) * width]
                        out += a * pre[g, h]
                        mix_ref[g * heads + h:g * heads + h + 1, :] += jnp.sum(a * qg, axis=0, keepdims=True)
                    acc[rows, 0:width] = out * 0.125
                dq = acc[:, 0:width].T.astype(bf16)
                dq_ref[mine, :] = dq
                own.wait()
                wacc[:, :model] += dot(n_own[...], dq, 0, 0)

                @pl.when(last >= 1)
                def _():
                    finish(leave(last - 1))

                finish(leave(last))

            return 0

        lax.fori_loop(0, 2, through, 0)
        every = jnp.sum(mix_ref[...], axis=1, keepdims=True)
        r = lax.broadcasted_iota(jnp.int32, mix_ref.shape, 0)
        c = lax.broadcasted_iota(jnp.int32, mix_ref.shape, 1)
        every = jnp.where(r % 128 == c, every, 0.0)
        mix_out[...] = jnp.zeros(mix_out.shape, f32)
        for i in range(-(-mix_ref.shape[0] // 128)):
            mix_out[i:i + 1, :] = jnp.sum(every[i * 128:(i + 1) * 128, :], axis=0, keepdims=True)
        for k in range(count):
            (keep_ref, give_ref)[k % 2][k // 2 * w_rows:(k // 2 + 1) * w_rows, :] = wacc[
                aligned(meta_ref[0] ^ k, w_rows), :
            ].astype(bf16)

    outs = [
        shaped((tokens, model)), shaped((2, length, model)), shaped((2, length, model)),
        shaped((8, 128), f32), shaped((count // 2 * w_rows, 3 * model)),
        shaped((count // 2 * w_rows, 3 * model)),
    ]
    scratch = [
        pltpu.VMEM((model, lanes), bf16), pltpu.VMEM((lanes, model), bf16), pltpu.VMEM((model, lanes), bf16),
        pltpu.VMEM((lanes, model), bf16), pltpu.VMEM((model, lanes), f32), pltpu.VMEM((CHUNK, lanes), bf16),
        pltpu.VMEM((length, lanes), bf16), pltpu.VMEM((1, lanes), f32), pltpu.VMEM((model, 3 * model), f32),
        pltpu.VMEM((2, 3, CHUNK, model), bf16), pltpu.VMEM((2, 2, CHUNK, model), bf16), pltpu.VMEM((width, model), bf16),
        pltpu.VMEM((2, model, half), bf16), pltpu.SemaphoreType.DMA((2, 3)), pltpu.SemaphoreType.DMA((2, 2)),
        pltpu.SemaphoreType.DMA, dma(2), pltpu.VMEM((heads, model), f32), pltpu.VMEM((heads, model), f32),
        pltpu.VMEM((tokens, model), bf16), pltpu.VMEM((tokens, model), bf16), pltpu.VMEM((2, 1, lanes), f32), dma(5),
        pltpu.VMEM((model, length), bf16), pltpu.VMEM((model, CHUNK), bf16),
        pltpu.VMEM((2 * heads * heads, width), f32),
    ]
    args = [pre_row, post_row, query, upstream, lse, normed, keys, values, ut]
    return call(
        body, "attend_back", outs, [meta, premix, postmix], args, scratch, 15 * length * model * lanes, after,
        tuple(range(9)), (1, 2),
    )


def input_back(meta, dq, dk, dv, w, x_pieces, gains, grad, after):
    count = len(x_pieces)
    x_arrays, x_spots = listed(x_pieces)
    width, model = x_arrays[0].shape[1:]
    length = dk.shape[1]
    chunks = length // CHUNK

    def body(meta_ref, dq_in, grad_in, gain_in, dk_hbm, dv_hbm, w_hbm, *refs):
        x_refs, refs = refs[:len(x_arrays)], refs[len(x_arrays):]
        keep_ref, give_ref, normed, dk_held, dv_held, w_ref, xs, sems, w_sem, x_sems = refs[:10]
        dq_ref, grad_ref, gain_ref, arg_sems, wt_ref = refs[10:]
        arg_copies = begin([(dq_in, dq_ref), (grad_in, grad_ref), (gain_in, gain_ref)], arg_sems)
        place = meta_ref[0]
        w_copy = pltpu.make_async_copy(w_hbm, w_ref, w_sem)
        w_copy.start()

        def fetch(slot, c):
            spot = aligned(c, CHUNK)
            return [
                pltpu.make_async_copy(a.at[slot, spot, :], b.at[slot, spot, :], sems.at[slot, c, i])
                for i, (a, b) in enumerate(((dk_hbm, dk_held), (dv_hbm, dv_held)))
            ]

        def start(slot, c):
            for copy in fetch(slot, c):
                copy.start()
            return 0

        for slot in range(2):
            block, active, row = slot_of(meta_ref, slot)
            needed = jnp.where(active, block // 2 + 1, 0)
            lax.fori_loop(0, needed, lambda c, unused, slot=slot: start(slot, c), 0)
        x_copies = begin([(views(x_refs, x_spots[k])[0], xs.at[k]) for k in range(count)], x_sems)
        w_copy.wait()
        for i in range(3):
            wt_ref[i] = w_ref[:, i * model:(i + 1) * model].T
        finish(arg_copies)

        finish(x_copies)

        def through(slot, unused):
            block, active, row = slot_of(meta_ref, slot)
            mine = aligned(slot, width)

            @pl.when(active)
            def _():
                def visit(c, unused):
                    spot = aligned(c, CHUNK)
                    finish(fetch(slot, c))
                    normed[spot, :] = dot(dk_held[slot, spot, :], wt_ref[1]) + dot(dv_held[slot, spot, :], wt_ref[2])
                    return 0

                lax.fori_loop(0, block // 2 + 1, visit, 0)
                normed[aligned(block, width), :] += dot(dq_ref[mine, :], wt_ref[0])

            def chip(i, unused):
                for k, out_ref in enumerate((keep_ref, give_ref)):
                    source = place ^ (2 * i + k)
                    spot = aligned(2 * i + row, width)
                    used = jnp.logical_and(active, source <= block)

                    @pl.when(jnp.logical_not(used))
                    def _():
                        out_ref[spot, :] = jnp.zeros((width, model), bf16)

                    @pl.when(used)
                    def _():
                        back = norm_back(
                            xs[2 * i + k, row].astype(f32), gain_ref[0:1, :], normed[aligned(source, width), :]
                        )
                        factor = jnp.where(source == block, 1.0, 0.0)
                        out_ref[spot, :] = (back + grad_ref[mine, :] * factor).astype(bf16)
                return 0

            lax.fori_loop(0, count // 2, chip, 0)
            return 0

        lax.fori_loop(0, 2, through, 0)

    half = count * width
    outs = [shaped((half, model)), shaped((half, model))]
    args = [dq, grad, gains, dk, dv, w] + x_arrays
    scratch = [
        pltpu.VMEM((length, model), f32), pltpu.VMEM((2, length, model), bf16), pltpu.VMEM((2, length, model), bf16),
        pltpu.VMEM((model, 3 * model), bf16), pltpu.VMEM((count, 2, width, model), bf16),
        pltpu.SemaphoreType.DMA((2, chunks, 2)), pltpu.SemaphoreType.DMA, dma(count),
        pltpu.VMEM(dq.shape, bf16), pltpu.VMEM(grad.shape, f32), pltpu.VMEM(gains.shape, f32), dma(3),
        pltpu.VMEM((3, model, model), bf16),
    ]
    return call(
        body, "input_back", outs, [meta], args, scratch, 8 * length * model * model, after,
        tuple(range(len(args))),
    )


def pair_sums(keep, got, count, later, after, name):
    blocks = count // 2
    rows, columns = keep.shape[0] // blocks, keep.shape[1]

    def body(keep_ref, got_ref, *refs):
        outs = refs[len(later):]
        for source, target in zip(refs, outs[blocks:]):
            target[...] = source[...]
        for i in range(blocks):
            spot = slice(i * rows, (i + 1) * rows)
            outs[i][...] = (keep_ref[spot, :].astype(f32) + got_ref[spot, :].astype(f32)).astype(outs[i].dtype)

    outs = [shaped((rows, columns))] * blocks
    outs += [shaped(a.shape, a.dtype) for a in later]
    made = call(body, name, outs, [], [keep, got] + list(later), (), 0, after)
    return made[:blocks], made[blocks:]


def halves_first(keep, got, pair, after, name):
    rows, columns = keep.shape[0] // 4, keep.shape[1]
    half = rows // 2

    def body(keep_ref, got_ref, *refs):
        if pair:
            refs[-1][...] = refs[0][...] + refs[1][...]
        two_ref, four_ref, rest_ref = refs[len(pair):len(pair) + 3]

        def part(i, b):
            spot = slice(i * rows + b * half, i * rows + (b + 1) * half)
            return keep_ref[spot, :].astype(f32) + got_ref[spot, :].astype(f32)

        for n, (i, b) in enumerate(((1, 0), (3, 0))):
            two_ref[n * half:(n + 1) * half, :] = part(i, b).astype(bf16)
        for n, (i, b) in enumerate(((2, 1), (3, 1))):
            four_ref[n * half:(n + 1) * half, :] = part(i, b).astype(bf16)
        for n, (i, b) in enumerate(((0, 0), (2, 0), (0, 1), (1, 1))):
            rest_ref[n * half:(n + 1) * half, :] = part(i, b)

    outs = [
        shaped((rows, columns)), shaped((rows, columns)), shaped((2 * rows, columns), f32),
    ] + [shaped(a.shape, f32) for a in pair[:1]]
    return call(body, name, outs, [], [keep, got, *pair], (), 0, after)


def halves_second(rest, from_two, from_four, pair, after, name):
    rows, columns = from_two.shape
    half = rows // 2

    def body(rest_ref, two_in, four_in, one, other, two_ref, four_ref, own_ref, sum_ref):
        sum_ref[...] = one[...] + other[...]
        own_ref[:half, :] = rest_ref[:half, :] + two_in[:half, :].astype(f32)
        four_ref[...] = (rest_ref[half:rows, :] + two_in[half:, :].astype(f32)).astype(bf16)
        own_ref[half:, :] = rest_ref[rows:rows + half, :] + four_in[:half, :].astype(f32)
        two_ref[...] = (rest_ref[rows + half:, :] + four_in[half:, :].astype(f32)).astype(bf16)

    outs = [
        shaped((half, columns)), shaped((half, columns)), shaped((rows, columns), f32), shaped(pair[0].shape, f32),
    ]
    return call(body, name, outs, [], [rest, from_two, from_four, *pair], (), 0, after)


def input_sum(own, from_four, from_two, shape):
    rows, width, model = shape

    def body(own_ref, four_ref, two_ref, out_ref):
        out_ref[0] = (own_ref[:width, :] + four_ref[...].astype(f32)).astype(bf16)
        out_ref[1] = (own_ref[width:, :] + two_ref[...].astype(f32)).astype(bf16)

    return call(body, "input_sum", [shaped(shape)], [], [own, from_four, from_two])[0]


def split_dp(meta, depth, parts, pair, after):
    joined, wide = parts[0].shape
    size = joined // depth
    halved = parts[1].shape[0] != joined

    def body(meta_ref, *refs):
        ins, (one, other), outs, sum_ref = refs[:len(parts)], refs[len(parts):len(parts) + 2], refs[len(parts) + 2:-2], refs[-2]
        total_ref = refs[-1]
        sum_ref[...] = one[...] + other[...]
        if halved:
            for i in range(2):
                spot = slice(i * joined // 2, (i + 1) * joined // 2)
                total_ref[spot, :] = (ins[0][spot, :] + ins[1 + i][...].astype(f32)).astype(bf16)
        else:
            total = ins[0][...].astype(f32)
            for ref in ins[1:]:
                total += ref[...].astype(f32)
            total_ref[...] = total.astype(bf16)
        for m in range(depth):
            r, c = picks(size, joined, 0, (meta_ref[1] ^ m) * size)
            outs[m][...] = dot(one_hot(r == c), total_ref[...]).astype(bf16)

    outs = [shaped((size, wide))] * depth + [shaped(pair[0].shape, f32)]
    scratch = [pltpu.VMEM((joined, wide), bf16)]
    made = call(body, "split_dp", outs, [meta], list(parts) + list(pair), scratch, 0, after)
    return made[:depth], made[depth]


def split_feed(meta, depth, grads, outer, size, middle, parts_out):
    count, joined, units = grads.shape
    joined //= 2
    bands = len(outer)
    band = outer[0].shape[0]
    shard = band // depth
    parts = 1 + GROUP
    out_rows = parts * size + shard
    tokens = middle.shape[0]
    width = tokens // 2

    def body(meta_ref, grad_in, *refs):
        o_ins, out_ins, refs = refs[:bands], refs[bands:bands + 4], refs[bands + 4:]
        outs, (total, grad_ref, outer_ref, middle_ref, part_ref, sems) = refs[:3], refs[3:]
        o_refs = [outer_ref.at[j] for j in range(bands)]
        pairs = [(out_ins[0], middle_ref)] + [(out_ins[1 + i].at[:tokens, :], part_ref.at[i]) for i in range(3)]
        copies = begin(pairs + [(grad_in, grad_ref)] + [(o_ins[j], o_refs[j]) for j in range(bands)], sems)
        finish(copies[:4])
        for slot in range(2):
            block, unused, row = slot_of(meta_ref, slot)
            spot = slice(slot * width, (slot + 1) * width)
            position = block * width + lax.broadcasted_iota(jnp.int32, (width, units), 0)
            value = middle_ref[spot, :]
            for i in range(3):
                value += part_ref[i, spot, :].astype(f32)
            value = jnp.where(position < meta_ref[5 + 4 * slot], value, 0.0).astype(bf16)
            for n in range(2):
                @pl.when(row == n)
                def _():
                    outs[1 + n][...] = value

        finish(copies[4:])
        section = grad_ref[0, :joined, :].astype(f32)
        for j in range(1, count):
            section += grad_ref[j, :joined, :].astype(f32)
        total[:joined, :] = section.astype(bf16)
        for t in range(GROUP):
            section = grad_ref[t, joined:, :].astype(f32)
            for j in range(1, bands):
                section += grad_ref[j * GROUP + t, joined:, :].astype(f32)
            total[(1 + t) * joined:(2 + t) * joined, :] = section.astype(bf16)
        rest = o_refs[0][...].astype(f32)
        for j in range(1, bands):
            rest += o_refs[j][...].astype(f32)
        total[parts * joined:, :] = rest.astype(bf16)
        for d in range(depth):
            for t in range(parts):
                outs[0][d, t * size:(t + 1) * size, :] = total[t * joined + d * size:t * joined + (d + 1) * size, :]
            start = parts * joined + d * shard
            outs[0][d, parts * size:, :] = total[start:start + shard, :]

    scratch = [
        pltpu.VMEM((parts * joined + band, units), bf16), pltpu.VMEM(grads.shape, bf16),
        pltpu.VMEM((bands, band, units), bf16), pltpu.VMEM((tokens, units), f32), pltpu.VMEM((3, tokens, units), bf16),
        dma(5 + bands),
    ]
    args = [grads] + list(outer) + [middle] + list(parts_out)
    outs = [shaped((depth, out_rows, units)), shaped((width, units)), shaped((width, units))]
    return call(body, "split_feed", outs, [meta], args, scratch, 0, (), tuple(range(len(args))))


def finish_projections(pieces, weights):
    size, wide = pieces[0].shape
    parts = 3
    model = wide // parts

    def body(*refs):
        ins, w_ins, outs = refs[:len(pieces)], refs[len(pieces):-6], refs[-6:-2]
        w_held, sems = refs[-2:]
        w_refs = [w_held.at[i] for i in range(parts)]
        finish(begin([(w_ins[i], w_refs[i]) for i in range(parts)], sems))
        along = jnp.zeros((size, 1), f32)
        for i in range(parts):
            part = slice(i * model, (i + 1) * model)
            total = ins[0][:, part].astype(f32)
            for ref in ins[1:]:
                total += ref[:, part].astype(f32)
            outs[i][...] = total
            along += jnp.sum(total * w_refs[i][...].astype(f32), axis=1, keepdims=True)
        outs[3][...] = along

    outs = [shaped((size, model), f32)] * parts + [shaped((size, 1), f32)]
    scratch = [pltpu.VMEM((parts, size, model), bf16), dma(parts)]
    args = list(pieces) + list(weights)
    return call(
        body, "finish_projections", outs, [], args, scratch, raw_args=tuple(range(len(pieces), len(args)))
    )


def finish_feed(pieces, weight, bands):
    size = weight.shape[0]
    depth, rows, units = pieces.shape
    band = units // bands

    def body(in_hbm, w_in, output_ref, inner_ref, outer_ref, along_ref, in_ref, w_ref, sems):
        finish(begin([(in_hbm, in_ref), (w_in, w_ref)], sems))
        total = in_ref[0].astype(f32)
        for d in range(1, depth):
            total += in_ref[d].astype(f32)
        output_ref[...] = total[:size, :]
        for t in range(GROUP):
            for y in range(bands):
                inner_ref[:, (y * GROUP + t) * band:(y * GROUP + t + 1) * band] = total[
                    (1 + t) * size:(2 + t) * size, y * band:(y + 1) * band
                ]
        outer_ref[...] = total[(1 + GROUP) * size:, :]
        along_ref[...] = jnp.sum(inner_ref[...] * w_ref[...].astype(f32), axis=1, keepdims=True)

    outs = [
        shaped((size, units), f32), shaped((size, GROUP * units), f32),
        shaped((rows - (1 + GROUP) * size, units), f32), shaped((size, 1), f32),
    ]
    scratch = [pltpu.VMEM(pieces.shape, bf16), pltpu.VMEM(weight.shape, bf16), dma(2)]
    return call(body, "finish_feed", outs, [], [pieces, weight], scratch, raw_args=(0, 1))


def swap(value, axis, mask):
    count = lax.axis_size(axis)
    return lax.ppermute(value, axis, [(i, i ^ mask) for i in range(count)])


def gather_dp(value):
    return [value] + [swap(value, "dp", m) for m in range(1, lax.axis_size("dp"))]


def gather_first(meta, inputs, first_w, inner, outer, after):
    count, depth = lax.axis_size("blk"), lax.axis_size("dp")
    pieces = gather_dp(first_w)
    x_links = [inputs, swap(inputs, "blk", 2), swap(inputs, "blk", 4)]
    shards = [outer] + [swap(outer, "blk", GROUP * j) for j in range(1, count // GROUP)]
    halves = [swap(x_links[2][0], "blk", 2), swap(x_links[1][1], "blk", 4)] if count == 8 else []
    w_own, x_core = join_dp(meta, pieces, x_links, after + shards[1:] + halves)
    feed = jnp.concatenate([inner] + shards, axis=0)
    if count == 8:
        w_links = [w_own, swap(w_own, "blk", 2), swap(w_own, "blk", 4)]
        x_core = swap(x_core, "blk", 1)
        w_on_two, w_on_four, w_core, x_across = forward_across(w_links, halves)
        w_across = [swap(w_on_two, "blk", 2), swap(w_on_four, "blk", 4)]
        w_core, x_far = swap(w_core, "blk", 1), swap(x_across, "blk", 1)
        w_far = [swap(part, "blk", 1) for part in w_across]
        xs = [[(a, None)] for a in x_links] + [[(x_across, None)]]
        ws = [[(a, None)] for a in w_links] + [[(a, None) for a in w_across]]
        xs_core = [[(x_core, i)] for i in range(3)] + [[(x_far, None)]]
        ws_core = [[(w_core, i)] for i in range(3)] + [[(a, None) for a in w_far]]
    else:
        x_links += [swap(inputs, "blk", k) for k in range(6, count, 2)]
        w_links = [w_own, swap(w_own, "blk", 2), swap(w_own, "blk", 4)]
        w_links += [swap(w_own, "blk", k) for k in range(6, count, 2)]
        xs, ws = [[(a, None)] for a in x_links], [[(a, None)] for a in w_links]
        xs_core, ws_core = [[(swap(a, "blk", 1), None)] for a in x_links], [[(swap(a, "blk", 1), None)] for a in w_links]
    x_pieces = [part for pair in zip(xs, xs_core) for part in pair]
    w_pieces = [part for pair in zip(ws, ws_core) for part in pair]
    return x_pieces, w_pieces, feed


def all_to_all(value, axis):
    return lax.all_to_all(value, axis, 0, 0, tiled=True)


def gather_group(value):
    two = swap(value, "blk", 2)
    return [value, swap(value, "blk", 1), two, swap(two, "blk", 1)]


def scatter_chips(parts):
    return [parts[0]] + [swap(part, "blk", 2 * i) for i, part in enumerate(parts) if i]


def on_device(
    inputs, lengths, prenorm, midnorm, query_proj, key_proj, value_proj, output_proj,
    premix, postmix, inner_proj, outer_proj, cotangent,
):
    count, depth = lax.axis_size("blk"), lax.axis_size("dp")
    place, zplace = lax.axis_index("blk"), lax.axis_index("dp")
    rows, width, model = inputs.shape
    shard = prenorm.shape[0]
    low = place < count // 2
    mirror = count - 1
    slot_rows = [jnp.where(low, 1, 0), jnp.where(low, 0, 1)]
    blocks = [jnp.maximum(place, place ^ mirror), jnp.minimum(place, place ^ mirror)]
    spans = [jnp.where(slot_rows[i] == 0, lengths[0], lengths[1]) for i in range(2)]
    meta = [place, zplace]
    for i in range(2):
        meta += [blocks[i], (blocks[i] * width < spans[i]).astype(jnp.int32), slot_rows[i], spans[i]]
    meta = jnp.stack(meta).astype(jnp.int32)

    head_size = model // premix.shape[0]
    pre_row = jnp.repeat(premix.T, head_size, axis=1)
    post_row = jnp.repeat(postmix, head_size, axis=1)
    bands = count // GROUP
    band_ff = depth * outer_proj.shape[0]
    first_w = pack_first([query_proj, key_proj, value_proj, output_proj], jnp.stack([prenorm, midnorm]))
    sections = inner_proj.reshape(shard, bands, GROUP, band_ff).transpose(2, 0, 1, 3).reshape(GROUP, shard, -1)
    sections = all_to_all(jnp.concatenate([sections] * bands), "blk").reshape(count * shard, -1)
    far_cotangent = swap(cotangent[1], "blk", mirror)
    x_pieces, w_pieces, second_w = gather_first(meta, inputs, first_w, sections, outer_proj, [sections])
    second_w = all_to_all(jnp.broadcast_to(second_w, (depth, *second_w.shape)), "dp")
    up = masked_cotangent(meta, cotangent, far_cotangent, [w_pieces[count - 2][0][0]])
    ups = gather_group(up)

    joined, second, middle, normed, keys, values, query, ut, lse, w, output_w, gain_rows = attend_forward(
        meta, premix, postmix, x_pieces, w_pieces, [up, pre_row, post_row]
    )
    seconds = gather_group(second)
    inner_w, outer_w = join_feed(meta, second_w, shard, count, [second, ups[2]])
    hidden, inner, (own, give, across), (out_own, out_give, out_across) = feed_forward(
        seconds, ups, inner_w, outer_w
    )
    got = swap(give, "blk", 1)
    tokens = rows * width
    across = (across.astype(f32) + got[tokens:].astype(f32)).astype(bf16)
    came = swap(across, "blk", 2)
    out_got = swap(out_give, "blk", 1)
    inner_grads, outer_grads = feed_weights(meta, seconds, ups, hidden, inner, bands, [across])

    grad, upstream, packed, out_across = before_attention_back(
        own, got, came, middle, up, gain_rows, output_w, joined, inner_grads, out_got, out_across, count, []
    )
    feed_grads = all_to_all(packed, "blk")
    outer_grads = [outer_grads[0]] + [swap(outer_grads[j], "blk", GROUP * j) for j in range(1, bands)]
    out_came = swap(out_across, "blk", 2)
    dq, dk, dv, mixes, keep, give = attend_back(
        meta, premix, postmix, pre_row, post_row, query, upstream, normed, keys, values, ut, lse, count, []
    )
    heads = premix.shape[0]
    cuts, near, far = split_feed(
        meta, depth, feed_grads, outer_grads, shard, middle, [out_own, out_got, out_came]
    )
    outputs = jnp.stack([near, swap(far, "blk", mirror)])
    input_keep, input_give = input_back(meta, dq, dk, dv, w, x_pieces, gain_rows, grad, [cuts])
    feed_sums = all_to_all(cuts, "dp")
    give, input_give = swap(give, "blk", 1), swap(input_give, "blk", 1)
    steps = [("blk", 1 << i) for i in range(count.bit_length() - 1)] + [("dp", 1 << i) for i in range(depth.bit_length() - 1)]

    def step(value):
        return value, swap(value, *steps.pop(0))

    if count == 8:
        two, four, rest = halves_first(keep, give, (), [input_keep], "halves_first_w")
        two, four = swap(two, "blk", 2), swap(four, "blk", 4)
        x_two, x_four, x_rest, mixes = halves_first(input_keep, input_give, step(mixes), [rest], "halves_first_x")
        x_two, x_four = swap(x_two, "blk", 2), swap(x_four, "blk", 4)
        two, four, rest, mixes = halves_second(rest, two, four, step(mixes), [x_rest], "halves_second_w")
        two, four = swap(two, "blk", 2), swap(four, "blk", 4)
        x_two, x_four, x_rest, mixes = halves_second(x_rest, x_two, x_four, step(mixes), [rest], "halves_second_x")
        x_two, x_four = swap(x_two, "blk", 2), swap(x_four, "blk", 4)
        cuts_w, mixes = split_dp(meta, depth, [rest, four, two], step(mixes), [x_rest])
        grad_inputs = input_sum(x_rest, x_four, x_two, inputs.shape)
    else:
        projected, unused = pair_sums(keep, give, count, [], [input_keep], "pair_sums_w")
        cuts_w, mixes = split_dp(meta, depth, scatter_chips(projected), step(mixes), [])
        parts, unused = pair_sums(input_keep, input_give, count, [], [], "pair_sums_x")
        grad_inputs = sum([part.astype(f32) for part in scatter_chips(parts)]).astype(bf16).reshape(inputs.shape)
    while steps:
        mixes = sum(step(mixes))
    mixes = mixes.reshape(-1)[:2 * heads * heads].reshape(2, heads, heads)
    output_sum, inner_sum, outer_sum, mid_gain = finish_feed(
        feed_sums, inner_proj, bands
    )
    cuts = cuts_w
    query_sum, key_sum, value_sum, pre_gain = finish_projections(
        [cuts[0]] + [swap(cuts[m], "dp", m) for m in range(1, depth)],
        [query_proj, key_proj, value_proj],
    )
    return (
        outputs,
        grad_inputs,
        pre_gain.reshape(-1) / prenorm.astype(f32),
        mid_gain.reshape(-1) / midnorm.astype(f32),
        query_sum,
        key_sum,
        value_sum,
        output_sum,
        mixes[0],
        mixes[1],
        inner_sum,
        outer_sum,
    )


def solution(mesh):
    weight = P(("blk", "dp"), None)
    vector = P(("blk", "dp"))
    tokens = P("dp", "blk", None)
    in_specs = (
        tokens, P("dp"), vector, vector, weight, weight, weight, weight, P(), P(), weight, weight, tokens,
    )
    out_specs = (
        tokens, tokens, vector, vector, weight, weight, weight, weight, P(), P(), weight, weight,
    )
    return jax.shard_map(on_device, mesh=mesh, in_specs=in_specs, out_specs=out_specs, check_vma=False)
```

```python
import jax
import jax.numpy as jnp
from jax import lax
from jax.experimental import pallas as pl
from jax.experimental.pallas import tpu as pltpu
from jax.sharding import PartitionSpec as P

EPSILON = 1e-06
GROUP = 4
CHUNK = 256
NEGATIVE = -1e30
VMEM_MOST = 60 * 1024 * 1024
VMEM_SPARE = 8 * 1024 * 1024
VMEM_WINDOWS = 18 * 1024 * 1024
GAIN_ROWS = 16
f32 = jnp.float32
bf16 = jnp.bfloat16
HIGH = lax.Precision.HIGHEST
ANY_SPEC = pl.BlockSpec(memory_space=pl.ANY)
VMEM_SPEC = pl.BlockSpec(memory_space=pltpu.VMEM)
HBM_SPEC = pl.BlockSpec(memory_space=pltpu.HBM)
SMEM_SPEC = pl.BlockSpec(memory_space=pltpu.SMEM)


def shaped(shape, dtype=bf16):
    return jax.ShapeDtypeStruct(shape, dtype)


def vmem_bytes(shape, dtype):
    lead, (rows, columns) = shape[:-2], shape[-2:]
    size = jnp.dtype(dtype).itemsize
    for extent in lead:
        size *= extent
    return size * -(-rows // 16) * 16 * -(-columns // 128) * 128


def call(body, name, outs, smem, args, scratch=(), flops=0, after=(), raw_args=(), raw_outs=(), extra=0):
    n_smem, n_args = len(smem), len(args)
    arrays = list(args) + list(outs)
    windows = [a for i, a in enumerate(args) if i not in raw_args] + [a for i, a in enumerate(outs) if i not in raw_outs]
    windows = sum(vmem_bytes(a.shape, a.dtype) for a in windows)
    held = sum(vmem_bytes(a.shape, a.dtype) for a in scratch if getattr(a, "memory_space", None) == pltpu.VMEM)
    held += VMEM_SPARE + extra + (windows if windows > VMEM_WINDOWS else 0)

    def kernel(*refs):
        first = n_smem + n_args
        body(*refs[:first], *refs[first + len(after):])

    return pl.pallas_call(
        kernel,
        out_shape=tuple(pltpu.HBM(a.shape, a.dtype) if i in raw_outs else a for i, a in enumerate(outs)),
        in_specs=[SMEM_SPEC] * n_smem
        + [HBM_SPEC if i in raw_args else VMEM_SPEC for i in range(n_args)] + [ANY_SPEC] * len(after),
        out_specs=tuple(HBM_SPEC if i in raw_outs else VMEM_SPEC for i in range(len(outs))),
        scratch_shapes=list(scratch),
        compiler_params=pltpu.CompilerParams(vmem_limit_bytes=min(VMEM_MOST, held)),
        cost_estimate=pl.CostEstimate(
            flops=flops, bytes_accessed=sum(a.size * a.dtype.itemsize for a in arrays), transcendentals=0
        ),
        name=name,
    )(
        *smem,
        *[pltpu.with_memory_space_constraint(a, pltpu.HBM) if i in raw_args else a for i, a in enumerate(args)],
        *after,
    )


def begin(pairs, sems):
    copies = [pltpu.make_async_copy(a, b, sems.at[i]) for i, (a, b) in enumerate(pairs)]
    for copy in copies:
        copy.start()
    return copies


def finish(copies):
    for copy in copies:
        copy.wait()


def dma(count):
    return pltpu.SemaphoreType.DMA((count,))


def dot(a, b, ca=1, cb=0):
    return lax.dot_general(a, b, (((ca,), (cb,)), ((), ())), preferred_element_type=f32)


def picks(rows, columns, start_row, start_column=0):
    r = lax.broadcasted_iota(jnp.int32, (rows, columns), 0) - start_row
    c = lax.broadcasted_iota(jnp.int32, (rows, columns), 1) - start_column
    return r, c


def one_hot(mask):
    return jnp.where(mask, 1.0, 0.0).astype(bf16)


def inverse_rms(values):
    return lax.rsqrt(jnp.mean(values * values, axis=-1, keepdims=True) + EPSILON)


def norm_back(values, gain, grad):
    inverse = inverse_rms(values)
    scaled = grad * gain
    mean = jnp.mean(scaled * values, axis=-1, keepdims=True)
    return inverse * (scaled - values * (inverse * inverse * mean))


def aligned(index, size):
    return pl.ds(pl.multiple_of(index * size, size), size)


def pack_first(weights, gains):
    size, model = weights[0].shape
    parts = len(weights)

    def body(*refs):
        gain_ref, out_ref, held, sems = refs[parts:]
        copies = begin([(refs[i], held.at[i]) for i in range(parts)], sems)
        r, c = picks(size, model, 0)
        along = dot(gain_ref[...], one_hot(r == c)).astype(bf16)
        r, c = picks(GAIN_ROWS, 2, 0)
        out_ref[parts * size:, :] = dot(one_hot(r == c), along).astype(bf16)
        finish(copies)
        for i in range(parts):
            out_ref[i * size:(i + 1) * size, :] = held[i]

    scratch = [pltpu.VMEM((parts, size, model), bf16), dma(parts)]
    outs = [shaped((parts * size + GAIN_ROWS, model))]
    return call(
        body, "pack_first", outs, [], list(weights) + [gains], scratch, raw_args=tuple(range(parts))
    )[0]


def join_dp(meta, pieces, x_links, after):
    depth = len(pieces)
    total_rows, model = pieces[0].shape
    size = (total_rows - GAIN_ROWS) // 4
    joined = size * depth
    links = len(x_links)
    lanes = 128

    def body(meta_ref, *refs):
        ins, x_refs, outs, sems = refs[:depth], refs[depth:depth + links], refs[depth + links:-1], refs[-1]
        copies = begin([(x_refs[i], outs[1].at[i]) for i in range(links)], sems)
        total = jnp.zeros((4 * joined, model), f32)
        gains = jnp.zeros((GAIN_ROWS, lanes), f32)
        for m in range(depth):
            d = meta_ref[1] ^ m
            r = lax.broadcasted_iota(jnp.int32, (4 * joined, total_rows), 0)
            c = lax.broadcasted_iota(jnp.int32, (4 * joined, total_rows), 1)
            want = jnp.where((r % joined) // size == d, (r // joined) * size + r % size, -1)
            total += dot(one_hot(c == want), ins[m][...])
            r, c = picks(lanes, lanes, 0, d * size)
            gains += dot(ins[m][4 * size:, :lanes], one_hot(jnp.logical_and(r == c, r < size)))
        outs[0][:4 * joined, :] = total.astype(bf16)
        outs[0][4 * joined:, :] = jnp.zeros((GAIN_ROWS, model), bf16)
        outs[0][4 * joined:, :lanes] = gains.astype(bf16)
        finish(copies)

    rows, width, model = x_links[0].shape
    whole = 4 * joined + GAIN_ROWS
    outs = [shaped((whole, model)), shaped((links, rows, width, model))]
    return call(
        body, "join_dp", outs, [meta], list(pieces) + list(x_links), [dma(links)], after=after,
        raw_args=tuple(range(depth, depth + links)),
    )


def forward_across(w_links, x_halves):
    total_rows, model = w_links[0].shape
    cut_at = (total_rows - GAIN_ROWS) // 2
    links = len(w_links)

    def body(*refs):
        w_refs, h_refs, outs = refs[:links], refs[links:links + 2], refs[links + 2:]
        outs[0][...] = w_refs[2][:cut_at, :]
        outs[1][...] = w_refs[1][cut_at:, :]
        for i in range(links):
            outs[2][i] = w_refs[i][:total_rows, :]
        for i in range(2):
            outs[3][i] = h_refs[i][...]

    outs = [
        shaped((cut_at, model)), shaped((total_rows - cut_at, model)), shaped((links, total_rows, model)),
        shaped((2, *x_halves[0].shape)),
    ]
    return call(body, "forward_across", outs, [], list(w_links) + list(x_halves))


def join_feed(meta, pieces, size, count, after):
    depth, total_rows, model = pieces.shape
    bands = count // GROUP
    band = (total_rows - count * size) // bands

    def body(meta_ref, in_ref, inner_ref, outer_ref, held, joined, sems):
        copies = begin([(in_ref.at[d], held.at[d]) for d in range(depth)], sems)
        for d in range(depth):
            copies[d].wait()
            for k in range(count):
                inner_ref[(k * depth + d) * size:(k * depth + d + 1) * size, :] = held[d, k * size:(k + 1) * size, :]
            for j in range(bands):
                start = count * size + j * band
                joined[j, d * band:(d + 1) * band, :] = held[d, start:start + band, :]
        for j in range(bands):
            outer_ref[aligned((meta_ref[0] // GROUP) ^ j, band * depth), :] = joined[j]

    outs = [shaped((count * depth * size, model)), shaped((bands * band * depth, model))]
    scratch = [
        pltpu.VMEM((depth, total_rows, model), bf16), pltpu.VMEM((bands, band * depth, model), bf16), dma(depth),
    ]
    return call(body, "join_feed", outs, [meta], [pieces], scratch, 0, after, (0,))


def slot_of(meta_ref, slot):
    return meta_ref[2 + 4 * slot], meta_ref[3 + 4 * slot] > 0, meta_ref[4 + 4 * slot]


def masked_cotangent(meta, own, far, after):
    rows, width, model = own.shape

    def body(meta_ref, own_ref, far_ref, out_ref):
        for slot in range(2):
            block, unused, row = slot_of(meta_ref, slot)
            length = meta_ref[5 + 4 * slot]
            position = block * width + lax.broadcasted_iota(jnp.int32, (width, model), 0)
            value = jnp.where(row == 0, own_ref[0].astype(f32), far_ref[...].astype(f32))
            out_ref[slot * width:(slot + 1) * width, :] = jnp.where(position < length, value, 0.0).astype(bf16)

    outs = [shaped((rows * width, model))]
    return call(body, "masked_cotangent", outs, [meta], [own, far], (), 0, after)[0]


def masked(tile, chunk, block, width, fill):
    rows, lanes = tile.shape
    key = chunk * CHUNK + lax.broadcasted_iota(jnp.int32, (rows, lanes), 0)
    query = block * width + lax.broadcasted_iota(jnp.int32, (rows, lanes), 1) % width
    return jnp.where(key <= query, tile, fill)


def mix_columns(vector_t, mix, out_ref, heads, heads_in, scale, by_row):
    model, width = vector_t.shape
    size = model // heads
    for i, h in enumerate(heads_in):
        for g in range(heads):
            factor = (mix[h, g] if by_row else mix[g, h]) * scale
            out_ref[g * size:(g + 1) * size, i * width:(i + 1) * width] = (
                vector_t[g * size:(g + 1) * size, :] * factor
            ).astype(bf16)


def lanes_at(index, size):
    return pl.ds(pl.multiple_of(index * size, size), size)


def over_keys(left_ref, right_ref, out_ref, used, lanes):
    for m in range(1, left_ref.shape[1] // CHUNK + 1):
        @pl.when(used == m)
        def _():
            def some(t, unused):
                part = lanes_at(t, lanes)
                out_ref[:, part] = dot(left_ref[:, :m * CHUNK], right_ref[:m * CHUNK, part])
                return 0

            lax.fori_loop(0, out_ref.shape[1] // lanes, some, 0)


def listed(pieces):
    arrays, spots = [], []
    for parts in pieces:
        spot = []
        for array, index in parts:
            known = [i for i, a in enumerate(arrays) if a is array]
            if not known:
                arrays.append(array)
            spot.append((known[0] if known else len(arrays) - 1, index))
        spots.append(spot)
    return arrays, spots


def views(refs, spot):
    return [refs[i] if index is None else refs[i].at[index] for i, index in spot]


def attend_forward(meta, premix, postmix, x_pieces, w_pieces, after):
    count = len(x_pieces)
    x_arrays, x_spots = listed(x_pieces)
    w_arrays, w_spots = listed(w_pieces)
    width, model = x_arrays[0].shape[1:]
    length = count * width
    chunks = length // CHUNK
    heads = premix.shape[0]
    size = model // heads
    pair = 2 * width
    lanes = heads * width
    half = lanes // 2
    w_rows = model // count
    mirror = count - 1

    def body(meta_ref, pre, post, *refs):
        x_refs, refs = refs[:len(x_arrays)], refs[len(x_arrays):]
        w_refs, refs = refs[:len(w_arrays)], refs[len(w_arrays):]
        joined_ref, second_ref, middle_ref, n_out, k_out, v_out, q_ref, ut_out, lse_ref, w_out, wo_out, gain_ref = refs[:12]
        qst, s_ref, acc, mx, total_out, n_ref, k_ref, v_ref, w_ref, wo_ref, ut_ref, xs, gains = refs[12:25]
        vt_ref, refs = refs[-1], refs[:-1]
        x_sems, w_sems, sems, w_sem, ut_sems = refs[25:]
        place = meta_ref[0]
        x_copies = begin([(views(x_refs, x_spots[k])[0], xs.at[k]) for k in range(count)], x_sems)
        pairs, gain_pairs = [], []
        for k in range(count):
            at, spot = 0, aligned(place ^ k, w_rows)
            for ref in views(w_refs, w_spots[k]):
                for start in range(0, ref.shape[0], w_rows):
                    if at > 4:
                        continue
                    if at < 3:
                        target = w_ref.at[spot, at * model:(at + 1) * model]
                        pairs.append((ref.at[start:start + w_rows, :], target))
                    elif at == 3:
                        pairs.append((ref.at[start:start + w_rows, :], wo_ref.at[spot, :]))
                    else:
                        gain_pairs.append((ref.at[start:start + GAIN_ROWS, :128], gains.at[k]))
                    at += 1
        w_copies = begin(gain_pairs + pairs, w_sems)
        finish(x_copies + w_copies[:count])
        gain = jnp.zeros((GAIN_ROWS, model), f32)
        for k in range(count):
            r, c = picks(128, model, 0, (place ^ k) * w_rows)
            gain += dot(gains[k], one_hot(jnp.logical_and(r == c, r < w_rows)))
        gain_ref[...] = gain[:8, :]
        out_copies = [
            pltpu.make_async_copy(w_ref, w_out, w_sem.at[0]), pltpu.make_async_copy(wo_ref, wo_out, w_sem.at[1])
        ]

        finish(w_copies[count:])
        for copy in out_copies:
            copy.start()

        def attend(slot, unused):
            block, active, row = slot_of(meta_ref, slot)
            last = block // 2
            mine = aligned(slot, width)
            ut_copies = [
                pltpu.make_async_copy(ut_ref.at[2 * slot + i], ut_out.at[2 * slot + i], ut_sems.at[2 * slot + i])
                for i in range(2)
            ]

            def leave(c):
                spot = aligned(c, CHUNK)
                pairs = ((n_ref, n_out), (k_ref, k_out), (v_ref, v_out))
                return [
                    pltpu.make_async_copy(a.at[spot, :], b.at[slot, spot, :], sems.at[i, c])
                    for i, (a, b) in enumerate(pairs)
                ]

            @pl.when(active)
            def _():
                for k in range(count):
                    @pl.when((place ^ k) // 2 <= last)
                    def _():
                        xb = xs[k, row].astype(f32)
                        n_ref[aligned(place ^ k, width), :] = (xb * inverse_rms(xb) * gain_ref[0:1, :]).astype(bf16)

            @pl.when(jnp.logical_not(active))
            def _():
                joined_ref[mine, :] = jnp.zeros((width, model), bf16)

            @pl.when(active)
            def _():
                def project(c, unused):
                    nc = n_ref[aligned(c, CHUNK), :]
                    k_ref[aligned(c, CHUNK), :] = dot(nc, w_ref[:, model:2 * model]).astype(bf16)
                    vc = dot(nc, w_ref[:, 2 * model:3 * model]).astype(bf16)
                    v_ref[aligned(c, CHUNK), :] = vc
                    vt_ref[c] = vc.T
                    for copy in leave(c):
                        copy.start()
                    return 0

                lax.fori_loop(0, last + 1, project, 0)
                query = dot(n_ref[aligned(block, width), :], w_ref[:, :model]).astype(bf16)
                q_ref[mine, :] = query
                query_t = query.astype(f32).T
                for part_of in range(2):
                    heads_in = range(part_of * heads // 2, (part_of + 1) * heads // 2)
                    mix_columns(query_t, pre, qst, heads, heads_in, 0.125, False)
                    mx[...] = jnp.full(mx.shape, NEGATIVE, f32)

                    def scores(c, unused):
                        kc = k_ref[aligned(c, CHUNK), :]
                        for t in range(half // pair):
                            part = slice(t * pair, (t + 1) * pair)
                            s = masked(dot(kc, qst[:, part]), c, block, width, NEGATIVE)
                            s_ref[aligned(c, CHUNK), part] = s
                            mx[:, part] = jnp.maximum(mx[:, part], jnp.max(s.reshape(CHUNK // 8, 8, pair), axis=0))
                        return 0

                    lax.fori_loop(0, last + 1, scores, 0)
                    peak = jnp.max(mx[...], axis=0, keepdims=True)
                    acc[...] = jnp.zeros(acc.shape, f32)
                    mx[...] = jnp.zeros(mx.shape, f32)

                    def weigh(c, unused):
                        vt = vt_ref[c]
                        for t in range(half // pair):
                            part = slice(t * pair, (t + 1) * pair)
                            p = jnp.exp(s_ref[aligned(c, CHUNK), part] - peak[:, part])
                            mx[:, part] += jnp.sum(p.reshape(CHUNK // 8, 8, pair), axis=0)
                            acc[:, part] += dot(vt, p.astype(bf16))
                        return 0

                    lax.fori_loop(0, last + 1, weigh, 0)
                    total = jnp.sum(mx[...], axis=0, keepdims=True)
                    lse_ref[slot, :, part_of * half:(part_of + 1) * half] = peak + jnp.log(total)
                    inverse = 1.0 / total
                    for k in range(heads):
                        rows = slice(k * size, (k + 1) * size)
                        out = jnp.zeros((size, width), f32)
                        for i, h in enumerate(heads_in):
                            cols = slice(i * width, (i + 1) * width)
                            u = acc[rows, cols] * inverse[:, cols]
                            ut_ref[2 * slot + part_of, rows, cols] = u.astype(bf16)
                            out += u * post[h, k]
                        if part_of == 0:
                            total_out[rows, :] = out
                        else:
                            total_out[rows, :] += out
                    ut_copies[part_of].start()
                joined_ref[mine, :] = total_out[...].T.astype(bf16)

                def gone(c, unused):
                    finish(leave(c))
                    return 0

                lax.fori_loop(0, last + 1, gone, 0)

            residual = jnp.where(row == 0, xs[0, 0].astype(f32), xs[mirror, 1].astype(f32))
            middle = residual + dot(joined_ref[mine, :], wo_ref[...])
            middle_ref[mine, :] = middle
            second_ref[mine, :] = (middle * inverse_rms(middle) * gain_ref[1:2, :]).astype(bf16)

            @pl.when(active)
            def _():
                finish(ut_copies)

            return 0

        lax.fori_loop(0, 2, attend, 0)
        finish(out_copies)

    tokens = 2 * width
    outs = [
        shaped((tokens, model)), shaped((tokens, model)), shaped((tokens, model), f32), shaped((2, length, model)),
        shaped((2, length, model)), shaped((2, length, model)), shaped((tokens, model)), shaped((4, model, half)),
        shaped((2, 1, lanes), f32), shaped((model, 3 * model)), shaped((model, model)), shaped((8, model), f32),
    ]
    scratch = [
        pltpu.VMEM((model, half), bf16), pltpu.VMEM((length, half), f32), pltpu.VMEM((model, half), f32),
        pltpu.VMEM((8, half), f32), pltpu.VMEM((model, width), f32), pltpu.VMEM((length, model), bf16),
        pltpu.VMEM((length, model), bf16), pltpu.VMEM((length, model), bf16), pltpu.VMEM((model, 3 * model), bf16),
        pltpu.VMEM((model, model), bf16), pltpu.VMEM((4, model, half), bf16),
        pltpu.VMEM((count, 2, width, model), bf16), pltpu.VMEM((count, GAIN_ROWS, 128), bf16),
        dma(count), dma(5 * count), pltpu.SemaphoreType.DMA((3, chunks)), dma(2), dma(4),
        pltpu.VMEM((chunks, model, CHUNK), bf16),
    ]
    args = x_arrays + w_arrays
    flops = 4 * length * model * (lanes + 2 * model)
    return call(
        body, "attend_forward", outs, [meta, premix, postmix], args, scratch, flops, after,
        tuple(range(len(args))), (3, 4, 5, 7, 9, 10),
    )


def feed_forward(seconds, ups, inner_w, outer_w):
    width, model = seconds[0].shape
    units = inner_w.shape[1]
    tokens = GROUP * width
    root = 0.7978845608028654
    tile = 256

    def body(*refs):
        s_refs, u_refs, (w1, w2), refs = refs[:GROUP], refs[GROUP:2 * GROUP], refs[2 * GROUP:2 * GROUP + 2], refs[2 * GROUP + 2:]
        hidden_ref, inner_ref, grads, outs, (tok, up, sems) = refs[0], refs[1], refs[2:5], refs[5:8], refs[8:]
        spots = [slice(i * width, (i + 1) * width) for i in range(GROUP)]
        pairs = [(s_refs[i], tok.at[spots[i], :]) for i in range(GROUP)]
        pairs += [(u_refs[i], up.at[spots[i], :]) for i in range(GROUP)]
        copies = begin(pairs, sems)
        finish(copies[:GROUP])
        for t in range(units // tile):
            part = slice(t * tile, (t + 1) * tile)
            v = dot(tok[...], w1[:, part])
            squared = v * v
            th = jnp.tanh(root * (v + 0.044715 * (squared * v)))
            hidden_ref[:, part] = (0.5 * v * (1.0 + th)).astype(bf16)
            slope = 0.5 * (1.0 + th) + 0.5 * v * (1.0 - th * th) * (root * (1.0 + 0.134145 * squared))
            if t == 0:
                finish(copies[GROUP:])
            inner_ref[:, part] = (dot(up[...], w2[part, :], 1, 1) * slope).astype(bf16)
        for (own_ref, give_ref, across_ref), made in (
            (grads, dot(inner_ref[...], w1[...], 1, 1)), (outs, dot(hidden_ref[...], w2[...]))
        ):
            made = made.astype(bf16)
            own_ref[...] = made[:width]
            give_ref[:width, :] = made[width:2 * width]
            give_ref[width:, :] = made[3 * width:]
            across_ref[...] = made[2 * width:3 * width]

    outs = [shaped((tokens, units)), shaped((tokens, units))]
    outs += [shaped((width, model)), shaped((2 * width, model)), shaped((width, model))] * 2
    scratch = [pltpu.VMEM((tokens, model), bf16), pltpu.VMEM((tokens, model), bf16), dma(2 * GROUP)]
    args = list(seconds) + list(ups) + [inner_w, outer_w]
    made = call(
        body, "feed_forward", outs, [], args, scratch, 8 * tokens * model * units, (), tuple(range(2 * GROUP))
    )
    return made[0], made[1], made[2:5], made[5:8]


def feed_weights(meta, seconds, ups, hidden, inner, bands, after):
    width, model = seconds[0].shape
    units = hidden.shape[1]
    tokens = GROUP * width
    rows_out = units // bands

    def body(meta_ref, *refs):
        s_refs, u_refs, (h_ref, i_ref), refs = refs[:GROUP], refs[GROUP:2 * GROUP], refs[2 * GROUP:2 * GROUP + 2], refs[2 * GROUP + 2:]
        inner_out, outer_j, (tok, up, grad, sems) = refs[0], refs[1:1 + bands], refs[1 + bands:]
        pairs = [(s_refs[i], tok.at[i * width:(i + 1) * width, :]) for i in range(GROUP)]
        pairs += [(u_refs[i], up.at[i * width:(i + 1) * width, :]) for i in range(GROUP)]
        copies = begin(pairs, sems)
        finish(copies[:GROUP])
        inner_out[...] = dot(tok[...], i_ref[...], 0, 0).astype(bf16)
        finish(copies[GROUP:])
        grad[...] = dot(h_ref[...], up[...], 0, 0).astype(bf16)
        for j in range(bands):
            outer_j[j][...] = grad[aligned((meta_ref[0] // GROUP) ^ j, rows_out), :]

    outs = [shaped((model, units))] + [shaped((rows_out, model))] * bands
    args = list(seconds) + list(ups) + [hidden, inner]
    scratch = [
        pltpu.VMEM((tokens, model), bf16), pltpu.VMEM((tokens, model), bf16), pltpu.VMEM((units, model), bf16),
        dma(2 * GROUP),
    ]
    made = call(
        body, "feed_weights", outs, [meta], args, scratch, 4 * tokens * model * units, after, tuple(range(2 * GROUP))
    )
    return made[0], list(made[1:])


def before_attention_back(own, got, came, middle, up, gains, w, joined, inner_grads, out_got, out_across, count, after):
    tokens, model = own.shape
    rows = model // count

    def body(own_ref, got_ref, came_ref, middle_ref, up_ref, gain_ref, w_in, joined_ref, inner_ref, out_got_ref, out_ref,
             grad_ref, upstream_ref, packed_ref, across_ref, w_ref, total_ref, sems):
        across_ref[...] = (out_ref[...].astype(f32) + out_got_ref[tokens:, :].astype(f32)).astype(bf16)
        copies = begin([(w_in, w_ref), (inner_ref, total_ref.at[:, rows:, :])], sems)
        second = own_ref[...].astype(f32) + got_ref[:tokens, :].astype(f32) + came_ref[...].astype(f32)
        back = norm_back(middle_ref[...], gain_ref[1:2, :], second)
        grad = up_ref[...].astype(f32) + back
        grad_ref[...] = grad
        cast = grad.astype(bf16)
        total = dot(joined_ref[...], cast, 0, 0)
        for j in range(count):
            total_ref[j, :rows, :] = total[j * rows:(j + 1) * rows, :].astype(bf16)
        copies[1].wait()
        last = pltpu.make_async_copy(total_ref, packed_ref, sems.at[2])
        last.start()
        copies[0].wait()
        upstream_ref[...] = dot(cast, w_ref[...], 1, 1).astype(bf16)
        last.wait()

    outs = [
        shaped((tokens, model), f32), shaped((tokens, model)), shaped((count, 2 * rows, model)), shaped((tokens, model)),
    ]
    args = [own, got, came, middle, up, gains, w, joined, inner_grads.reshape(count, rows, model), out_got, out_across]
    scratch = [pltpu.VMEM((model, model), bf16), pltpu.VMEM((count, 2 * rows, model), bf16), dma(3)]
    return call(
        body, "before_attention_back", outs, [], args, scratch, 4 * tokens * model * model, after, (6, 8), (2,)
    )


def attend_back(meta, premix, postmix, pre_row, post_row, query, upstream, normed, keys, values, ut, lse, count, after):
    tokens, model = query.shape
    width = tokens // 2
    length = keys.shape[1]
    heads = premix.shape[0]
    size = model // heads
    pair = 2 * width
    lanes = heads * width
    half = lanes // 2
    w_rows = model // count

    def body(meta_ref, pre, post, pre_in, post_in, q_in, up_in, lse_in, n_hbm, k_hbm, v_hbm, ut_hbm,
             dq_ref, dk_hbm, dv_hbm, mix_out, keep_ref, give_ref,
             qst, qs, ust, us, acc, pbuf, lbuf, dots, wacc, cin, cout, n_own, ut_held, in_sems, out_sems, own_sem, ut_sems,
             pre_row, post_row, q_ref, up_ref, lse_ref, arg_sems, kt_ref, nt_ref, mix_ref):
        args = begin(
            [(pre_in, pre_row), (post_in, post_row), (q_in, q_ref), (up_in, up_ref), (lse_in, lse_ref)], arg_sems
        )
        wacc[...] = jnp.zeros(wacc.shape, f32)
        mix_ref[...] = jnp.zeros(mix_ref.shape, f32)
        finish(args)

        def through(slot, unused):
            block, active, unused_row = slot_of(meta_ref, slot)
            last = block // 2
            mine = aligned(slot, width)
            ut_copies = [
                pltpu.make_async_copy(ut_hbm.at[2 * slot + i], ut_held.at[i], ut_sems.at[i]) for i in range(2)
            ]

            @pl.when(jnp.logical_not(active))
            def _():
                dq_ref[mine, :] = jnp.zeros((width, model), bf16)

            @pl.when(active)
            def _():
                def fetch(c):
                    return [
                        pltpu.make_async_copy(
                            a.at[slot, aligned(c, CHUNK), :], cin.at[c % 2, i], in_sems.at[c % 2, i]
                        )
                        for i, a in enumerate((k_hbm, v_hbm, n_hbm))
                    ]

                def leave(c):
                    return [
                        pltpu.make_async_copy(
                            cout.at[c % 2, i], a.at[slot, aligned(c, CHUNK), :], out_sems.at[c % 2, i]
                        )
                        for i, a in enumerate((dk_hbm, dv_hbm))
                    ]

                own = pltpu.make_async_copy(n_hbm.at[slot, aligned(block, width), :], n_own, own_sem)
                own.start()
                for copy in ut_copies + fetch(0):
                    copy.start()
                q = q_ref[mine, :].astype(f32)
                up = up_ref[mine, :].astype(f32)
                qt, upt = q.T, up.T
                mix_columns(qt, pre, qst, heads, range(heads), 0.125, False)
                mix_columns(upt, post, ust, heads, range(heads), 1.0, True)
                for h in range(heads):
                    spot = slice(h * width, (h + 1) * width)
                    qs[spot, :] = (q * (pre_row[h:h + 1, :] * 0.125)).astype(bf16)
                    us[spot, :] = (up * post_row[h:h + 1, :]).astype(bf16)
                finish(ut_copies)
                for h in range(heads):
                    spot = slice(h * width, (h + 1) * width)
                    column = h % (heads // 2) * width
                    u = ut_held[h // (heads // 2), :, column:column + width].astype(f32)
                    t = jnp.sum((u * upt).reshape(heads, size, width), axis=1)
                    mix_ref[(heads + h) * heads:(heads + h + 1) * heads, :] += t
                    d = jnp.zeros((1, width), f32)
                    for k in range(heads):
                        d += t[k:k + 1, :] * post[h, k]
                    dots[:, spot] = d

                def visit(c, unused):
                    finish(fetch(c))

                    @pl.when(c < last)
                    def _():
                        for copy in fetch(c + 1):
                            copy.start()

                    kc, vc = cin[c % 2, 0], cin[c % 2, 1]
                    kt_ref[:, lanes_at(c, CHUNK)] = kc.T
                    nt_ref[...] = cin[c % 2, 2].T
                    for t in range(heads // 2):
                        part = slice(t * pair, (t + 1) * pair)
                        p = masked(jnp.exp(dot(kc, qst[:, part]) - lse_ref[slot, :, part]), c, block, width, 0.0)
                        grad = (p * (dot(vc, ust[:, part]) - dots[:, part])).astype(bf16)
                        pbuf[:, part] = p.astype(bf16)
                        lbuf[aligned(c, CHUNK), part] = grad

                    @pl.when(c >= 2)
                    def _():
                        finish(leave(c - 2))

                    dk = dot(lbuf[aligned(c, CHUNK), :], qs[...]).astype(bf16)
                    dv = dot(pbuf[...], us[...]).astype(bf16)
                    cout[c % 2, 0] = dk
                    cout[c % 2, 1] = dv
                    for copy in leave(c):
                        copy.start()
                    wacc[:, model:2 * model] += dot(nt_ref[...], dk)
                    wacc[:, 2 * model:] += dot(nt_ref[...], dv)
                    return 0

                lax.fori_loop(0, last + 1, visit, 0)
                over_keys(kt_ref, lbuf, acc, last + 1, pair)
                for g in range(heads):
                    rows = slice(g * size, (g + 1) * size)
                    out = jnp.zeros((size, width), f32)
                    qg = qt[rows, :] * 0.125
                    for h in range(heads):
                        a = acc[rows, h * width:(h + 1) * width]
                        out += a * pre[g, h]
                        mix_ref[g * heads + h:g * heads + h + 1, :] += jnp.sum(a * qg, axis=0, keepdims=True)
                    acc[rows, 0:width] = out * 0.125
                dq = acc[:, 0:width].T.astype(bf16)
                dq_ref[mine, :] = dq
                own.wait()
                wacc[:, :model] += dot(n_own[...], dq, 0, 0)

                @pl.when(last >= 1)
                def _():
                    finish(leave(last - 1))

                finish(leave(last))

            return 0

        lax.fori_loop(0, 2, through, 0)
        every = jnp.sum(mix_ref[...], axis=1, keepdims=True)
        r = lax.broadcasted_iota(jnp.int32, mix_ref.shape, 0)
        c = lax.broadcasted_iota(jnp.int32, mix_ref.shape, 1)
        every = jnp.where(r % 128 == c, every, 0.0)
        mix_out[...] = jnp.zeros(mix_out.shape, f32)
        for i in range(-(-mix_ref.shape[0] // 128)):
            mix_out[i:i + 1, :] = jnp.sum(every[i * 128:(i + 1) * 128, :], axis=0, keepdims=True)
        for k in range(count):
            (keep_ref, give_ref)[k % 2][k // 2 * w_rows:(k // 2 + 1) * w_rows, :] = wacc[
                aligned(meta_ref[0] ^ k, w_rows), :
            ].astype(bf16)

    outs = [
        shaped((tokens, model)), shaped((2, length, model)), shaped((2, length, model)),
        shaped((8, 128), f32), shaped((count // 2 * w_rows, 3 * model)),
        shaped((count // 2 * w_rows, 3 * model)),
    ]
    scratch = [
        pltpu.VMEM((model, lanes), bf16), pltpu.VMEM((lanes, model), bf16), pltpu.VMEM((model, lanes), bf16),
        pltpu.VMEM((lanes, model), bf16), pltpu.VMEM((model, lanes), f32), pltpu.VMEM((CHUNK, lanes), bf16),
        pltpu.VMEM((length, lanes), bf16), pltpu.VMEM((1, lanes), f32), pltpu.VMEM((model, 3 * model), f32),
        pltpu.VMEM((2, 3, CHUNK, model), bf16), pltpu.VMEM((2, 2, CHUNK, model), bf16), pltpu.VMEM((width, model), bf16),
        pltpu.VMEM((2, model, half), bf16), pltpu.SemaphoreType.DMA((2, 3)), pltpu.SemaphoreType.DMA((2, 2)),
        pltpu.SemaphoreType.DMA, dma(2), pltpu.VMEM((heads, model), f32), pltpu.VMEM((heads, model), f32),
        pltpu.VMEM((tokens, model), bf16), pltpu.VMEM((tokens, model), bf16), pltpu.VMEM((2, 1, lanes), f32), dma(5),
        pltpu.VMEM((model, length), bf16), pltpu.VMEM((model, CHUNK), bf16),
        pltpu.VMEM((2 * heads * heads, width), f32),
    ]
    args = [pre_row, post_row, query, upstream, lse, normed, keys, values, ut]
    return call(
        body, "attend_back", outs, [meta, premix, postmix], args, scratch, 15 * length * model * lanes, after,
        tuple(range(9)), (1, 2),
    )


def input_back(meta, dq, dk, dv, w, x_pieces, gains, grad, after):
    count = len(x_pieces)
    x_arrays, x_spots = listed(x_pieces)
    width, model = x_arrays[0].shape[1:]
    length = dk.shape[1]
    chunks = length // CHUNK

    def body(meta_ref, dq_in, grad_in, gain_in, dk_hbm, dv_hbm, w_hbm, *refs):
        x_refs, refs = refs[:len(x_arrays)], refs[len(x_arrays):]
        keep_ref, give_ref, normed, dk_held, dv_held, w_ref, xs, sems, w_sem, x_sems = refs[:10]
        dq_ref, grad_ref, gain_ref, arg_sems, wt_ref = refs[10:]
        arg_copies = begin([(dq_in, dq_ref), (grad_in, grad_ref), (gain_in, gain_ref)], arg_sems)
        place = meta_ref[0]
        w_copy = pltpu.make_async_copy(w_hbm, w_ref, w_sem)
        w_copy.start()

        def fetch(slot, c):
            spot = aligned(c, CHUNK)
            return [
                pltpu.make_async_copy(a.at[slot, spot, :], b.at[slot, spot, :], sems.at[slot, c, i])
                for i, (a, b) in enumerate(((dk_hbm, dk_held), (dv_hbm, dv_held)))
            ]

        def start(slot, c):
            for copy in fetch(slot, c):
                copy.start()
            return 0

        for slot in range(2):
            block, active, row = slot_of(meta_ref, slot)
            needed = jnp.where(active, block // 2 + 1, 0)
            lax.fori_loop(0, needed, lambda c, unused, slot=slot: start(slot, c), 0)
        x_copies = begin([(views(x_refs, x_spots[k])[0], xs.at[k]) for k in range(count)], x_sems)
        w_copy.wait()
        for i in range(3):
            wt_ref[i] = w_ref[:, i * model:(i + 1) * model].T
        finish(arg_copies)

        def through(slot, unused):
            block, active, row = slot_of(meta_ref, slot)
            mine = aligned(slot, width)

            @pl.when(active)
            def _():
                def visit(c, unused):
                    spot = aligned(c, CHUNK)
                    finish(fetch(slot, c))
                    normed[spot, :] = dot(dk_held[slot, spot, :], wt_ref[1]) + dot(dv_held[slot, spot, :], wt_ref[2])
                    return 0

                lax.fori_loop(0, block // 2 + 1, visit, 0)
                normed[aligned(block, width), :] += dot(dq_ref[mine, :], wt_ref[0])

            @pl.when(slot == 0)
            def _():
                finish(x_copies)

            def chip(i, unused):
                for k, out_ref in enumerate((keep_ref, give_ref)):
                    source = place ^ (2 * i + k)
                    spot = aligned(2 * i + row, width)
                    used = jnp.logical_and(active, source <= block)

                    @pl.when(jnp.logical_not(used))
                    def _():
                        out_ref[spot, :] = jnp.zeros((width, model), bf16)

                    @pl.when(used)
                    def _():
                        back = norm_back(
                            xs[2 * i + k, row].astype(f32), gain_ref[0:1, :], normed[aligned(source, width), :]
                        )
                        factor = jnp.where(source == block, 1.0, 0.0)
                        out_ref[spot, :] = (back + grad_ref[mine, :] * factor).astype(bf16)
                return 0

            lax.fori_loop(0, count // 2, chip, 0)
            return 0

        lax.fori_loop(0, 2, through, 0)

    half = count * width
    outs = [shaped((half, model)), shaped((half, model))]
    args = [dq, grad, gains, dk, dv, w] + x_arrays
    scratch = [
        pltpu.VMEM((length, model), f32), pltpu.VMEM((2, length, model), bf16), pltpu.VMEM((2, length, model), bf16),
        pltpu.VMEM((model, 3 * model), bf16), pltpu.VMEM((count, 2, width, model), bf16),
        pltpu.SemaphoreType.DMA((2, chunks, 2)), pltpu.SemaphoreType.DMA, dma(count),
        pltpu.VMEM(dq.shape, bf16), pltpu.VMEM(grad.shape, f32), pltpu.VMEM(gains.shape, f32), dma(3),
        pltpu.VMEM((3, model, model), bf16),
    ]
    return call(
        body, "input_back", outs, [meta], args, scratch, 8 * length * model * model, after,
        tuple(range(len(args))),
    )


def pair_sums(keep, got, count, later, after, name):
    blocks = count // 2
    rows, columns = keep.shape[0] // blocks, keep.shape[1]

    def body(keep_ref, got_ref, *refs):
        outs = refs[len(later):]
        for source, target in zip(refs, outs[blocks:]):
            target[...] = source[...]
        for i in range(blocks):
            spot = slice(i * rows, (i + 1) * rows)
            outs[i][...] = (keep_ref[spot, :].astype(f32) + got_ref[spot, :].astype(f32)).astype(outs[i].dtype)

    outs = [shaped((rows, columns))] * blocks
    outs += [shaped(a.shape, a.dtype) for a in later]
    made = call(body, name, outs, [], [keep, got] + list(later), (), 0, after)
    return made[:blocks], made[blocks:]


def halves_first(keep, got, pair, after, name):
    rows, columns = keep.shape[0] // 4, keep.shape[1]
    half = rows // 2

    def body(keep_ref, got_ref, *refs):
        if pair:
            refs[-1][...] = refs[0][...] + refs[1][...]
        two_ref, four_ref, rest_ref = refs[len(pair):len(pair) + 3]

        def part(i, b):
            spot = slice(i * rows + b * half, i * rows + (b + 1) * half)
            return keep_ref[spot, :].astype(f32) + got_ref[spot, :].astype(f32)

        for n, (i, b) in enumerate(((1, 0), (3, 0))):
            two_ref[n * half:(n + 1) * half, :] = part(i, b).astype(bf16)
        for n, (i, b) in enumerate(((2, 1), (3, 1))):
            four_ref[n * half:(n + 1) * half, :] = part(i, b).astype(bf16)
        for n, (i, b) in enumerate(((0, 0), (2, 0), (0, 1), (1, 1))):
            rest_ref[n * half:(n + 1) * half, :] = part(i, b)

    outs = [
        shaped((rows, columns)), shaped((rows, columns)), shaped((2 * rows, columns), f32),
    ] + [shaped(a.shape, f32) for a in pair[:1]]
    return call(body, name, outs, [], [keep, got, *pair], (), 0, after)


def halves_second(rest, from_two, from_four, pair, after, name):
    rows, columns = from_two.shape
    half = rows // 2

    def body(rest_ref, two_in, four_in, one, other, two_ref, four_ref, own_ref, sum_ref):
        sum_ref[...] = one[...] + other[...]
        own_ref[:half, :] = rest_ref[:half, :] + two_in[:half, :].astype(f32)
        four_ref[...] = (rest_ref[half:rows, :] + two_in[half:, :].astype(f32)).astype(bf16)
        own_ref[half:, :] = rest_ref[rows:rows + half, :] + four_in[:half, :].astype(f32)
        two_ref[...] = (rest_ref[rows + half:, :] + four_in[half:, :].astype(f32)).astype(bf16)

    outs = [
        shaped((half, columns)), shaped((half, columns)), shaped((rows, columns), f32), shaped(pair[0].shape, f32),
    ]
    return call(body, name, outs, [], [rest, from_two, from_four, *pair], (), 0, after)


def input_sum(own, from_four, from_two, shape):
    rows, width, model = shape

    def body(own_ref, four_ref, two_ref, out_ref):
        out_ref[0] = (own_ref[:width, :] + four_ref[...].astype(f32)).astype(bf16)
        out_ref[1] = (own_ref[width:, :] + two_ref[...].astype(f32)).astype(bf16)

    return call(body, "input_sum", [shaped(shape)], [], [own, from_four, from_two])[0]


def split_dp(meta, depth, parts, pair, after):
    joined, wide = parts[0].shape
    size = joined // depth
    halved = parts[1].shape[0] != joined

    def body(meta_ref, *refs):
        ins, (one, other), outs, sum_ref = refs[:len(parts)], refs[len(parts):len(parts) + 2], refs[len(parts) + 2:-2], refs[-2]
        total_ref = refs[-1]
        sum_ref[...] = one[...] + other[...]
        if halved:
            for i in range(2):
                spot = slice(i * joined // 2, (i + 1) * joined // 2)
                total_ref[spot, :] = (ins[0][spot, :] + ins[1 + i][...].astype(f32)).astype(bf16)
        else:
            total = ins[0][...].astype(f32)
            for ref in ins[1:]:
                total += ref[...].astype(f32)
            total_ref[...] = total.astype(bf16)
        for m in range(depth):
            r, c = picks(size, joined, 0, (meta_ref[1] ^ m) * size)
            outs[m][...] = dot(one_hot(r == c), total_ref[...]).astype(bf16)

    outs = [shaped((size, wide))] * depth + [shaped(pair[0].shape, f32)]
    scratch = [pltpu.VMEM((joined, wide), bf16)]
    made = call(body, "split_dp", outs, [meta], list(parts) + list(pair), scratch, 0, after)
    return made[:depth], made[depth]


def split_feed(meta, depth, grads, outer, size, middle, parts_out):
    count, joined, units = grads.shape
    joined //= 2
    bands = len(outer)
    band = outer[0].shape[0]
    shard = band // depth
    parts = 1 + GROUP
    out_rows = parts * size + shard
    tokens = middle.shape[0]
    width = tokens // 2

    def body(meta_ref, grad_in, *refs):
        o_ins, out_ins, refs = refs[:bands], refs[bands:bands + 4], refs[bands + 4:]
        outs, (total, grad_ref, outer_ref, middle_ref, part_ref, sems) = refs[:3], refs[3:]
        o_refs = [outer_ref.at[j] for j in range(bands)]
        pairs = [(out_ins[0], middle_ref)] + [(out_ins[1 + i].at[:tokens, :], part_ref.at[i]) for i in range(3)]
        copies = begin(pairs + [(grad_in, grad_ref)] + [(o_ins[j], o_refs[j]) for j in range(bands)], sems)
        finish(copies[:4])
        for slot in range(2):
            block, unused, row = slot_of(meta_ref, slot)
            spot = slice(slot * width, (slot + 1) * width)
            position = block * width + lax.broadcasted_iota(jnp.int32, (width, units), 0)
            value = middle_ref[spot, :]
            for i in range(3):
                value += part_ref[i, spot, :].astype(f32)
            value = jnp.where(position < meta_ref[5 + 4 * slot], value, 0.0).astype(bf16)
            for n in range(2):
                @pl.when(row == n)
                def _():
                    outs[1 + n][...] = value

        finish(copies[4:])
        section = grad_ref[0, :joined, :].astype(f32)
        for j in range(1, count):
            section += grad_ref[j, :joined, :].astype(f32)
        total[:joined, :] = section.astype(bf16)
        for t in range(GROUP):
            section = grad_ref[t, joined:, :].astype(f32)
            for j in range(1, bands):
                section += grad_ref[j * GROUP + t, joined:, :].astype(f32)
            total[(1 + t) * joined:(2 + t) * joined, :] = section.astype(bf16)
        rest = o_refs[0][...].astype(f32)
        for j in range(1, bands):
            rest += o_refs[j][...].astype(f32)
        total[parts * joined:, :] = rest.astype(bf16)
        for d in range(depth):
            for t in range(parts):
                outs[0][d, t * size:(t + 1) * size, :] = total[t * joined + d * size:t * joined + (d + 1) * size, :]
            start = parts * joined + d * shard
            outs[0][d, parts * size:, :] = total[start:start + shard, :]

    scratch = [
        pltpu.VMEM((parts * joined + band, units), bf16), pltpu.VMEM(grads.shape, bf16),
        pltpu.VMEM((bands, band, units), bf16), pltpu.VMEM((tokens, units), f32), pltpu.VMEM((3, tokens, units), bf16),
        dma(5 + bands),
    ]
    args = [grads] + list(outer) + [middle] + list(parts_out)
    outs = [shaped((depth, out_rows, units)), shaped((width, units)), shaped((width, units))]
    return call(body, "split_feed", outs, [meta], args, scratch, 0, (), tuple(range(len(args))))


def finish_projections(pieces, weights):
    size, wide = pieces[0].shape
    parts = 3
    model = wide // parts

    def body(*refs):
        ins, w_ins, outs = refs[:len(pieces)], refs[len(pieces):-6], refs[-6:-2]
        w_held, sems = refs[-2:]
        w_refs = [w_held.at[i] for i in range(parts)]
        finish(begin([(w_ins[i], w_refs[i]) for i in range(parts)], sems))
        along = jnp.zeros((size, 1), f32)
        for i in range(parts):
            part = slice(i * model, (i + 1) * model)
            total = ins[0][:, part].astype(f32)
            for ref in ins[1:]:
                total += ref[:, part].astype(f32)
            outs[i][...] = total
            along += jnp.sum(total * w_refs[i][...].astype(f32), axis=1, keepdims=True)
        outs[3][...] = along

    outs = [shaped((size, model), f32)] * parts + [shaped((size, 1), f32)]
    scratch = [pltpu.VMEM((parts, size, model), bf16), dma(parts)]
    args = list(pieces) + list(weights)
    return call(
        body, "finish_projections", outs, [], args, scratch, raw_args=tuple(range(len(pieces), len(args)))
    )


def finish_feed(pieces, weight, bands):
    size = weight.shape[0]
    depth, rows, units = pieces.shape
    band = units // bands

    def body(in_hbm, w_in, output_ref, inner_ref, outer_ref, along_ref, in_ref, w_ref, sems):
        finish(begin([(in_hbm, in_ref), (w_in, w_ref)], sems))
        total = in_ref[0].astype(f32)
        for d in range(1, depth):
            total += in_ref[d].astype(f32)
        output_ref[...] = total[:size, :]
        for t in range(GROUP):
            for y in range(bands):
                inner_ref[:, (y * GROUP + t) * band:(y * GROUP + t + 1) * band] = total[
                    (1 + t) * size:(2 + t) * size, y * band:(y + 1) * band
                ]
        outer_ref[...] = total[(1 + GROUP) * size:, :]
        along_ref[...] = jnp.sum(inner_ref[...] * w_ref[...].astype(f32), axis=1, keepdims=True)

    outs = [
        shaped((size, units), f32), shaped((size, GROUP * units), f32),
        shaped((rows - (1 + GROUP) * size, units), f32), shaped((size, 1), f32),
    ]
    scratch = [pltpu.VMEM(pieces.shape, bf16), pltpu.VMEM(weight.shape, bf16), dma(2)]
    return call(body, "finish_feed", outs, [], [pieces, weight], scratch, raw_args=(0, 1))


def swap(value, axis, mask):
    count = lax.axis_size(axis)
    return lax.ppermute(value, axis, [(i, i ^ mask) for i in range(count)])


def gather_dp(value):
    return [value] + [swap(value, "dp", m) for m in range(1, lax.axis_size("dp"))]


def gather_first(meta, inputs, first_w, inner, outer, after):
    count, depth = lax.axis_size("blk"), lax.axis_size("dp")
    pieces = gather_dp(first_w)
    x_links = [inputs, swap(inputs, "blk", 2), swap(inputs, "blk", 4)]
    shards = [outer] + [swap(outer, "blk", GROUP * j) for j in range(1, count // GROUP)]
    halves = [swap(x_links[2][0], "blk", 2), swap(x_links[1][1], "blk", 4)] if count == 8 else []
    w_own, x_core = join_dp(meta, pieces, x_links, after + shards[1:] + halves)
    feed = jnp.concatenate([inner] + shards, axis=0)
    if count == 8:
        w_links = [w_own, swap(w_own, "blk", 2), swap(w_own, "blk", 4)]
        x_core = swap(x_core, "blk", 1)
        w_on_two, w_on_four, w_core, x_across = forward_across(w_links, halves)
        w_across = [swap(w_on_two, "blk", 2), swap(w_on_four, "blk", 4)]
        w_core, x_far = swap(w_core, "blk", 1), swap(x_across, "blk", 1)
        w_far = [swap(part, "blk", 1) for part in w_across]
        xs = [[(a, None)] for a in x_links] + [[(x_across, None)]]
        ws = [[(a, None)] for a in w_links] + [[(a, None) for a in w_across]]
        xs_core = [[(x_core, i)] for i in range(3)] + [[(x_far, None)]]
        ws_core = [[(w_core, i)] for i in range(3)] + [[(a, None) for a in w_far]]
    else:
        x_links += [swap(inputs, "blk", k) for k in range(6, count, 2)]
        w_links = [w_own, swap(w_own, "blk", 2), swap(w_own, "blk", 4)]
        w_links += [swap(w_own, "blk", k) for k in range(6, count, 2)]
        xs, ws = [[(a, None)] for a in x_links], [[(a, None)] for a in w_links]
        xs_core, ws_core = [[(swap(a, "blk", 1), None)] for a in x_links], [[(swap(a, "blk", 1), None)] for a in w_links]
    x_pieces = [part for pair in zip(xs, xs_core) for part in pair]
    w_pieces = [part for pair in zip(ws, ws_core) for part in pair]
    return x_pieces, w_pieces, feed


def all_to_all(value, axis):
    return lax.all_to_all(value, axis, 0, 0, tiled=True)


def gather_group(value):
    two = swap(value, "blk", 2)
    return [value, swap(value, "blk", 1), two, swap(two, "blk", 1)]


def scatter_chips(parts):
    return [parts[0]] + [swap(part, "blk", 2 * i) for i, part in enumerate(parts) if i]


def on_device(
    inputs, lengths, prenorm, midnorm, query_proj, key_proj, value_proj, output_proj,
    premix, postmix, inner_proj, outer_proj, cotangent,
):
    count, depth = lax.axis_size("blk"), lax.axis_size("dp")
    place, zplace = lax.axis_index("blk"), lax.axis_index("dp")
    rows, width, model = inputs.shape
    shard = prenorm.shape[0]
    low = place < count // 2
    mirror = count - 1
    slot_rows = [jnp.where(low, 1, 0), jnp.where(low, 0, 1)]
    blocks = [jnp.maximum(place, place ^ mirror), jnp.minimum(place, place ^ mirror)]
    spans = [jnp.where(slot_rows[i] == 0, lengths[0], lengths[1]) for i in range(2)]
    meta = [place, zplace]
    for i in range(2):
        meta += [blocks[i], (blocks[i] * width < spans[i]).astype(jnp.int32), slot_rows[i], spans[i]]
    meta = jnp.stack(meta).astype(jnp.int32)

    head_size = model // premix.shape[0]
    pre_row = jnp.repeat(premix.T, head_size, axis=1)
    post_row = jnp.repeat(postmix, head_size, axis=1)
    bands = count // GROUP
    band_ff = depth * outer_proj.shape[0]
    first_w = pack_first([query_proj, key_proj, value_proj, output_proj], jnp.stack([prenorm, midnorm]))
    sections = inner_proj.reshape(shard, bands, GROUP, band_ff).transpose(2, 0, 1, 3).reshape(GROUP, shard, -1)
    sections = all_to_all(jnp.concatenate([sections] * bands), "blk").reshape(count * shard, -1)
    far_cotangent = swap(cotangent[1], "blk", mirror)
    x_pieces, w_pieces, second_w = gather_first(meta, inputs, first_w, sections, outer_proj, [sections])
    second_w = all_to_all(jnp.broadcast_to(second_w, (depth, *second_w.shape)), "dp")
    up = masked_cotangent(meta, cotangent, far_cotangent, [w_pieces[count - 2][0][0]])
    ups = gather_group(up)

    joined, second, middle, normed, keys, values, query, ut, lse, w, output_w, gain_rows = attend_forward(
        meta, premix, postmix, x_pieces, w_pieces, [up, pre_row, post_row]
    )
    seconds = gather_group(second)
    inner_w, outer_w = join_feed(meta, second_w, shard, count, [second, ups[2]])
    hidden, inner, (own, give, across), (out_own, out_give, out_across) = feed_forward(
        seconds, ups, inner_w, outer_w
    )
    got = swap(give, "blk", 1)
    tokens = rows * width
    across = (across.astype(f32) + got[tokens:].astype(f32)).astype(bf16)
    came = swap(across, "blk", 2)
    out_got = swap(out_give, "blk", 1)
    inner_grads, outer_grads = feed_weights(meta, seconds, ups, hidden, inner, bands, [across])

    grad, upstream, packed, out_across = before_attention_back(
        own, got, came, middle, up, gain_rows, output_w, joined, inner_grads, out_got, out_across, count, []
    )
    feed_grads = all_to_all(packed, "blk")
    outer_grads = [outer_grads[0]] + [swap(outer_grads[j], "blk", GROUP * j) for j in range(1, bands)]
    out_came = swap(out_across, "blk", 2)
    dq, dk, dv, mixes, keep, give = attend_back(
        meta, premix, postmix, pre_row, post_row, query, upstream, normed, keys, values, ut, lse, count, []
    )
    heads = premix.shape[0]
    cuts, near, far = split_feed(
        meta, depth, feed_grads, outer_grads, shard, middle, [out_own, out_got, out_came]
    )
    outputs = jnp.stack([near, swap(far, "blk", mirror)])
    input_keep, input_give = input_back(meta, dq, dk, dv, w, x_pieces, gain_rows, grad, [cuts])
    feed_sums = all_to_all(cuts, "dp")
    give, input_give = swap(give, "blk", 1), swap(input_give, "blk", 1)
    steps = [("blk", 1 << i) for i in range(count.bit_length() - 1)] + [("dp", 1 << i) for i in range(depth.bit_length() - 1)]

    def step(value):
        return value, swap(value, *steps.pop(0))

    if count == 8:
        two, four, rest = halves_first(keep, give, (), [input_keep], "halves_first_w")
        two, four = swap(two, "blk", 2), swap(four, "blk", 4)
        x_two, x_four, x_rest, mixes = halves_first(input_keep, input_give, step(mixes), [rest], "halves_first_x")
        x_two, x_four = swap(x_two, "blk", 2), swap(x_four, "blk", 4)
        two, four, rest, mixes = halves_second(rest, two, four, step(mixes), [x_rest], "halves_second_w")
        two, four = swap(two, "blk", 2), swap(four, "blk", 4)
        x_two, x_four, x_rest, mixes = halves_second(x_rest, x_two, x_four, step(mixes), [rest], "halves_second_x")
        x_two, x_four = swap(x_two, "blk", 2), swap(x_four, "blk", 4)
        cuts_w, mixes = split_dp(meta, depth, [rest, four, two], step(mixes), [x_rest])
        grad_inputs = input_sum(x_rest, x_four, x_two, inputs.shape)
    else:
        projected, unused = pair_sums(keep, give, count, [], [input_keep], "pair_sums_w")
        cuts_w, mixes = split_dp(meta, depth, scatter_chips(projected), step(mixes), [])
        parts, unused = pair_sums(input_keep, input_give, count, [], [], "pair_sums_x")
        grad_inputs = sum([part.astype(f32) for part in scatter_chips(parts)]).astype(bf16).reshape(inputs.shape)
    while steps:
        mixes = sum(step(mixes))
    mixes = mixes.reshape(-1)[:2 * heads * heads].reshape(2, heads, heads)
    output_sum, inner_sum, outer_sum, mid_gain = finish_feed(
        feed_sums, inner_proj, bands
    )
    cuts = cuts_w
    query_sum, key_sum, value_sum, pre_gain = finish_projections(
        [cuts[0]] + [swap(cuts[m], "dp", m) for m in range(1, depth)],
        [query_proj, key_proj, value_proj],
    )
    return (
        outputs,
        grad_inputs,
        pre_gain.reshape(-1) / prenorm.astype(f32),
        mid_gain.reshape(-1) / midnorm.astype(f32),
        query_sum,
        key_sum,
        value_sum,
        output_sum,
        mixes[0],
        mixes[1],
        inner_sum,
        outer_sum,
    )


def solution(mesh):
    weight = P(("blk", "dp"), None)
    vector = P(("blk", "dp"))
    tokens = P("dp", "blk", None)
    in_specs = (
        tokens, P("dp"), vector, vector, weight, weight, weight, weight, P(), P(), weight, weight, tokens,
    )
    out_specs = (
        tokens, tokens, vector, vector, weight, weight, weight, weight, P(), P(), weight, weight,
    )
    return jax.shard_map(on_device, mesh=mesh, in_specs=in_specs, out_specs=out_specs, check_vma=False)
```
